32 devices in a mesh: grp: 2 (over x), dev: 16 (over z, y, core).
Axes of the slice: x: 2, y: 2, z: 4, core: 2. Of those that a mesh axis runs over, the one named last changes fastest.
Arguments:
- embeddings: bfloat16 [16384, 768], P(('grp', 'dev')), parts along dimension 0, as said below
- position: int32 [16384], P(('grp', 'dev')), parts along dimension 0, may hold values from 0 to 8191, as said below
- cluster_ids: int32 [16384], P(('grp', 'dev')), parts along dimension 0, may hold values from 0 to 8191, as said below
Outputs:
- weight: float32 [16384], P(('grp', 'dev')), parts along dimension 0
The draws below stay inside these ranges and needn't reach their ends.
There are 2 independent parts, one for each index of `grp`. The reference program is written for one: setup_inputs(seed, part) draws one part's arguments, and reference() takes and returns one part's arrays. A program takes and returns all parts, laid end to end along the dimension named above; each array names one. Nothing has to cross between parts.
Inputs may be any that keep to these rules, and one draw needn't show every extreme that they name: `position`: a permutation; the 512 documents of every device take exactly 32 positions in the range of positions of every device. `cluster_ids`: never falling along positions; each cluster holds 1 to 2048 consecutive positions, and one holds exactly 2048; the cluster at the first position is numbered 0, the cluster at the last position 8191, and each other cluster one more than the cluster before it. `embeddings`: rows are not normalized.
All inputs are finite; a program needn't handle non-finite values.
Results may differ from the reference program's by a relative error of at most 0.0003.
Values may be sent and summed in bfloat16 or wider, within the bound.
No kernel may reach another device: no remote copies, remote signals or barrier semaphores. Data moves between devices by JAX's collectives and lax.ppermute only.
A program may use at most 64 MiB of HBM per device.

```python
import math
import jax
import jax.numpy as jnp
from jax import lax

D = 768
BLOCK = 256
DOC_DEV = 512
MOST = 2048
DOC = 8192
N_DEV = 16


def cluster_layout(key):
    layout_key = jax.random.fold_in(key, 101)
    ratio_key, giant_key = jax.random.split(layout_key)
    ratios = jax.random.randint(ratio_key, (DOC,), 1, 65)
    cluster_sizes = jnp.maximum(MOST // ratios, 1)
    giant_index = jax.random.randint(giant_key, (), 0, 2)
    cluster_sizes = jnp.where(jnp.arange(DOC) == giant_index, MOST, cluster_sizes)
    cluster_ends = jnp.cumsum(cluster_sizes)
    raw_ids = jnp.searchsorted(cluster_ends, jnp.arange(DOC), side='right').astype(jnp.int32)
    return jnp.where(raw_ids == raw_ids[DOC - 1], DOC - 1, raw_ids).astype(jnp.int32)


def placement(key):
    place_key = jax.random.fold_in(key, 202)
    source_key, slot_key = jax.random.split(place_key)
    per_peer = DOC_DEV // N_DEV
    source_perm = jax.vmap(lambda subkey: jax.random.permutation(subkey, DOC_DEV))(jax.random.split(source_key, N_DEV))
    slot_perm = jax.vmap(lambda subkey: jax.random.permutation(subkey, DOC_DEV))(jax.random.split(slot_key, N_DEV))
    rank_values = jnp.arange(DOC_DEV, dtype=jnp.int32)
    slot_rank = jax.vmap(lambda shuffled: jnp.zeros((DOC_DEV,), jnp.int32).at[shuffled].set(rank_values))(slot_perm)
    source_ids = jnp.arange(N_DEV)[:, None, None]
    target_ids = jnp.arange(N_DEV)[None, :, None]
    member = jnp.arange(per_peer)[None, None, :]
    local_doc = source_perm[source_ids, target_ids * per_peer + member]
    slot_index = slot_rank[target_ids, source_ids * per_peer + member]
    documents = (source_ids * DOC_DEV + local_doc).reshape(-1)
    document_positions = (target_ids * DOC_DEV + slot_index).reshape(-1).astype(jnp.int32)
    return jnp.zeros((DOC,), jnp.int32).at[documents].set(document_positions)


def draw_embeddings(key, part):
    own_key = jax.random.fold_in(key, 7)
    labels = cluster_layout(key)
    position = placement(key)
    center_key, jitter_key, spread_key = jax.random.split(own_key, 3)
    doc_cluster = labels[position]
    centers = jax.vmap(lambda cluster: jax.random.normal(jax.random.fold_in(center_key, cluster), (D,), jnp.float32))(doc_cluster)
    jitter = jax.random.normal(jitter_key, (DOC, D), jnp.float32)
    spread = jnp.exp(jax.random.uniform(spread_key, (DOC, 1), jnp.float32, math.log(0.25), math.log(0.9)))
    return (centers + spread * jitter).astype(jnp.bfloat16)


def draw_position(key, part):
    return placement(key)


def draw_cluster_ids(key, part):
    return cluster_layout(key)


def setup_inputs(seed: int = 0, part: int = 0) -> dict:
    splits = jax.random.split(jax.random.key(seed), 4)
    part_keys = jax.random.split(jax.random.fold_in(splits[3], part), 4)
    embeddings = draw_embeddings(jax.random.fold_in(jax.random.fold_in(splits[3], part), 71), part)
    position = draw_position(jax.random.fold_in(jax.random.fold_in(splits[3], part), 71), part)
    cluster_ids = draw_cluster_ids(jax.random.fold_in(jax.random.fold_in(splits[3], part), 71), part)
    return {"embeddings": embeddings, "position": position, "cluster_ids": cluster_ids}


SIMILARITY_CUTOFF = 0.9
SOFTMAX_HEAT = 0.02

def inverse_norms(matrix):
    wide = matrix.astype(jnp.float32)
    return lax.rsqrt(lax.optimization_barrier(jnp.sum(wide * wide, axis=1)) + 1e-06)

def block_terms(window, inverse, labels, left_start, right_start, offset):
    left_rows = lax.dynamic_slice_in_dim(window, left_start, BLOCK, 0)
    right_rows = lax.dynamic_slice_in_dim(window, right_start, BLOCK, 0)
    products = lax.dot_general(left_rows, right_rows, (((1,), (1,)), ((), ())), preferred_element_type=jnp.float32)
    left_inverse = lax.dynamic_slice_in_dim(inverse, left_start, BLOCK, 0)
    right_inverse = lax.dynamic_slice_in_dim(inverse, right_start, BLOCK, 0)
    cosine_similarity = products * left_inverse[:, None] * right_inverse[None, :]
    left_labels = lax.dynamic_slice_in_dim(labels, left_start, BLOCK, 0)
    right_labels = lax.dynamic_slice_in_dim(labels, right_start, BLOCK, 0)
    across = lax.broadcasted_iota(jnp.int32, (BLOCK, BLOCK), 0) != lax.broadcasted_iota(jnp.int32, (BLOCK, BLOCK), 1)
    same_cluster_mask = (left_labels[:, None] == right_labels[None, :]) & (across | (offset != 0))
    return jnp.where(same_cluster_mask, jnp.exp((cosine_similarity - SIMILARITY_CUTOFF) / SOFTMAX_HEAT), 0.0)

def add_at(totals, start, values):
    current = lax.dynamic_slice_in_dim(totals, start, values.shape[0], 0)
    return lax.dynamic_update_slice_in_dim(totals, current + values, start, 0)

def reference(embeddings, position, cluster_ids):
    doc_total = embeddings.shape[0]
    ordered = jnp.zeros_like(embeddings).at[position].set(embeddings)
    inverse = inverse_norms(ordered)
    window = jnp.concatenate([ordered, jnp.zeros((MOST, embeddings.shape[1]), embeddings.dtype)], axis=0)
    inverse = jnp.concatenate([inverse, jnp.zeros((MOST,), jnp.float32)], axis=0)
    labels = jnp.concatenate([cluster_ids, jnp.full((MOST,), -1, jnp.int32)], axis=0)
    block_total = doc_total // BLOCK
    block_reach = MOST // BLOCK

    def task(totals, task_index):
        left_block = (task_index // (block_reach + 1)).astype(jnp.int32)
        offset = (task_index % (block_reach + 1)).astype(jnp.int32)
        right_block = left_block + offset
        live_pairs = (offset == 0) | (labels[(left_block + 1) * BLOCK - 1] == labels[right_block * BLOCK])

        def compute_pair(totals):
            pair_terms = block_terms(window, inverse, labels, left_block * BLOCK, right_block * BLOCK, offset)
            row_part = lax.optimization_barrier(jnp.sum(pair_terms, axis=1))
            column_part = jnp.where(offset > 0, lax.optimization_barrier(jnp.sum(pair_terms, axis=0)), 0.0)
            totals = add_at(totals, left_block * BLOCK, row_part)
            return add_at(totals, right_block * BLOCK, column_part)
        return (lax.cond(live_pairs, compute_pair, lambda carried: carried, totals), None)
    totals, _ = lax.scan(task, jnp.zeros((doc_total + MOST,), jnp.float32), jnp.arange(block_total * (block_reach + 1), dtype=jnp.int32))
    sorted_weight = 1.0 / (1.0 + totals[:doc_total])
    return sorted_weight[position]
```

```python
import functools
import math

import jax
import jax.numpy as jnp
from jax import lax
from jax.experimental import pallas as pl
from jax.experimental.pallas import tpu as pltpu
from jax.sharding import PartitionSpec as P

MOST = 2048
HALF = MOST // 2
SIMILARITY_CUTOFF = 0.9
SOFTMAX_HEAT = 0.02
SCALE = math.log2(math.e) / SOFTMAX_HEAT
SHIFT = SIMILARITY_CUTOFF * SCALE
QUAD = 4
CHUNK = 256
LANES = 128
VMEM_LIMIT = 48 * 1024 * 1024

NT = (((1,), (1,)), ((), ()))
TN = (((0,), (0,)), ((), ()))


def iota(shape, dim):
    return lax.broadcasted_iota(jnp.int32, shape, dim)


def call(kernel, out_shape, **extra):
    return pl.pallas_call(
        kernel,
        out_shape=out_shape,
        compiler_params=pltpu.CompilerParams(vmem_limit_bytes=VMEM_LIMIT),
        **extra,
    )


def arrange_kernel(per_half, halves, position_ref, rows_ref, out_ref, rank_ref):
    n = rows_ref.shape[0]
    half = position_ref[...] // HALF
    kinds = iota((halves, n), 0) == half
    earlier = iota((n, n), 0) < iota((n, n), 1)
    counts = jnp.dot(
        kinds.astype(jnp.bfloat16),
        earlier.astype(jnp.bfloat16),
        preferred_element_type=jnp.float32,
    )
    count = jnp.sum(jnp.where(kinds, counts, 0.0), axis=0, keepdims=True)
    rank = half * per_half + count.astype(jnp.int32)
    rank_ref[...] = rank
    pick = (iota((n, n), 0) == rank).astype(jnp.bfloat16)
    out_ref[...] = jnp.dot(
        pick, rows_ref[...], preferred_element_type=jnp.float32
    ).astype(out_ref.dtype)


def facts_kernel(position_ref, ids_ref, rank_ref, arranged_ref, out_ref):
    n = arranged_ref.shape[0]
    eye = iota((n, n), 0) == iota((n, n), 1)
    pick = iota((n, n), 0) == rank_ref[...]
    where_to = position_ref[...].astype(jnp.float32)
    column = jnp.sum(jnp.where(pick, where_to, 0.0), axis=1, keepdims=True)
    wide = arranged_ref[...].astype(jnp.float32)
    inverse = lax.rsqrt(jnp.sum(wide * wide, axis=1, keepdims=True) + 1e-06)
    out_ref[0:1, :] = jnp.sum(jnp.where(eye, column, 0.0), axis=0, keepdims=True)
    out_ref[1:2, :] = jnp.sum(jnp.where(eye, inverse, 0.0), axis=0, keepdims=True)
    out_ref[2:3, :] = ids_ref[...].astype(jnp.float32)
    out_ref[3:4, :] = jnp.zeros((1, n), jnp.float32)


def labels_kernel(place_ref, table_ref, out_ref):
    place = place_ref[...]
    depth = table_ref.shape[0]
    n = place.shape[1]
    table = table_ref[...]
    high = jnp.floor(table * (1.0 / 256.0))
    low = table - high * 256.0
    line = (iota((depth, n), 0) == place // LANES).astype(jnp.bfloat16)
    high = lax.dot_general(
        high.astype(jnp.bfloat16), line, TN, preferred_element_type=jnp.float32
    )
    low = lax.dot_general(
        low.astype(jnp.bfloat16), line, TN, preferred_element_type=jnp.float32
    )
    here = iota((LANES, n), 0) == place % LANES
    out_ref[...] = jnp.sum(jnp.where(here, high * 256.0 + low, 0.0), axis=0, keepdims=True)


def masses_kernel(b0, b1, b2, h0, h1, rows_ref, columns_ref, out_ref):
    n = b0.shape[0]
    blocks = (b0, b1, b2)

    def terms(other, start, size, other_at, own, label_row):
        at = own * n
        products = lax.dot_general(
            other[start : start + size, :],
            blocks[own][...],
            NT,
            preferred_element_type=jnp.float32,
        )
        scale = columns_ref[other_at : other_at + size, 0:1]
        label = columns_ref[other_at : other_at + size, 1:2]
        own_scale = rows_ref[0:1, at : at + n]
        own_label = rows_ref[label_row : label_row + 1, at : at + n]
        power = products * scale * own_scale - SHIFT
        return label == own_label, jnp.exp2(power)

    def summed(mask, values):
        return jnp.sum(jnp.where(mask, values, 0.0), axis=0, keepdims=True)

    totals = [jnp.zeros((1, n), jnp.float32) for _ in blocks]
    for start in range(0, n, CHUNK):
        mask, values = terms(b0, start, CHUNK, start, 0, 1)
        mask &= iota((CHUNK, n), 0) + start != iota((CHUNK, n), 1)
        totals[0] += summed(mask, values)
        for other in (1, 2):
            totals[0] += summed(*terms(blocks[other], start, CHUNK, other * n + start, 0, 1))
        totals[1] += summed(*terms(b2, start, CHUNK, 2 * n + start, 1, 1))
    for k, halo in enumerate((h0, h1)):
        for start in range(0, n, CHUNK):
            across = jnp.zeros((CHUNK, LANES), jnp.float32)
            for own in (0, 2):
                mask, values = terms(
                    halo, start, CHUNK, (3 + k) * n + start, own, 1 if start < n // 2 else 2
                )
                values = jnp.where(mask, values, 0.0)
                totals[own] += jnp.sum(values, axis=0, keepdims=True)
                for lane in range(0, n, LANES):
                    across += values[:, lane : lane + LANES]
            out_ref[3 + k : 4 + k, start : start + CHUNK] = jnp.sum(
                across.T, axis=0, keepdims=True
            )
    for k, total in enumerate(totals):
        out_ref[k : k + 1, :] = total


def weights_kernel(per_half, rank_ref, returned_ref, out_ref):
    peers, width = returned_ref.shape
    rank = rank_ref[...]
    n = rank.shape[1]
    slab = rank // (2 * per_half)
    member = rank % (2 * per_half)
    upper = member >= per_half
    returned = returned_ref[...]
    plane = iota((peers, n), 0) // QUAD
    beside = jnp.where(upper, slab + 1, slab - 1)
    beside_member = jnp.where(upper, member + per_half, member + 3 * per_half)

    def chosen(which, lane):
        picked = lax.dot_general(
            returned,
            (plane == which).astype(jnp.float32),
            TN,
            precision=lax.Precision.HIGHEST,
            preferred_element_type=jnp.float32,
        )
        return jnp.sum(
            jnp.where(iota((width, n), 0) == lane, picked, 0.0), axis=0, keepdims=True
        )

    mass = chosen(slab, member) + chosen(beside, beside_member)
    out_ref[...] = 1.0 / (1.0 + mass)


def shards(embeddings, position, cluster_ids):
    n, width = embeddings.shape
    peers = lax.axis_size("dev")
    me = lax.axis_index("dev")
    planes = peers // QUAD
    slab, lane = me // QUAD, me % QUAD
    per_half = n // (2 * planes)
    per_slab = 2 * per_half
    f32 = jnp.float32

    where_to = position.reshape(1, n)
    arranged, rank = call(
        functools.partial(arrange_kernel, per_half, 2 * planes),
        (
            jax.ShapeDtypeStruct((n, width), embeddings.dtype),
            jax.ShapeDtypeStruct((1, n), jnp.int32),
        ),
    )(where_to, embeddings)
    lines = [[p * QUAD + q for p in range(planes)] for q in range(QUAD)]
    block = lax.all_to_all(
        arranged, "dev", split_axis=0, concat_axis=0, axis_index_groups=lines, tiled=True
    )

    facts = call(facts_kernel, jax.ShapeDtypeStruct((4, n), f32))(
        where_to, cluster_ids.reshape(1, n), rank, arranged
    )
    facts = lax.all_gather(facts, "dev", axis=0, tiled=False)

    ids = jnp.pad(facts[:, 2].reshape(peers * n), (MOST, MOST))
    ids = lax.dynamic_slice_in_dim(ids, slab * MOST, 3 * MOST, 0)
    by_slab = facts[:, :2].reshape(planes, QUAD, 2, planes, 2, per_half)
    by_slab = jnp.pad(by_slab, ((0, 0),) * 3 + ((1, 1),) + ((0, 0),) * 2)
    near = lax.dynamic_slice_in_dim(by_slab, slab, 3, 3)
    flipped = jnp.where(lane % 2 == 1, near.reshape(planes, 2, 2, 2, 3, 2, per_half)[:, :, ::-1], near.reshape(planes, 2, 2, 2, 3, 2, per_half))
    flipped = jnp.where(lane // 2 == 1, flipped[:, ::-1], flipped)
    near = flipped.reshape(planes, QUAD, 2, 3, 2, per_half).transpose(2, 1, 3, 0, 4, 5)
    own = near[:, :3, 1].reshape(2, 3 * n)
    halo = jnp.stack([near[:, :2, 0, :, 1], near[:, :2, 2, :, 0]], axis=2).reshape(2, 2 * n)
    near = jnp.concatenate([own, halo], axis=1)
    total = 5 * n
    place = near[0].astype(jnp.int32) - (slab - 1) * MOST
    label = call(labels_kernel, jax.ShapeDtypeStruct((1, total), f32))(
        place.reshape(1, total), ids.reshape(3 * MOST // LANES, LANES)
    )[0]
    at = jnp.arange(total)
    is_halo = at >= 3 * n
    is_after = at % n >= n // 2
    absent = is_halo & jnp.where(is_after, slab == planes - 1, slab == 0)
    label = jnp.where(absent, -1.0, label)
    in_upper = at % per_slab >= per_half
    rows = jnp.stack([near[1], label, jnp.where(in_upper, -2.0, label), jnp.zeros_like(label)])
    columns = jnp.stack([near[1] * SCALE, label], axis=1)

    def passed(rows_, by):
        pairs = [(i, i + by) for i in range(peers) if 0 <= i + by < peers]
        return lax.ppermute(rows_, "dev", pairs)

    def swapped(rows_, bit):
        return lax.ppermute(rows_, "dev", [(i, i ^ bit) for i in range(peers)])

    across = swapped(block, 2)
    parts = block.reshape(planes, 2, per_half, width)
    before = passed(parts[:, 1].reshape(n // 2, width), QUAD)
    after = passed(parts[:, 0].reshape(n // 2, width), -QUAD)
    beside = swapped(block, 1)
    halo = jnp.concatenate([before, after], axis=0)
    halo_beside = swapped(halo, 1)

    masses = call(masses_kernel, jax.ShapeDtypeStruct((8, n), f32))(
        block, beside, across, halo, halo_beside, rows, columns
    )
    none = jnp.zeros((n,), f32)
    slabs = jnp.stack([masses[0], masses[1], masses[2], none])
    halos = jnp.stack([masses[3], masses[4], none, none])
    slabs = slabs.reshape(2, 2, planes, per_slab)
    halos = halos.reshape(2, 2, 2, planes, per_half)
    outgoing = jnp.concatenate([slabs, halos[:, :, 0], halos[:, :, 1]], axis=-1)
    outgoing = jnp.where(lane % 2 == 1, outgoing[:, ::-1], outgoing)
    outgoing = jnp.where(lane // 2 == 1, outgoing[::-1], outgoing)
    outgoing = outgoing.reshape(QUAD, planes, 4 * per_half).transpose(1, 0, 2)
    returned = lax.all_to_all(
        outgoing.reshape(peers, 4 * per_half), "dev", split_axis=0, concat_axis=0, tiled=True
    )
    weight = call(
        functools.partial(weights_kernel, per_half), jax.ShapeDtypeStruct((1, n), f32)
    )(rank, returned)
    return weight.reshape(n)


def solution(mesh):
    return jax.shard_map(
        shards,
        mesh=mesh,
        in_specs=(P(("grp", "dev"), None), P(("grp", "dev")), P(("grp", "dev"))),
        out_specs=P(("grp", "dev")),
        check_vma=False,
    )
```

```python
import functools
import math

import jax
import jax.numpy as jnp
from jax import lax
from jax.experimental import pallas as pl
from jax.experimental.pallas import tpu as pltpu
from jax.sharding import PartitionSpec as P

MOST = 2048
HALF = MOST // 2
SIMILARITY_CUTOFF = 0.9
SOFTMAX_HEAT = 0.02
SCALE = math.log2(math.e) / SOFTMAX_HEAT
SHIFT = SIMILARITY_CUTOFF * SCALE
QUAD = 4
CHUNK = 256
LANES = 128
VMEM_LIMIT = 48 * 1024 * 1024

NT = (((1,), (1,)), ((), ()))
TN = (((0,), (0,)), ((), ()))


def iota(shape, dim):
    return lax.broadcasted_iota(jnp.int32, shape, dim)


def call(kernel, out_shape, **extra):
    return pl.pallas_call(
        kernel,
        out_shape=out_shape,
        compiler_params=pltpu.CompilerParams(vmem_limit_bytes=VMEM_LIMIT),
        **extra,
    )


def arrange_kernel(per_half, halves, position_ref, rows_ref, out_ref, rank_ref):
    n = rows_ref.shape[0]
    half = position_ref[...] // HALF
    kinds = iota((halves, n), 0) == half
    earlier = iota((n, n), 0) < iota((n, n), 1)
    counts = jnp.dot(
        kinds.astype(jnp.bfloat16),
        earlier.astype(jnp.bfloat16),
        preferred_element_type=jnp.float32,
    )
    count = jnp.sum(jnp.where(kinds, counts, 0.0), axis=0, keepdims=True)
    rank = half * per_half + count.astype(jnp.int32)
    rank_ref[...] = rank
    pick = (iota((n, n), 0) == rank).astype(jnp.bfloat16)
    out_ref[...] = jnp.dot(
        pick, rows_ref[...], preferred_element_type=jnp.float32
    ).astype(out_ref.dtype)


def facts_kernel(position_ref, ids_ref, rank_ref, arranged_ref, out_ref):
    n = arranged_ref.shape[0]
    eye = iota((n, n), 0) == iota((n, n), 1)
    pick = iota((n, n), 0) == rank_ref[...]
    where_to = position_ref[...].astype(jnp.float32)
    column = jnp.sum(jnp.where(pick, where_to, 0.0), axis=1, keepdims=True)
    wide = arranged_ref[...].astype(jnp.float32)
    inverse = lax.rsqrt(jnp.sum(wide * wide, axis=1, keepdims=True) + 1e-06)
    out_ref[0:1, :] = jnp.sum(jnp.where(eye, column, 0.0), axis=0, keepdims=True)
    out_ref[1:2, :] = jnp.sum(jnp.where(eye, inverse, 0.0), axis=0, keepdims=True)
    out_ref[2:3, :] = ids_ref[...].astype(jnp.float32)
    out_ref[3:4, :] = jnp.zeros((1, n), jnp.float32)


def labels_kernel(place_ref, table_ref, out_ref):
    place = place_ref[...]
    depth = table_ref.shape[0]
    n = place.shape[1]
    table = table_ref[...]
    high = jnp.floor(table * (1.0 / 256.0))
    low = table - high * 256.0
    line = (iota((depth, n), 0) == place // LANES).astype(jnp.bfloat16)
    high = lax.dot_general(
        high.astype(jnp.bfloat16), line, TN, preferred_element_type=jnp.float32
    )
    low = lax.dot_general(
        low.astype(jnp.bfloat16), line, TN, preferred_element_type=jnp.float32
    )
    here = iota((LANES, n), 0) == place % LANES
    out_ref[...] = jnp.sum(jnp.where(here, high * 256.0 + low, 0.0), axis=0, keepdims=True)


class Terms:
    def __init__(self, rows_ref, columns_ref):
        self.rows, self.columns = rows_ref, columns_ref

    def of(self, other, start, other_at, own, own_at, label_row):
        n = own.shape[0]
        products = lax.dot_general(
            other[start : start + CHUNK, :], own[...], NT, preferred_element_type=jnp.float32
        )
        scale = self.columns[other_at : other_at + CHUNK, 0:1]
        label = self.columns[other_at : other_at + CHUNK, 1:2]
        own_scale = self.rows[0:1, own_at : own_at + n]
        own_label = self.rows[label_row : label_row + 1, own_at : own_at + n]
        values = jnp.exp2(products * scale * own_scale - SHIFT)
        return jnp.where(label == own_label, values, 0.0)

    def block(self, other, other_at, own, own_at, same=False):
        n = own.shape[0]
        total = jnp.zeros((1, n), jnp.float32)
        for start in range(0, n, CHUNK):
            values = self.of(other, start, other_at + start, own, own_at, 1)
            if same:
                apart = iota((CHUNK, n), 0) + start != iota((CHUNK, n), 1)
                values = jnp.where(apart, values, 0.0)
            total += jnp.sum(values, axis=0, keepdims=True)
        return total

    def halo(self, halo, first, halo_at, own, own_at):
        n = own.shape[0]
        total = jnp.zeros((1, n), jnp.float32)
        sides = []
        for start in range(0, n, CHUNK):
            values = self.of(
                halo, first + start, halo_at + start, own, own_at, 1 if start < n // 2 else 2
            )
            total += jnp.sum(values, axis=0, keepdims=True)
            side = jnp.zeros((CHUNK, LANES), jnp.float32)
            for lane in range(0, n, LANES):
                side += values[:, lane : lane + LANES]
            sides.append(jnp.sum(side.T, axis=0, keepdims=True))
        return total, jnp.concatenate(sides, axis=1)


def masses_kernel(b0, h0, partner, rows_ref, columns_ref, out_ref):
    n = b0.shape[0]
    t = Terms(rows_ref, columns_ref)
    total = t.block(b0, 0, b0, 0, same=True) + t.block(partner, n, b0, 0)
    for k, (halo, first) in enumerate(((h0, 0), (partner, n))):
        more, side = t.halo(halo, first, (3 + k) * n, b0, 0)
        total += more
        out_ref[3 + k : 4 + k, :] = side
    out_ref[0:1, :] = total
    out_ref[1:3, :] = jnp.zeros((2, n), jnp.float32)


def masses_across_kernel(b0, h0, partner, b2, rows_ref, columns_ref, last_ref, out_ref):
    n = b0.shape[0]
    t = Terms(rows_ref, columns_ref)
    out_ref[0:1, :] = last_ref[0:1, :] + t.block(b2, 2 * n, b0, 0)
    total = t.block(partner, n, b2, 2 * n)
    for k, (halo, first) in enumerate(((h0, 0), (partner, n))):
        more, side = t.halo(halo, first, (3 + k) * n, b2, 2 * n)
        total += more
        out_ref[3 + k : 4 + k, :] = last_ref[3 + k : 4 + k, :] + side
    out_ref[1:2, :] = jnp.zeros((1, n), jnp.float32)
    out_ref[2:3, :] = total


def weights_kernel(per_half, rank_ref, returned_ref, out_ref):
    peers, width = returned_ref.shape
    rank = rank_ref[...]
    n = rank.shape[1]
    slab = rank // (2 * per_half)
    member = rank % (2 * per_half)
    upper = member >= per_half
    returned = returned_ref[...]
    plane = iota((peers, n), 0) // QUAD
    beside = jnp.where(upper, slab + 1, slab - 1)
    beside_member = jnp.where(upper, member + per_half, member + 3 * per_half)

    def chosen(which, lane):
        picked = lax.dot_general(
            returned,
            (plane == which).astype(jnp.float32),
            TN,
            precision=lax.Precision.HIGHEST,
            preferred_element_type=jnp.float32,
        )
        return jnp.sum(
            jnp.where(iota((width, n), 0) == lane, picked, 0.0), axis=0, keepdims=True
        )

    mass = chosen(slab, member) + chosen(beside, beside_member)
    out_ref[...] = 1.0 / (1.0 + mass)


def shards(embeddings, position, cluster_ids):
    n, width = embeddings.shape
    peers = lax.axis_size("dev")
    me = lax.axis_index("dev")
    planes = peers // QUAD
    slab, lane = me // QUAD, me % QUAD
    per_half = n // (2 * planes)
    per_slab = 2 * per_half
    f32 = jnp.float32

    where_to = position.reshape(1, n)
    arranged, rank = call(
        functools.partial(arrange_kernel, per_half, 2 * planes),
        (
            jax.ShapeDtypeStruct((n, width), embeddings.dtype),
            jax.ShapeDtypeStruct((1, n), jnp.int32),
        ),
    )(where_to, embeddings)
    lines = [[p * QUAD + q for p in range(planes)] for q in range(QUAD)]
    block = lax.all_to_all(
        arranged, "dev", split_axis=0, concat_axis=0, axis_index_groups=lines, tiled=True
    )

    facts = call(facts_kernel, jax.ShapeDtypeStruct((4, n), f32))(
        where_to, cluster_ids.reshape(1, n), rank, arranged
    )
    facts = lax.all_to_all(
        jnp.broadcast_to(facts, (peers, 4, n)), "dev", split_axis=0, concat_axis=0, tiled=True
    )

    ids = jnp.pad(facts[:, 2].reshape(peers * n), (MOST, MOST))
    ids = lax.dynamic_slice_in_dim(ids, slab * MOST, 3 * MOST, 0)
    by_slab = facts[:, :2].reshape(planes, QUAD, 2, planes, 2, per_half)
    by_slab = jnp.pad(by_slab, ((0, 0),) * 3 + ((1, 1),) + ((0, 0),) * 2)
    near = lax.dynamic_slice_in_dim(by_slab, slab, 3, 3)
    flipped = jnp.where(lane % 2 == 1, near.reshape(planes, 2, 2, 2, 3, 2, per_half)[:, :, ::-1], near.reshape(planes, 2, 2, 2, 3, 2, per_half))
    flipped = jnp.where(lane // 2 == 1, flipped[:, ::-1], flipped)
    near = flipped.reshape(planes, QUAD, 2, 3, 2, per_half).transpose(2, 1, 3, 0, 4, 5)
    own = near[:, :3, 1].reshape(2, 3 * n)
    halo = jnp.stack([near[:, :2, 0, :, 1], near[:, :2, 2, :, 0]], axis=2).reshape(2, 2 * n)
    near = jnp.concatenate([own, halo], axis=1)
    total = 5 * n
    place = near[0].astype(jnp.int32) - (slab - 1) * MOST
    label = call(labels_kernel, jax.ShapeDtypeStruct((1, total), f32))(
        place.reshape(1, total), ids.reshape(3 * MOST // LANES, LANES)
    )[0]
    at = jnp.arange(total)
    is_halo = at >= 3 * n
    is_after = at % n >= n // 2
    absent = is_halo & jnp.where(is_after, slab == planes - 1, slab == 0)
    label = jnp.where(absent, -1.0, label)
    in_upper = at % per_slab >= per_half
    rows = jnp.stack([near[1], label, jnp.where(in_upper, -2.0, label), jnp.zeros_like(label)])
    columns = jnp.stack([near[1] * SCALE, label], axis=1)

    def passed(rows_, by):
        pairs = [(i, i + by) for i in range(peers) if 0 <= i + by < peers]
        return lax.ppermute(rows_, "dev", pairs)

    def swapped(rows_, bit):
        return lax.ppermute(rows_, "dev", [(i, i ^ bit) for i in range(peers)])

    across = swapped(block, 2)
    parts = block.reshape(planes, 2, per_half, width)
    before = passed(parts[:, 1].reshape(n // 2, width), QUAD)
    after = passed(parts[:, 0].reshape(n // 2, width), -QUAD)
    halo = jnp.concatenate([before, after], axis=0)
    partner = swapped(jnp.concatenate([block, halo], axis=0), 1)

    sums = jax.ShapeDtypeStruct((8, n), f32)
    masses = call(masses_kernel, sums)(block, halo, partner, rows, columns)
    masses = call(masses_across_kernel, sums)(
        block, halo, partner, across, rows, columns, masses
    )
    none = jnp.zeros((n,), f32)
    slabs = jnp.stack([masses[0], masses[1], masses[2], none])
    halos = jnp.stack([masses[3], masses[4], none, none])
    slabs = slabs.reshape(2, 2, planes, per_slab)
    halos = halos.reshape(2, 2, 2, planes, per_half)
    outgoing = jnp.concatenate([slabs, halos[:, :, 0], halos[:, :, 1]], axis=-1)
    outgoing = jnp.where(lane % 2 == 1, outgoing[:, ::-1], outgoing)
    outgoing = jnp.where(lane // 2 == 1, outgoing[::-1], outgoing)
    outgoing = outgoing.reshape(QUAD, planes, 4 * per_half).transpose(1, 0, 2)
    returned = lax.all_to_all(
        outgoing.reshape(peers, 4 * per_half), "dev", split_axis=0, concat_axis=0, tiled=True
    )
    weight = call(
        functools.partial(weights_kernel, per_half), jax.ShapeDtypeStruct((1, n), f32)
    )(rank, returned)
    return weight.reshape(n)


def solution(mesh):
    return jax.shard_map(
        shards,
        mesh=mesh,
        in_specs=(P(("grp", "dev"), None), P(("grp", "dev")), P(("grp", "dev"))),
        out_specs=P(("grp", "dev")),
        check_vma=False,
    )
```

```python
import functools
import math

import jax
import jax.numpy as jnp
from jax import lax
from jax.experimental import pallas as pl
from jax.experimental.pallas import tpu as pltpu
from jax.sharding import PartitionSpec as P

MOST = 2048
HALF = MOST // 2
SIMILARITY_CUTOFF = 0.9
SOFTMAX_HEAT = 0.02
SCALE = math.log2(math.e) / SOFTMAX_HEAT
SHIFT = SIMILARITY_CUTOFF * SCALE
QUAD = 4
CHUNK = 256
LANES = 128
VMEM_LIMIT = 48 * 1024 * 1024

NT = (((1,), (1,)), ((), ()))
TN = (((0,), (0,)), ((), ()))


def iota(shape, dim):
    return lax.broadcasted_iota(jnp.int32, shape, dim)


def call(kernel, out_shape, **extra):
    return pl.pallas_call(
        kernel,
        out_shape=out_shape,
        compiler_params=pltpu.CompilerParams(vmem_limit_bytes=VMEM_LIMIT),
        **extra,
    )


def arrange_kernel(per_half, halves, position_hbm, rows_hbm, *refs):
    *outs, rank_ref, place, rows, sems = refs
    copies = [
        pltpu.make_async_copy(position_hbm, place, sems.at[0]),
        pltpu.make_async_copy(rows_hbm, rows, sems.at[1]),
    ]
    for copy in copies:
        copy.start()
    n = rows.shape[0]
    earlier = (iota((n, n), 0) < iota((n, n), 1)).astype(jnp.bfloat16)
    copies[0].wait()
    half = place[...] // HALF
    kinds = iota((halves, n), 0) == half
    counts = jnp.dot(kinds.astype(jnp.bfloat16), earlier, preferred_element_type=jnp.float32)
    count = jnp.sum(jnp.where(kinds, counts, 0.0), axis=0, keepdims=True).astype(jnp.int32)
    rank_ref[...] = half * per_half + count
    if len(outs) > 1:
        half = half ^ (2 * (lax.axis_index("dev") // QUAD))
    rank = half * per_half + count
    size = n // len(outs)
    copies[1].wait()
    for k, out in enumerate(outs):
        pick = (iota((size, n), 0) + k * size == rank).astype(jnp.bfloat16)
        out[...] = jnp.dot(pick, rows[...], preferred_element_type=jnp.float32).astype(out.dtype)


def facts_kernel(position_ref, ids_ref, rank_ref, *refs):
    *pieces, out_ref = refs
    n = position_ref.shape[1]
    size = n // len(pieces)
    mine = 0
    if len(pieces) > 1:
        mine = lax.axis_index("dev") // QUAD
    pick = iota((n, n), 0) == rank_ref[...]
    where_to = position_ref[...].astype(jnp.float32)
    column = jnp.sum(jnp.where(pick, where_to, 0.0), axis=1, keepdims=True)
    eye = iota((n, n), 0) == iota((n, n), 1)
    out_ref[0:1, :] = jnp.sum(jnp.where(eye, column, 0.0), axis=0, keepdims=True)
    total = jnp.zeros((1, n), jnp.float32)
    for k, piece in enumerate(pieces):
        wide = piece[...].astype(jnp.float32)
        inverse = lax.rsqrt(jnp.sum(wide * wide, axis=1, keepdims=True) + 1e-06)
        here = iota((size, n), 0) + (mine ^ k) * size == iota((size, n), 1)
        total += jnp.sum(jnp.where(here, inverse, 0.0), axis=0, keepdims=True)
    out_ref[1:2, :] = total
    out_ref[2:3, :] = ids_ref[...].astype(jnp.float32)
    out_ref[3:4, :] = jnp.zeros((1, n), jnp.float32)


def labels_kernel(place_ref, table_ref, out_ref):
    place = place_ref[...]
    depth = table_ref.shape[0]
    n = place.shape[1]
    table = table_ref[...]
    high = jnp.floor(table * (1.0 / 256.0))
    low = table - high * 256.0
    line = (iota((depth, n), 0) == place // LANES).astype(jnp.bfloat16)
    high = lax.dot_general(
        high.astype(jnp.bfloat16), line, TN, preferred_element_type=jnp.float32
    )
    low = lax.dot_general(
        low.astype(jnp.bfloat16), line, TN, preferred_element_type=jnp.float32
    )
    here = iota((LANES, n), 0) == place % LANES
    out_ref[...] = jnp.sum(jnp.where(here, high * 256.0 + low, 0.0), axis=0, keepdims=True)


OFFSETS = {"b0": 0, "b1": 2, "b2": 4, "h0": 6, "h1": 8}
SUMS = {"b0": 0, "b1": 1, "b2": 2, "h0": 3, "h1": 4}


class Terms:
    def __init__(self, arrays, rows_ref, columns_ref, out_ref, last_ref):
        self.arrays, self.rows, self.columns, self.out = arrays, rows_ref, columns_ref, out_ref
        self.n = out_ref.shape[1]
        self.last = last_ref
        self.sums = {}

    def add(self, name, at, values):
        key = (name, at)
        self.sums[key] = self.sums[key] + values if key in self.sums else values

    def offset(self, name):
        return OFFSETS[name] * self.n // 2

    def whole(self, name):
        refs = self.arrays[name]
        parts = [ref[...] for ref in refs]
        return parts[0] if len(parts) == 1 else jnp.concatenate(parts, axis=0)

    def tiles(self, other, own, label_row):
        block = self.whole(own)
        n, own_at = block.shape[0], self.offset(own)
        own_scale = self.rows[0:1, own_at : own_at + n]
        at = 0
        for ref in self.arrays[other]:
            size = min(CHUNK, ref.shape[0])
            for start in range(0, ref.shape[0], size):
                products = lax.dot_general(
                    ref[start : start + size, :], block, NT, preferred_element_type=jnp.float32
                )
                facts = self.offset(other) + at
                scale = self.columns[facts : facts + size, 0:1]
                label = self.columns[facts : facts + size, 1:2]
                row = label_row(at)
                own_label = self.rows[row : row + 1, own_at : own_at + n]
                values = jnp.exp2(products * scale * own_scale - SHIFT)
                yield at, size, jnp.where(label == own_label, values, 0.0)
                at += size

    def block(self, other, own):
        for at, size, values in self.tiles(other, own, lambda at: 1):
            if other == own:
                shape = values.shape
                values = jnp.where(iota(shape, 0) + at != iota(shape, 1), values, 0.0)
            self.add(own, 0, jnp.sum(values, axis=0, keepdims=True))

    def halo(self, other, own):
        for at, size, values in self.tiles(other, own, lambda at: 1 if at < self.n // 2 else 2):
            self.add(own, 0, jnp.sum(values, axis=0, keepdims=True))
            side = jnp.zeros((size, LANES), jnp.float32)
            for lane in range(0, values.shape[1], LANES):
                side += values[:, lane : lane + LANES]
            self.add(other, at, side)

    def write(self):
        written = set()
        for (name, at), values in self.sums.items():
            if values.shape[0] > 1:
                values = jnp.sum(values.T, axis=0, keepdims=True)
            k, size = SUMS[name], values.shape[1]
            if self.last is not None:
                values += self.last[k : k + 1, at : at + size]
            self.out[k : k + 1, at : at + size] = values
            written.add(k)
        for k in range(5):
            if k not in written:
                row = jnp.zeros((1, self.n), jnp.float32)
                self.out[k : k + 1, :] = row if self.last is None else self.last[k : k + 1, :]


def masses_call(jobs, arrays, rows, columns, last=None):
    names = sorted({name for job in jobs for name in job})
    counts = [len(arrays[name]) for name in names]

    def kernel(*refs):
        refs = list(refs)
        held = {name: [refs.pop(0) for _ in range(k)] for name, k in zip(names, counts)}
        rows_ref, columns_ref = refs.pop(0), refs.pop(0)
        last_ref = refs.pop(0) if last is not None else None
        t = Terms(held, rows_ref, columns_ref, refs.pop(0), last_ref)
        for other, own in jobs:
            (t.halo if other in ("h0", "h1") else t.block)(other, own)
        t.write()

    operands = [array for name in names for array in arrays[name]] + [rows, columns]
    if last is not None:
        operands.append(last)
    n = rows.shape[1] // 5
    return call(kernel, jax.ShapeDtypeStruct((8, n), jnp.float32))(*operands)


def weights_kernel(per_half, rank_ref, returned_ref, out_ref):
    peers, width = returned_ref.shape
    rank = rank_ref[...]
    n = rank.shape[1]
    slab = rank // (2 * per_half)
    member = rank % (2 * per_half)
    upper = member >= per_half
    returned = returned_ref[...]
    plane = iota((peers, n), 0) // QUAD
    beside = jnp.where(upper, slab + 1, slab - 1)
    beside_member = jnp.where(upper, member + per_half, member + 3 * per_half)

    def chosen(which, lane):
        picked = lax.dot_general(
            returned,
            (plane == which).astype(jnp.float32),
            TN,
            precision=lax.Precision.HIGHEST,
            preferred_element_type=jnp.float32,
        )
        return jnp.sum(
            jnp.where(iota((width, n), 0) == lane, picked, 0.0), axis=0, keepdims=True
        )

    mass = chosen(slab, member) + chosen(beside, beside_member)
    out_ref[...] = 1.0 / (1.0 + mass)


def xor_order(array, axis, bits):
    count = array.shape[axis]
    for k in range(count.bit_length() - 1):
        step = 1 << k
        shape = array.shape[:axis] + (count // (2 * step), 2, step) + array.shape[axis + 1 :]
        split = array.reshape(shape)
        split = jnp.where((bits >> k) & 1 == 1, jnp.flip(split, axis + 1), split)
        array = split.reshape(array.shape)
    return array


def shards(embeddings, position, cluster_ids):
    n, width = embeddings.shape
    peers = lax.axis_size("dev")
    me = lax.axis_index("dev")
    planes = peers // QUAD
    slab, lane = me // QUAD, me % QUAD
    per_half = n // (2 * planes)
    per_slab = 2 * per_half
    f32 = jnp.float32
    by_permutes = planes == 4
    pieces = planes if by_permutes else 1

    def swapped(rows_, bit):
        return lax.ppermute(rows_, "dev", [(i, i ^ bit) for i in range(peers)])

    def passed(rows_, by):
        pairs = [(i, i + by) for i in range(peers) if 0 <= i + by < peers]
        return lax.ppermute(rows_, "dev", pairs)

    where_to = position.reshape(1, n)
    in_hbm = pl.BlockSpec(memory_space=pl.ANY)
    *arranged, rank = call(
        functools.partial(arrange_kernel, per_half, 2 * planes),
        [jax.ShapeDtypeStruct((n // pieces, width), embeddings.dtype)] * pieces
        + [jax.ShapeDtypeStruct((1, n), jnp.int32)],
        in_specs=[in_hbm, in_hbm],
        scratch_shapes=[
            pltpu.VMEM((1, n), jnp.int32),
            pltpu.VMEM((n, width), embeddings.dtype),
            pltpu.SemaphoreType.DMA((2,)),
        ],
    )(where_to, embeddings)
    if by_permutes:
        block = [arranged[0]]
        across = [swapped(block[0], 2)]
        later = {k: swapped(arranged[k], k * QUAD) for k in (3, 2, 1)}
        for k in (1, 2, 3):
            block.append(later[k])
            across.append(swapped(later[k], 2))
    else:
        lines = [[p * QUAD + q for p in range(planes)] for q in range(QUAD)]
        block = [
            lax.all_to_all(
                arranged[0], "dev", split_axis=0, concat_axis=0, axis_index_groups=lines, tiled=True
            )
        ]
        across = [swapped(block[0], 2)]

    facts = call(facts_kernel, jax.ShapeDtypeStruct((4, n), f32))(
        where_to, cluster_ids.reshape(1, n), rank, *arranged
    )
    facts = lax.all_to_all(
        jnp.broadcast_to(facts, (peers, 4, n)), "dev", split_axis=0, concat_axis=0, tiled=True
    )

    ids = jnp.pad(facts[:, 2].reshape(peers * n), (MOST, MOST))
    ids = lax.dynamic_slice_in_dim(ids, slab * MOST, 3 * MOST, 0)
    by_slab = facts[:, :2].reshape(planes, QUAD, 2, planes, 2, per_half)
    by_slab = jnp.pad(by_slab, ((0, 0),) * 3 + ((1, 1),) + ((0, 0),) * 2)
    near = lax.dynamic_slice_in_dim(by_slab, slab, 3, 3)
    near = xor_order(near, 1, lane)
    near = near.transpose(2, 1, 3, 0, 4, 5)

    def as_received(values, axis, plane):
        return xor_order(values, axis, plane) if by_permutes else values

    own = as_received(near[:, :3, 1], 2, slab).reshape(2, 3 * n)
    before = as_received(near[:, :2, 0, :, 1], 2, slab - 1)
    after = as_received(near[:, :2, 2, :, 0], 2, slab + 1)
    halo = jnp.stack([before, after], axis=2).reshape(2, 2 * n)
    near = jnp.concatenate([own, halo], axis=1)
    total = 5 * n
    place = near[0].astype(jnp.int32) - (slab - 1) * MOST
    label = call(labels_kernel, jax.ShapeDtypeStruct((1, total), f32))(
        place.reshape(1, total), ids.reshape(3 * MOST // LANES, LANES)
    )[0]
    at = jnp.arange(total)
    is_halo = at >= 3 * n
    is_after = at % n >= n // 2
    absent = is_halo & jnp.where(is_after, slab == planes - 1, slab == 0)
    label = jnp.where(absent, -1.0, label)
    in_upper = at % per_slab >= per_half
    rows = jnp.stack([near[1], label, jnp.where(in_upper, -2.0, label), jnp.zeros_like(label)])
    columns = jnp.stack([near[1] * SCALE, label], axis=1)

    halves = [piece.reshape(-1, 2, per_half, width) for piece in block]
    upper = jnp.concatenate([h[:, 1] for h in halves], axis=0).reshape(n // 2, width)
    lower = jnp.concatenate([h[:, 0] for h in halves], axis=0).reshape(n // 2, width)
    before = passed(upper, QUAD)
    after = passed(lower, -QUAD)
    beside = swapped(jnp.concatenate(block, axis=0), 1)
    halo_beside = swapped(jnp.concatenate([before, after], axis=0), 1)

    arrays = {
        "b0": block,
        "b1": [beside],
        "b2": across,
        "h0": [before, after],
        "h1": [halo_beside],
    }
    masses = masses_call([("b0", "b0"), ("b1", "b0"), ("h0", "b0")], arrays, rows, columns)
    masses = masses_call(
        [("b2", "b0"), ("b1", "b2"), ("h0", "b2"), ("h1", "b0"), ("h1", "b2")],
        arrays, rows, columns, masses,
    )

    none = jnp.zeros((n,), f32)
    slabs = jnp.stack([masses[0], masses[1], masses[2], none])
    halos = jnp.stack([masses[3], masses[4], none, none])
    slabs = slabs.reshape(QUAD, planes, per_slab)
    halos = halos.reshape(QUAD, 2, planes, per_half)
    outgoing = jnp.concatenate(
        [
            as_received(slabs, 1, slab),
            as_received(halos[:, 0], 1, slab - 1),
            as_received(halos[:, 1], 1, slab + 1),
        ],
        axis=-1,
    )
    outgoing = xor_order(outgoing, 0, lane)
    outgoing = outgoing.transpose(1, 0, 2)
    returned = lax.all_to_all(
        outgoing.reshape(peers, 4 * per_half), "dev", split_axis=0, concat_axis=0, tiled=True
    )
    weight = call(
        functools.partial(weights_kernel, per_half), jax.ShapeDtypeStruct((1, n), f32)
    )(rank, returned)
    return weight.reshape(n)


def solution(mesh):
    return jax.shard_map(
        shards,
        mesh=mesh,
        in_specs=(P(("grp", "dev"), None), P(("grp", "dev")), P(("grp", "dev"))),
        out_specs=P(("grp", "dev")),
        check_vma=False,
    )
```

```python
import functools
import math

import jax
import jax.numpy as jnp
from jax import lax
from jax.experimental import pallas as pl
from jax.experimental.pallas import tpu as pltpu
from jax.sharding import PartitionSpec as P

MOST = 2048
HALF = MOST // 2
SIMILARITY_CUTOFF = 0.9
SOFTMAX_HEAT = 0.02
SCALE = math.log2(math.e) / SOFTMAX_HEAT
SHIFT = SIMILARITY_CUTOFF * SCALE
QUAD = 4
CHUNK = 256
LANES = 128
VMEM_LIMIT = 16 * 1024 * 1024

NT = (((1,), (1,)), ((), ()))
TN = (((0,), (0,)), ((), ()))


def iota(shape, dim):
    return lax.broadcasted_iota(jnp.int32, shape, dim)


def call(kernel, out_shape, **extra):
    return pl.pallas_call(
        kernel,
        out_shape=out_shape,
        compiler_params=pltpu.CompilerParams(vmem_limit_bytes=VMEM_LIMIT),
        **extra,
    )


def arrange_kernel(per_half, halves, position_hbm, rows_hbm, *refs):
    *outs, rank_ref, place, rows, sems = refs
    copies = [
        pltpu.make_async_copy(position_hbm, place, sems.at[0]),
        pltpu.make_async_copy(rows_hbm, rows, sems.at[1]),
    ]
    for copy in copies:
        copy.start()
    n = rows.shape[0]
    earlier = (iota((n, n), 0) < iota((n, n), 1)).astype(jnp.bfloat16)
    copies[0].wait()
    half = place[...] // HALF
    kinds = iota((halves, n), 0) == half
    counts = jnp.dot(kinds.astype(jnp.bfloat16), earlier, preferred_element_type=jnp.float32)
    count = jnp.sum(jnp.where(kinds, counts, 0.0), axis=0, keepdims=True).astype(jnp.int32)
    rank_ref[...] = half * per_half + count
    rank = half * per_half + count
    if len(outs) > 1:
        plane = (half // 2) ^ (lax.axis_index("dev") // QUAD)
        rank = ((1 - half % 2) * (halves // 2) + plane) * per_half + count
    pick = (iota((n, n), 0) == rank).astype(jnp.bfloat16)
    copies[1].wait()
    picked = jnp.dot(pick, rows[...], preferred_element_type=jnp.float32)
    size = n // len(outs)
    for k, out in enumerate(outs):
        out[...] = picked[k * size : (k + 1) * size, :].astype(out.dtype)


def facts_kernel(halves, position_ref, ids_ref, rank_ref, *refs):
    *pieces, out_ref = refs
    n = position_ref.shape[1]
    size = n // len(pieces)
    pick = iota((n, n), 0) == rank_ref[...]
    where_to = position_ref[...].astype(jnp.float32)
    column = jnp.sum(jnp.where(pick, where_to, 0.0), axis=1, keepdims=True)
    eye = iota((n, n), 0) == iota((n, n), 1)
    out_ref[0:1, :] = jnp.sum(jnp.where(eye, column, 0.0), axis=0, keepdims=True)
    total = jnp.zeros((1, n), jnp.float32)
    for k, piece in enumerate(pieces):
        wide = piece[...].astype(jnp.float32)
        inverse = lax.rsqrt(jnp.sum(wide * wide, axis=1, keepdims=True) + 1e-06)
        first = 0
        if len(pieces) > 1:
            plane = (k % (halves // 2)) ^ (lax.axis_index("dev") // QUAD)
            first = (2 * plane + 1 - k // (halves // 2)) * size
        here = iota((size, n), 0) + first == iota((size, n), 1)
        total += jnp.sum(jnp.where(here, inverse, 0.0), axis=0, keepdims=True)
    out_ref[1:2, :] = total
    out_ref[2:3, :] = ids_ref[...].astype(jnp.float32)
    out_ref[3:4, :] = jnp.zeros((1, n), jnp.float32)


def labels_kernel(place_ref, table_ref, out_ref):
    place = place_ref[...]
    depth = table_ref.shape[0]
    n = place.shape[1]
    table = table_ref[...]
    high = jnp.floor(table * (1.0 / 256.0))
    low = table - high * 256.0
    line = (iota((depth, n), 0) == place // LANES).astype(jnp.bfloat16)
    high = lax.dot_general(
        high.astype(jnp.bfloat16), line, TN, preferred_element_type=jnp.float32
    )
    low = lax.dot_general(
        low.astype(jnp.bfloat16), line, TN, preferred_element_type=jnp.float32
    )
    here = iota((LANES, n), 0) == place % LANES
    out_ref[...] = jnp.sum(jnp.where(here, high * 256.0 + low, 0.0), axis=0, keepdims=True)


NAMES = ("b0h", "b0l", "b1h", "b1l", "b2h", "b2l", "u", "l", "u1", "l1")
SUMS = ("b0h", "b0l", "b2h", "b2l", "u", "l", "u1", "l1")


class Terms:
    def __init__(self, arrays, rows_ref, columns_ref, out_ref, last_ref):
        self.arrays, self.rows, self.columns, self.out = arrays, rows_ref, columns_ref, out_ref
        self.last = last_ref
        self.sums = {}

    def add(self, name, values):
        self.sums[name] = self.sums[name] + values if name in self.sums else values

    def job(self, down, across):
        n = self.arrays[down].shape[0]
        products = lax.dot_general(
            self.arrays[down][...],
            self.arrays[across][...],
            NT,
            preferred_element_type=jnp.float32,
        )
        at, to = NAMES.index(down) * n, NAMES.index(across) * n
        scale = self.columns[at : at + n, 0:1]
        label = self.columns[at : at + n, 1:2]
        power = products * scale * self.rows[0:1, to : to + n] - SHIFT
        mask = label == self.rows[1:2, to : to + n]
        if down == across:
            mask &= iota((n, n), 0) != iota((n, n), 1)
        values = jnp.where(mask, jnp.exp2(power), 0.0)
        self.add(across, jnp.sum(values, axis=0, keepdims=True))
        if down in ("u", "l", "u1", "l1") or (down, across) == ("b0h", "b0l"):
            side = jnp.zeros((n, LANES), jnp.float32)
            for lane in range(0, n, LANES):
                side += values[:, lane : lane + LANES]
            self.add(down, jnp.sum(side.T, axis=0, keepdims=True))

    def write(self):
        for k, name in enumerate(SUMS):
            values = self.sums.get(name)
            last = self.last[k : k + 1, :] if self.last is not None else None
            if values is None:
                values = jnp.zeros((1, self.out.shape[1]), jnp.float32) if last is None else last
            elif last is not None:
                values += last
            self.out[k : k + 1, :] = values


def masses_call(jobs, arrays, rows, columns, last=None):
    names = [name for name in NAMES if any(name in job for job in jobs)]

    def kernel(*refs):
        refs = list(refs)
        held = {name: refs.pop(0) for name in names}
        rows_ref, columns_ref = refs.pop(0), refs.pop(0)
        last_ref = refs.pop(0) if last is not None else None
        t = Terms(held, rows_ref, columns_ref, refs.pop(0), last_ref)
        for job in jobs:
            t.job(*job)
        t.write()

    operands = [arrays[name] for name in names] + [rows, columns]
    if last is not None:
        operands.append(last)
    n, width = operands[0].shape
    return call(
        kernel,
        jax.ShapeDtypeStruct((len(SUMS), n), jnp.float32),
        cost_estimate=pl.CostEstimate(
            flops=2 * len(jobs) * n * n * width,
            transcendentals=len(jobs) * n * n,
            bytes_accessed=2 * len(names) * n * width,
        ),
    )(*operands)


def weights_kernel(per_half, rank_ref, returned_ref, out_ref):
    peers, width = returned_ref.shape
    rank = rank_ref[...]
    n = rank.shape[1]
    slab = rank // (2 * per_half)
    member = rank % (2 * per_half)
    upper = member >= per_half
    returned = returned_ref[...]
    plane = iota((peers, n), 0) // QUAD
    beside = jnp.where(upper, slab + 1, slab - 1)
    beside_member = jnp.where(upper, member + per_half, member + 3 * per_half)

    def chosen(which, lane):
        picked = lax.dot_general(
            returned,
            (plane == which).astype(jnp.float32),
            TN,
            precision=lax.Precision.HIGHEST,
            preferred_element_type=jnp.float32,
        )
        return jnp.sum(
            jnp.where(iota((width, n), 0) == lane, picked, 0.0), axis=0, keepdims=True
        )

    mass = chosen(slab, member) + chosen(beside, beside_member)
    out_ref[...] = 1.0 / (1.0 + mass)


def xor_order(array, axis, bits):
    count = array.shape[axis]
    for k in range(count.bit_length() - 1):
        step = 1 << k
        shape = array.shape[:axis] + (count // (2 * step), 2, step) + array.shape[axis + 1 :]
        split = array.reshape(shape)
        split = jnp.where((bits >> k) & 1 == 1, jnp.flip(split, axis + 1), split)
        array = split.reshape(array.shape)
    return array


def shards(embeddings, position, cluster_ids):
    n, width = embeddings.shape
    peers = lax.axis_size("dev")
    me = lax.axis_index("dev")
    planes = peers // QUAD
    slab, lane = me // QUAD, me % QUAD
    per_half = n // (2 * planes)
    by_permutes = planes == 4
    pieces = 2 * planes if by_permutes else 1
    f32 = jnp.float32

    def swapped(rows_, bit):
        return lax.ppermute(rows_, "dev", [(i, i ^ bit) for i in range(peers)])

    def passed(rows_, by):
        pairs = [(i, i + by) for i in range(peers) if 0 <= i + by < peers]
        return lax.ppermute(rows_, "dev", pairs)

    def as_received(values, axis, plane):
        return xor_order(values, axis, plane) if by_permutes else values

    where_to = position.reshape(1, n)
    in_hbm = pl.BlockSpec(memory_space=pltpu.HBM)
    *arranged, rank = call(
        functools.partial(arrange_kernel, per_half, 2 * planes),
        [jax.ShapeDtypeStruct((n // pieces, width), embeddings.dtype)] * pieces
        + [jax.ShapeDtypeStruct((1, n), jnp.int32)],
        in_specs=[in_hbm, in_hbm],
        scratch_shapes=[
            pltpu.VMEM((1, n), jnp.int32),
            pltpu.VMEM((n, width), embeddings.dtype),
            pltpu.SemaphoreType.DMA((2,)),
        ],
    )(where_to, embeddings)
    if by_permutes:
        sent = [
            arranged[k] if k % planes == 0 else swapped(arranged[k], (k % planes) * QUAD)
            for k in range(pieces)
        ]
        upper = jnp.concatenate(sent[:planes], axis=0)
        lower = jnp.concatenate(sent[planes:], axis=0)
    else:
        lines = [[p * QUAD + q for p in range(planes)] for q in range(QUAD)]
        block = lax.all_to_all(
            arranged[0], "dev", split_axis=0, concat_axis=0, axis_index_groups=lines, tiled=True
        ).reshape(planes, 2, per_half, width)
        upper = block[:, 1].reshape(n // 2, width)
        lower = block[:, 0].reshape(n // 2, width)

    facts = call(functools.partial(facts_kernel, 2 * planes), jax.ShapeDtypeStruct((4, n), f32))(
        where_to, cluster_ids.reshape(1, n), rank, *arranged
    )
    seen = jnp.pad(facts[:2], ((0, 0), (per_half, per_half)))
    seen = jnp.stack(
        [seen[:, 2 * p * per_half : (2 * p + 4) * per_half] for p in range(planes)]
    ).reshape(planes, 1, 8 * per_half)
    facts = jnp.concatenate(
        [
            jnp.broadcast_to(seen, (planes, QUAD, 8 * per_half)),
            jnp.broadcast_to(facts[2], (planes, QUAD, n)),
        ],
        axis=2,
    )
    facts = lax.all_to_all(
        facts.reshape(peers, 8 * per_half + n), "dev", split_axis=0, concat_axis=0, tiled=True
    )
    ids = jnp.pad(facts[:, 8 * per_half :].reshape(peers * n), (MOST, MOST))
    ids = lax.dynamic_slice_in_dim(ids, slab * MOST, 3 * MOST, 0)
    near = facts[:, : 8 * per_half].reshape(planes, QUAD, 2, 4, per_half)
    near = xor_order(near, 1, lane).transpose(2, 1, 3, 0, 4)
    before = as_received(near[:, :2, 0], 2, slab - 1)
    after = as_received(near[:, :2, 3], 2, slab + 1)
    own = as_received(near[:, :3, 1:3], 3, slab)
    near = jnp.concatenate(
        [
            jnp.stack([own[:, :, 1], own[:, :, 0]], axis=2).reshape(2, 3 * n),
            jnp.stack([before, after], axis=2).reshape(2, 2 * n),
        ],
        axis=1,
    )
    total = 5 * n
    place = near[0].astype(jnp.int32) - (slab - 1) * MOST
    label = call(labels_kernel, jax.ShapeDtypeStruct((1, total), f32))(
        place.reshape(1, total), ids.reshape(3 * MOST // LANES, LANES)
    )[0]
    at = jnp.arange(total)
    absent = (at >= 3 * n) & jnp.where(at % n >= n // 2, slab == planes - 1, slab == 0)
    label = jnp.where(absent, -1.0, label)
    rows = jnp.stack([near[1], label])
    columns = jnp.stack([near[1] * SCALE, label], axis=1)

    arrays = {"b0h": upper, "b0l": lower}
    arrays["b2h"] = swapped(upper, 2)
    arrays["b1h"] = swapped(upper, 1)
    arrays["u"] = passed(upper, QUAD)
    arrays["l"] = passed(lower, -QUAD)
    arrays["b2l"] = swapped(lower, 2)
    arrays["b1l"] = swapped(lower, 1)
    arrays["u1"] = swapped(arrays["u"], 1)
    arrays["l1"] = swapped(arrays["l"], 1)

    first = [("b0h", "b0h"), ("b1h", "b0h"), ("b2h", "b0h"), ("b1h", "b2h")]
    second = [("b0l", "b0l"), ("b0h", "b0l"), ("b1h", "b0l"), ("b2h", "b0l")]
    second += [("b1l", "b0h"), ("b1l", "b0l"), ("b1l", "b2h")]
    second += [(u, b) for u in ("u", "u1") for b in ("b0h", "b0l", "b2h")]
    third = [("b2l", "b0h"), ("b2l", "b0l"), ("b1h", "b2l"), ("b1l", "b2l")]
    third += [("u", "b2l"), ("u1", "b2l"), ("l", "b0l"), ("l", "b2l")]
    fourth = [("l1", "b0l"), ("l1", "b2l")]
    masses = None
    for jobs in (first, second, third, fourth):
        masses = masses_call(jobs, arrays, rows, columns, masses)

    masses = masses.reshape(4, 2, planes, per_half)
    slabs = as_received(masses[:2], 2, slab)
    before = as_received(masses[2:, 0], 1, slab - 1)
    after = as_received(masses[2:, 1], 1, slab + 1)
    none = jnp.zeros_like(before[0])
    outgoing = jnp.stack(
        [
            jnp.stack([slabs[0, 1], none, slabs[1, 1], none]),
            jnp.stack([slabs[0, 0], none, slabs[1, 0], none]),
            jnp.stack([before[0], before[1], none, none]),
            jnp.stack([after[0], after[1], none, none]),
        ],
        axis=2,
    )
    outgoing = xor_order(outgoing, 0, lane).transpose(1, 0, 2, 3)
    returned = lax.all_to_all(
        outgoing.reshape(peers, 4 * per_half), "dev", split_axis=0, concat_axis=0, tiled=True
    )
    weight = call(
        functools.partial(weights_kernel, per_half), jax.ShapeDtypeStruct((1, n), f32)
    )(rank, returned)
    return weight.reshape(n)


def solution(mesh):
    return jax.shard_map(
        shards,
        mesh=mesh,
        in_specs=(P(("grp", "dev"), None), P(("grp", "dev")), P(("grp", "dev"))),
        out_specs=P(("grp", "dev")),
        check_vma=False,
    )
```

```python
import functools
import math

import jax
import jax.numpy as jnp
from jax import lax
from jax.experimental import pallas as pl
from jax.experimental.pallas import tpu as pltpu
from jax.sharding import PartitionSpec as P

MOST = 2048
HALF = MOST // 2
SIMILARITY_CUTOFF = 0.9
SOFTMAX_HEAT = 0.02
SCALE = math.log2(math.e) / SOFTMAX_HEAT
SHIFT = SIMILARITY_CUTOFF * SCALE
QUAD = 4
CHUNK = 256
LANES = 128
VMEM_LIMIT = 16 * 1024 * 1024

NT = (((1,), (1,)), ((), ()))
TN = (((0,), (0,)), ((), ()))


def iota(shape, dim):
    return lax.broadcasted_iota(jnp.int32, shape, dim)


def call(kernel, out_shape, limit=VMEM_LIMIT, **extra):
    return pl.pallas_call(
        kernel,
        out_shape=out_shape,
        compiler_params=pltpu.CompilerParams(vmem_limit_bytes=limit),
        **extra,
    )


def arrange_kernel(per_half, halves, position_hbm, rows_hbm, *refs):
    *outs, rank_ref, place, rows, sems = refs
    copies = [
        pltpu.make_async_copy(position_hbm, place, sems.at[0]),
        pltpu.make_async_copy(rows_hbm, rows, sems.at[1]),
    ]
    for copy in copies:
        copy.start()
    n = rows.shape[0]
    earlier = (iota((n, n), 0) < iota((n, n), 1)).astype(jnp.bfloat16)
    copies[0].wait()
    half = place[...] // HALF
    kinds = iota((halves, n), 0) == half
    counts = jnp.dot(kinds.astype(jnp.bfloat16), earlier, preferred_element_type=jnp.float32)
    count = jnp.sum(jnp.where(kinds, counts, 0.0), axis=0, keepdims=True).astype(jnp.int32)
    rank_ref[...] = half * per_half + count
    rank = half * per_half + count
    if len(outs) > 1:
        plane = (half // 2) ^ (lax.axis_index("dev") // QUAD)
        rank = (2 * plane + 1 - half % 2) * per_half + count
    pick = (iota((n, n), 0) == rank).astype(jnp.bfloat16)
    copies[1].wait()
    picked = jnp.dot(pick, rows[...], preferred_element_type=jnp.float32)
    at = 0
    for out in outs:
        out[...] = picked[at : at + out.shape[0], :].astype(out.dtype)
        at += out.shape[0]


def facts_kernel(position_ref, ids_ref, rank_ref, rows_ref, out_ref):
    n = rows_ref.shape[0]
    pick = iota((n, n), 0) == rank_ref[...]
    eye = iota((n, n), 0) == iota((n, n), 1)
    wide = rows_ref[...].astype(jnp.float32)
    inverse = lax.rsqrt(jnp.sum(wide * wide, axis=1, keepdims=True) + 1e-06)
    inverse = jnp.sum(jnp.where(eye, inverse, 0.0), axis=0, keepdims=True)
    for k, values in enumerate((position_ref[...].astype(jnp.float32), inverse)):
        column = jnp.sum(jnp.where(pick, values, 0.0), axis=1, keepdims=True)
        out_ref[k : k + 1, :] = jnp.sum(jnp.where(eye, column, 0.0), axis=0, keepdims=True)
    out_ref[2:3, :] = ids_ref[...].astype(jnp.float32)
    out_ref[3:4, :] = jnp.zeros((1, n), jnp.float32)


def labels_kernel(place_ref, table_ref, out_ref):
    place = place_ref[...]
    depth = table_ref.shape[0]
    n = place.shape[1]
    table = table_ref[...]
    high = jnp.floor(table * (1.0 / 256.0))
    low = table - high * 256.0
    line = (iota((depth, n), 0) == place // LANES).astype(jnp.bfloat16)
    high = lax.dot_general(
        high.astype(jnp.bfloat16), line, TN, preferred_element_type=jnp.float32
    )
    low = lax.dot_general(
        low.astype(jnp.bfloat16), line, TN, preferred_element_type=jnp.float32
    )
    here = iota((LANES, n), 0) == place % LANES
    out_ref[...] = jnp.sum(jnp.where(here, high * 256.0 + low, 0.0), axis=0, keepdims=True)


NAMES = ("b0h", "b0l", "b1h", "b1l", "b2h", "b2l", "u", "l", "u1", "l1")
SUMS = ("b0h", "b0l", "b2h", "b2l", "u", "l", "u1", "l1")


class Terms:
    def __init__(self, arrays, rows_ref, columns_ref, out_ref, last_ref):
        self.arrays, self.rows, self.columns, self.out = arrays, rows_ref, columns_ref, out_ref
        self.last = last_ref
        self.sums = {}

    def add(self, name, values):
        self.sums[name] = self.sums[name] + values if name in self.sums else values

    def job(self, down, across):
        n = self.arrays[down].shape[0]
        products = lax.dot_general(
            self.arrays[down][...],
            self.arrays[across][...],
            NT,
            preferred_element_type=jnp.float32,
        )
        at, to = NAMES.index(down) * n, NAMES.index(across) * n
        scale = self.columns[at : at + n, 0:1]
        label = self.columns[at : at + n, 1:2]
        power = products * scale * self.rows[0:1, to : to + n] - SHIFT
        mask = label == self.rows[1:2, to : to + n]
        if down == across:
            mask &= iota((n, n), 0) != iota((n, n), 1)
        values = jnp.where(mask, jnp.exp2(power), 0.0)
        self.add(across, jnp.sum(values, axis=0, keepdims=True))
        if down in ("u", "l", "u1", "l1") or (down, across) == ("b0h", "b0l"):
            side = jnp.zeros((n, LANES), jnp.float32)
            for lane in range(0, n, LANES):
                side += values[:, lane : lane + LANES]
            self.add(down, jnp.sum(side.T, axis=0, keepdims=True))

    def write(self):
        for k, name in enumerate(SUMS):
            values = self.sums.get(name)
            last = self.last[k : k + 1, :] if self.last is not None else None
            if values is None:
                values = jnp.zeros((1, self.out.shape[1]), jnp.float32) if last is None else last
            elif last is not None:
                values += last
            self.out[k : k + 1, :] = values


def masses_call(jobs, arrays, rows, columns, last=None):
    names = [name for name in NAMES if any(name in job for job in jobs)]

    def kernel(*refs):
        refs = list(refs)
        held = {name: refs.pop(0) for name in names}
        rows_ref, columns_ref = refs.pop(0), refs.pop(0)
        last_ref = refs.pop(0) if last is not None else None
        t = Terms(held, rows_ref, columns_ref, refs.pop(0), last_ref)
        for job in jobs:
            t.job(*job)
        t.write()

    operands = [arrays[name] for name in names] + [rows, columns]
    if last is not None:
        operands.append(last)
    n, width = operands[0].shape
    return call(
        kernel,
        jax.ShapeDtypeStruct((len(SUMS), n), jnp.float32),
        cost_estimate=pl.CostEstimate(flops=0, transcendentals=0, bytes_accessed=0),
    )(*operands)


def weights_kernel(per_half, rank_ref, returned_ref, out_ref):
    peers, width = returned_ref.shape
    rank = rank_ref[...]
    n = rank.shape[1]
    slab = rank // (2 * per_half)
    member = rank % (2 * per_half)
    upper = member >= per_half
    returned = returned_ref[...]
    plane = iota((peers, n), 0) // QUAD
    beside = jnp.where(upper, slab + 1, slab - 1)
    beside_member = jnp.where(upper, member + per_half, member + 3 * per_half)

    def chosen(which, lane):
        picked = lax.dot_general(
            returned,
            (plane == which).astype(jnp.float32),
            TN,
            precision=lax.Precision.HIGHEST,
            preferred_element_type=jnp.float32,
        )
        return jnp.sum(
            jnp.where(iota((width, n), 0) == lane, picked, 0.0), axis=0, keepdims=True
        )

    mass = chosen(slab, member) + chosen(beside, beside_member)
    out_ref[...] = 1.0 / (1.0 + mass)


def xor_order(array, axis, bits):
    count = array.shape[axis]
    for k in range(count.bit_length() - 1):
        step = 1 << k
        shape = array.shape[:axis] + (count // (2 * step), 2, step) + array.shape[axis + 1 :]
        split = array.reshape(shape)
        split = jnp.where((bits >> k) & 1 == 1, jnp.flip(split, axis + 1), split)
        array = split.reshape(array.shape)
    return array


def shards(embeddings, position, cluster_ids):
    n, width = embeddings.shape
    peers = lax.axis_size("dev")
    me = lax.axis_index("dev")
    planes = peers // QUAD
    slab, lane = me // QUAD, me % QUAD
    per_half = n // (2 * planes)
    by_permutes = planes == 4
    pieces = [per_half] * 2 + [2 * per_half] + [per_half] * 4 if by_permutes else [n]
    f32 = jnp.float32

    def swapped(rows_, bit):
        return lax.ppermute(rows_, "dev", [(i, i ^ bit) for i in range(peers)])

    def passed(rows_, by):
        pairs = [(i, i + by) for i in range(peers) if 0 <= i + by < peers]
        return lax.ppermute(rows_, "dev", pairs)

    def as_received(values, axis, plane):
        return xor_order(values, axis, plane) if by_permutes else values

    where_to = position.reshape(1, n)
    in_hbm = pl.BlockSpec(memory_space=pltpu.HBM)
    *arranged, rank = call(
        functools.partial(arrange_kernel, per_half, 2 * planes),
        [jax.ShapeDtypeStruct((size, width), embeddings.dtype) for size in pieces]
        + [jax.ShapeDtypeStruct((1, n), jnp.int32)],
        limit=60 * 1024 * 1024,
        in_specs=[in_hbm, in_hbm],
        scratch_shapes=[
            pltpu.VMEM((1, n), jnp.int32),
            pltpu.VMEM((n, width), embeddings.dtype),
            pltpu.SemaphoreType.DMA((2,)),
        ],
    )(where_to, embeddings)
    if by_permutes:
        own_upper, own_lower, to_1, upper_2, lower_2, upper_3, lower_3 = arranged
        upper_3 = swapped(upper_3, 3 * QUAD)
        upper_2 = swapped(upper_2, 2 * QUAD)
        both_1 = swapped(to_1, QUAD)
        lower_3 = swapped(lower_3, 3 * QUAD)
        lower_2 = swapped(lower_2, 2 * QUAD)
        upper = jnp.concatenate([own_upper, both_1[:per_half], upper_2, upper_3], axis=0)
        lower = jnp.concatenate([own_lower, both_1[per_half:], lower_2, lower_3], axis=0)
    else:
        lines = [[p * QUAD + q for p in range(planes)] for q in range(QUAD)]
        block = lax.all_to_all(
            arranged[0], "dev", split_axis=0, concat_axis=0, axis_index_groups=lines, tiled=True
        ).reshape(planes, 2, per_half, width)
        upper = block[:, 1].reshape(n // 2, width)
        lower = block[:, 0].reshape(n // 2, width)

    facts = call(facts_kernel, jax.ShapeDtypeStruct((4, n), f32))(
        where_to, cluster_ids.reshape(1, n), rank, embeddings
    )
    seen = jnp.pad(facts[:2], ((0, 0), (per_half, per_half)))
    seen = jnp.stack(
        [seen[:, 2 * p * per_half : (2 * p + 4) * per_half] for p in range(planes)]
    ).reshape(planes, 1, 8 * per_half)
    facts = jnp.concatenate(
        [
            jnp.broadcast_to(seen, (planes, QUAD, 8 * per_half)),
            jnp.broadcast_to(facts[2], (planes, QUAD, n)),
        ],
        axis=2,
    )
    facts = lax.all_to_all(
        facts.reshape(peers, 8 * per_half + n), "dev", split_axis=0, concat_axis=0, tiled=True
    )
    ids = jnp.pad(facts[:, 8 * per_half :].reshape(peers * n), (MOST, MOST))
    ids = lax.dynamic_slice_in_dim(ids, slab * MOST, 3 * MOST, 0)
    near = facts[:, : 8 * per_half].reshape(planes, QUAD, 2, 4, per_half)
    near = xor_order(near, 1, lane).transpose(2, 1, 3, 0, 4)
    before = as_received(near[:, :2, 0], 2, slab - 1)
    after = as_received(near[:, :2, 3], 2, slab + 1)
    own = as_received(near[:, :3, 1:3], 3, slab)
    near = jnp.concatenate(
        [
            jnp.stack([own[:, :, 1], own[:, :, 0]], axis=2).reshape(2, 3 * n),
            jnp.stack([before, after], axis=2).reshape(2, 2 * n),
        ],
        axis=1,
    )
    total = 5 * n
    place = near[0].astype(jnp.int32) - (slab - 1) * MOST
    label = call(labels_kernel, jax.ShapeDtypeStruct((1, total), f32))(
        place.reshape(1, total), ids.reshape(3 * MOST // LANES, LANES)
    )[0]
    at = jnp.arange(total)
    absent = (at >= 3 * n) & jnp.where(at % n >= n // 2, slab == planes - 1, slab == 0)
    label = jnp.where(absent, -1.0, label)
    rows = jnp.stack([near[1], label])
    columns = jnp.stack([near[1] * SCALE, label], axis=1)

    def after_all(value, *others):
        return lax.optimization_barrier((value, *others))[0]

    arrays = {"b0h": upper}
    arrays["b1h"] = swapped(upper, 1)
    arrays["b2h"] = swapped(upper, 2)
    lower = after_all(lower, arrays["b1h"])
    arrays["b0l"] = lower
    arrays["u"] = passed(upper, QUAD)
    arrays["b2l"] = swapped(lower, 2)
    arrays["l"] = passed(lower, -QUAD)
    arrays["b1l"] = swapped(lower, 1)

    def masses_after(jobs, last=None):
        return masses_call(jobs, arrays, rows, columns, last)

    masses = masses_after(
        [("b0h", "b0h"), ("b1h", "b0h"), ("b2h", "b0h"), ("b1h", "b2h")]
        + [("b0l", "b0l"), ("b0h", "b0l"), ("b1h", "b0l"), ("b2h", "b0l")]
        + [("b1l", "b0h"), ("b1l", "b0l"), ("b1l", "b2h")]
    )
    arrays["u1"] = swapped(arrays["u"], 1)
    masses = masses_after([(u, b) for u in ("u", "u1") for b in ("b0h", "b0l", "b2h")], masses)
    arrays["l1"] = swapped(after_all(arrays["l"], masses, arrays["b2l"]), 1)
    masses = masses_after(
        [("b2l", "b0h"), ("b2l", "b0l"), ("b1h", "b2l"), ("b1l", "b2l")]
        + [("u", "b2l"), ("u1", "b2l"), ("l", "b0l"), ("l", "b2l")],
        masses,
    )
    masses = masses_after([("l1", "b0l"), ("l1", "b2l")], masses)

    masses = masses.reshape(4, 2, planes, per_half)
    slabs = as_received(masses[:2], 2, slab)
    before = as_received(masses[2:, 0], 1, slab - 1)
    after = as_received(masses[2:, 1], 1, slab + 1)
    none = jnp.zeros_like(before[0])
    outgoing = jnp.stack(
        [
            jnp.stack([slabs[0, 1], none, slabs[1, 1], none]),
            jnp.stack([slabs[0, 0], none, slabs[1, 0], none]),
            jnp.stack([before[0], before[1], none, none]),
            jnp.stack([after[0], after[1], none, none]),
        ],
        axis=2,
    )
    outgoing = xor_order(outgoing, 0, lane).transpose(1, 0, 2, 3)
    returned = lax.all_to_all(
        outgoing.reshape(peers, 4 * per_half), "dev", split_axis=0, concat_axis=0, tiled=True
    )
    weight = call(
        functools.partial(weights_kernel, per_half), jax.ShapeDtypeStruct((1, n), f32)
    )(rank, returned)
    return weight.reshape(n)


def solution(mesh):
    return jax.shard_map(
        shards,
        mesh=mesh,
        in_specs=(P(("grp", "dev"), None), P(("grp", "dev")), P(("grp", "dev"))),
        out_specs=P(("grp", "dev")),
        check_vma=False,
    )
```

```python
import functools
import math

import jax
import jax.numpy as jnp
from jax import lax
from jax.experimental import pallas as pl
from jax.experimental.pallas import tpu as pltpu
from jax.sharding import PartitionSpec as P

MOST = 2048
HALF = MOST // 2
SIMILARITY_CUTOFF = 0.9
SOFTMAX_HEAT = 0.02
SCALE = math.log2(math.e) / SOFTMAX_HEAT
SHIFT = SIMILARITY_CUTOFF * SCALE
QUAD = 4
CHUNK = 256
LANES = 128
VMEM_LIMIT = 16 * 1024 * 1024

NT = (((1,), (1,)), ((), ()))
TN = (((0,), (0,)), ((), ()))


def iota(shape, dim):
    return lax.broadcasted_iota(jnp.int32, shape, dim)


def call(kernel, out_shape, limit=VMEM_LIMIT, **extra):
    return pl.pallas_call(
        kernel,
        out_shape=out_shape,
        compiler_params=pltpu.CompilerParams(vmem_limit_bytes=limit),
        **extra,
    )


def arrange_kernel(per_half, halves, position_hbm, rows_hbm, *refs):
    *outs, rank_ref, place, rows, sems = refs
    copies = [
        pltpu.make_async_copy(position_hbm, place, sems.at[0]),
        pltpu.make_async_copy(rows_hbm, rows, sems.at[1]),
    ]
    for copy in copies:
        copy.start()
    n = rows.shape[0]
    earlier = (iota((n, n), 0) < iota((n, n), 1)).astype(jnp.bfloat16)
    copies[0].wait()
    half = place[...] // HALF
    kinds = iota((halves, n), 0) == half
    counts = jnp.dot(kinds.astype(jnp.bfloat16), earlier, preferred_element_type=jnp.float32)
    count = jnp.sum(jnp.where(kinds, counts, 0.0), axis=0, keepdims=True).astype(jnp.int32)
    rank_ref[...] = half * per_half + count
    rank = half * per_half + count
    if len(outs) > 1:
        plane = (half // 2) ^ (lax.axis_index("dev") // QUAD)
        rank = (2 * plane + 1 - half % 2) * per_half + count
    pick = (iota((n, n), 0) == rank).astype(jnp.bfloat16)
    copies[1].wait()
    picked = jnp.dot(pick, rows[...], preferred_element_type=jnp.float32)
    at = 0
    for out in outs:
        out[...] = picked[at : at + out.shape[0], :].astype(out.dtype)
        at += out.shape[0]


def facts_kernel(per_half, position_ref, ids_ref, rank_ref, *refs):
    *pieces, out_ref = refs
    n = position_ref.shape[1]
    pick = iota((n, n), 0) == rank_ref[...]
    where_to = position_ref[...].astype(jnp.float32)
    column = jnp.sum(jnp.where(pick, where_to, 0.0), axis=1, keepdims=True)
    eye = iota((n, n), 0) == iota((n, n), 1)
    out_ref[0:1, :] = jnp.sum(jnp.where(eye, column, 0.0), axis=0, keepdims=True)
    total = jnp.zeros((1, n), jnp.float32)
    k = 0
    for piece in pieces:
        size = n if len(pieces) == 1 else per_half
        for start in range(0, piece.shape[0], size):
            wide = piece[start : start + size, :].astype(jnp.float32)
            inverse = lax.rsqrt(jnp.sum(wide * wide, axis=1, keepdims=True) + 1e-06)
            first = 0
            if len(pieces) > 1:
                plane = (k // 2) ^ (lax.axis_index("dev") // QUAD)
                first = (2 * plane + 1 - k % 2) * per_half
            here = iota((size, n), 0) + first == iota((size, n), 1)
            total += jnp.sum(jnp.where(here, inverse, 0.0), axis=0, keepdims=True)
            k += 1
    out_ref[1:2, :] = total
    out_ref[2:3, :] = ids_ref[...].astype(jnp.float32)
    out_ref[3:4, :] = jnp.zeros((1, n), jnp.float32)


def labels_kernel(place_ref, table_ref, out_ref):
    place = place_ref[...]
    depth = table_ref.shape[0]
    n = place.shape[1]
    table = table_ref[...]
    high = jnp.floor(table * (1.0 / 256.0))
    low = table - high * 256.0
    line = (iota((depth, n), 0) == place // LANES).astype(jnp.bfloat16)
    high = lax.dot_general(
        high.astype(jnp.bfloat16), line, TN, preferred_element_type=jnp.float32
    )
    low = lax.dot_general(
        low.astype(jnp.bfloat16), line, TN, preferred_element_type=jnp.float32
    )
    here = iota((LANES, n), 0) == place % LANES
    out_ref[...] = jnp.sum(jnp.where(here, high * 256.0 + low, 0.0), axis=0, keepdims=True)


NAMES = ("b0h", "b0l", "b1h", "b1l", "b2h", "b2l", "u", "l", "u1", "l1")
SUMS = ("b0h", "b0l", "b2h", "b2l", "u", "l", "u1", "l1")


class Terms:
    def __init__(self, arrays, rows_ref, columns_ref, out_ref, last_ref):
        self.arrays, self.rows, self.columns, self.out = arrays, rows_ref, columns_ref, out_ref
        self.last = last_ref
        self.sums = {}

    def add(self, name, values):
        self.sums[name] = self.sums[name] + values if name in self.sums else values

    def job(self, down, across):
        n = self.arrays[down].shape[0]
        products = lax.dot_general(
            self.arrays[down][...],
            self.arrays[across][...],
            NT,
            preferred_element_type=jnp.float32,
        )
        at, to = NAMES.index(down) * n, NAMES.index(across) * n
        scale = self.columns[at : at + n, 0:1]
        label = self.columns[at : at + n, 1:2]
        power = products * scale * self.rows[0:1, to : to + n] - SHIFT
        mask = label == self.rows[1:2, to : to + n]
        if down == across:
            mask &= iota((n, n), 0) != iota((n, n), 1)
        values = jnp.where(mask, jnp.exp2(power), 0.0)
        self.add(across, jnp.sum(values, axis=0, keepdims=True))
        if down in ("u", "l", "u1", "l1") or (down, across) == ("b0h", "b0l"):
            side = jnp.zeros((n, LANES), jnp.float32)
            for lane in range(0, n, LANES):
                side += values[:, lane : lane + LANES]
            self.add(down, jnp.sum(side.T, axis=0, keepdims=True))

    def write(self):
        for k, name in enumerate(SUMS):
            values = self.sums.get(name)
            last = self.last[k : k + 1, :] if self.last is not None else None
            if values is None:
                values = jnp.zeros((1, self.out.shape[1]), jnp.float32) if last is None else last
            elif last is not None:
                values += last
            self.out[k : k + 1, :] = values


def masses_call(jobs, arrays, rows, columns, last=None):
    names = [name for name in NAMES if any(name in job for job in jobs)]

    def kernel(*refs):
        refs = list(refs)
        held = {name: refs.pop(0) for name in names}
        rows_ref, columns_ref = refs.pop(0), refs.pop(0)
        last_ref = refs.pop(0) if last is not None else None
        t = Terms(held, rows_ref, columns_ref, refs.pop(0), last_ref)
        for job in jobs:
            t.job(*job)
        t.write()

    operands = [arrays[name] for name in names] + [rows, columns]
    if last is not None:
        operands.append(last)
    n, width = operands[0].shape
    return call(
        kernel,
        jax.ShapeDtypeStruct((len(SUMS), n), jnp.float32),
        cost_estimate=pl.CostEstimate(flops=0, transcendentals=0, bytes_accessed=0),
    )(*operands)


def weights_kernel(per_half, rank_ref, returned_ref, out_ref):
    peers, width = returned_ref.shape
    rank = rank_ref[...]
    n = rank.shape[1]
    slab = rank // (2 * per_half)
    member = rank % (2 * per_half)
    upper = member >= per_half
    returned = returned_ref[...]
    plane = iota((peers, n), 0) // QUAD
    beside = jnp.where(upper, slab + 1, slab - 1)
    beside_member = jnp.where(upper, member + per_half, member + 3 * per_half)

    def chosen(which, lane):
        picked = lax.dot_general(
            returned,
            (plane == which).astype(jnp.float32),
            TN,
            precision=lax.Precision.HIGHEST,
            preferred_element_type=jnp.float32,
        )
        return jnp.sum(
            jnp.where(iota((width, n), 0) == lane, picked, 0.0), axis=0, keepdims=True
        )

    mass = chosen(slab, member) + chosen(beside, beside_member)
    out_ref[...] = 1.0 / (1.0 + mass)


def xor_order(array, axis, bits):
    count = array.shape[axis]
    for k in range(count.bit_length() - 1):
        step = 1 << k
        shape = array.shape[:axis] + (count // (2 * step), 2, step) + array.shape[axis + 1 :]
        split = array.reshape(shape)
        split = jnp.where((bits >> k) & 1 == 1, jnp.flip(split, axis + 1), split)
        array = split.reshape(array.shape)
    return array


def shards(embeddings, position, cluster_ids):
    n, width = embeddings.shape
    peers = lax.axis_size("dev")
    me = lax.axis_index("dev")
    planes = peers // QUAD
    slab, lane = me // QUAD, me % QUAD
    per_half = n // (2 * planes)
    by_permutes = planes == 4
    pieces = [per_half] * 2 + [2 * per_half] + [per_half] * 4 if by_permutes else [n]
    f32 = jnp.float32

    def swapped(rows_, bit):
        return lax.ppermute(rows_, "dev", [(i, i ^ bit) for i in range(peers)])

    def passed(rows_, by):
        pairs = [(i, i + by) for i in range(peers) if 0 <= i + by < peers]
        return lax.ppermute(rows_, "dev", pairs)

    def as_received(values, axis, plane):
        return xor_order(values, axis, plane) if by_permutes else values

    where_to = position.reshape(1, n)
    in_hbm = pl.BlockSpec(memory_space=pltpu.HBM)
    *arranged, rank = call(
        functools.partial(arrange_kernel, per_half, 2 * planes),
        [jax.ShapeDtypeStruct((size, width), embeddings.dtype) for size in pieces]
        + [jax.ShapeDtypeStruct((1, n), jnp.int32)],
        in_specs=[in_hbm, in_hbm],
        scratch_shapes=[
            pltpu.VMEM((1, n), jnp.int32),
            pltpu.VMEM((n, width), embeddings.dtype),
            pltpu.SemaphoreType.DMA((2,)),
        ],
    )(where_to, embeddings)
    if by_permutes:
        own_upper, own_lower, to_1, upper_2, lower_2, upper_3, lower_3 = arranged
        upper_3 = swapped(upper_3, 3 * QUAD)
        upper_2 = swapped(upper_2, 2 * QUAD)
        both_1 = swapped(to_1, QUAD)
        lower_3 = swapped(lower_3, 3 * QUAD)
        lower_2 = swapped(lower_2, 2 * QUAD)
        upper = jnp.concatenate([own_upper, both_1[:per_half], upper_2, upper_3], axis=0)
        lower = jnp.concatenate([own_lower, both_1[per_half:], lower_2, lower_3], axis=0)
    else:
        lines = [[p * QUAD + q for p in range(planes)] for q in range(QUAD)]
        block = lax.all_to_all(
            arranged[0], "dev", split_axis=0, concat_axis=0, axis_index_groups=lines, tiled=True
        ).reshape(planes, 2, per_half, width)
        upper = block[:, 1].reshape(n // 2, width)
        lower = block[:, 0].reshape(n // 2, width)

    facts = call(
        functools.partial(facts_kernel, per_half), jax.ShapeDtypeStruct((4, n), f32)
    )(where_to, cluster_ids.reshape(1, n), rank, *arranged)
    seen = jnp.pad(facts[:2], ((0, 0), (per_half, per_half)))
    seen = jnp.stack(
        [seen[:, 2 * p * per_half : (2 * p + 4) * per_half] for p in range(planes)]
    ).reshape(planes, 1, 8 * per_half)
    facts = jnp.concatenate(
        [
            jnp.broadcast_to(seen, (planes, QUAD, 8 * per_half)),
            jnp.broadcast_to(facts[2], (planes, QUAD, n)),
        ],
        axis=2,
    )
    facts = lax.all_to_all(
        facts.reshape(peers, 8 * per_half + n), "dev", split_axis=0, concat_axis=0, tiled=True
    )
    ids = jnp.pad(facts[:, 8 * per_half :].reshape(peers * n), (MOST, MOST))
    ids = lax.dynamic_slice_in_dim(ids, slab * MOST, 3 * MOST, 0)
    near = facts[:, : 8 * per_half].reshape(planes, QUAD, 2, 4, per_half)
    near = xor_order(near, 1, lane).transpose(2, 1, 3, 0, 4)
    before = as_received(near[:, :2, 0], 2, slab - 1)
    after = as_received(near[:, :2, 3], 2, slab + 1)
    own = as_received(near[:, :3, 1:3], 3, slab)
    near = jnp.concatenate(
        [
            jnp.stack([own[:, :, 1], own[:, :, 0]], axis=2).reshape(2, 3 * n),
            jnp.stack([before, after], axis=2).reshape(2, 2 * n),
        ],
        axis=1,
    )
    total = 5 * n
    place = near[0].astype(jnp.int32) - (slab - 1) * MOST
    label = call(labels_kernel, jax.ShapeDtypeStruct((1, total), f32))(
        place.reshape(1, total), ids.reshape(3 * MOST // LANES, LANES)
    )[0]
    at = jnp.arange(total)
    absent = (at >= 3 * n) & jnp.where(at % n >= n // 2, slab == planes - 1, slab == 0)
    label = jnp.where(absent, -1.0, label)
    rows = jnp.stack([near[1], label])
    columns = jnp.stack([near[1] * SCALE, label], axis=1)

    def after_all(value, *others):
        return lax.optimization_barrier((value, *others))[0]

    arrays = {"b0h": upper}
    arrays["b2h"] = swapped(upper, 2)
    arrays["b1h"] = swapped(upper, 1)
    lower = after_all(lower, arrays["b1h"])
    arrays["b0l"] = lower
    arrays["u"] = passed(upper, QUAD)
    arrays["b2l"] = swapped(lower, 2)
    arrays["l"] = passed(lower, -QUAD)
    arrays["b1l"] = swapped(lower, 1)

    def masses_after(jobs, last=None):
        return masses_call(jobs, arrays, rows, columns, last)

    masses = masses_after(
        [("b0h", "b0h"), ("b1h", "b0h"), ("b2h", "b0h"), ("b1h", "b2h")]
        + [("b0l", "b0l"), ("b0h", "b0l"), ("b1h", "b0l"), ("b2h", "b0l")]
        + [("b1l", "b0h"), ("b1l", "b0l"), ("b1l", "b2h")]
    )
    arrays["u1"] = swapped(after_all(arrays['u'], arrays["b2h"]), 1)
    masses = masses_after([(u, b) for u in ("u", "u1") for b in ("b0h", "b0l", "b2h")], masses)
    arrays["l1"] = swapped(after_all(arrays["l"], masses, arrays["b2l"]), 1)
    masses = masses_after(
        [("b2l", "b0h"), ("b2l", "b0l"), ("b1h", "b2l"), ("b1l", "b2l")]
        + [("u", "b2l"), ("u1", "b2l"), ("l", "b0l"), ("l", "b2l")],
        masses,
    )
    masses = masses_after([("l1", "b0l"), ("l1", "b2l")], masses)

    masses = masses.reshape(4, 2, planes, per_half)
    slabs = as_received(masses[:2], 2, slab)
    before = as_received(masses[2:, 0], 1, slab - 1)
    after = as_received(masses[2:, 1], 1, slab + 1)
    none = jnp.zeros_like(before[0])
    outgoing = jnp.stack(
        [
            jnp.stack([slabs[0, 1], none, slabs[1, 1], none]),
            jnp.stack([slabs[0, 0], none, slabs[1, 0], none]),
            jnp.stack([before[0], before[1], none, none]),
            jnp.stack([after[0], after[1], none, none]),
        ],
        axis=2,
    )
    outgoing = xor_order(outgoing, 0, lane).transpose(1, 0, 2, 3)
    returned = lax.all_to_all(
        outgoing.reshape(peers, 4 * per_half), "dev", split_axis=0, concat_axis=0, tiled=True
    )
    weight = call(
        functools.partial(weights_kernel, per_half), jax.ShapeDtypeStruct((1, n), f32)
    )(rank, returned)
    return weight.reshape(n)


def solution(mesh):
    return jax.shard_map(
        shards,
        mesh=mesh,
        in_specs=(P(("grp", "dev"), None), P(("grp", "dev")), P(("grp", "dev"))),
        out_specs=P(("grp", "dev")),
        check_vma=False,
    )
```

```python
import functools
import math

import jax
import jax.numpy as jnp
from jax import lax
from jax.experimental import pallas as pl
from jax.experimental.pallas import tpu as pltpu
from jax.sharding import PartitionSpec as P

MOST = 2048
HALF = MOST // 2
SIMILARITY_CUTOFF = 0.9
SOFTMAX_HEAT = 0.02
SCALE = math.log2(math.e) / SOFTMAX_HEAT
SHIFT = SIMILARITY_CUTOFF * SCALE
QUAD = 4
CHUNK = 256
LANES = 128
VMEM_LIMIT = 16 * 1024 * 1024

NT = (((1,), (1,)), ((), ()))
TN = (((0,), (0,)), ((), ()))


def iota(shape, dim):
    return lax.broadcasted_iota(jnp.int32, shape, dim)


def call(kernel, out_shape, limit=VMEM_LIMIT, **extra):
    return pl.pallas_call(
        kernel,
        out_shape=out_shape,
        compiler_params=pltpu.CompilerParams(vmem_limit_bytes=limit),
        **extra,
    )


def arrange_kernel(per_half, halves, position_hbm, rows_hbm, *refs):
    *outs, rank_ref, place, rows, sems = refs
    copies = [
        pltpu.make_async_copy(position_hbm, place, sems.at[0]),
        pltpu.make_async_copy(rows_hbm, rows, sems.at[1]),
    ]
    for copy in copies:
        copy.start()
    n = rows.shape[0]
    earlier = (iota((n, n), 0) < iota((n, n), 1)).astype(jnp.bfloat16)
    copies[0].wait()
    half = place[...] // HALF
    kinds = iota((halves, n), 0) == half
    counts = jnp.dot(kinds.astype(jnp.bfloat16), earlier, preferred_element_type=jnp.float32)
    count = jnp.sum(jnp.where(kinds, counts, 0.0), axis=0, keepdims=True).astype(jnp.int32)
    rank_ref[...] = half * per_half + count
    rank = half * per_half + count
    if len(outs) > 1:
        plane = (half // 2) ^ (lax.axis_index("dev") // QUAD)
        rank = (2 * plane + 1 - half % 2) * per_half + count
    pick = (iota((n, n), 0) == rank).astype(jnp.bfloat16)
    copies[1].wait()
    picked = jnp.dot(pick, rows[...], preferred_element_type=jnp.float32)
    at = 0
    for out in outs:
        out[...] = picked[at : at + out.shape[0], :].astype(out.dtype)
        at += out.shape[0]


def facts_kernel(per_half, position_ref, ids_ref, rank_ref, *refs):
    *pieces, out_ref = refs
    n = position_ref.shape[1]
    pick = iota((n, n), 0) == rank_ref[...]
    where_to = position_ref[...].astype(jnp.float32)
    column = jnp.sum(jnp.where(pick, where_to, 0.0), axis=1, keepdims=True)
    eye = iota((n, n), 0) == iota((n, n), 1)
    out_ref[0:1, :] = jnp.sum(jnp.where(eye, column, 0.0), axis=0, keepdims=True)
    total = jnp.zeros((1, n), jnp.float32)
    k = 0
    for piece in pieces:
        size = n if len(pieces) == 1 else per_half
        for start in range(0, piece.shape[0], size):
            wide = piece[start : start + size, :].astype(jnp.float32)
            inverse = lax.rsqrt(jnp.sum(wide * wide, axis=1, keepdims=True) + 1e-06)
            first = 0
            if len(pieces) > 1:
                plane = (k // 2) ^ (lax.axis_index("dev") // QUAD)
                first = (2 * plane + 1 - k % 2) * per_half
            here = iota((size, n), 0) + first == iota((size, n), 1)
            total += jnp.sum(jnp.where(here, inverse, 0.0), axis=0, keepdims=True)
            k += 1
    out_ref[1:2, :] = total
    out_ref[2:3, :] = ids_ref[...].astype(jnp.float32)
    out_ref[3:4, :] = jnp.zeros((1, n), jnp.float32)


def labels_kernel(place_ref, table_ref, out_ref):
    place = place_ref[...]
    depth = table_ref.shape[0]
    n = place.shape[1]
    table = table_ref[...]
    high = jnp.floor(table * (1.0 / 256.0))
    low = table - high * 256.0
    line = (iota((depth, n), 0) == place // LANES).astype(jnp.bfloat16)
    high = lax.dot_general(
        high.astype(jnp.bfloat16), line, TN, preferred_element_type=jnp.float32
    )
    low = lax.dot_general(
        low.astype(jnp.bfloat16), line, TN, preferred_element_type=jnp.float32
    )
    here = iota((LANES, n), 0) == place % LANES
    out_ref[...] = jnp.sum(jnp.where(here, high * 256.0 + low, 0.0), axis=0, keepdims=True)


NAMES = ("b0h", "b0l", "b1h", "b1l", "b2h", "b2l", "u", "l", "u1", "l1")
SUMS = ("b0h", "b0l", "b2h", "b2l", "u", "l", "u1", "l1")


class Terms:
    def __init__(self, arrays, rows_ref, columns_ref, out_ref, last_ref):
        self.arrays, self.rows, self.columns, self.out = arrays, rows_ref, columns_ref, out_ref
        self.last = last_ref
        self.sums = {}

    def add(self, name, values):
        self.sums[name] = self.sums[name] + values if name in self.sums else values

    def job(self, down, across):
        n = self.arrays[down].shape[0]
        products = lax.dot_general(
            self.arrays[down][...],
            self.arrays[across][...],
            NT,
            preferred_element_type=jnp.float32,
        )
        at, to = NAMES.index(down) * n, NAMES.index(across) * n
        scale = self.columns[at : at + n, 0:1]
        label = self.columns[at : at + n, 1:2]
        power = products * scale * self.rows[0:1, to : to + n] - SHIFT
        mask = label == self.rows[1:2, to : to + n]
        if down == across:
            mask &= iota((n, n), 0) != iota((n, n), 1)
        values = jnp.where(mask, jnp.exp2(power), 0.0)
        self.add(across, jnp.sum(values, axis=0, keepdims=True))
        if down in ("u", "l", "u1", "l1") or (down, across) == ("b0h", "b0l"):
            side = jnp.zeros((n, LANES), jnp.float32)
            for lane in range(0, n, LANES):
                side += values[:, lane : lane + LANES]
            self.add(down, jnp.sum(side.T, axis=0, keepdims=True))

    def write(self):
        for k, name in enumerate(SUMS):
            values = self.sums.get(name)
            last = self.last[k : k + 1, :] if self.last is not None else None
            if values is None:
                values = jnp.zeros((1, self.out.shape[1]), jnp.float32) if last is None else last
            elif last is not None:
                values += last
            self.out[k : k + 1, :] = values


def masses_call(jobs, arrays, rows, columns, last=None):
    names = [name for name in NAMES if any(name in job for job in jobs)]

    def kernel(*refs):
        refs = list(refs)
        held = {name: refs.pop(0) for name in names}
        rows_ref, columns_ref = refs.pop(0), refs.pop(0)
        last_ref = refs.pop(0) if last is not None else None
        t = Terms(held, rows_ref, columns_ref, refs.pop(0), last_ref)
        for job in jobs:
            t.job(*job)
        t.write()

    operands = [arrays[name] for name in names] + [rows, columns]
    if last is not None:
        operands.append(last)
    n, width = operands[0].shape
    return call(
        kernel,
        jax.ShapeDtypeStruct((len(SUMS), n), jnp.float32),
        cost_estimate=pl.CostEstimate(flops=0, transcendentals=0, bytes_accessed=0),
    )(*operands)


def weights_kernel(per_half, rank_ref, returned_ref, out_ref):
    peers, width = returned_ref.shape
    rank = rank_ref[...]
    n = rank.shape[1]
    slab = rank // (2 * per_half)
    member = rank % (2 * per_half)
    upper = member >= per_half
    returned = returned_ref[...]
    plane = iota((peers, n), 0) // QUAD
    beside = jnp.where(upper, slab + 1, slab - 1)
    beside_member = jnp.where(upper, member + per_half, member + 3 * per_half)

    def chosen(which, lane):
        picked = lax.dot_general(
            returned,
            (plane == which).astype(jnp.float32),
            TN,
            precision=lax.Precision.HIGHEST,
            preferred_element_type=jnp.float32,
        )
        return jnp.sum(
            jnp.where(iota((width, n), 0) == lane, picked, 0.0), axis=0, keepdims=True
        )

    mass = chosen(slab, member) + chosen(beside, beside_member)
    out_ref[...] = 1.0 / (1.0 + mass)


def xor_order(array, axis, bits):
    count = array.shape[axis]
    for k in range(count.bit_length() - 1):
        step = 1 << k
        shape = array.shape[:axis] + (count // (2 * step), 2, step) + array.shape[axis + 1 :]
        split = array.reshape(shape)
        split = jnp.where((bits >> k) & 1 == 1, jnp.flip(split, axis + 1), split)
        array = split.reshape(array.shape)
    return array


def shards(embeddings, position, cluster_ids):
    n, width = embeddings.shape
    peers = lax.axis_size("dev")
    me = lax.axis_index("dev")
    planes = peers // QUAD
    slab, lane = me // QUAD, me % QUAD
    per_half = n // (2 * planes)
    by_permutes = planes == 4
    pieces = [per_half] * 2 + [2 * per_half] + [per_half] * 4 if by_permutes else [n]
    f32 = jnp.float32

    def swapped(rows_, bit):
        return lax.ppermute(rows_, "dev", [(i, i ^ bit) for i in range(peers)])

    def passed(rows_, by):
        pairs = [(i, i + by) for i in range(peers) if 0 <= i + by < peers]
        return lax.ppermute(rows_, "dev", pairs)

    def after_all(value, *others):
        return lax.optimization_barrier((value, *others))[0]

    def as_received(values, axis, plane):
        return xor_order(values, axis, plane) if by_permutes else values

    where_to = position.reshape(1, n)
    in_hbm = pl.BlockSpec(memory_space=pltpu.HBM)
    *arranged, rank = call(
        functools.partial(arrange_kernel, per_half, 2 * planes),
        [jax.ShapeDtypeStruct((size, width), embeddings.dtype) for size in pieces]
        + [jax.ShapeDtypeStruct((1, n), jnp.int32)],
        in_specs=[in_hbm, in_hbm],
        scratch_shapes=[
            pltpu.VMEM((1, n), jnp.int32),
            pltpu.VMEM((n, width), embeddings.dtype),
            pltpu.SemaphoreType.DMA((2,)),
        ],
    )(where_to, embeddings)
    if by_permutes:
        own_upper, own_lower, to_1, upper_2, lower_2, upper_3, lower_3 = arranged
        upper_3 = swapped(upper_3, 3 * QUAD)
        upper_2 = swapped(upper_2, 2 * QUAD)
        both_1 = swapped(to_1, QUAD)
        lower_3 = swapped(lower_3, 3 * QUAD)
        lower_2 = swapped(lower_2, 2 * QUAD)
        upper = jnp.concatenate([own_upper, both_1[:per_half], upper_2, upper_3], axis=0)
        lower = jnp.concatenate([own_lower, both_1[per_half:], lower_2, lower_3], axis=0)
    else:
        lines = [[p * QUAD + q for p in range(planes)] for q in range(QUAD)]
        block = lax.all_to_all(
            arranged[0], "dev", split_axis=0, concat_axis=0, axis_index_groups=lines, tiled=True
        ).reshape(planes, 2, per_half, width)
        upper = block[:, 1].reshape(n // 2, width)
        lower = block[:, 0].reshape(n // 2, width)

    facts = call(
        functools.partial(facts_kernel, per_half), jax.ShapeDtypeStruct((4, n), f32)
    )(where_to, cluster_ids.reshape(1, n), after_all(rank, both_1 if by_permutes else block), *arranged)
    seen = jnp.pad(facts[:2], ((0, 0), (per_half, per_half)))
    seen = jnp.stack(
        [seen[:, 2 * p * per_half : (2 * p + 4) * per_half] for p in range(planes)]
    ).reshape(planes, 1, 8 * per_half)
    facts = jnp.concatenate(
        [
            jnp.broadcast_to(seen, (planes, QUAD, 8 * per_half)),
            jnp.broadcast_to(facts[2], (planes, QUAD, n)),
        ],
        axis=2,
    )
    facts = lax.all_to_all(
        facts.reshape(peers, 8 * per_half + n), "dev", split_axis=0, concat_axis=0, tiled=True
    )
    ids = jnp.pad(facts[:, 8 * per_half :].reshape(peers * n), (MOST, MOST))
    ids = lax.dynamic_slice_in_dim(ids, slab * MOST, 3 * MOST, 0)
    near = facts[:, : 8 * per_half].reshape(planes, QUAD, 2, 4, per_half)
    near = xor_order(near, 1, lane).transpose(2, 1, 3, 0, 4)
    before = as_received(near[:, :2, 0], 2, slab - 1)
    after = as_received(near[:, :2, 3], 2, slab + 1)
    own = as_received(near[:, :3, 1:3], 3, slab)
    near = jnp.concatenate(
        [
            jnp.stack([own[:, :, 1], own[:, :, 0]], axis=2).reshape(2, 3 * n),
            jnp.stack([before, after], axis=2).reshape(2, 2 * n),
        ],
        axis=1,
    )
    total = 5 * n
    place = near[0].astype(jnp.int32) - (slab - 1) * MOST
    label = call(labels_kernel, jax.ShapeDtypeStruct((1, total), f32))(
        place.reshape(1, total), ids.reshape(3 * MOST // LANES, LANES)
    )[0]
    at = jnp.arange(total)
    absent = (at >= 3 * n) & jnp.where(at % n >= n // 2, slab == planes - 1, slab == 0)
    label = jnp.where(absent, -1.0, label)
    rows = jnp.stack([near[1], label])
    columns = jnp.stack([near[1] * SCALE, label], axis=1)

    arrays = {"b0h": upper}
    arrays["b2h"] = swapped(upper, 2)
    arrays["b1h"] = swapped(upper, 1)
    lower = after_all(lower, arrays["b1h"])
    arrays["b0l"] = lower
    arrays["u"] = passed(upper, QUAD)
    arrays["b2l"] = swapped(lower, 2)
    arrays["l"] = passed(lower, -QUAD)
    arrays["b1l"] = swapped(lower, 1)

    def masses_after(jobs, last=None):
        return masses_call(jobs, arrays, rows, columns, last)

    masses = masses_after(
        [("b0h", "b0h"), ("b1h", "b0h"), ("b2h", "b0h"), ("b1h", "b2h")]
        + [("b0l", "b0l"), ("b0h", "b0l"), ("b1h", "b0l"), ("b2h", "b0l")]
        + [("b1l", "b0h"), ("b1l", "b0l"), ("b1l", "b2h")]
    )
    arrays["u1"] = swapped(after_all(arrays['u'], arrays["b2h"]), 1)
    masses = masses_after([(u, b) for u in ("u", "u1") for b in ("b0h", "b0l", "b2h")], masses)
    arrays["l1"] = swapped(after_all(arrays["l"], masses, arrays["b2l"]), 1)
    masses = masses_after(
        [("b2l", "b0h"), ("b2l", "b0l"), ("b1h", "b2l"), ("b1l", "b2l")]
        + [("u", "b2l"), ("u1", "b2l"), ("l", "b0l"), ("l", "b2l")],
        masses,
    )
    masses = masses_after([("l1", "b0l"), ("l1", "b2l")], masses)

    masses = masses.reshape(4, 2, planes, per_half)
    slabs = as_received(masses[:2], 2, slab)
    before = as_received(masses[2:, 0], 1, slab - 1)
    after = as_received(masses[2:, 1], 1, slab + 1)
    none = jnp.zeros_like(before[0])
    outgoing = jnp.stack(
        [
            jnp.stack([slabs[0, 1], none, slabs[1, 1], none]),
            jnp.stack([slabs[0, 0], none, slabs[1, 0], none]),
            jnp.stack([before[0], before[1], none, none]),
            jnp.stack([after[0], after[1], none, none]),
        ],
        axis=2,
    )
    outgoing = xor_order(outgoing, 0, lane).transpose(1, 0, 2, 3)
    returned = lax.all_to_all(
        outgoing.reshape(peers, 4 * per_half), "dev", split_axis=0, concat_axis=0, tiled=True
    )
    weight = call(
        functools.partial(weights_kernel, per_half), jax.ShapeDtypeStruct((1, n), f32)
    )(rank, returned)
    return weight.reshape(n)


def solution(mesh):
    return jax.shard_map(
        shards,
        mesh=mesh,
        in_specs=(P(("grp", "dev"), None), P(("grp", "dev")), P(("grp", "dev"))),
        out_specs=P(("grp", "dev")),
        check_vma=False,
    )
```

```python
import functools
import math

import jax
import jax.numpy as jnp
from jax import lax
from jax.experimental import pallas as pl
from jax.experimental.pallas import tpu as pltpu
from jax.sharding import PartitionSpec as P

MOST = 2048
HALF = MOST // 2
SIMILARITY_CUTOFF = 0.9
SOFTMAX_HEAT = 0.02
SCALE = math.log2(math.e) / SOFTMAX_HEAT
SHIFT = SIMILARITY_CUTOFF * SCALE
QUAD = 4
CHUNK = 256
LANES = 128
VMEM_LIMIT = 16 * 1024 * 1024

NT = (((1,), (1,)), ((), ()))
TN = (((0,), (0,)), ((), ()))


def iota(shape, dim):
    return lax.broadcasted_iota(jnp.int32, shape, dim)


def call(kernel, out_shape, limit=VMEM_LIMIT, **extra):
    return pl.pallas_call(
        kernel,
        out_shape=out_shape,
        compiler_params=pltpu.CompilerParams(vmem_limit_bytes=limit),
        **extra,
    )


def arrange_kernel(per_half, halves, position_hbm, rows_hbm, *refs):
    *outs, rank_ref, place, rows, sems = refs
    copies = [
        pltpu.make_async_copy(position_hbm, place, sems.at[0]),
        pltpu.make_async_copy(rows_hbm, rows, sems.at[1]),
    ]
    for copy in copies:
        copy.start()
    n = rows.shape[0]
    earlier = (iota((n, n), 0) < iota((n, n), 1)).astype(jnp.bfloat16)
    copies[0].wait()
    half = place[...] // HALF
    kinds = iota((halves, n), 0) == half
    counts = jnp.dot(kinds.astype(jnp.bfloat16), earlier, preferred_element_type=jnp.float32)
    count = jnp.sum(jnp.where(kinds, counts, 0.0), axis=0, keepdims=True).astype(jnp.int32)
    rank_ref[...] = half * per_half + count
    rank = half * per_half + count
    if len(outs) > 1:
        plane = (half // 2) ^ (lax.axis_index("dev") // QUAD)
        rank = (2 * plane + 1 - half % 2) * per_half + count
    pick = (iota((n, n), 0) == rank).astype(jnp.bfloat16)
    copies[1].wait()
    picked = jnp.dot(pick, rows[...], preferred_element_type=jnp.float32)
    at = 0
    for out in outs:
        out[...] = picked[at : at + out.shape[0], :].astype(out.dtype)
        at += out.shape[0]


def facts_kernel(position_ref, ids_ref, rows_ref, out_ref):
    n = rows_ref.shape[0]
    wide = rows_ref[...].astype(jnp.float32)
    inverse = lax.rsqrt(jnp.sum(wide * wide, axis=1, keepdims=True) + 1e-06)
    eye = iota((n, n), 0) == iota((n, n), 1)
    out_ref[0:1, :] = position_ref[...].astype(jnp.float32)
    out_ref[1:2, :] = jnp.sum(jnp.where(eye, inverse, 0.0), axis=0, keepdims=True)
    out_ref[2:3, :] = ids_ref[...].astype(jnp.float32)
    out_ref[3:4, :] = jnp.zeros((1, n), jnp.float32)


def in_bf16(values, count):
    parts = []
    for _ in range(count):
        parts.append(values.astype(jnp.bfloat16))
        values = values - parts[-1].astype(jnp.float32)
    return parts


def places_kernel(per_half, planes, facts_ref, out_ref):
    n = facts_ref.shape[-1]
    slab = lax.axis_index("dev") // QUAD
    earlier = (iota((n, n), 0) < iota((n, n), 1)).astype(jnp.bfloat16)
    half = facts_ref[0 : 3 * planes, 0, :].astype(jnp.int32) // HALF
    slot = jnp.full(half.shape, -1, jnp.int32)
    for k, which in enumerate((2 * slab, 2 * slab + 1, 2 * slab - 1, 2 * slab + 2)):
        mask = half == which
        ones = jnp.where(mask, 1.0, 0.0).astype(jnp.bfloat16)
        count = jnp.dot(ones, earlier, preferred_element_type=jnp.float32).astype(jnp.int32)
        slot = jnp.where(mask, count + k * per_half, slot)
    for k in range(3):
        groups = 2 if k == 2 else 4
        for x in range(planes):
            at = k * planes + x
            pick = (iota((groups * per_half, n), 0) == slot[at : at + 1, :]).astype(jnp.bfloat16)
            position = facts_ref[at, 0:1, :]
            inverse = facts_ref[at, 1:2, :]
            parts = in_bf16(position, 2) + in_bf16(inverse, 3)
            parts.append(jnp.zeros((3, n), jnp.bfloat16))
            picked = lax.dot_general(
                jnp.concatenate(parts, axis=0), pick, NT, preferred_element_type=jnp.float32
            )
            width = groups * per_half
            out_ref[k, 0, x : x + 1, 0:width] = picked[0:1, :] + picked[1:2, :]
            out_ref[k, 1, x : x + 1, 0:width] = picked[2:3, :] + picked[3:4, :] + picked[4:5, :]
            if groups == 2:
                out_ref[k, 0, x : x + 1, width:] = jnp.zeros((1, width), jnp.float32)
                out_ref[k, 1, x : x + 1, width:] = jnp.zeros((1, width), jnp.float32)


def labels_kernel(per_device, planes, place_ref, table_ref, out_ref):
    place = place_ref[...].astype(jnp.int32)
    depth = table_ref.shape[0]
    n = place.shape[1]
    table = table_ref[...]
    high = jnp.floor(table * (1.0 / 256.0))
    low = table - high * 256.0
    owner = place // per_device ^ lax.axis_index("dev")
    owner = owner % QUAD * planes + owner // QUAD
    line = owner * (per_device // LANES) + place % per_device // LANES
    line = (iota((depth, n), 0) == line).astype(jnp.bfloat16)
    high = lax.dot_general(
        high.astype(jnp.bfloat16), line, TN, preferred_element_type=jnp.float32
    )
    low = lax.dot_general(
        low.astype(jnp.bfloat16), line, TN, preferred_element_type=jnp.float32
    )
    here = iota((LANES, n), 0) == place % LANES
    out_ref[...] = jnp.sum(jnp.where(here, high * 256.0 + low, 0.0), axis=0, keepdims=True)


NAMES = ("b0h", "b0l", "b1h", "b1l", "b2h", "b2l", "u", "l", "u1", "l1")
SUMS = ("b0h", "b0l", "b2h", "b2l", "u", "l", "u1", "l1")


class Terms:
    def __init__(self, arrays, rows_ref, columns_ref, out_ref, last_ref):
        self.arrays, self.rows, self.columns, self.out = arrays, rows_ref, columns_ref, out_ref
        self.last = last_ref
        self.sums = {}

    def add(self, name, values):
        self.sums[name] = self.sums[name] + values if name in self.sums else values

    def job(self, down, across):
        n = self.arrays[down].shape[0]
        products = lax.dot_general(
            self.arrays[down][...],
            self.arrays[across][...],
            NT,
            preferred_element_type=jnp.float32,
        )
        at, to = NAMES.index(down) * n, NAMES.index(across) * n
        scale = self.columns[at : at + n, 0:1]
        label = self.columns[at : at + n, 1:2]
        power = products * scale * self.rows[0:1, to : to + n] - SHIFT
        mask = label == self.rows[1:2, to : to + n]
        if down == across:
            mask &= iota((n, n), 0) != iota((n, n), 1)
        values = jnp.where(mask, jnp.exp2(power), 0.0)
        self.add(across, jnp.sum(values, axis=0, keepdims=True))
        if down in ("u", "l", "u1", "l1") or (down, across) == ("b0h", "b0l"):
            side = jnp.zeros((n, LANES), jnp.float32)
            for lane in range(0, n, LANES):
                side += values[:, lane : lane + LANES]
            self.add(down, jnp.sum(side.T, axis=0, keepdims=True))

    def write(self):
        for k, name in enumerate(SUMS):
            values = self.sums.get(name)
            last = self.last[k : k + 1, :] if self.last is not None else None
            if values is None:
                values = jnp.zeros((1, self.out.shape[1]), jnp.float32) if last is None else last
            elif last is not None:
                values += last
            self.out[k : k + 1, :] = values


def masses_call(jobs, arrays, rows, columns, last=None):
    names = [name for name in NAMES if any(name in job for job in jobs)]

    def kernel(*refs):
        refs = list(refs)
        held = {name: refs.pop(0) for name in names}
        rows_ref, columns_ref = refs.pop(0), refs.pop(0)
        last_ref = refs.pop(0) if last is not None else None
        t = Terms(held, rows_ref, columns_ref, refs.pop(0), last_ref)
        for job in jobs:
            t.job(*job)
        t.write()

    operands = [arrays[name] for name in names] + [rows, columns]
    if last is not None:
        operands.append(last)
    n, width = operands[0].shape
    return call(
        kernel,
        jax.ShapeDtypeStruct((len(SUMS), n), jnp.float32),
        cost_estimate=pl.CostEstimate(flops=0, transcendentals=0, bytes_accessed=0),
    )(*operands)


def weights_kernel(per_half, rank_ref, returned_ref, out_ref):
    peers, width = returned_ref.shape
    rank = rank_ref[...]
    n = rank.shape[1]
    slab = rank // (2 * per_half)
    member = rank % (2 * per_half)
    upper = member >= per_half
    returned = returned_ref[...]
    plane = iota((peers, n), 0) // QUAD
    beside = jnp.where(upper, slab + 1, slab - 1)
    beside_member = jnp.where(upper, member + per_half, member + 3 * per_half)

    def chosen(which, lane):
        picked = lax.dot_general(
            returned,
            (plane == which).astype(jnp.float32),
            TN,
            precision=lax.Precision.HIGHEST,
            preferred_element_type=jnp.float32,
        )
        return jnp.sum(
            jnp.where(iota((width, n), 0) == lane, picked, 0.0), axis=0, keepdims=True
        )

    mass = chosen(slab, member) + chosen(beside, beside_member)
    out_ref[...] = 1.0 / (1.0 + mass)


def xor_order(array, axis, bits):
    count = array.shape[axis]
    for k in range(count.bit_length() - 1):
        step = 1 << k
        shape = array.shape[:axis] + (count // (2 * step), 2, step) + array.shape[axis + 1 :]
        split = array.reshape(shape)
        split = jnp.where((bits >> k) & 1 == 1, jnp.flip(split, axis + 1), split)
        array = split.reshape(array.shape)
    return array


def shards(embeddings, position, cluster_ids):
    n, width = embeddings.shape
    peers = lax.axis_size("dev")
    me = lax.axis_index("dev")
    planes = peers // QUAD
    slab, lane = me // QUAD, me % QUAD
    per_half = n // (2 * planes)
    by_permutes = planes == 4
    pieces = [per_half] * 2 + [2 * per_half] + [per_half] * 4 if by_permutes else [n]
    f32 = jnp.float32

    def swapped(rows_, bit):
        return lax.ppermute(rows_, "dev", [(i, i ^ bit) for i in range(peers)])

    def passed(rows_, by):
        pairs = [(i, i + by) for i in range(peers) if 0 <= i + by < peers]
        return lax.ppermute(rows_, "dev", pairs)

    def after_all(value, *others):
        return lax.optimization_barrier((value, *others))[0]

    def as_received(values, axis, plane):
        return xor_order(values, axis, plane) if by_permutes else values

    def from_own(values, axis, plane):
        if by_permutes:
            return values if plane is slab else xor_order(values, axis, slab ^ plane)
        return xor_order(values, axis, slab)

    where_to = position.reshape(1, n)
    in_hbm = pl.BlockSpec(memory_space=pltpu.HBM)
    *arranged, rank = call(
        functools.partial(arrange_kernel, per_half, 2 * planes),
        [jax.ShapeDtypeStruct((size, width), embeddings.dtype) for size in pieces]
        + [jax.ShapeDtypeStruct((1, n), jnp.int32)],
        in_specs=[in_hbm, in_hbm],
        scratch_shapes=[
            pltpu.VMEM((1, n), jnp.int32),
            pltpu.VMEM((n, width), embeddings.dtype),
            pltpu.SemaphoreType.DMA((2,)),
        ],
    )(where_to, embeddings)
    if by_permutes:
        own_upper, own_lower, to_1, upper_2, lower_2, upper_3, lower_3 = arranged
        upper_3 = swapped(upper_3, 3 * QUAD)
        upper_2 = swapped(upper_2, 2 * QUAD)
        both_1 = swapped(to_1, QUAD)
        lower_3 = swapped(lower_3, 3 * QUAD)
        lower_2 = swapped(lower_2, 2 * QUAD)
        upper = jnp.concatenate([own_upper, both_1[:per_half], upper_2, upper_3], axis=0)
        lower = jnp.concatenate([own_lower, both_1[per_half:], lower_2, lower_3], axis=0)
    else:
        lines = [[p * QUAD + q for p in range(planes)] for q in range(QUAD)]
        block = lax.all_to_all(
            arranged[0], "dev", split_axis=0, concat_axis=0, axis_index_groups=lines, tiled=True
        ).reshape(planes, 2, per_half, width)
        upper = block[:, 1].reshape(n // 2, width)
        lower = block[:, 0].reshape(n // 2, width)

    facts = call(facts_kernel, jax.ShapeDtypeStruct((4, n), f32))(
        where_to, cluster_ids.reshape(1, n), embeddings
    )
    facts = facts.reshape(1, 4, n)
    bit = QUAD
    while bit < peers:
        facts = jnp.concatenate([facts, swapped(facts, bit)], axis=0)
        bit *= 2
    facts = after_all(facts, both_1 if by_permutes else block)
    for bit in (1, 2):
        facts = jnp.concatenate([facts, swapped(facts, bit)], axis=0)
    near = call(
        functools.partial(places_kernel, per_half, planes),
        jax.ShapeDtypeStruct((3, 2, planes, 4 * per_half), f32),
    )(facts)
    near = near.reshape(3, 2, planes, 4, per_half).transpose(1, 0, 3, 2, 4)
    own = from_own(near[:, :, :2], 3, slab)
    before = from_own(near[:, :2, 2], 2, slab - 1)
    after = from_own(near[:, :2, 3], 2, slab + 1)
    near = jnp.concatenate(
        [
            jnp.stack([own[:, :, 1], own[:, :, 0]], axis=2).reshape(2, 3 * n),
            jnp.stack([before, after], axis=2).reshape(2, 2 * n),
        ],
        axis=1,
    )
    total = 5 * n
    label = call(
        functools.partial(labels_kernel, n, planes), jax.ShapeDtypeStruct((1, total), f32)
    )(near[:1], facts[:, 2].reshape(peers * n // LANES, LANES))[0]
    at = jnp.arange(total)
    absent = (at >= 3 * n) & jnp.where(at % n >= n // 2, slab == planes - 1, slab == 0)
    label = jnp.where(absent, -1.0, label)
    rows = jnp.stack([near[1], label])
    columns = jnp.stack([near[1] * SCALE, label], axis=1)

    arrays = {"b0h": upper}
    arrays["b2h"] = swapped(upper, 2)
    arrays["b1h"] = swapped(upper, 1)
    lower = after_all(lower, arrays["b1h"])
    arrays["b0l"] = lower
    arrays["u"] = passed(upper, QUAD)
    arrays["b2l"] = swapped(lower, 2)
    arrays["l"] = passed(lower, -QUAD)
    arrays["b1l"] = swapped(lower, 1)

    def masses_after(jobs, last=None):
        return masses_call(jobs, arrays, rows, columns, last)

    masses = masses_after(
        [("b0h", "b0h"), ("b1h", "b0h"), ("b2h", "b0h"), ("b1h", "b2h")]
        + [("b0l", "b0l"), ("b0h", "b0l"), ("b1h", "b0l"), ("b2h", "b0l")]
        + [("b1l", "b0h"), ("b1l", "b0l"), ("b1l", "b2h")]
    )
    arrays["u1"] = swapped(after_all(arrays['u'], arrays["b2h"]), 1)
    masses = masses_after([(u, b) for u in ("u", "u1") for b in ("b0h", "b0l", "b2h")], masses)
    arrays["l1"] = swapped(after_all(arrays["l"], masses, arrays["b2l"]), 1)
    masses = masses_after(
        [("b2l", "b0h"), ("b2l", "b0l"), ("b1h", "b2l"), ("b1l", "b2l")]
        + [("u", "b2l"), ("u1", "b2l"), ("l", "b0l"), ("l", "b2l")],
        masses,
    )
    masses = masses_after([("l1", "b0l"), ("l1", "b2l")], masses)

    masses = masses.reshape(4, 2, planes, per_half)
    slabs = as_received(masses[:2], 2, slab)
    before = as_received(masses[2:, 0], 1, slab - 1)
    after = as_received(masses[2:, 1], 1, slab + 1)
    none = jnp.zeros_like(before[0])
    outgoing = jnp.stack(
        [
            jnp.stack([slabs[0, 1], none, slabs[1, 1], none]),
            jnp.stack([slabs[0, 0], none, slabs[1, 0], none]),
            jnp.stack([before[0], before[1], none, none]),
            jnp.stack([after[0], after[1], none, none]),
        ],
        axis=2,
    )
    outgoing = xor_order(outgoing, 0, lane).transpose(1, 0, 2, 3)
    returned = lax.all_to_all(
        outgoing.reshape(peers, 4 * per_half), "dev", split_axis=0, concat_axis=0, tiled=True
    )
    weight = call(
        functools.partial(weights_kernel, per_half), jax.ShapeDtypeStruct((1, n), f32)
    )(rank, returned)
    return weight.reshape(n)


def solution(mesh):
    return jax.shard_map(
        shards,
        mesh=mesh,
        in_specs=(P(("grp", "dev"), None), P(("grp", "dev")), P(("grp", "dev"))),
        out_specs=P(("grp", "dev")),
        check_vma=False,
    )
```

```python
import functools
import math

import jax
import jax.numpy as jnp
from jax import lax
from jax.experimental import pallas as pl
from jax.experimental.pallas import tpu as pltpu
from jax.sharding import PartitionSpec as P

MOST = 2048
HALF = MOST // 2
SIMILARITY_CUTOFF = 0.9
SOFTMAX_HEAT = 0.02
SCALE = math.log2(math.e) / SOFTMAX_HEAT
SHIFT = SIMILARITY_CUTOFF * SCALE
QUAD = 4
CHUNK = 256
LANES = 128
VMEM_LIMIT = 16 * 1024 * 1024

NT = (((1,), (1,)), ((), ()))
TN = (((0,), (0,)), ((), ()))


def iota(shape, dim):
    return lax.broadcasted_iota(jnp.int32, shape, dim)


def call(kernel, out_shape, limit=VMEM_LIMIT, **extra):
    return pl.pallas_call(
        kernel,
        out_shape=out_shape,
        compiler_params=pltpu.CompilerParams(vmem_limit_bytes=limit),
        **extra,
    )


def in_bf16(values, count):
    parts = []
    for _ in range(count):
        parts.append(values.astype(jnp.bfloat16))
        values = values - parts[-1].astype(jnp.float32)
    return parts


def facts_of(position, ids, partner_ids, rows):
    n = rows.shape[0]
    wide = rows.astype(jnp.float32)
    inverse = lax.rsqrt(jnp.sum(wide * wide, axis=1, keepdims=True) + 1e-06)
    eye = iota((n, n), 0) == iota((n, n), 1)
    inverse = jnp.sum(jnp.where(eye, inverse, 0.0), axis=0, keepdims=True)
    ids = [values.astype(jnp.float32) for values in (ids, partner_ids)]
    return position.astype(jnp.float32), inverse, *ids


def ranks(per_half, halves, position):
    n = position.shape[1]
    earlier = (iota((n, n), 0) < iota((n, n), 1)).astype(jnp.bfloat16)
    half = position // HALF
    kinds = iota((halves, n), 0) == half
    counts = jnp.dot(kinds.astype(jnp.bfloat16), earlier, preferred_element_type=jnp.float32)
    count = jnp.sum(jnp.where(kinds, counts, 0.0), axis=0, keepdims=True).astype(jnp.int32)
    return half, count


def arrange_kernel(per_half, halves, position_ref, rows_ref, out_ref, rank_ref):
    n = rows_ref.shape[0]
    half, count = ranks(per_half, halves, position_ref[...])
    rank = half * per_half + count
    rank_ref[...] = rank
    pick = (iota((n, n), 0) == rank).astype(jnp.bfloat16)
    out_ref[...] = jnp.dot(
        pick, rows_ref[...], preferred_element_type=jnp.float32
    ).astype(out_ref.dtype)


PARTS = (2, 3, 2, 2)
FACT_ROWS = 16


def arrange_pieces_kernel(per_half, halves, position_ref, ids_ref, partner_ids_ref, rows_ref, *refs):
    *outs, rank_ref, facts_ref = refs
    n, width = rows_ref.shape
    position = position_ref[...]
    half, count = ranks(per_half, halves, position)
    rank_ref[...] = half * per_half + count
    plane = (half // 2) ^ (lax.axis_index("dev") // QUAD)
    rank = (2 * plane + 1 - half % 2) * per_half + count
    pick = (iota((n, n), 0) == rank).astype(jnp.bfloat16)
    rows = rows_ref[...]
    picked = jnp.dot(pick, rows, preferred_element_type=jnp.float32)
    facts = facts_of(position, ids_ref[...], partner_ids_ref[...], rows)
    parts = []
    for k, (values, amount) in enumerate(zip(facts, PARTS)):
        facts_ref[k : k + 1, :] = values
        parts += [part.astype(jnp.float32) for part in in_bf16(values, amount)]
    parts.append(jnp.zeros((FACT_ROWS - len(parts), n), jnp.float32))
    parts = jnp.concatenate(parts, axis=0)
    parts = jnp.concatenate([parts, jnp.zeros((FACT_ROWS, width - n), jnp.float32)], axis=1)
    at = 0
    for out in outs:
        size = out.shape[0]
        if size % per_half:
            size -= FACT_ROWS
            out[size:, :] = parts.astype(out.dtype)
        out[0:size, :] = picked[at : at + size, :].astype(out.dtype)
        at += size


def unpack_kernel(facts_ref, *refs):
    *pieces, out_ref = refs
    n = facts_ref.shape[1]
    out_ref[0, :, :] = facts_ref[...]
    for x, piece in enumerate(pieces):
        parts = piece[piece.shape[0] - FACT_ROWS :, :].astype(jnp.float32)[:, 0:n]
        at = 0
        for k, amount in enumerate(PARTS):
            total = parts[at : at + 1, :]
            for j in range(1, amount):
                total += parts[at + j : at + j + 1, :]
            out_ref[x + 1, k : k + 1, :] = total
            at += amount


def facts_kernel(position_ref, ids_ref, partner_ids_ref, rows_ref, out_ref):
    facts = facts_of(position_ref[...], ids_ref[...], partner_ids_ref[...], rows_ref[...])
    for k, values in enumerate(facts):
        out_ref[k : k + 1, :] = values


def places_kernel(per_half, planes, facts_ref, out_ref):
    n = facts_ref.shape[-1]
    slab = lax.axis_index("dev") // QUAD
    earlier = (iota((n, n), 0) < iota((n, n), 1)).astype(jnp.bfloat16)
    half = facts_ref[0 : 3 * planes, 0, :].astype(jnp.int32) // HALF
    slot = jnp.full(half.shape, -1, jnp.int32)
    for k, which in enumerate((2 * slab, 2 * slab + 1, 2 * slab - 1, 2 * slab + 2)):
        mask = half == which
        ones = jnp.where(mask, 1.0, 0.0).astype(jnp.bfloat16)
        count = jnp.dot(ones, earlier, preferred_element_type=jnp.float32).astype(jnp.int32)
        slot = jnp.where(mask, count + k * per_half, slot)
    for k in range(3):
        groups = 2 if k == 2 else 4
        for x in range(planes):
            at = k * planes + x
            pick = (iota((groups * per_half, n), 0) == slot[at : at + 1, :]).astype(jnp.bfloat16)
            position = facts_ref[at, 0:1, :]
            inverse = facts_ref[at, 1:2, :]
            parts = in_bf16(position, 2) + in_bf16(inverse, 3)
            parts.append(jnp.zeros((3, n), jnp.bfloat16))
            picked = lax.dot_general(
                jnp.concatenate(parts, axis=0), pick, NT, preferred_element_type=jnp.float32
            )
            width = groups * per_half
            out_ref[k, 0, x : x + 1, 0:width] = picked[0:1, :] + picked[1:2, :]
            out_ref[k, 1, x : x + 1, 0:width] = picked[2:3, :] + picked[3:4, :] + picked[4:5, :]
            if groups == 2:
                out_ref[k, 0, x : x + 1, width:] = jnp.zeros((1, width), jnp.float32)
                out_ref[k, 1, x : x + 1, width:] = jnp.zeros((1, width), jnp.float32)


def labels_kernel(per_device, planes, place_ref, table_ref, out_ref):
    place = place_ref[...].astype(jnp.int32)
    depth = table_ref.shape[0]
    n = place.shape[1]
    table = table_ref[...]
    high = jnp.floor(table * (1.0 / 256.0))
    low = table - high * 256.0
    owner = place // per_device ^ lax.axis_index("dev")
    owner = owner % QUAD * planes + owner // QUAD
    line = owner * (per_device // LANES) + place % per_device // LANES
    line = (iota((depth, n), 0) == line).astype(jnp.bfloat16)
    high = lax.dot_general(
        high.astype(jnp.bfloat16), line, TN, preferred_element_type=jnp.float32
    )
    low = lax.dot_general(
        low.astype(jnp.bfloat16), line, TN, preferred_element_type=jnp.float32
    )
    here = iota((LANES, n), 0) == place % LANES
    out_ref[...] = jnp.sum(jnp.where(here, high * 256.0 + low, 0.0), axis=0, keepdims=True)


NAMES = ("b0h", "b0l", "b1h", "b1l", "b2h", "b2l", "u", "l", "u1", "l1")
SUMS = ("b0h", "b0l", "b2h", "b2l", "u", "l", "u1", "l1")


class Terms:
    def __init__(self, arrays, rows_ref, columns_ref, out_ref, last_ref):
        self.arrays, self.rows, self.columns, self.out = arrays, rows_ref, columns_ref, out_ref
        self.last = last_ref
        self.sums = {}

    def add(self, name, values):
        self.sums[name] = self.sums[name] + values if name in self.sums else values

    def job(self, down, across):
        n = self.arrays[down].shape[0]
        products = lax.dot_general(
            self.arrays[down][...],
            self.arrays[across][...],
            NT,
            preferred_element_type=jnp.float32,
        )
        at, to = NAMES.index(down) * n, NAMES.index(across) * n
        scale = self.columns[at : at + n, 0:1]
        label = self.columns[at : at + n, 1:2]
        power = products * scale * self.rows[0:1, to : to + n] - SHIFT
        mask = label == self.rows[1:2, to : to + n]
        if down == across:
            mask &= iota((n, n), 0) != iota((n, n), 1)
        values = jnp.where(mask, jnp.exp2(power), 0.0)
        self.add(across, jnp.sum(values, axis=0, keepdims=True))
        if down in ("u", "l", "u1", "l1") or (down, across) == ("b0h", "b0l"):
            side = jnp.zeros((n, LANES), jnp.float32)
            for lane in range(0, n, LANES):
                side += values[:, lane : lane + LANES]
            self.add(down, jnp.sum(side.T, axis=0, keepdims=True))

    def write(self):
        for k, name in enumerate(SUMS):
            values = self.sums.get(name)
            last = self.last[k : k + 1, :] if self.last is not None else None
            if values is None:
                values = jnp.zeros((1, self.out.shape[1]), jnp.float32) if last is None else last
            elif last is not None:
                values += last
            self.out[k : k + 1, :] = values


def masses_call(jobs, arrays, rows, columns, last=None):
    names = [name for name in NAMES if any(name in job for job in jobs)]

    def kernel(*refs):
        refs = list(refs)
        held = {name: refs.pop(0) for name in names}
        rows_ref, columns_ref = refs.pop(0), refs.pop(0)
        last_ref = refs.pop(0) if last is not None else None
        t = Terms(held, rows_ref, columns_ref, refs.pop(0), last_ref)
        for job in jobs:
            t.job(*job)
        t.write()

    operands = [arrays[name] for name in names] + [rows, columns]
    if last is not None:
        operands.append(last)
    n, width = operands[0].shape
    return call(
        kernel,
        jax.ShapeDtypeStruct((len(SUMS), n), jnp.float32),
        cost_estimate=pl.CostEstimate(flops=0, transcendentals=0, bytes_accessed=0),
    )(*operands)


def weights_kernel(per_half, rank_ref, returned_ref, out_ref):
    peers, width = returned_ref.shape
    rank = rank_ref[...]
    n = rank.shape[1]
    slab = rank // (2 * per_half)
    member = rank % (2 * per_half)
    upper = member >= per_half
    returned = returned_ref[...]
    plane = iota((peers, n), 0) // QUAD
    beside = jnp.where(upper, slab + 1, slab - 1)
    beside_member = jnp.where(upper, member + per_half, member + 3 * per_half)

    def chosen(which, lane):
        picked = lax.dot_general(
            returned,
            (plane == which).astype(jnp.float32),
            TN,
            precision=lax.Precision.HIGHEST,
            preferred_element_type=jnp.float32,
        )
        return jnp.sum(
            jnp.where(iota((width, n), 0) == lane, picked, 0.0), axis=0, keepdims=True
        )

    mass = chosen(slab, member) + chosen(beside, beside_member)
    out_ref[...] = 1.0 / (1.0 + mass)


def xor_order(array, axis, bits):
    count = array.shape[axis]
    for k in range(count.bit_length() - 1):
        step = 1 << k
        shape = array.shape[:axis] + (count // (2 * step), 2, step) + array.shape[axis + 1 :]
        split = array.reshape(shape)
        split = jnp.where((bits >> k) & 1 == 1, jnp.flip(split, axis + 1), split)
        array = split.reshape(array.shape)
    return array


def shards(embeddings, position, cluster_ids):
    n, width = embeddings.shape
    peers = lax.axis_size("dev")
    me = lax.axis_index("dev")
    planes = peers // QUAD
    slab, lane = me // QUAD, me % QUAD
    per_half = n // (2 * planes)
    per_slab = 2 * per_half
    f32 = jnp.float32
    by_permutes = planes == 4
    def swapped(rows_, bit):
        return lax.ppermute(rows_, "dev", [(i, i ^ bit) for i in range(peers)])

    def passed(rows_, by):
        pairs = [(i, i + by) for i in range(peers) if 0 <= i + by < peers]
        return lax.ppermute(rows_, "dev", pairs)

    def after_all(value, *others):
        return lax.optimization_barrier((value, *others))[0]

    def as_received(values, axis, plane):
        return xor_order(values, axis, plane) if by_permutes else values

    def from_own(values, axis, plane):
        if by_permutes:
            return values if plane is slab else xor_order(values, axis, slab ^ plane)
        return xor_order(values, axis, slab)

    where_to = position.reshape(1, n)
    own_ids = cluster_ids.reshape(1, n)
    partner_ids = swapped(own_ids, 1)
    rank_shape = jax.ShapeDtypeStruct((1, n), jnp.int32)
    facts_shape = jax.ShapeDtypeStruct((4, n), f32)

    def rows_shape(size):
        return jax.ShapeDtypeStruct((size, width), embeddings.dtype)

    if by_permutes:
        more = per_half + FACT_ROWS
        sizes = [per_half, per_half, per_half + more, more, per_half, more, per_half]
        *arranged, rank, facts = call(
            functools.partial(arrange_pieces_kernel, per_half, 2 * planes),
            [rows_shape(size) for size in sizes] + [rank_shape, facts_shape],
        )(where_to, own_ids, partner_ids, embeddings)
        own_upper, own_lower, to_1, upper_2, lower_2, upper_3, lower_3 = arranged
        both_1 = swapped(to_1, QUAD)
        upper_2 = swapped(upper_2, 2 * QUAD)
        upper_3 = swapped(upper_3, 3 * QUAD)
        lower_2 = swapped(lower_2, 2 * QUAD)
        lower_3 = swapped(lower_3, 3 * QUAD)
        upper = jnp.concatenate(
            [own_upper, both_1[:per_half], upper_2[:per_half], upper_3[:per_half]], axis=0
        )
        lower = jnp.concatenate(
            [own_lower, both_1[per_half:per_slab], lower_2, lower_3], axis=0
        )
        facts = call(unpack_kernel, jax.ShapeDtypeStruct((planes, 4, n), f32))(
            facts, both_1, upper_2, upper_3
        )
    else:
        arranged, rank = call(
            functools.partial(arrange_kernel, per_half, 2 * planes), [rows_shape(n), rank_shape]
        )(where_to, embeddings)
        lines = [[p * QUAD + q for p in range(planes)] for q in range(QUAD)]
        block = lax.all_to_all(
            arranged, "dev", split_axis=0, concat_axis=0, axis_index_groups=lines, tiled=True
        ).reshape(planes, 2, per_half, width)
        upper = block[:, 1].reshape(n // 2, width)
        lower = block[:, 0].reshape(n // 2, width)
        facts = call(facts_kernel, facts_shape)(where_to, own_ids, partner_ids, embeddings).reshape(1, 4, n)
        bit = QUAD
        while bit < peers:
            facts = jnp.concatenate([facts, swapped(facts, bit)], axis=0)
            bit *= 2
    beside, across = swapped(facts, 1), swapped(facts, 2)
    ids = jnp.concatenate([facts[:, 2], facts[:, 3], across[:, 2], across[:, 3]], axis=0)
    facts = jnp.concatenate([facts, beside, across], axis=0)
    arrays = {"b0h": upper}
    arrays["b2h"] = swapped(upper, 2)
    arrays["b1h"] = swapped(after_all(upper, beside), 1)
    lower = after_all(lower, arrays["b1h"])
    arrays["b0l"] = lower
    arrays["u"] = passed(after_all(upper, lower), QUAD)
    arrays["b2l"] = swapped(lower, 2)
    arrays["l"] = passed(lower, -QUAD)
    arrays["b1l"] = swapped(lower, 1)

    facts = after_all(facts, arrays["b1l"])
    near = call(
        functools.partial(places_kernel, per_half, planes),
        jax.ShapeDtypeStruct((3, 2, planes, 4 * per_half), f32),
    )(facts)
    near = near.reshape(3, 2, planes, 4, per_half).transpose(1, 0, 3, 2, 4)
    own = from_own(near[:, :, :2], 3, slab)
    before = from_own(near[:, :2, 2], 2, slab - 1)
    after = from_own(near[:, :2, 3], 2, slab + 1)
    near = jnp.concatenate(
        [
            jnp.stack([own[:, :, 1], own[:, :, 0]], axis=2).reshape(2, 3 * n),
            jnp.stack([before, after], axis=2).reshape(2, 2 * n),
        ],
        axis=1,
    )
    total = 5 * n
    label = call(
        functools.partial(labels_kernel, n, planes), jax.ShapeDtypeStruct((1, total), f32)
    )(near[:1], ids.reshape(peers * n // LANES, LANES))[0]
    at = jnp.arange(total)
    absent = (at >= 3 * n) & jnp.where(at % n >= n // 2, slab == planes - 1, slab == 0)
    label = jnp.where(absent, -1.0, label)
    rows = jnp.stack([near[1], label])
    columns = jnp.stack([near[1] * SCALE, label], axis=1)

    def masses_after(jobs, last=None):
        return masses_call(jobs, arrays, rows, columns, last)

    masses = masses_after(
        [("b0h", "b0h"), ("b1h", "b0h"), ("b2h", "b0h"), ("b1h", "b2h")]
        + [("b0l", "b0l"), ("b0h", "b0l"), ("b1h", "b0l"), ("b2h", "b0l")]
        + [("b1l", "b0h"), ("b1l", "b0l"), ("b1l", "b2h")]
    )
    arrays["u1"] = swapped(after_all(arrays['u'], arrays["b2h"]), 1)
    masses = masses_after([(u, b) for u in ("u", "u1") for b in ("b0h", "b0l", "b2h")], masses)
    arrays["l1"] = swapped(after_all(arrays["l"], masses, arrays["b2l"]), 1)
    masses = masses_after(
        [("b2l", "b0h"), ("b2l", "b0l"), ("b1h", "b2l"), ("b1l", "b2l")]
        + [("u", "b2l"), ("u1", "b2l"), ("l", "b0l"), ("l", "b2l")],
        masses,
    )
    masses = masses_after([("l1", "b0l"), ("l1", "b2l")], masses)

    masses = masses.reshape(4, 2, planes, per_half)
    slabs = as_received(masses[:2], 2, slab)
    before = as_received(masses[2:, 0], 1, slab - 1)
    after = as_received(masses[2:, 1], 1, slab + 1)
    none = jnp.zeros_like(before[0])
    outgoing = jnp.stack(
        [
            jnp.stack([slabs[0, 1], none, slabs[1, 1], none]),
            jnp.stack([slabs[0, 0], none, slabs[1, 0], none]),
            jnp.stack([before[0], before[1], none, none]),
            jnp.stack([after[0], after[1], none, none]),
        ],
        axis=2,
    )
    outgoing = xor_order(outgoing, 0, lane).transpose(1, 0, 2, 3)
    returned = lax.all_to_all(
        outgoing.reshape(peers, 4 * per_half), "dev", split_axis=0, concat_axis=0, tiled=True
    )
    weight = call(
        functools.partial(weights_kernel, per_half), jax.ShapeDtypeStruct((1, n), f32)
    )(rank, returned)
    return weight.reshape(n)


def solution(mesh):
    return jax.shard_map(
        shards,
        mesh=mesh,
        in_specs=(P(("grp", "dev"), None), P(("grp", "dev")), P(("grp", "dev"))),
        out_specs=P(("grp", "dev")),
        check_vma=False,
    )
```

```python
import functools
import math

import jax
import jax.numpy as jnp
from jax import lax
from jax.experimental import pallas as pl
from jax.experimental.pallas import tpu as pltpu
from jax.sharding import PartitionSpec as P

MOST = 2048
HALF = MOST // 2
SIMILARITY_CUTOFF = 0.9
SOFTMAX_HEAT = 0.02
SCALE = math.log2(math.e) / SOFTMAX_HEAT
SHIFT = SIMILARITY_CUTOFF * SCALE
QUAD = 4
CHUNK = 256
LANES = 128
VMEM_LIMIT = 16 * 1024 * 1024

NT = (((1,), (1,)), ((), ()))
TN = (((0,), (0,)), ((), ()))


def iota(shape, dim):
    return lax.broadcasted_iota(jnp.int32, shape, dim)


def call(kernel, out_shape, limit=VMEM_LIMIT, **extra):
    return pl.pallas_call(
        kernel,
        out_shape=out_shape,
        compiler_params=pltpu.CompilerParams(vmem_limit_bytes=limit),
        **extra,
    )


def arrange_kernel(per_half, halves, position_hbm, rows_hbm, *refs):
    *outs, rank_ref, place, rows, sems = refs
    copies = [
        pltpu.make_async_copy(position_hbm, place, sems.at[0]),
        pltpu.make_async_copy(rows_hbm, rows, sems.at[1]),
    ]
    for copy in copies:
        copy.start()
    n = rows.shape[0]
    earlier = (iota((n, n), 0) < iota((n, n), 1)).astype(jnp.bfloat16)
    copies[0].wait()
    half = place[...] // HALF
    kinds = iota((halves, n), 0) == half
    counts = jnp.dot(kinds.astype(jnp.bfloat16), earlier, preferred_element_type=jnp.float32)
    count = jnp.sum(jnp.where(kinds, counts, 0.0), axis=0, keepdims=True).astype(jnp.int32)
    rank_ref[...] = half * per_half + count
    rank = half * per_half + count
    if len(outs) > 1:
        plane = (half // 2) ^ (lax.axis_index("dev") // QUAD)
        rank = (2 * plane + 1 - half % 2) * per_half + count
    pick = (iota((n, n), 0) == rank).astype(jnp.bfloat16)
    copies[1].wait()
    picked = jnp.dot(pick, rows[...], preferred_element_type=jnp.float32)
    at = 0
    for out in outs:
        out[...] = picked[at : at + out.shape[0], :].astype(out.dtype)
        at += out.shape[0]


def facts_kernel(per_half, position_ref, ids_ref, rank_ref, *refs):
    *pieces, out_ref = refs
    n = position_ref.shape[1]
    pick = iota((n, n), 0) == rank_ref[...]
    where_to = position_ref[...].astype(jnp.float32)
    column = jnp.sum(jnp.where(pick, where_to, 0.0), axis=1, keepdims=True)
    eye = iota((n, n), 0) == iota((n, n), 1)
    out_ref[0:1, :] = jnp.sum(jnp.where(eye, column, 0.0), axis=0, keepdims=True)
    total = jnp.zeros((1, n), jnp.float32)
    k = 0
    for piece in pieces:
        size = n if len(pieces) == 1 else per_half
        for start in range(0, piece.shape[0], size):
            wide = piece[start : start + size, :].astype(jnp.float32)
            inverse = lax.rsqrt(jnp.sum(wide * wide, axis=1, keepdims=True) + 1e-06)
            first = 0
            if len(pieces) > 1:
                plane = (k // 2) ^ (lax.axis_index("dev") // QUAD)
                first = (2 * plane + 1 - k % 2) * per_half
            here = iota((size, n), 0) + first == iota((size, n), 1)
            total += jnp.sum(jnp.where(here, inverse, 0.0), axis=0, keepdims=True)
            k += 1
    out_ref[1:2, :] = total
    out_ref[2:3, :] = ids_ref[...].astype(jnp.float32)
    out_ref[3:4, :] = jnp.zeros((1, n), jnp.float32)


def labels_kernel(place_ref, table_ref, out_ref):
    place = place_ref[...]
    depth = table_ref.shape[0]
    n = place.shape[1]
    table = table_ref[...]
    high = jnp.floor(table * (1.0 / 256.0))
    low = table - high * 256.0
    line = (iota((depth, n), 0) == place // LANES).astype(jnp.bfloat16)
    high = lax.dot_general(
        high.astype(jnp.bfloat16), line, TN, preferred_element_type=jnp.float32
    )
    low = lax.dot_general(
        low.astype(jnp.bfloat16), line, TN, preferred_element_type=jnp.float32
    )
    here = iota((LANES, n), 0) == place % LANES
    out_ref[...] = jnp.sum(jnp.where(here, high * 256.0 + low, 0.0), axis=0, keepdims=True)


NAMES = ("b0p", "b0q", "b1p", "b1q", "b2p", "b2q", "u", "l", "u1", "l1")
SUMS = ("b0p", "b0q", "b2p", "b2q", "u", "l", "u1", "l1")


class Terms:
    def __init__(self, arrays, rows_ref, columns_ref, out_ref, last_ref):
        self.arrays, self.rows, self.columns, self.out = arrays, rows_ref, columns_ref, out_ref
        self.last = last_ref
        self.sums = {}

    def add(self, name, values):
        self.sums[name] = self.sums[name] + values if name in self.sums else values

    def job(self, down, across):
        n = self.arrays[down].shape[0]
        products = lax.dot_general(
            self.arrays[down][...],
            self.arrays[across][...],
            NT,
            preferred_element_type=jnp.float32,
        )
        at, to = NAMES.index(down) * n, NAMES.index(across) * n
        scale = self.columns[at : at + n, 0:1]
        label = self.columns[at : at + n, 1:2]
        power = products * scale * self.rows[0:1, to : to + n] - SHIFT
        row = 2 if down in ("l", "l1") else 1
        mask = label == self.rows[row : row + 1, to : to + n]
        if down == across:
            mask &= iota((n, n), 0) != iota((n, n), 1)
        values = jnp.where(mask, jnp.exp2(power), 0.0)
        self.add(across, jnp.sum(values, axis=0, keepdims=True))
        if down in ("u", "l", "u1", "l1") or (down, across) == ("b0p", "b0q"):
            side = jnp.zeros((n, LANES), jnp.float32)
            for lane in range(0, n, LANES):
                side += values[:, lane : lane + LANES]
            self.add(down, jnp.sum(side.T, axis=0, keepdims=True))

    def write(self):
        for k, name in enumerate(SUMS):
            values = self.sums.get(name)
            last = self.last[k : k + 1, :] if self.last is not None else None
            if values is None:
                values = jnp.zeros((1, self.out.shape[1]), jnp.float32) if last is None else last
            elif last is not None:
                values += last
            self.out[k : k + 1, :] = values


def masses_call(jobs, arrays, rows, columns, last=None):
    names = [name for name in NAMES if any(name in job for job in jobs)]

    def kernel(*refs):
        refs = list(refs)
        held = {name: refs.pop(0) for name in names}
        rows_ref, columns_ref = refs.pop(0), refs.pop(0)
        last_ref = refs.pop(0) if last is not None else None
        t = Terms(held, rows_ref, columns_ref, refs.pop(0), last_ref)
        for job in jobs:
            t.job(*job)
        t.write()

    operands = [arrays[name] for name in names] + [rows, columns]
    if last is not None:
        operands.append(last)
    n, width = operands[0].shape
    return call(
        kernel,
        jax.ShapeDtypeStruct((len(SUMS), n), jnp.float32),
        cost_estimate=pl.CostEstimate(flops=0, transcendentals=0, bytes_accessed=0),
    )(*operands)


def weights_kernel(per_half, rank_ref, returned_ref, out_ref):
    peers, width = returned_ref.shape
    rank = rank_ref[...]
    n = rank.shape[1]
    slab = rank // (2 * per_half)
    member = rank % (2 * per_half)
    upper = member >= per_half
    returned = returned_ref[...]
    plane = iota((peers, n), 0) // QUAD
    beside = jnp.where(upper, slab + 1, slab - 1)
    beside_member = jnp.where(upper, member + per_half, member + 3 * per_half)

    def chosen(which, lane):
        picked = lax.dot_general(
            returned,
            (plane == which).astype(jnp.float32),
            TN,
            precision=lax.Precision.HIGHEST,
            preferred_element_type=jnp.float32,
        )
        return jnp.sum(
            jnp.where(iota((width, n), 0) == lane, picked, 0.0), axis=0, keepdims=True
        )

    mass = chosen(slab, member) + chosen(beside, beside_member)
    out_ref[...] = 1.0 / (1.0 + mass)


def xor_order(array, axis, bits):
    count = array.shape[axis]
    for k in range(count.bit_length() - 1):
        step = 1 << k
        shape = array.shape[:axis] + (count // (2 * step), 2, step) + array.shape[axis + 1 :]
        split = array.reshape(shape)
        split = jnp.where((bits >> k) & 1 == 1, jnp.flip(split, axis + 1), split)
        array = split.reshape(array.shape)
    return array


def shards(embeddings, position, cluster_ids):
    n, width = embeddings.shape
    peers = lax.axis_size("dev")
    me = lax.axis_index("dev")
    planes = peers // QUAD
    slab, lane = me // QUAD, me % QUAD
    per_half = n // (2 * planes)
    per_slab = 2 * per_half
    by_permutes = planes == 4
    pieces = [2 * per_half] * planes if by_permutes else [n]
    f32 = jnp.float32

    def swapped(rows_, bit):
        return lax.ppermute(rows_, "dev", [(i, i ^ bit) for i in range(peers)])

    def passed(rows_, by):
        pairs = [(i, i + by) for i in range(peers) if 0 <= i + by < peers]
        return lax.ppermute(rows_, "dev", pairs)

    def after_all(value, *others):
        return lax.optimization_barrier((value, *others))[0]

    def as_received(values, axis, plane):
        return xor_order(values, axis, plane) if by_permutes else values

    where_to = position.reshape(1, n)
    in_hbm = pl.BlockSpec(memory_space=pltpu.HBM)
    *arranged, rank = call(
        functools.partial(arrange_kernel, per_half, 2 * planes),
        [jax.ShapeDtypeStruct((size, width), embeddings.dtype) for size in pieces]
        + [jax.ShapeDtypeStruct((1, n), jnp.int32)],
        in_specs=[in_hbm, in_hbm],
        scratch_shapes=[
            pltpu.VMEM((1, n), jnp.int32),
            pltpu.VMEM((n, width), embeddings.dtype),
            pltpu.SemaphoreType.DMA((2,)),
        ],
    )(where_to, embeddings)
    if by_permutes:
        block = [arranged[0]] + [swapped(arranged[x], x * QUAD) for x in range(1, planes)]
        halves = [piece.reshape(2, per_half, width) for piece in block]
        parts = [jnp.concatenate(block[:2], axis=0), jnp.concatenate(block[2:], axis=0)]
        upper = jnp.concatenate([piece[0] for piece in halves], axis=0)
        lower = jnp.concatenate([piece[1] for piece in halves], axis=0)
        first = block[1]
    else:
        lines = [[p * QUAD + q for p in range(planes)] for q in range(QUAD)]
        block = lax.all_to_all(
            arranged[0], "dev", split_axis=0, concat_axis=0, axis_index_groups=lines, tiled=True
        ).reshape(planes, 2, per_half, width)[:, ::-1]
        parts = [part.reshape(n // 2, width) for part in jnp.split(block, 2)]
        upper = block[:, 0].reshape(n // 2, width)
        lower = block[:, 1].reshape(n // 2, width)
        first = lower

    arrays = {"b0p": parts[0], "b0q": parts[1]}
    arrays["b2p"] = swapped(parts[0], 2)
    arrays["b1p"] = swapped(parts[0], 1)

    facts = call(
        functools.partial(facts_kernel, per_half), jax.ShapeDtypeStruct((4, n), f32)
    )(where_to, cluster_ids.reshape(1, n), after_all(rank, arrays["b1p"]), *arranged)
    seen = jnp.pad(facts[:2], ((0, 0), (per_half, per_half)))
    seen = jnp.stack(
        [seen[:, 2 * p * per_half : (2 * p + 4) * per_half] for p in range(planes)]
    ).reshape(planes, 1, 8 * per_half)
    facts = jnp.concatenate(
        [
            jnp.broadcast_to(seen, (planes, QUAD, 8 * per_half)),
            jnp.broadcast_to(facts[2], (planes, QUAD, n)),
        ],
        axis=2,
    )
    facts = lax.all_to_all(
        facts.reshape(peers, 8 * per_half + n), "dev", split_axis=0, concat_axis=0, tiled=True
    )
    ids = jnp.pad(facts[:, 8 * per_half :].reshape(peers * n), (MOST, MOST))
    ids = lax.dynamic_slice_in_dim(ids, slab * MOST, 3 * MOST, 0)
    near = facts[:, : 8 * per_half].reshape(planes, QUAD, 2, 4, per_half)
    near = xor_order(near, 1, lane).transpose(2, 1, 3, 0, 4)
    before = as_received(near[:, :2, 0], 2, slab - 1)
    after = as_received(near[:, :2, 3], 2, slab + 1)
    own = as_received(near[:, :3, 1:3], 3, slab)
    near = jnp.concatenate(
        [
            jnp.stack([own[:, :, 1], own[:, :, 0]], axis=3).reshape(2, 3 * n),
            jnp.stack([before, after], axis=2).reshape(2, 2 * n),
        ],
        axis=1,
    )
    total = 5 * n
    place = near[0].astype(jnp.int32) - (slab - 1) * MOST
    label = call(labels_kernel, jax.ShapeDtypeStruct((1, total), f32))(
        place.reshape(1, total), ids.reshape(3 * MOST // LANES, LANES)
    )[0]
    at = jnp.arange(total)
    absent = (at >= 3 * n) & jnp.where(at % n >= n // 2, slab == planes - 1, slab == 0)
    label = jnp.where(absent, -1.0, label)
    rows = jnp.stack([near[1], label, jnp.where(at % per_slab < per_half, -2.0, label)])
    columns = jnp.stack([near[1] * SCALE, label], axis=1)

    arrays["b2q"] = swapped(parts[1], 2)
    arrays["u"] = passed(upper, QUAD)
    arrays["l"] = passed(lower, -QUAD)
    arrays["b1q"] = swapped(parts[1], 1)

    def masses_after(jobs, last=None):
        return masses_call(jobs, arrays, rows, columns, last)

    masses = masses_after(
        [(down, across) for across in ("b0p", "b0q") for down in ("b0p", "b0q", "b1p", "b1q", "b2p")
         if (down, across) != ("b0q", "b0p")]
        + [("b1p", "b2p"), ("b1q", "b2p")]
    )
    masses = masses_after(
        [("b2q", "b0p"), ("b2q", "b0q"), ("b1p", "b2q"), ("b1q", "b2q")], masses
    )
    everywhere = ("b0p", "b0q", "b2p", "b2q")
    arrays["u1"] = swapped(arrays["u"], 1)
    arrays["l1"] = swapped(arrays["l"], 1)
    masses = masses_after([(side, b) for side in ("u", "l") for b in everywhere], masses)
    masses = masses_after([(side, b) for side in ("u1", "l1") for b in everywhere], masses)

    slabs = masses[:4].reshape(2, planes, 2, per_half)
    slabs = as_received(slabs, 1, slab).transpose(0, 2, 1, 3)
    masses = masses.reshape(4, 2, planes, per_half)
    before = as_received(masses[2:, 0], 1, slab - 1)
    after = as_received(masses[2:, 1], 1, slab + 1)
    none = jnp.zeros_like(before[0])
    outgoing = jnp.stack(
        [
            jnp.stack([slabs[0, 1], none, slabs[1, 1], none]),
            jnp.stack([slabs[0, 0], none, slabs[1, 0], none]),
            jnp.stack([before[0], before[1], none, none]),
            jnp.stack([after[0], after[1], none, none]),
        ],
        axis=2,
    )
    outgoing = xor_order(outgoing, 0, lane).transpose(1, 0, 2, 3)
    returned = lax.all_to_all(
        outgoing.reshape(peers, 4 * per_half), "dev", split_axis=0, concat_axis=0, tiled=True
    )
    weight = call(
        functools.partial(weights_kernel, per_half), jax.ShapeDtypeStruct((1, n), f32)
    )(rank, returned)
    return weight.reshape(n)


def solution(mesh):
    return jax.shard_map(
        shards,
        mesh=mesh,
        in_specs=(P(("grp", "dev"), None), P(("grp", "dev")), P(("grp", "dev"))),
        out_specs=P(("grp", "dev")),
        check_vma=False,
    )
```

```python
import functools
import math

import jax
import jax.numpy as jnp
from jax import lax
from jax.experimental import pallas as pl
from jax.experimental.pallas import tpu as pltpu
from jax.sharding import PartitionSpec as P

MOST = 2048
HALF = MOST // 2
SIMILARITY_CUTOFF = 0.9
SOFTMAX_HEAT = 0.02
SCALE = math.log2(math.e) / SOFTMAX_HEAT
SHIFT = SIMILARITY_CUTOFF * SCALE
QUAD = 4
CHUNK = 256
LANES = 128
VMEM_LIMIT = 16 * 1024 * 1024

NT = (((1,), (1,)), ((), ()))
TN = (((0,), (0,)), ((), ()))


def iota(shape, dim):
    return lax.broadcasted_iota(jnp.int32, shape, dim)


def call(kernel, out_shape, limit=VMEM_LIMIT, **extra):
    return pl.pallas_call(
        kernel,
        out_shape=out_shape,
        compiler_params=pltpu.CompilerParams(vmem_limit_bytes=limit),
        **extra,
    )


def arrange_kernel(per_half, halves, position_hbm, rows_hbm, *refs):
    *outs, rank_ref, place, rows, sems = refs
    copies = [
        pltpu.make_async_copy(position_hbm, place, sems.at[0]),
        pltpu.make_async_copy(rows_hbm, rows, sems.at[1]),
    ]
    for copy in copies:
        copy.start()
    n = rows.shape[0]
    earlier = (iota((n, n), 0) < iota((n, n), 1)).astype(jnp.bfloat16)
    copies[0].wait()
    half = place[...] // HALF
    kinds = iota((halves, n), 0) == half
    counts = jnp.dot(kinds.astype(jnp.bfloat16), earlier, preferred_element_type=jnp.float32)
    count = jnp.sum(jnp.where(kinds, counts, 0.0), axis=0, keepdims=True).astype(jnp.int32)
    rank_ref[...] = half * per_half + count
    rank = half * per_half + count
    if len(outs) > 1:
        plane = (half // 2) ^ (lax.axis_index("dev") // QUAD)
        rank = (2 * plane + 1 - half % 2) * per_half + count
    pick = (iota((n, n), 0) == rank).astype(jnp.bfloat16)
    copies[1].wait()
    picked = jnp.dot(pick, rows[...], preferred_element_type=jnp.float32)
    at = 0
    for out in outs:
        out[...] = picked[at : at + out.shape[0], :].astype(out.dtype)
        at += out.shape[0]


def facts_kernel(per_half, position_ref, ids_ref, rank_ref, *refs):
    *pieces, out_ref = refs
    n = position_ref.shape[1]
    pick = iota((n, n), 0) == rank_ref[...]
    where_to = position_ref[...].astype(jnp.float32)
    column = jnp.sum(jnp.where(pick, where_to, 0.0), axis=1, keepdims=True)
    eye = iota((n, n), 0) == iota((n, n), 1)
    out_ref[0:1, :] = jnp.sum(jnp.where(eye, column, 0.0), axis=0, keepdims=True)
    total = jnp.zeros((1, n), jnp.float32)
    k = 0
    for piece in pieces:
        size = n if len(pieces) == 1 else per_half
        for start in range(0, piece.shape[0], size):
            wide = piece[start : start + size, :].astype(jnp.float32)
            inverse = lax.rsqrt(jnp.sum(wide * wide, axis=1, keepdims=True) + 1e-06)
            first = 0
            if len(pieces) > 1:
                plane = (k // 2) ^ (lax.axis_index("dev") // QUAD)
                first = (2 * plane + 1 - k % 2) * per_half
            here = iota((size, n), 0) + first == iota((size, n), 1)
            total += jnp.sum(jnp.where(here, inverse, 0.0), axis=0, keepdims=True)
            k += 1
    out_ref[1:2, :] = total
    out_ref[2:3, :] = ids_ref[...].astype(jnp.float32)
    out_ref[3:4, :] = jnp.zeros((1, n), jnp.float32)


def labels_kernel(place_ref, table_ref, out_ref):
    place = place_ref[...]
    depth = table_ref.shape[0]
    n = place.shape[1]
    table = table_ref[...]
    high = jnp.floor(table * (1.0 / 256.0))
    low = table - high * 256.0
    line = (iota((depth, n), 0) == place // LANES).astype(jnp.bfloat16)
    high = lax.dot_general(
        high.astype(jnp.bfloat16), line, TN, preferred_element_type=jnp.float32
    )
    low = lax.dot_general(
        low.astype(jnp.bfloat16), line, TN, preferred_element_type=jnp.float32
    )
    here = iota((LANES, n), 0) == place % LANES
    out_ref[...] = jnp.sum(jnp.where(here, high * 256.0 + low, 0.0), axis=0, keepdims=True)


NAMES = ("b0p", "b0q", "b1p", "b1q", "b2p", "b2q", "u", "l", "u1", "l1")
SUMS = ("b0p", "b0q", "b2p", "b2q", "u", "l", "u1", "l1")


class Terms:
    def __init__(self, arrays, rows_ref, columns_ref, out_ref, last_ref):
        self.arrays, self.rows, self.columns, self.out = arrays, rows_ref, columns_ref, out_ref
        self.last = last_ref
        self.sums = {}

    def add(self, name, values):
        self.sums[name] = self.sums[name] + values if name in self.sums else values

    def job(self, down, across):
        n = self.arrays[down].shape[0]
        products = lax.dot_general(
            self.arrays[down][...],
            self.arrays[across][...],
            NT,
            preferred_element_type=jnp.float32,
        )
        at, to = NAMES.index(down) * n, NAMES.index(across) * n
        scale = self.columns[at : at + n, 0:1]
        label = self.columns[at : at + n, 1:2]
        power = products * scale * self.rows[0:1, to : to + n] - SHIFT
        row = 2 if down in ("l", "l1") else 1
        mask = label == self.rows[row : row + 1, to : to + n]
        if down == across:
            mask &= iota((n, n), 0) != iota((n, n), 1)
        values = jnp.where(mask, jnp.exp2(power), 0.0)
        self.add(across, jnp.sum(values, axis=0, keepdims=True))
        if down in ("u", "l", "u1", "l1") or (down, across) == ("b0p", "b0q"):
            side = jnp.zeros((n, LANES), jnp.float32)
            for lane in range(0, n, LANES):
                side += values[:, lane : lane + LANES]
            self.add(down, jnp.sum(side.T, axis=0, keepdims=True))

    def write(self):
        for k, name in enumerate(SUMS):
            values = self.sums.get(name)
            last = self.last[k : k + 1, :] if self.last is not None else None
            if values is None:
                values = jnp.zeros((1, self.out.shape[1]), jnp.float32) if last is None else last
            elif last is not None:
                values += last
            self.out[k : k + 1, :] = values


def masses_call(jobs, arrays, rows, columns, last=None):
    names = [name for name in NAMES if any(name in job for job in jobs)]

    def kernel(*refs):
        refs = list(refs)
        held = {name: refs.pop(0) for name in names}
        rows_ref, columns_ref = refs.pop(0), refs.pop(0)
        last_ref = refs.pop(0) if last is not None else None
        t = Terms(held, rows_ref, columns_ref, refs.pop(0), last_ref)
        for job in jobs:
            t.job(*job)
        t.write()

    operands = [arrays[name] for name in names] + [rows, columns]
    if last is not None:
        operands.append(last)
    n, width = operands[0].shape
    return call(
        kernel,
        jax.ShapeDtypeStruct((len(SUMS), n), jnp.float32),
        cost_estimate=pl.CostEstimate(flops=0, transcendentals=0, bytes_accessed=0),
    )(*operands)


def weights_kernel(per_half, rank_ref, returned_ref, out_ref):
    peers, width = returned_ref.shape
    rank = rank_ref[...]
    n = rank.shape[1]
    slab = rank // (2 * per_half)
    member = rank % (2 * per_half)
    upper = member >= per_half
    returned = returned_ref[...]
    plane = iota((peers, n), 0) // QUAD
    beside = jnp.where(upper, slab + 1, slab - 1)
    beside_member = jnp.where(upper, member + per_half, member + 3 * per_half)

    def chosen(which, lane):
        picked = lax.dot_general(
            returned,
            (plane == which).astype(jnp.float32),
            TN,
            precision=lax.Precision.HIGHEST,
            preferred_element_type=jnp.float32,
        )
        return jnp.sum(
            jnp.where(iota((width, n), 0) == lane, picked, 0.0), axis=0, keepdims=True
        )

    mass = chosen(slab, member) + chosen(beside, beside_member)
    out_ref[...] = 1.0 / (1.0 + mass)


def xor_order(array, axis, bits):
    count = array.shape[axis]
    for k in range(count.bit_length() - 1):
        step = 1 << k
        shape = array.shape[:axis] + (count // (2 * step), 2, step) + array.shape[axis + 1 :]
        split = array.reshape(shape)
        split = jnp.where((bits >> k) & 1 == 1, jnp.flip(split, axis + 1), split)
        array = split.reshape(array.shape)
    return array


def shards(embeddings, position, cluster_ids):
    n, width = embeddings.shape
    peers = lax.axis_size("dev")
    me = lax.axis_index("dev")
    planes = peers // QUAD
    slab, lane = me // QUAD, me % QUAD
    per_half = n // (2 * planes)
    per_slab = 2 * per_half
    by_permutes = planes == 4
    pieces = [2 * per_half] * planes if by_permutes else [n]
    f32 = jnp.float32

    def swapped(rows_, bit):
        return lax.ppermute(rows_, "dev", [(i, i ^ bit) for i in range(peers)])

    def passed(rows_, by):
        pairs = [(i, i + by) for i in range(peers) if 0 <= i + by < peers]
        return lax.ppermute(rows_, "dev", pairs)

    def after_all(value, *others):
        return lax.optimization_barrier((value, *others))[0]

    def as_received(values, axis, plane):
        return xor_order(values, axis, plane) if by_permutes else values

    where_to = position.reshape(1, n)
    in_hbm = pl.BlockSpec(memory_space=pltpu.HBM)
    *arranged, rank = call(
        functools.partial(arrange_kernel, per_half, 2 * planes),
        [jax.ShapeDtypeStruct((size, width), embeddings.dtype) for size in pieces]
        + [jax.ShapeDtypeStruct((1, n), jnp.int32)],
        in_specs=[in_hbm, in_hbm],
        scratch_shapes=[
            pltpu.VMEM((1, n), jnp.int32),
            pltpu.VMEM((n, width), embeddings.dtype),
            pltpu.SemaphoreType.DMA((2,)),
        ],
    )(where_to, embeddings)
    if by_permutes:
        block = [arranged[0]] + [swapped(arranged[x], x * QUAD) for x in range(1, planes)]
        halves = [piece.reshape(2, per_half, width) for piece in block]
        parts = [jnp.concatenate(block[:2], axis=0), jnp.concatenate(block[2:], axis=0)]
        upper = jnp.concatenate([piece[0] for piece in halves], axis=0)
        lower = jnp.concatenate([piece[1] for piece in halves], axis=0)
        first = block[1]
    else:
        lines = [[p * QUAD + q for p in range(planes)] for q in range(QUAD)]
        block = lax.all_to_all(
            arranged[0], "dev", split_axis=0, concat_axis=0, axis_index_groups=lines, tiled=True
        ).reshape(planes, 2, per_half, width)[:, ::-1]
        parts = [part.reshape(n // 2, width) for part in jnp.split(block, 2)]
        upper = block[:, 0].reshape(n // 2, width)
        lower = block[:, 1].reshape(n // 2, width)
        first = lower

    arrays = {"b0p": parts[0], "b0q": parts[1]}
    if by_permutes:
        own_across = swapped(block[0], 2)
        rest_across = swapped(after_all(block[1], own_across), 2)
        arrays["b2p"] = jnp.concatenate([own_across, rest_across], axis=0)
    else:
        arrays["b2p"] = swapped(parts[0], 2)
    arrays["b1p"] = swapped(parts[0], 1)

    facts = call(
        functools.partial(facts_kernel, per_half), jax.ShapeDtypeStruct((4, n), f32)
    )(where_to, cluster_ids.reshape(1, n), after_all(rank, first), *arranged)
    seen = jnp.pad(facts[:2], ((0, 0), (per_half, per_half)))
    seen = jnp.stack(
        [seen[:, 2 * p * per_half : (2 * p + 4) * per_half] for p in range(planes)]
    ).reshape(planes, 1, 8 * per_half)
    facts = jnp.concatenate(
        [
            jnp.broadcast_to(seen, (planes, QUAD, 8 * per_half)),
            jnp.broadcast_to(facts[2], (planes, QUAD, n)),
        ],
        axis=2,
    )
    facts = lax.all_to_all(
        facts.reshape(peers, 8 * per_half + n), "dev", split_axis=0, concat_axis=0, tiled=True
    )
    ids = jnp.pad(facts[:, 8 * per_half :].reshape(peers * n), (MOST, MOST))
    ids = lax.dynamic_slice_in_dim(ids, slab * MOST, 3 * MOST, 0)
    near = facts[:, : 8 * per_half].reshape(planes, QUAD, 2, 4, per_half)
    near = xor_order(near, 1, lane).transpose(2, 1, 3, 0, 4)
    before = as_received(near[:, :2, 0], 2, slab - 1)
    after = as_received(near[:, :2, 3], 2, slab + 1)
    own = as_received(near[:, :3, 1:3], 3, slab)
    near = jnp.concatenate(
        [
            jnp.stack([own[:, :, 1], own[:, :, 0]], axis=3).reshape(2, 3 * n),
            jnp.stack([before, after], axis=2).reshape(2, 2 * n),
        ],
        axis=1,
    )
    total = 5 * n
    place = near[0].astype(jnp.int32) - (slab - 1) * MOST
    label = call(labels_kernel, jax.ShapeDtypeStruct((1, total), f32))(
        place.reshape(1, total), ids.reshape(3 * MOST // LANES, LANES)
    )[0]
    at = jnp.arange(total)
    absent = (at >= 3 * n) & jnp.where(at % n >= n // 2, slab == planes - 1, slab == 0)
    label = jnp.where(absent, -1.0, label)
    rows = jnp.stack([near[1], label, jnp.where(at % per_slab < per_half, -2.0, label)])
    columns = jnp.stack([near[1] * SCALE, label], axis=1)

    part = after_all(parts[1], arrays["b1p"])
    arrays["b2q"] = swapped(part, 2)
    arrays["u"] = passed(upper, QUAD)
    arrays["l"] = passed(lower, -QUAD)
    arrays["b1q"] = swapped(part, 1)

    def masses_after(jobs, last=None):
        return masses_call(jobs, arrays, rows, columns, last)

    masses = masses_after(
        [(down, across) for across in ("b0p", "b0q") for down in ("b0p", "b0q", "b1p", "b1q", "b2p")
         if (down, across) != ("b0q", "b0p")]
        + [("b1p", "b2p"), ("b1q", "b2p")]
    )
    arrays["u1"] = swapped(after_all(arrays["u"], masses), 1)
    arrays["l1"] = swapped(after_all(arrays["l"], masses), 1)
    masses = masses_after(
        [("b2q", "b0p"), ("b2q", "b0q"), ("b1p", "b2q"), ("b1q", "b2q")], masses
    )
    everywhere = ("b0p", "b0q", "b2p", "b2q")
    masses = masses_after([(side, b) for side in ("u", "l") for b in everywhere], masses)
    masses = masses_after([(side, b) for side in ("u1", "l1") for b in everywhere], masses)

    slabs = masses[:4].reshape(2, planes, 2, per_half)
    slabs = as_received(slabs, 1, slab).transpose(0, 2, 1, 3)
    masses = masses.reshape(4, 2, planes, per_half)
    before = as_received(masses[2:, 0], 1, slab - 1)
    after = as_received(masses[2:, 1], 1, slab + 1)
    none = jnp.zeros_like(before[0])
    outgoing = jnp.stack(
        [
            jnp.stack([slabs[0, 1], none, slabs[1, 1], none]),
            jnp.stack([slabs[0, 0], none, slabs[1, 0], none]),
            jnp.stack([before[0], before[1], none, none]),
            jnp.stack([after[0], after[1], none, none]),
        ],
        axis=2,
    )
    outgoing = xor_order(outgoing, 0, lane).transpose(1, 0, 2, 3)
    returned = lax.all_to_all(
        outgoing.reshape(peers, 4 * per_half), "dev", split_axis=0, concat_axis=0, tiled=True
    )
    weight = call(
        functools.partial(weights_kernel, per_half), jax.ShapeDtypeStruct((1, n), f32)
    )(rank, returned)
    return weight.reshape(n)


def solution(mesh):
    return jax.shard_map(
        shards,
        mesh=mesh,
        in_specs=(P(("grp", "dev"), None), P(("grp", "dev")), P(("grp", "dev"))),
        out_specs=P(("grp", "dev")),
        check_vma=False,
    )
```

```python
import functools
import math

import jax
import jax.numpy as jnp
from jax import lax
from jax.experimental import pallas as pl
from jax.experimental.pallas import tpu as pltpu
from jax.sharding import PartitionSpec as P

MOST = 2048
HALF = MOST // 2
SIMILARITY_CUTOFF = 0.9
SOFTMAX_HEAT = 0.02
SCALE = math.log2(math.e) / SOFTMAX_HEAT
SHIFT = SIMILARITY_CUTOFF * SCALE
QUAD = 4
CHUNK = 256
LANES = 128
VMEM_LIMIT = 16 * 1024 * 1024

NT = (((1,), (1,)), ((), ()))
TN = (((0,), (0,)), ((), ()))


def iota(shape, dim):
    return lax.broadcasted_iota(jnp.int32, shape, dim)


def call(kernel, out_shape, limit=VMEM_LIMIT, **extra):
    return pl.pallas_call(
        kernel,
        out_shape=out_shape,
        compiler_params=pltpu.CompilerParams(vmem_limit_bytes=limit),
        **extra,
    )


def arrange_kernel(per_half, halves, position_hbm, rows_hbm, *refs):
    *outs, rank_ref, place, rows, sems = refs
    copies = [
        pltpu.make_async_copy(position_hbm, place, sems.at[0]),
        pltpu.make_async_copy(rows_hbm, rows, sems.at[1]),
    ]
    for copy in copies:
        copy.start()
    n = rows.shape[0]
    earlier = (iota((n, n), 0) < iota((n, n), 1)).astype(jnp.bfloat16)
    copies[0].wait()
    half = place[...] // HALF
    kinds = iota((halves, n), 0) == half
    counts = jnp.dot(kinds.astype(jnp.bfloat16), earlier, preferred_element_type=jnp.float32)
    count = jnp.sum(jnp.where(kinds, counts, 0.0), axis=0, keepdims=True).astype(jnp.int32)
    rank_ref[...] = half * per_half + count
    rank = half * per_half + count
    if len(outs) > 1:
        plane = (half // 2) ^ (lax.axis_index("dev") // QUAD)
        rank = (2 * plane + 1 - half % 2) * per_half + count
    pick = (iota((n, n), 0) == rank).astype(jnp.bfloat16)
    copies[1].wait()
    picked = jnp.dot(pick, rows[...], preferred_element_type=jnp.float32)
    at = 0
    for out in outs:
        out[...] = picked[at : at + out.shape[0], :].astype(out.dtype)
        at += out.shape[0]


def facts_kernel(per_half, position_ref, ids_ref, rank_ref, *refs):
    *pieces, out_ref = refs
    n = position_ref.shape[1]
    pick = iota((n, n), 0) == rank_ref[...]
    where_to = position_ref[...].astype(jnp.float32)
    column = jnp.sum(jnp.where(pick, where_to, 0.0), axis=1, keepdims=True)
    eye = iota((n, n), 0) == iota((n, n), 1)
    out_ref[0:1, :] = jnp.sum(jnp.where(eye, column, 0.0), axis=0, keepdims=True)
    total = jnp.zeros((1, n), jnp.float32)
    k = 0
    for piece in pieces:
        size = n if len(pieces) == 1 else per_half
        for start in range(0, piece.shape[0], size):
            wide = piece[start : start + size, :].astype(jnp.float32)
            inverse = lax.rsqrt(jnp.sum(wide * wide, axis=1, keepdims=True) + 1e-06)
            first = 0
            if len(pieces) > 1:
                plane = (k // 2) ^ (lax.axis_index("dev") // QUAD)
                first = (2 * plane + 1 - k % 2) * per_half
            here = iota((size, n), 0) + first == iota((size, n), 1)
            total += jnp.sum(jnp.where(here, inverse, 0.0), axis=0, keepdims=True)
            k += 1
    out_ref[1:2, :] = total
    out_ref[2:3, :] = ids_ref[...].astype(jnp.float32)
    out_ref[3:4, :] = jnp.zeros((1, n), jnp.float32)


def labels_kernel(place_ref, table_ref, out_ref):
    place = place_ref[...]
    depth = table_ref.shape[0]
    n = place.shape[1]
    table = table_ref[...]
    high = jnp.floor(table * (1.0 / 256.0))
    low = table - high * 256.0
    line = (iota((depth, n), 0) == place // LANES).astype(jnp.bfloat16)
    high = lax.dot_general(
        high.astype(jnp.bfloat16), line, TN, preferred_element_type=jnp.float32
    )
    low = lax.dot_general(
        low.astype(jnp.bfloat16), line, TN, preferred_element_type=jnp.float32
    )
    here = iota((LANES, n), 0) == place % LANES
    out_ref[...] = jnp.sum(jnp.where(here, high * 256.0 + low, 0.0), axis=0, keepdims=True)


NAMES = ("b0h", "b0l", "b1h", "b1l", "b2h", "b2l", "u", "l", "u1", "l1")
SUMS = ("b0h", "b0l", "b2h", "b2l", "u", "l", "u1", "l1")


class Terms:
    def __init__(self, arrays, rows_ref, columns_ref, out_ref, last_ref):
        self.arrays, self.rows, self.columns, self.out = arrays, rows_ref, columns_ref, out_ref
        self.last = last_ref
        self.sums = {}

    def add(self, name, values):
        self.sums[name] = self.sums[name] + values if name in self.sums else values

    def job(self, down, across):
        n = self.arrays[down].shape[0]
        products = lax.dot_general(
            self.arrays[down][...],
            self.arrays[across][...],
            NT,
            preferred_element_type=jnp.float32,
        )
        at, to = NAMES.index(down) * n, NAMES.index(across) * n
        scale = self.columns[at : at + n, 0:1]
        label = self.columns[at : at + n, 1:2]
        power = products * scale * self.rows[0:1, to : to + n] - SHIFT
        mask = label == self.rows[1:2, to : to + n]
        if down == across:
            mask &= iota((n, n), 0) != iota((n, n), 1)
        values = jnp.where(mask, jnp.exp2(power), 0.0)
        self.add(across, jnp.sum(values, axis=0, keepdims=True))
        if down in ("u", "l", "u1", "l1") or (down, across) == ("b0h", "b0l"):
            side = jnp.zeros((n, LANES), jnp.float32)
            for lane in range(0, n, LANES):
                side += values[:, lane : lane + LANES]
            self.add(down, jnp.sum(side.T, axis=0, keepdims=True))

    def write(self):
        for k, name in enumerate(SUMS):
            values = self.sums.get(name)
            last = self.last[k : k + 1, :] if self.last is not None else None
            if values is None:
                values = jnp.zeros((1, self.out.shape[1]), jnp.float32) if last is None else last
            elif last is not None:
                values += last
            self.out[k : k + 1, :] = values


def masses_call(jobs, arrays, rows, columns, last=None):
    names = [name for name in NAMES if any(name in job for job in jobs)]

    def kernel(*refs):
        refs = list(refs)
        held = {name: refs.pop(0) for name in names}
        rows_ref, columns_ref = refs.pop(0), refs.pop(0)
        last_ref = refs.pop(0) if last is not None else None
        t = Terms(held, rows_ref, columns_ref, refs.pop(0), last_ref)
        for job in jobs:
            t.job(*job)
        t.write()

    operands = [arrays[name] for name in names] + [rows, columns]
    if last is not None:
        operands.append(last)
    n, width = operands[0].shape
    return call(
        kernel,
        jax.ShapeDtypeStruct((len(SUMS), n), jnp.float32),
        cost_estimate=pl.CostEstimate(flops=0, transcendentals=0, bytes_accessed=0),
    )(*operands)


def combine_kernel(masses_ref, across_ref, beside_ref, *out_refs):
    slab = lax.axis_index("dev") // QUAD
    upper = masses_ref[0:1, :] + across_ref[0:1, :]
    lower = masses_ref[1:2, :] + across_ref[1:2, :]
    before = masses_ref[4:5, :] + beside_ref[0:1, :]
    after = masses_ref[5:6, :] + beside_ref[1:2, :]
    m = out_refs[0].shape[1]

    def piece(values, x):
        return values[:, x * m : (x + 1) * m]

    for x, out in enumerate(out_refs):
        out[0:1, :] = piece(lower, x)
        out[1:2, :] = piece(upper, x)
        out[2:3, :] = jnp.where(slab == 2, piece(before, x ^ 3), piece(before, x ^ 1))
        out[3:4, :] = jnp.where(slab == 1, piece(after, x ^ 3), piece(after, x ^ 1))


def weights_kernel(relative, rank_ref, *refs):
    *returned, out_ref = refs
    parts = [ref[...] for ref in returned]
    returned = parts[0] if len(parts) == 1 else jnp.concatenate(parts, axis=0)
    count, m = returned.shape
    rank = rank_ref[...]
    n = rank.shape[1]
    slab, upper, member = rank // (2 * m), rank // m % 2 == 1, rank % m
    shape = (count, n)
    plane = iota(shape, 0) // (count * 2 * m // n)
    if relative:
        plane = plane ^ (lax.axis_index("dev") // QUAD)
    kind = iota(shape, 0) % 4
    own = (plane == slab) & (kind == jnp.where(upper, 1, 0))
    halo = (plane == jnp.where(upper, slab + 1, slab - 1)) & (kind == jnp.where(upper, 2, 3))
    picked = lax.dot_general(
        returned,
        jnp.where(own | halo, 1.0, 0.0),
        TN,
        precision=lax.Precision.HIGHEST,
        preferred_element_type=jnp.float32,
    )
    mass = jnp.sum(jnp.where(iota((m, n), 0) == member, picked, 0.0), axis=0, keepdims=True)
    out_ref[...] = 1.0 / (1.0 + mass)


def xor_order(array, axis, bits):
    count = array.shape[axis]
    for k in range(count.bit_length() - 1):
        step = 1 << k
        shape = array.shape[:axis] + (count // (2 * step), 2, step) + array.shape[axis + 1 :]
        split = array.reshape(shape)
        split = jnp.where((bits >> k) & 1 == 1, jnp.flip(split, axis + 1), split)
        array = split.reshape(array.shape)
    return array


def shards(embeddings, position, cluster_ids):
    n, width = embeddings.shape
    peers = lax.axis_size("dev")
    me = lax.axis_index("dev")
    planes = peers // QUAD
    slab, lane = me // QUAD, me % QUAD
    per_half = n // (2 * planes)
    by_permutes = planes == 4
    pieces = [per_half] * 2 + [2 * per_half] + [per_half] * 4 if by_permutes else [n]
    f32 = jnp.float32

    def swapped(rows_, bit):
        return lax.ppermute(rows_, "dev", [(i, i ^ bit) for i in range(peers)])

    def passed(rows_, by):
        pairs = [(i, i + by) for i in range(peers) if 0 <= i + by < peers]
        return lax.ppermute(rows_, "dev", pairs)

    def after_all(value, *others):
        return lax.optimization_barrier((value, *others))[0]

    def as_received(values, axis, plane):
        return xor_order(values, axis, plane) if by_permutes else values

    where_to = position.reshape(1, n)
    in_hbm = pl.BlockSpec(memory_space=pltpu.HBM)
    *arranged, rank = call(
        functools.partial(arrange_kernel, per_half, 2 * planes),
        [jax.ShapeDtypeStruct((size, width), embeddings.dtype) for size in pieces]
        + [jax.ShapeDtypeStruct((1, n), jnp.int32)],
        in_specs=[in_hbm, in_hbm],
        scratch_shapes=[
            pltpu.VMEM((1, n), jnp.int32),
            pltpu.VMEM((n, width), embeddings.dtype),
            pltpu.SemaphoreType.DMA((2,)),
        ],
    )(where_to, embeddings)
    if by_permutes:
        own_upper, own_lower, to_1, upper_2, lower_2, upper_3, lower_3 = arranged
        upper_3 = swapped(upper_3, 3 * QUAD)
        upper_2 = swapped(upper_2, 2 * QUAD)
        both_1 = swapped(to_1, QUAD)
        lower_3 = swapped(lower_3, 3 * QUAD)
        lower_2 = swapped(lower_2, 2 * QUAD)
        upper = jnp.concatenate([own_upper, both_1[:per_half], upper_2, upper_3], axis=0)
        lower = jnp.concatenate([own_lower, both_1[per_half:], lower_2, lower_3], axis=0)
    else:
        lines = [[p * QUAD + q for p in range(planes)] for q in range(QUAD)]
        block = lax.all_to_all(
            arranged[0], "dev", split_axis=0, concat_axis=0, axis_index_groups=lines, tiled=True
        ).reshape(planes, 2, per_half, width)
        upper = block[:, 1].reshape(n // 2, width)
        lower = block[:, 0].reshape(n // 2, width)

    facts = call(
        functools.partial(facts_kernel, per_half), jax.ShapeDtypeStruct((4, n), f32)
    )(where_to, cluster_ids.reshape(1, n), rank, *arranged)
    seen = jnp.pad(facts[:2], ((0, 0), (per_half, per_half)))
    seen = jnp.stack(
        [seen[:, 2 * p * per_half : (2 * p + 4) * per_half] for p in range(planes)]
    ).reshape(planes, 1, 8 * per_half)
    facts = jnp.concatenate(
        [
            jnp.broadcast_to(seen, (planes, QUAD, 8 * per_half)),
            jnp.broadcast_to(facts[2], (planes, QUAD, n)),
        ],
        axis=2,
    )
    facts = after_all(facts, both_1 if by_permutes else block)
    facts = lax.all_to_all(
        facts.reshape(peers, 8 * per_half + n), "dev", split_axis=0, concat_axis=0, tiled=True
    )
    arrays = {"b0h": upper}
    arrays["b2h"] = swapped(upper, 2)
    arrays["b1h"] = swapped(upper, 1)
    lower = after_all(lower, arrays["b1h"])
    arrays["b0l"] = lower
    arrays["u"] = passed(upper, QUAD)
    arrays["b2l"] = swapped(lower, 2)
    arrays["l"] = passed(lower, -QUAD)
    arrays["b1l"] = swapped(lower, 1)

    facts = after_all(facts, arrays["b1h"])
    ids = jnp.pad(facts[:, 8 * per_half :].reshape(peers * n), (MOST, MOST))
    ids = lax.dynamic_slice_in_dim(ids, slab * MOST, 3 * MOST, 0)
    near = facts[:, : 8 * per_half].reshape(planes, QUAD, 2, 4, per_half)
    near = xor_order(near, 1, lane).transpose(2, 1, 3, 0, 4)
    before = as_received(near[:, :2, 0], 2, slab - 1)
    after = as_received(near[:, :2, 3], 2, slab + 1)
    own = as_received(near[:, :3, 1:3], 3, slab)
    near = jnp.concatenate(
        [
            jnp.stack([own[:, :, 1], own[:, :, 0]], axis=2).reshape(2, 3 * n),
            jnp.stack([before, after], axis=2).reshape(2, 2 * n),
        ],
        axis=1,
    )
    total = 5 * n
    place = near[0].astype(jnp.int32) - (slab - 1) * MOST
    label = call(labels_kernel, jax.ShapeDtypeStruct((1, total), f32))(
        place.reshape(1, total), ids.reshape(3 * MOST // LANES, LANES)
    )[0]
    at = jnp.arange(total)
    absent = (at >= 3 * n) & jnp.where(at % n >= n // 2, slab == planes - 1, slab == 0)
    label = jnp.where(absent, -1.0, label)
    rows = jnp.stack([near[1], label])
    columns = jnp.stack([near[1] * SCALE, label], axis=1)

    def masses_after(jobs, last=None):
        return masses_call(jobs, arrays, rows, columns, last)

    masses = masses_after(
        [("b0h", "b0h"), ("b1h", "b0h"), ("b2h", "b0h"), ("b1h", "b2h")]
        + [("b0l", "b0l"), ("b0h", "b0l"), ("b1h", "b0l"), ("b2h", "b0l")]
        + [("b1l", "b0h"), ("b1l", "b0l"), ("b1l", "b2h")]
    )
    arrays["u1"] = swapped(after_all(arrays['u'], arrays["b2h"]), 1)
    masses = masses_after([(u, b) for u in ("u", "u1") for b in ("b0h", "b0l", "b2h")], masses)
    arrays["l1"] = swapped(after_all(arrays["l"], masses, arrays["b2l"]), 1)
    masses = masses_after(
        [("b2l", "b0h"), ("b2l", "b0l"), ("b1h", "b2l"), ("b1l", "b2l")]
        + [("u", "b2l"), ("u1", "b2l"), ("l", "b0l"), ("l", "b2l")],
        masses,
    )
    masses = masses_after([("l1", "b0l"), ("l1", "b2l")], masses)

    if by_permutes:
        across = swapped(masses[2:4], 2)
        beside = swapped(masses[6:8], 1)
        sums = call(combine_kernel, [jax.ShapeDtypeStruct((4, per_half), f32)] * planes)(
            masses, across, beside
        )
        returned = [sums[0]] + [swapped(sums[x], x * QUAD) for x in range(1, planes)]
    else:
        masses = masses.reshape(4, 2, planes, per_half)
        slabs = as_received(masses[:2], 2, slab)
        before = as_received(masses[2:, 0], 1, slab - 1)
        after = as_received(masses[2:, 1], 1, slab + 1)
        none = jnp.zeros_like(before[0])
        outgoing = jnp.stack(
            [
                jnp.stack([slabs[0, 1], none, slabs[1, 1], none]),
                jnp.stack([slabs[0, 0], none, slabs[1, 0], none]),
                jnp.stack([before[0], before[1], none, none]),
                jnp.stack([after[0], after[1], none, none]),
            ],
            axis=2,
        )
        outgoing = xor_order(outgoing, 0, lane).transpose(1, 0, 2, 3)
        returned = lax.all_to_all(
            outgoing.reshape(peers, 4 * per_half), "dev", split_axis=0, concat_axis=0, tiled=True
        )
        returned = [returned.reshape(4 * peers, per_half)]
    weight = call(
        functools.partial(weights_kernel, by_permutes), jax.ShapeDtypeStruct((1, n), f32)
    )(rank, *returned)
    return weight.reshape(n)


def solution(mesh):
    return jax.shard_map(
        shards,
        mesh=mesh,
        in_specs=(P(("grp", "dev"), None), P(("grp", "dev")), P(("grp", "dev"))),
        out_specs=P(("grp", "dev")),
        check_vma=False,
    )
```

```python
import functools
import math

import jax
import jax.numpy as jnp
from jax import lax
from jax.experimental import pallas as pl
from jax.experimental.pallas import tpu as pltpu
from jax.sharding import PartitionSpec as P

MOST = 2048
HALF = MOST // 2
SIMILARITY_CUTOFF = 0.9
SOFTMAX_HEAT = 0.02
SCALE = math.log2(math.e) / SOFTMAX_HEAT
SHIFT = SIMILARITY_CUTOFF * SCALE
QUAD = 4
CHUNK = 256
LANES = 128
VMEM_LIMIT = 16 * 1024 * 1024

NT = (((1,), (1,)), ((), ()))
TN = (((0,), (0,)), ((), ()))


def iota(shape, dim):
    return lax.broadcasted_iota(jnp.int32, shape, dim)


def call(kernel, out_shape, limit=VMEM_LIMIT, **extra):
    return pl.pallas_call(
        kernel,
        out_shape=out_shape,
        compiler_params=pltpu.CompilerParams(vmem_limit_bytes=limit),
        **extra,
    )


def arrange_kernel(per_half, halves, position_hbm, rows_hbm, *refs):
    *outs, rank_ref, place, rows, sems = refs
    copies = [
        pltpu.make_async_copy(position_hbm, place, sems.at[0]),
        pltpu.make_async_copy(rows_hbm, rows, sems.at[1]),
    ]
    for copy in copies:
        copy.start()
    n = rows.shape[0]
    earlier = (iota((n, n), 0) < iota((n, n), 1)).astype(jnp.bfloat16)
    copies[0].wait()
    half = place[...] // HALF
    kinds = iota((halves, n), 0) == half
    counts = jnp.dot(kinds.astype(jnp.bfloat16), earlier, preferred_element_type=jnp.float32)
    count = jnp.sum(jnp.where(kinds, counts, 0.0), axis=0, keepdims=True).astype(jnp.int32)
    rank_ref[...] = half * per_half + count
    rank = half * per_half + count
    if len(outs) > 1:
        plane = (half // 2) ^ (lax.axis_index("dev") // QUAD)
        rank = (2 * plane + 1 - half % 2) * per_half + count
    pick = (iota((n, n), 0) == rank).astype(jnp.bfloat16)
    copies[1].wait()
    picked = jnp.dot(pick, rows[...], preferred_element_type=jnp.float32)
    at = 0
    for out in outs:
        out[...] = picked[at : at + out.shape[0], :].astype(out.dtype)
        at += out.shape[0]


def facts_kernel(per_half, position_ref, ids_ref, rank_ref, *refs):
    *pieces, out_ref = refs
    n = position_ref.shape[1]
    pick = iota((n, n), 0) == rank_ref[...]
    where_to = position_ref[...].astype(jnp.float32)
    column = jnp.sum(jnp.where(pick, where_to, 0.0), axis=1, keepdims=True)
    eye = iota((n, n), 0) == iota((n, n), 1)
    out_ref[0:1, :] = jnp.sum(jnp.where(eye, column, 0.0), axis=0, keepdims=True)
    total = jnp.zeros((1, n), jnp.float32)
    k = 0
    for piece in pieces:
        size = n if len(pieces) == 1 else per_half
        for start in range(0, piece.shape[0], size):
            wide = piece[start : start + size, :].astype(jnp.float32)
            inverse = lax.rsqrt(jnp.sum(wide * wide, axis=1, keepdims=True) + 1e-06)
            first = 0
            if len(pieces) > 1:
                plane = (k // 2) ^ (lax.axis_index("dev") // QUAD)
                first = (2 * plane + 1 - k % 2) * per_half
            here = iota((size, n), 0) + first == iota((size, n), 1)
            total += jnp.sum(jnp.where(here, inverse, 0.0), axis=0, keepdims=True)
            k += 1
    out_ref[1:2, :] = total
    out_ref[2:3, :] = ids_ref[...].astype(jnp.float32)
    out_ref[3:4, :] = jnp.zeros((1, n), jnp.float32)


def labels_kernel(place_ref, table_ref, out_ref):
    place = place_ref[...]
    depth = table_ref.shape[0]
    n = place.shape[1]
    table = table_ref[...]
    high = jnp.floor(table * (1.0 / 256.0))
    low = table - high * 256.0
    line = (iota((depth, n), 0) == place // LANES).astype(jnp.bfloat16)
    high = lax.dot_general(
        high.astype(jnp.bfloat16), line, TN, preferred_element_type=jnp.float32
    )
    low = lax.dot_general(
        low.astype(jnp.bfloat16), line, TN, preferred_element_type=jnp.float32
    )
    here = iota((LANES, n), 0) == place % LANES
    out_ref[...] = jnp.sum(jnp.where(here, high * 256.0 + low, 0.0), axis=0, keepdims=True)


NAMES = ("b0h", "b0l", "b1h", "b1l", "b2h", "b2l", "u", "l", "u1", "l1")
SUMS = ("b0h", "b0l", "b2h", "b2l", "u", "l", "u1", "l1")


class Terms:
    def __init__(self, arrays, rows_ref, columns_ref, out_ref, last_ref):
        self.arrays, self.rows, self.columns, self.out = arrays, rows_ref, columns_ref, out_ref
        self.last = last_ref
        self.sums = {}

    def add(self, name, values):
        self.sums[name] = self.sums[name] + values if name in self.sums else values

    def job(self, down, across):
        n = self.arrays[down].shape[0]
        products = lax.dot_general(
            self.arrays[down][...],
            self.arrays[across][...],
            NT,
            preferred_element_type=jnp.float32,
        )
        at, to = NAMES.index(down) * n, NAMES.index(across) * n
        scale = self.columns[at : at + n, 0:1]
        label = self.columns[at : at + n, 1:2]
        power = products * scale * self.rows[0:1, to : to + n] - SHIFT
        mask = label == self.rows[1:2, to : to + n]
        if down == across:
            mask &= iota((n, n), 0) != iota((n, n), 1)
        values = jnp.where(mask, jnp.exp2(power), 0.0)
        self.add(across, jnp.sum(values, axis=0, keepdims=True))
        if down in ("u", "l", "u1", "l1") or (down, across) == ("b0h", "b0l"):
            side = jnp.zeros((n, LANES), jnp.float32)
            for lane in range(0, n, LANES):
                side += values[:, lane : lane + LANES]
            self.add(down, jnp.sum(side.T, axis=0, keepdims=True))

    def write(self):
        for k, name in enumerate(SUMS):
            values = self.sums.get(name)
            last = self.last[k : k + 1, :] if self.last is not None else None
            if values is None:
                values = jnp.zeros((1, self.out.shape[1]), jnp.float32) if last is None else last
            elif last is not None:
                values += last
            self.out[k : k + 1, :] = values


def masses_call(jobs, arrays, rows, columns, last=None):
    names = [name for name in NAMES if any(name in job for job in jobs)]

    def kernel(*refs):
        refs = list(refs)
        held = {name: refs.pop(0) for name in names}
        rows_ref, columns_ref = refs.pop(0), refs.pop(0)
        last_ref = refs.pop(0) if last is not None else None
        t = Terms(held, rows_ref, columns_ref, refs.pop(0), last_ref)
        for job in jobs:
            t.job(*job)
        t.write()

    operands = [arrays[name] for name in names] + [rows, columns]
    if last is not None:
        operands.append(last)
    n, width = operands[0].shape
    return call(
        kernel,
        jax.ShapeDtypeStruct((len(SUMS), n), jnp.float32),
        cost_estimate=pl.CostEstimate(flops=0, transcendentals=0, bytes_accessed=0),
    )(*operands)


def weights_kernel(rank_ref, returned_ref, out_ref):
    returned = returned_ref[...]
    count, m = returned.shape
    rank = rank_ref[...]
    n = rank.shape[1]
    slab, upper, member = rank // (2 * m), rank // m % 2 == 1, rank % m
    shape = (count, n)
    plane = iota(shape, 0) // (count * 2 * m // n)
    kind = iota(shape, 0) % 4
    own = (plane == slab) & (kind == jnp.where(upper, 1, 0))
    halo = (plane == jnp.where(upper, slab + 1, slab - 1)) & (kind == jnp.where(upper, 2, 3))
    picked = lax.dot_general(
        returned,
        jnp.where(own | halo, 1.0, 0.0),
        TN,
        precision=lax.Precision.HIGHEST,
        preferred_element_type=jnp.float32,
    )
    mass = jnp.sum(jnp.where(iota((m, n), 0) == member, picked, 0.0), axis=0, keepdims=True)
    out_ref[...] = 1.0 / (1.0 + mass)


def xor_order(array, axis, bits):
    count = array.shape[axis]
    for k in range(count.bit_length() - 1):
        step = 1 << k
        shape = array.shape[:axis] + (count // (2 * step), 2, step) + array.shape[axis + 1 :]
        split = array.reshape(shape)
        split = jnp.where((bits >> k) & 1 == 1, jnp.flip(split, axis + 1), split)
        array = split.reshape(array.shape)
    return array


def shards(embeddings, position, cluster_ids):
    n, width = embeddings.shape
    peers = lax.axis_size("dev")
    me = lax.axis_index("dev")
    planes = peers // QUAD
    slab, lane = me // QUAD, me % QUAD
    per_half = n // (2 * planes)
    by_permutes = planes == 4
    pieces = [per_half] * 2 + [2 * per_half] + [per_half] * 4 if by_permutes else [n]
    f32 = jnp.float32

    def swapped(rows_, bit):
        return lax.ppermute(rows_, "dev", [(i, i ^ bit) for i in range(peers)])

    def passed(rows_, by):
        pairs = [(i, i + by) for i in range(peers) if 0 <= i + by < peers]
        return lax.ppermute(rows_, "dev", pairs)

    def after_all(value, *others):
        return lax.optimization_barrier((value, *others))[0]

    def as_received(values, axis, plane):
        return xor_order(values, axis, plane) if by_permutes else values

    where_to = position.reshape(1, n)
    in_hbm = pl.BlockSpec(memory_space=pltpu.HBM)
    *arranged, rank = call(
        functools.partial(arrange_kernel, per_half, 2 * planes),
        [jax.ShapeDtypeStruct((size, width), embeddings.dtype) for size in pieces]
        + [jax.ShapeDtypeStruct((1, n), jnp.int32)],
        in_specs=[in_hbm, in_hbm],
        scratch_shapes=[
            pltpu.VMEM((1, n), jnp.int32),
            pltpu.VMEM((n, width), embeddings.dtype),
            pltpu.SemaphoreType.DMA((2,)),
        ],
    )(where_to, embeddings)
    if by_permutes:
        own_upper, own_lower, to_1, upper_2, lower_2, upper_3, lower_3 = arranged
        upper_3 = swapped(upper_3, 3 * QUAD)
        upper_2 = swapped(upper_2, 2 * QUAD)
        both_1 = swapped(to_1, QUAD)
        lower_3 = swapped(lower_3, 3 * QUAD)
        lower_2 = swapped(lower_2, 2 * QUAD)
        upper = jnp.concatenate([own_upper, both_1[:per_half], upper_2, upper_3], axis=0)
        lower = jnp.concatenate([own_lower, both_1[per_half:], lower_2, lower_3], axis=0)
    else:
        lines = [[p * QUAD + q for p in range(planes)] for q in range(QUAD)]
        block = lax.all_to_all(
            arranged[0], "dev", split_axis=0, concat_axis=0, axis_index_groups=lines, tiled=True
        ).reshape(planes, 2, per_half, width)
        upper = block[:, 1].reshape(n // 2, width)
        lower = block[:, 0].reshape(n // 2, width)

    facts = call(
        functools.partial(facts_kernel, per_half), jax.ShapeDtypeStruct((4, n), f32)
    )(where_to, cluster_ids.reshape(1, n), rank, *arranged)
    seen = jnp.pad(facts[:2], ((0, 0), (per_half, per_half)))
    seen = jnp.stack(
        [seen[:, 2 * p * per_half : (2 * p + 4) * per_half] for p in range(planes)]
    ).reshape(planes, 1, 8 * per_half)
    facts = jnp.concatenate(
        [
            jnp.broadcast_to(seen, (planes, QUAD, 8 * per_half)),
            jnp.broadcast_to(facts[2], (planes, QUAD, n)),
        ],
        axis=2,
    )
    facts = after_all(facts, both_1 if by_permutes else block)
    facts = lax.all_to_all(
        facts.reshape(peers, 8 * per_half + n), "dev", split_axis=0, concat_axis=0, tiled=True
    )
    arrays = {"b0h": upper}
    arrays["b2h"] = swapped(upper, 2)
    arrays["b1h"] = swapped(upper, 1)
    lower = after_all(lower, arrays["b1h"])
    arrays["b0l"] = lower
    arrays["u"] = passed(upper, QUAD)
    arrays["b2l"] = swapped(lower, 2)
    arrays["l"] = passed(lower, -QUAD)
    arrays["b1l"] = swapped(lower, 1)

    ids = jnp.pad(facts[:, 8 * per_half :].reshape(peers * n), (MOST, MOST))
    ids = lax.dynamic_slice_in_dim(ids, slab * MOST, 3 * MOST, 0)
    near = facts[:, : 8 * per_half].reshape(planes, QUAD, 2, 4, per_half)
    near = xor_order(near, 1, lane).transpose(2, 1, 3, 0, 4)
    before = as_received(near[:, :2, 0], 2, slab - 1)
    after = as_received(near[:, :2, 3], 2, slab + 1)
    own = as_received(near[:, :3, 1:3], 3, slab)
    near = jnp.concatenate(
        [
            jnp.stack([own[:, :, 1], own[:, :, 0]], axis=2).reshape(2, 3 * n),
            jnp.stack([before, after], axis=2).reshape(2, 2 * n),
        ],
        axis=1,
    )
    total = 5 * n
    place = near[0].astype(jnp.int32) - (slab - 1) * MOST
    label = call(labels_kernel, jax.ShapeDtypeStruct((1, total), f32))(
        place.reshape(1, total), ids.reshape(3 * MOST // LANES, LANES)
    )[0]
    at = jnp.arange(total)
    absent = (at >= 3 * n) & jnp.where(at % n >= n // 2, slab == planes - 1, slab == 0)
    label = jnp.where(absent, -1.0, label)
    rows = jnp.stack([near[1], label])
    columns = jnp.stack([near[1] * SCALE, label], axis=1)

    def masses_after(jobs, last=None):
        return masses_call(jobs, arrays, rows, columns, last)

    masses = masses_after(
        [("b0h", "b0h"), ("b1h", "b0h"), ("b2h", "b0h"), ("b1h", "b2h")]
        + [("b0l", "b0l"), ("b0h", "b0l"), ("b1h", "b0l"), ("b2h", "b0l")]
        + [("b1l", "b0h"), ("b1l", "b0l"), ("b1l", "b2h")]
    )
    arrays["u1"] = swapped(after_all(arrays['u'], arrays["b2h"]), 1)
    masses = masses_after([(u, b) for u in ("u", "u1") for b in ("b0h", "b0l", "b2h")], masses)
    arrays["l1"] = swapped(after_all(arrays["l"], masses, arrays["b2l"]), 1)
    masses = masses_after(
        [("b2l", "b0h"), ("b2l", "b0l"), ("b1h", "b2l"), ("b1l", "b2l")]
        + [("u", "b2l"), ("u1", "b2l"), ("l", "b0l"), ("l", "b2l")],
        masses,
    )
    masses = masses_after([("l1", "b0l"), ("l1", "b2l")], masses)

    masses = masses.reshape(4, 2, planes, per_half)
    slabs = as_received(masses[:2], 2, slab)
    before = as_received(masses[2:, 0], 1, slab - 1)
    after = as_received(masses[2:, 1], 1, slab + 1)
    none = jnp.zeros_like(before[0])
    outgoing = jnp.stack(
        [
            jnp.stack([slabs[0, 1], none, slabs[1, 1], none]),
            jnp.stack([slabs[0, 0], none, slabs[1, 0], none]),
            jnp.stack([before[0], before[1], none, none]),
            jnp.stack([after[0], after[1], none, none]),
        ],
        axis=2,
    )
    outgoing = xor_order(outgoing, 0, lane).transpose(1, 0, 2, 3)
    returned = lax.all_to_all(
        outgoing.reshape(peers, 4 * per_half), "dev", split_axis=0, concat_axis=0, tiled=True
    )
    returned = returned.reshape(4 * peers, per_half)
    weight = call(
        weights_kernel, jax.ShapeDtypeStruct((1, n), f32)
    )(rank, returned)
    return weight.reshape(n)


def solution(mesh):
    return jax.shard_map(
        shards,
        mesh=mesh,
        in_specs=(P(("grp", "dev"), None), P(("grp", "dev")), P(("grp", "dev"))),
        out_specs=P(("grp", "dev")),
        check_vma=False,
    )
```

```python
import functools
import math

import jax
import jax.numpy as jnp
from jax import lax
from jax.experimental import pallas as pl
from jax.experimental.pallas import tpu as pltpu
from jax.sharding import PartitionSpec as P

MOST = 2048
HALF = MOST // 2
SIMILARITY_CUTOFF = 0.9
SOFTMAX_HEAT = 0.02
SCALE = math.log2(math.e) / SOFTMAX_HEAT
SHIFT = SIMILARITY_CUTOFF * SCALE
QUAD = 4
CHUNK = 256
LANES = 128
VMEM_LIMIT = 16 * 1024 * 1024

NT = (((1,), (1,)), ((), ()))
TN = (((0,), (0,)), ((), ()))


def iota(shape, dim):
    return lax.broadcasted_iota(jnp.int32, shape, dim)


def call(kernel, out_shape, limit=VMEM_LIMIT, **extra):
    return pl.pallas_call(
        kernel,
        out_shape=out_shape,
        compiler_params=pltpu.CompilerParams(vmem_limit_bytes=limit),
        **extra,
    )


def arrange_kernel(per_half, halves, position_hbm, rows_hbm, *refs):
    *outs, rank_ref, place, rows, sems = refs
    copies = [
        pltpu.make_async_copy(position_hbm, place, sems.at[0]),
        pltpu.make_async_copy(rows_hbm, rows, sems.at[1]),
    ]
    for copy in copies:
        copy.start()
    n = rows.shape[0]
    earlier = (iota((n, n), 0) < iota((n, n), 1)).astype(jnp.bfloat16)
    copies[0].wait()
    half = place[...] // HALF
    kinds = iota((halves, n), 0) == half
    counts = jnp.dot(kinds.astype(jnp.bfloat16), earlier, preferred_element_type=jnp.float32)
    count = jnp.sum(jnp.where(kinds, counts, 0.0), axis=0, keepdims=True).astype(jnp.int32)
    rank_ref[...] = half * per_half + count
    rank = half * per_half + count
    if len(outs) > 1:
        plane = (half // 2) ^ (lax.axis_index("dev") // QUAD)
        rank = (2 * plane + 1 - half % 2) * per_half + count
    pick = (iota((n, n), 0) == rank).astype(jnp.bfloat16)
    copies[1].wait()
    picked = jnp.dot(pick, rows[...], preferred_element_type=jnp.float32)
    at = 0
    for out in outs:
        out[...] = picked[at : at + out.shape[0], :].astype(out.dtype)
        at += out.shape[0]


def facts_kernel(per_half, position_ref, ids_ref, rank_ref, *refs):
    *pieces, out_ref = refs
    n = position_ref.shape[1]
    pick = iota((n, n), 0) == rank_ref[...]
    where_to = position_ref[...].astype(jnp.float32)
    column = jnp.sum(jnp.where(pick, where_to, 0.0), axis=1, keepdims=True)
    eye = iota((n, n), 0) == iota((n, n), 1)
    out_ref[0:1, :] = jnp.sum(jnp.where(eye, column, 0.0), axis=0, keepdims=True)
    total = jnp.zeros((1, n), jnp.float32)
    k = 0
    for piece in pieces:
        size = n if len(pieces) == 1 else per_half
        for start in range(0, piece.shape[0], size):
            wide = piece[start : start + size, :].astype(jnp.float32)
            inverse = lax.rsqrt(jnp.sum(wide * wide, axis=1, keepdims=True) + 1e-06)
            first = 0
            if len(pieces) > 1:
                plane = (k // 2) ^ (lax.axis_index("dev") // QUAD)
                first = (2 * plane + 1 - k % 2) * per_half
            here = iota((size, n), 0) + first == iota((size, n), 1)
            total += jnp.sum(jnp.where(here, inverse, 0.0), axis=0, keepdims=True)
            k += 1
    out_ref[1:2, :] = total
    out_ref[2:3, :] = ids_ref[...].astype(jnp.float32)
    out_ref[3:4, :] = jnp.zeros((1, n), jnp.float32)


def labels_kernel(place_ref, table_ref, out_ref):
    place = place_ref[...]
    depth = table_ref.shape[0]
    n = place.shape[1]
    table = table_ref[...]
    high = jnp.floor(table * (1.0 / 256.0))
    low = table - high * 256.0
    line = (iota((depth, n), 0) == place // LANES).astype(jnp.bfloat16)
    high = lax.dot_general(
        high.astype(jnp.bfloat16), line, TN, preferred_element_type=jnp.float32
    )
    low = lax.dot_general(
        low.astype(jnp.bfloat16), line, TN, preferred_element_type=jnp.float32
    )
    here = iota((LANES, n), 0) == place % LANES
    out_ref[...] = jnp.sum(jnp.where(here, high * 256.0 + low, 0.0), axis=0, keepdims=True)


NAMES = ("b0p", "b0q", "b1p", "b1q", "b2p", "b2q", "u", "l", "u1", "l1")
SUMS = ("b0p", "b0q", "b2p", "b2q", "u", "l", "u1", "l1")


class Terms:
    def __init__(self, arrays, rows_ref, columns_ref, out_ref, last_ref):
        self.arrays, self.rows, self.columns, self.out = arrays, rows_ref, columns_ref, out_ref
        self.last = last_ref
        self.sums = {}

    def add(self, name, values):
        self.sums[name] = self.sums[name] + values if name in self.sums else values

    def job(self, down, across):
        n = self.arrays[down].shape[0]
        products = lax.dot_general(
            self.arrays[down][...],
            self.arrays[across][...],
            NT,
            preferred_element_type=jnp.float32,
        )
        at, to = NAMES.index(down) * n, NAMES.index(across) * n
        scale = self.columns[at : at + n, 0:1]
        label = self.columns[at : at + n, 1:2]
        power = products * scale * self.rows[0:1, to : to + n] - SHIFT
        row = 2 if down in ("l", "l1") else 1
        mask = label == self.rows[row : row + 1, to : to + n]
        if down == across:
            mask &= iota((n, n), 0) != iota((n, n), 1)
        values = jnp.where(mask, jnp.exp2(power), 0.0)
        self.add(across, jnp.sum(values, axis=0, keepdims=True))
        if down in ("u", "l", "u1", "l1") or (down, across) == ("b0p", "b0q"):
            side = jnp.zeros((n, LANES), jnp.float32)
            for lane in range(0, n, LANES):
                side += values[:, lane : lane + LANES]
            self.add(down, jnp.sum(side.T, axis=0, keepdims=True))

    def write(self):
        for k, name in enumerate(SUMS):
            values = self.sums.get(name)
            last = self.last[k : k + 1, :] if self.last is not None else None
            if values is None:
                values = jnp.zeros((1, self.out.shape[1]), jnp.float32) if last is None else last
            elif last is not None:
                values += last
            self.out[k : k + 1, :] = values


def masses_call(jobs, arrays, rows, columns, last=None):
    names = [name for name in NAMES if any(name in job for job in jobs)]

    def kernel(*refs):
        refs = list(refs)
        held = {name: refs.pop(0) for name in names}
        rows_ref, columns_ref = refs.pop(0), refs.pop(0)
        last_ref = refs.pop(0) if last is not None else None
        t = Terms(held, rows_ref, columns_ref, refs.pop(0), last_ref)
        for job in jobs:
            t.job(*job)
        t.write()

    operands = [arrays[name] for name in names] + [rows, columns]
    if last is not None:
        operands.append(last)
    n, width = operands[0].shape
    return call(
        kernel,
        jax.ShapeDtypeStruct((len(SUMS), n), jnp.float32),
        cost_estimate=pl.CostEstimate(flops=0, transcendentals=0, bytes_accessed=0),
    )(*operands)


def weights_kernel(rank_ref, returned_ref, out_ref):
    returned = returned_ref[...]
    count, m = returned.shape
    rank = rank_ref[...]
    n = rank.shape[1]
    slab, upper, member = rank // (2 * m), rank // m % 2 == 1, rank % m
    shape = (count, n)
    plane = iota(shape, 0) // (count * 2 * m // n)
    kind = iota(shape, 0) % 4
    own = (plane == slab) & (kind == jnp.where(upper, 1, 0))
    halo = (plane == jnp.where(upper, slab + 1, slab - 1)) & (kind == jnp.where(upper, 2, 3))
    picked = lax.dot_general(
        returned,
        jnp.where(own | halo, 1.0, 0.0),
        TN,
        precision=lax.Precision.HIGHEST,
        preferred_element_type=jnp.float32,
    )
    mass = jnp.sum(jnp.where(iota((m, n), 0) == member, picked, 0.0), axis=0, keepdims=True)
    out_ref[...] = 1.0 / (1.0 + mass)


def xor_order(array, axis, bits):
    count = array.shape[axis]
    for k in range(count.bit_length() - 1):
        step = 1 << k
        shape = array.shape[:axis] + (count // (2 * step), 2, step) + array.shape[axis + 1 :]
        split = array.reshape(shape)
        split = jnp.where((bits >> k) & 1 == 1, jnp.flip(split, axis + 1), split)
        array = split.reshape(array.shape)
    return array


def shards(embeddings, position, cluster_ids):
    n, width = embeddings.shape
    peers = lax.axis_size("dev")
    me = lax.axis_index("dev")
    planes = peers // QUAD
    slab, lane = me // QUAD, me % QUAD
    per_half = n // (2 * planes)
    per_slab = 2 * per_half
    by_permutes = planes == 4
    pieces = [2 * per_half] * planes if by_permutes else [n]
    f32 = jnp.float32

    def swapped(rows_, bit):
        return lax.ppermute(rows_, "dev", [(i, i ^ bit) for i in range(peers)])

    def passed(rows_, by):
        pairs = [(i, i + by) for i in range(peers) if 0 <= i + by < peers]
        return lax.ppermute(rows_, "dev", pairs)

    def after_all(value, *others):
        return lax.optimization_barrier((value, *others))[0]

    def as_received(values, axis, plane):
        return xor_order(values, axis, plane) if by_permutes else values

    where_to = position.reshape(1, n)
    in_hbm = pl.BlockSpec(memory_space=pltpu.HBM)
    *arranged, rank = call(
        functools.partial(arrange_kernel, per_half, 2 * planes),
        [jax.ShapeDtypeStruct((size, width), embeddings.dtype) for size in pieces]
        + [jax.ShapeDtypeStruct((1, n), jnp.int32)],
        in_specs=[in_hbm, in_hbm],
        scratch_shapes=[
            pltpu.VMEM((1, n), jnp.int32),
            pltpu.VMEM((n, width), embeddings.dtype),
            pltpu.SemaphoreType.DMA((2,)),
        ],
    )(where_to, embeddings)
    if by_permutes:
        block = [arranged[0]] + [swapped(arranged[x], x * QUAD) for x in range(1, planes)]
        halves = [piece.reshape(2, per_half, width) for piece in block]
        parts = [jnp.concatenate(block[:2], axis=0), jnp.concatenate(block[2:], axis=0)]
        upper = jnp.concatenate([piece[0] for piece in halves], axis=0)
        lower = jnp.concatenate([piece[1] for piece in halves], axis=0)
        first = block[1]
    else:
        lines = [[p * QUAD + q for p in range(planes)] for q in range(QUAD)]
        block = lax.all_to_all(
            arranged[0], "dev", split_axis=0, concat_axis=0, axis_index_groups=lines, tiled=True
        ).reshape(planes, 2, per_half, width)[:, ::-1]
        parts = [part.reshape(n // 2, width) for part in jnp.split(block, 2)]
        upper = block[:, 0].reshape(n // 2, width)
        lower = block[:, 1].reshape(n // 2, width)
        first = lower

    arrays = {"b0p": parts[0], "b0q": parts[1]}
    if by_permutes:
        own_across = swapped(block[0], 2)
        rest_across = swapped(after_all(block[1], own_across), 2)
        arrays["b2p"] = jnp.concatenate([own_across, rest_across], axis=0)
    else:
        arrays["b2p"] = swapped(parts[0], 2)
    arrays["b1p"] = swapped(parts[0], 1)

    facts = call(
        functools.partial(facts_kernel, per_half), jax.ShapeDtypeStruct((4, n), f32)
    )(where_to, cluster_ids.reshape(1, n), rank, *arranged)
    seen = jnp.pad(facts[:2], ((0, 0), (per_half, per_half)))
    seen = jnp.stack(
        [seen[:, 2 * p * per_half : (2 * p + 4) * per_half] for p in range(planes)]
    ).reshape(planes, 1, 8 * per_half)
    facts = jnp.concatenate(
        [
            jnp.broadcast_to(seen, (planes, QUAD, 8 * per_half)),
            jnp.broadcast_to(facts[2], (planes, QUAD, n)),
        ],
        axis=2,
    )
    facts = after_all(facts, first)
    facts = lax.all_to_all(
        facts.reshape(peers, 8 * per_half + n), "dev", split_axis=0, concat_axis=0, tiled=True
    )
    arrays["b2q"] = swapped(parts[1], 2)
    arrays["u"] = passed(upper, QUAD)
    arrays["l"] = passed(lower, -QUAD)
    arrays["b1q"] = swapped(after_all(parts[1], arrays["b1p"]), 1)
    facts = after_all(facts, arrays["b1q"])
    ids = jnp.pad(facts[:, 8 * per_half :].reshape(peers * n), (MOST, MOST))
    ids = lax.dynamic_slice_in_dim(ids, slab * MOST, 3 * MOST, 0)
    near = facts[:, : 8 * per_half].reshape(planes, QUAD, 2, 4, per_half)
    near = xor_order(near, 1, lane).transpose(2, 1, 3, 0, 4)
    before = as_received(near[:, :2, 0], 2, slab - 1)
    after = as_received(near[:, :2, 3], 2, slab + 1)
    own = as_received(near[:, :3, 1:3], 3, slab)
    near = jnp.concatenate(
        [
            jnp.stack([own[:, :, 1], own[:, :, 0]], axis=3).reshape(2, 3 * n),
            jnp.stack([before, after], axis=2).reshape(2, 2 * n),
        ],
        axis=1,
    )
    total = 5 * n
    place = near[0].astype(jnp.int32) - (slab - 1) * MOST
    label = call(labels_kernel, jax.ShapeDtypeStruct((1, total), f32))(
        place.reshape(1, total), ids.reshape(3 * MOST // LANES, LANES)
    )[0]
    at = jnp.arange(total)
    absent = (at >= 3 * n) & jnp.where(at % n >= n // 2, slab == planes - 1, slab == 0)
    label = jnp.where(absent, -1.0, label)
    rows = jnp.stack([near[1], label, jnp.where(at % per_slab < per_half, -2.0, label)])
    columns = jnp.stack([near[1] * SCALE, label], axis=1)


    def masses_after(jobs, last=None):
        return masses_call(jobs, arrays, rows, columns, last)

    masses = masses_after(
        [(down, across) for across in ("b0p", "b0q") for down in ("b0p", "b0q", "b1p", "b1q", "b2p")
         if (down, across) != ("b0q", "b0p")]
        + [("b1p", "b2p"), ("b1q", "b2p")]
    )
    arrays["u1"] = swapped(after_all(arrays["u"], masses), 1)
    arrays["l1"] = swapped(after_all(arrays["l"], masses), 1)
    masses = masses_after(
        [("b2q", "b0p"), ("b2q", "b0q"), ("b1p", "b2q"), ("b1q", "b2q")], masses
    )
    everywhere = ("b0p", "b0q", "b2p", "b2q")
    masses = masses_after([(side, b) for side in ("u", "l") for b in everywhere], masses)
    masses = masses_after([(side, b) for side in ("u1", "l1") for b in everywhere], masses)

    slabs = masses[:4].reshape(2, planes, 2, per_half)
    slabs = as_received(slabs, 1, slab).transpose(0, 2, 1, 3)
    masses = masses.reshape(4, 2, planes, per_half)
    before = as_received(masses[2:, 0], 1, slab - 1)
    after = as_received(masses[2:, 1], 1, slab + 1)
    none = jnp.zeros_like(before[0])
    outgoing = jnp.stack(
        [
            jnp.stack([slabs[0, 1], none, slabs[1, 1], none]),
            jnp.stack([slabs[0, 0], none, slabs[1, 0], none]),
            jnp.stack([before[0], before[1], none, none]),
            jnp.stack([after[0], after[1], none, none]),
        ],
        axis=2,
    )
    outgoing = xor_order(outgoing, 0, lane).transpose(1, 0, 2, 3)
    returned = lax.all_to_all(
        outgoing.reshape(peers, 4 * per_half), "dev", split_axis=0, concat_axis=0, tiled=True
    )
    weight = call(weights_kernel, jax.ShapeDtypeStruct((1, n), f32))(
        rank, returned.reshape(4 * peers, per_half)
    )
    return weight.reshape(n)


def solution(mesh):
    return jax.shard_map(
        shards,
        mesh=mesh,
        in_specs=(P(("grp", "dev"), None), P(("grp", "dev")), P(("grp", "dev"))),
        out_specs=P(("grp", "dev")),
        check_vma=False,
    )
```

```python
import functools
import math

import jax
import jax.numpy as jnp
from jax import lax
from jax.experimental import pallas as pl
from jax.experimental.pallas import tpu as pltpu
from jax.sharding import PartitionSpec as P

MOST = 2048
HALF = MOST // 2
SIMILARITY_CUTOFF = 0.9
SOFTMAX_HEAT = 0.02
SCALE = math.log2(math.e) / SOFTMAX_HEAT
SHIFT = SIMILARITY_CUTOFF * SCALE
QUAD = 4
CHUNK = 256
LANES = 128
VMEM_LIMIT = 16 * 1024 * 1024

NT = (((1,), (1,)), ((), ()))
TN = (((0,), (0,)), ((), ()))


def iota(shape, dim):
    return lax.broadcasted_iota(jnp.int32, shape, dim)


def call(kernel, out_shape, limit=VMEM_LIMIT, **extra):
    return pl.pallas_call(
        kernel,
        out_shape=out_shape,
        compiler_params=pltpu.CompilerParams(vmem_limit_bytes=limit),
        **extra,
    )


def arrange_kernel(per_half, halves, position_hbm, rows_hbm, *refs):
    *outs, rank_ref, place, rows, sems = refs
    copies = [
        pltpu.make_async_copy(position_hbm, place, sems.at[0]),
        pltpu.make_async_copy(rows_hbm, rows, sems.at[1]),
    ]
    for copy in copies:
        copy.start()
    n = rows.shape[0]
    earlier = (iota((n, n), 0) < iota((n, n), 1)).astype(jnp.bfloat16)
    copies[0].wait()
    half = place[...] // HALF
    kinds = iota((halves, n), 0) == half
    counts = jnp.dot(kinds.astype(jnp.bfloat16), earlier, preferred_element_type=jnp.float32)
    count = jnp.sum(jnp.where(kinds, counts, 0.0), axis=0, keepdims=True).astype(jnp.int32)
    rank_ref[...] = half * per_half + count
    rank = half * per_half + count
    if len(outs) > 1:
        plane = (half // 2) ^ (lax.axis_index("dev") // QUAD)
        rank = (2 * plane + 1 - half % 2) * per_half + count
    pick = (iota((n, n), 0) == rank).astype(jnp.bfloat16)
    copies[1].wait()
    picked = jnp.dot(pick, rows[...], preferred_element_type=jnp.float32)
    at = 0
    for out in outs:
        out[...] = picked[at : at + out.shape[0], :].astype(out.dtype)
        at += out.shape[0]


def facts_kernel(per_half, position_ref, ids_ref, rank_ref, *refs):
    *pieces, out_ref = refs
    n = position_ref.shape[1]
    pick = iota((n, n), 0) == rank_ref[...]
    where_to = position_ref[...].astype(jnp.float32)
    column = jnp.sum(jnp.where(pick, where_to, 0.0), axis=1, keepdims=True)
    eye = iota((n, n), 0) == iota((n, n), 1)
    out_ref[0:1, :] = jnp.sum(jnp.where(eye, column, 0.0), axis=0, keepdims=True)
    total = jnp.zeros((1, n), jnp.float32)
    k = 0
    for piece in pieces:
        size = n if len(pieces) == 1 else per_half
        for start in range(0, piece.shape[0], size):
            wide = piece[start : start + size, :].astype(jnp.float32)
            inverse = lax.rsqrt(jnp.sum(wide * wide, axis=1, keepdims=True) + 1e-06)
            first = 0
            if len(pieces) > 1:
                plane = (k // 2) ^ (lax.axis_index("dev") // QUAD)
                first = (2 * plane + 1 - k % 2) * per_half
            here = iota((size, n), 0) + first == iota((size, n), 1)
            total += jnp.sum(jnp.where(here, inverse, 0.0), axis=0, keepdims=True)
            k += 1
    out_ref[1:2, :] = total
    out_ref[2:3, :] = ids_ref[...].astype(jnp.float32)
    out_ref[3:4, :] = jnp.zeros((1, n), jnp.float32)


def labels_kernel(place_ref, table_ref, out_ref):
    place = place_ref[...]
    depth = table_ref.shape[0]
    n = place.shape[1]
    table = table_ref[...]
    high = jnp.floor(table * (1.0 / 256.0))
    low = table - high * 256.0
    line = (iota((depth, n), 0) == place // LANES).astype(jnp.bfloat16)
    high = lax.dot_general(
        high.astype(jnp.bfloat16), line, TN, preferred_element_type=jnp.float32
    )
    low = lax.dot_general(
        low.astype(jnp.bfloat16), line, TN, preferred_element_type=jnp.float32
    )
    here = iota((LANES, n), 0) == place % LANES
    out_ref[...] = jnp.sum(jnp.where(here, high * 256.0 + low, 0.0), axis=0, keepdims=True)


NAMES = ("b0h", "b0l", "b1h", "b1l", "b2h", "b2l", "u", "l", "u1", "l1")
SUMS = ("b0h", "b0l", "b2h", "b2l", "u", "l", "u1", "l1")


class Terms:
    def __init__(self, arrays, rows_ref, columns_ref, out_ref, last_ref):
        self.arrays, self.rows, self.columns, self.out = arrays, rows_ref, columns_ref, out_ref
        self.last = last_ref
        self.sums = {}

    def add(self, name, values):
        self.sums[name] = self.sums[name] + values if name in self.sums else values

    def job(self, down, across):
        n = self.arrays[down].shape[0]
        products = lax.dot_general(
            self.arrays[down][...],
            self.arrays[across][...],
            NT,
            preferred_element_type=jnp.float32,
        )
        at, to = NAMES.index(down) * n, NAMES.index(across) * n
        scale = self.columns[at : at + n, 0:1]
        label = self.columns[at : at + n, 1:2]
        power = products * scale * self.rows[0:1, to : to + n] - SHIFT
        mask = label == self.rows[1:2, to : to + n]
        if down == across:
            mask &= iota((n, n), 0) != iota((n, n), 1)
        values = jnp.where(mask, jnp.exp2(power), 0.0)
        self.add(across, jnp.sum(values, axis=0, keepdims=True))
        if down in ("u", "l", "u1", "l1") or (down, across) == ("b0h", "b0l"):
            side = jnp.zeros((n, LANES), jnp.float32)
            for lane in range(0, n, LANES):
                side += values[:, lane : lane + LANES]
            self.add(down, jnp.sum(side.T, axis=0, keepdims=True))

    def totals(self):
        totals = {}
        for k, name in enumerate(SUMS):
            values = self.sums.get(name)
            last = self.last[k : k + 1, :] if self.last is not None else None
            if values is None:
                n = self.arrays["b0l"].shape[0]
                values = jnp.zeros((1, n), jnp.float32) if last is None else last
            elif last is not None:
                values += last
            totals[name] = values
        return totals

    def write(self):
        for k, values in enumerate(self.totals().values()):
            self.out[k : k + 1, :] = values


def lay_out(sums, m, out_ref):
    me = lax.axis_index("dev")
    slab, lane = me // QUAD, me % QUAD
    planes = sums["u"].shape[1] // m
    out_ref[...] = jnp.zeros_like(out_ref)
    places = {
        "b0l": (slab, 0, 0), "b0h": (slab, 0, 1), "u": (slab - 1, 0, 2), "l": (slab + 1, 0, 3),
        "b2l": (slab, 2, 0), "b2h": (slab, 2, 1), "u1": (slab - 1, 1, 2), "l1": (slab + 1, 1, 3),
    }
    for name, (order, line, kind) in places.items():
        for x in range(planes):
            plane = (order % planes) ^ x
            at = (plane * QUAD + (lane ^ line)) * 4 + kind
            out_ref[pl.ds(at, 1), :] = sums[name][:, x * m : (x + 1) * m]


def masses_call(jobs, arrays, rows, columns, last=None, layout=None):
    names = [name for name in NAMES if any(name in job for job in jobs)]

    def kernel(*refs):
        refs = list(refs)
        held = {name: refs.pop(0) for name in names}
        rows_ref, columns_ref = refs.pop(0), refs.pop(0)
        last_ref = refs.pop(0) if last is not None else None
        t = Terms(held, rows_ref, columns_ref, refs.pop(0), last_ref)
        for job in jobs:
            t.job(*job)
        if layout is None:
            t.write()
        else:
            lay_out(t.totals(), layout[1], t.out)

    operands = [arrays[name] for name in names] + [rows, columns]
    if last is not None:
        operands.append(last)
    n, width = operands[0].shape
    return call(
        kernel,
        jax.ShapeDtypeStruct(layout or (len(SUMS), n), jnp.float32),
        cost_estimate=pl.CostEstimate(flops=0, transcendentals=0, bytes_accessed=0),
    )(*operands)


def weights_kernel(rank_ref, returned_ref, out_ref):
    returned = returned_ref[...]
    count, m = returned.shape
    rank = rank_ref[...]
    n = rank.shape[1]
    slab, upper, member = rank // (2 * m), rank // m % 2 == 1, rank % m
    shape = (count, n)
    plane = iota(shape, 0) // (count * 2 * m // n)
    kind = iota(shape, 0) % 4
    own = (plane == slab) & (kind == jnp.where(upper, 1, 0))
    halo = (plane == jnp.where(upper, slab + 1, slab - 1)) & (kind == jnp.where(upper, 2, 3))
    picked = lax.dot_general(
        returned,
        jnp.where(own | halo, 1.0, 0.0),
        TN,
        precision=lax.Precision.HIGHEST,
        preferred_element_type=jnp.float32,
    )
    mass = jnp.sum(jnp.where(iota((m, n), 0) == member, picked, 0.0), axis=0, keepdims=True)
    out_ref[...] = 1.0 / (1.0 + mass)


def xor_order(array, axis, bits):
    count = array.shape[axis]
    for k in range(count.bit_length() - 1):
        step = 1 << k
        shape = array.shape[:axis] + (count // (2 * step), 2, step) + array.shape[axis + 1 :]
        split = array.reshape(shape)
        split = jnp.where((bits >> k) & 1 == 1, jnp.flip(split, axis + 1), split)
        array = split.reshape(array.shape)
    return array


def shards(embeddings, position, cluster_ids):
    n, width = embeddings.shape
    peers = lax.axis_size("dev")
    me = lax.axis_index("dev")
    planes = peers // QUAD
    slab, lane = me // QUAD, me % QUAD
    per_half = n // (2 * planes)
    by_permutes = planes == 4
    pieces = [per_half] * 2 + [2 * per_half] + [per_half] * 4 if by_permutes else [n]
    f32 = jnp.float32

    def swapped(rows_, bit):
        return lax.ppermute(rows_, "dev", [(i, i ^ bit) for i in range(peers)])

    def passed(rows_, by):
        pairs = [(i, i + by) for i in range(peers) if 0 <= i + by < peers]
        return lax.ppermute(rows_, "dev", pairs)

    def after_all(value, *others):
        return lax.optimization_barrier((value, *others))[0]

    def as_received(values, axis, plane):
        return xor_order(values, axis, plane) if by_permutes else values

    where_to = position.reshape(1, n)
    in_hbm = pl.BlockSpec(memory_space=pltpu.HBM)
    *arranged, rank = call(
        functools.partial(arrange_kernel, per_half, 2 * planes),
        [jax.ShapeDtypeStruct((size, width), embeddings.dtype) for size in pieces]
        + [jax.ShapeDtypeStruct((1, n), jnp.int32)],
        in_specs=[in_hbm, in_hbm],
        scratch_shapes=[
            pltpu.VMEM((1, n), jnp.int32),
            pltpu.VMEM((n, width), embeddings.dtype),
            pltpu.SemaphoreType.DMA((2,)),
        ],
    )(where_to, embeddings)
    if by_permutes:
        own_upper, own_lower, to_1, upper_2, lower_2, upper_3, lower_3 = arranged
        upper_3 = swapped(upper_3, 3 * QUAD)
        upper_2 = swapped(upper_2, 2 * QUAD)
        both_1 = swapped(to_1, QUAD)
        lower_3 = swapped(lower_3, 3 * QUAD)
        lower_2 = swapped(lower_2, 2 * QUAD)
        upper = jnp.concatenate([own_upper, both_1[:per_half], upper_2, upper_3], axis=0)
        lower = jnp.concatenate([own_lower, both_1[per_half:], lower_2, lower_3], axis=0)
    else:
        lines = [[p * QUAD + q for p in range(planes)] for q in range(QUAD)]
        block = lax.all_to_all(
            arranged[0], "dev", split_axis=0, concat_axis=0, axis_index_groups=lines, tiled=True
        ).reshape(planes, 2, per_half, width)
        upper = block[:, 1].reshape(n // 2, width)
        lower = block[:, 0].reshape(n // 2, width)

    facts = call(
        functools.partial(facts_kernel, per_half), jax.ShapeDtypeStruct((4, n), f32)
    )(where_to, cluster_ids.reshape(1, n), rank, *arranged)
    seen = jnp.pad(facts[:2], ((0, 0), (per_half, per_half)))
    seen = jnp.stack(
        [seen[:, 2 * p * per_half : (2 * p + 4) * per_half] for p in range(planes)]
    ).reshape(planes, 1, 8 * per_half)
    facts = jnp.concatenate(
        [
            jnp.broadcast_to(seen, (planes, QUAD, 8 * per_half)),
            jnp.broadcast_to(facts[2], (planes, QUAD, n)),
        ],
        axis=2,
    )
    facts = after_all(facts, both_1 if by_permutes else block)
    facts = lax.all_to_all(
        facts.reshape(peers, 8 * per_half + n), "dev", split_axis=0, concat_axis=0, tiled=True
    )
    arrays = {"b0h": upper}
    arrays["b2h"] = swapped(upper, 2)
    arrays["b1h"] = swapped(upper, 1)
    lower = after_all(lower, arrays["b1h"])
    arrays["b0l"] = lower
    arrays["u"] = passed(after_all(upper, facts), QUAD)
    arrays["b2l"] = swapped(lower, 2)
    arrays["l"] = passed(lower, -QUAD)
    arrays["b1l"] = swapped(lower, 1)

    facts = after_all(facts, arrays["b1l"])
    ids = jnp.pad(facts[:, 8 * per_half :].reshape(peers * n), (MOST, MOST))
    ids = lax.dynamic_slice_in_dim(ids, slab * MOST, 3 * MOST, 0)
    near = facts[:, : 8 * per_half].reshape(planes, QUAD, 2, 4, per_half)
    near = xor_order(near, 1, lane).transpose(2, 1, 3, 0, 4)
    before = as_received(near[:, :2, 0], 2, slab - 1)
    after = as_received(near[:, :2, 3], 2, slab + 1)
    own = as_received(near[:, :3, 1:3], 3, slab)
    near = jnp.concatenate(
        [
            jnp.stack([own[:, :, 1], own[:, :, 0]], axis=2).reshape(2, 3 * n),
            jnp.stack([before, after], axis=2).reshape(2, 2 * n),
        ],
        axis=1,
    )
    total = 5 * n
    place = near[0].astype(jnp.int32) - (slab - 1) * MOST
    label = call(labels_kernel, jax.ShapeDtypeStruct((1, total), f32))(
        place.reshape(1, total), ids.reshape(3 * MOST // LANES, LANES)
    )[0]
    at = jnp.arange(total)
    absent = (at >= 3 * n) & jnp.where(at % n >= n // 2, slab == planes - 1, slab == 0)
    label = jnp.where(absent, -1.0, label)
    rows = jnp.stack([near[1], label])
    columns = jnp.stack([near[1] * SCALE, label], axis=1)

    def masses_after(jobs, last=None):
        return masses_call(jobs, arrays, rows, columns, last)

    masses = masses_after(
        [("b0h", "b0h"), ("b1h", "b0h"), ("b2h", "b0h"), ("b1h", "b2h")]
        + [("b0l", "b0l"), ("b0h", "b0l"), ("b1h", "b0l"), ("b2h", "b0l")]
        + [("b1l", "b0h"), ("b1l", "b0l"), ("b1l", "b2h")]
    )
    arrays["u1"] = swapped(after_all(arrays['u'], arrays["b2h"]), 1)
    masses = masses_after([(u, b) for u in ("u", "u1") for b in ("b0h", "b0l", "b2h")], masses)
    arrays["l1"] = swapped(after_all(arrays["l"], masses, arrays["b2l"]), 1)
    masses = masses_after(
        [("b2l", "b0h"), ("b2l", "b0l"), ("b1h", "b2l"), ("b1l", "b2l"), ("u", "b2l"), ("u1", "b2l")],
        masses,
    )
    last = [("l", "b0l"), ("l", "b2l"), ("l1", "b0l"), ("l1", "b2l")]
    if by_permutes:
        outgoing = masses_call(last, arrays, rows, columns, masses, (4 * peers, per_half))
    else:
        masses = masses_after(last, masses)
        masses = masses.reshape(4, 2, planes, per_half)
        slabs = as_received(masses[:2], 2, slab)
        before = as_received(masses[2:, 0], 1, slab - 1)
        after = as_received(masses[2:, 1], 1, slab + 1)
        none = jnp.zeros_like(before[0])
        outgoing = jnp.stack(
            [
                jnp.stack([slabs[0, 1], none, slabs[1, 1], none]),
                jnp.stack([slabs[0, 0], none, slabs[1, 0], none]),
                jnp.stack([before[0], before[1], none, none]),
                jnp.stack([after[0], after[1], none, none]),
            ],
            axis=2,
        )
        outgoing = xor_order(outgoing, 0, lane).transpose(1, 0, 2, 3)
        outgoing = outgoing.reshape(4 * peers, per_half)
    returned = lax.all_to_all(outgoing, "dev", split_axis=0, concat_axis=0, tiled=True)
    weight = call(
        weights_kernel, jax.ShapeDtypeStruct((1, n), f32)
    )(rank, returned)
    return weight.reshape(n)


def solution(mesh):
    return jax.shard_map(
        shards,
        mesh=mesh,
        in_specs=(P(("grp", "dev"), None), P(("grp", "dev")), P(("grp", "dev"))),
        out_specs=P(("grp", "dev")),
        check_vma=False,
    )
```

```python
import functools
import math

import jax
import jax.numpy as jnp
from jax import lax
from jax.experimental import pallas as pl
from jax.experimental.pallas import tpu as pltpu
from jax.sharding import PartitionSpec as P

MOST = 2048
HALF = MOST // 2
SIMILARITY_CUTOFF = 0.9
SOFTMAX_HEAT = 0.02
SCALE = math.log2(math.e) / SOFTMAX_HEAT
SHIFT = SIMILARITY_CUTOFF * SCALE
QUAD = 4
CHUNK = 256
LANES = 128
VMEM_LIMIT = 16 * 1024 * 1024

NT = (((1,), (1,)), ((), ()))
TN = (((0,), (0,)), ((), ()))


def iota(shape, dim):
    return lax.broadcasted_iota(jnp.int32, shape, dim)


def call(kernel, out_shape, limit=VMEM_LIMIT, **extra):
    return pl.pallas_call(
        kernel,
        out_shape=out_shape,
        compiler_params=pltpu.CompilerParams(vmem_limit_bytes=limit),
        **extra,
    )


def arrange_kernel(per_half, halves, position_hbm, rows_hbm, *refs):
    *outs, rank_ref, place, rows, sems = refs
    copies = [
        pltpu.make_async_copy(position_hbm, place, sems.at[0]),
        pltpu.make_async_copy(rows_hbm, rows, sems.at[1]),
    ]
    for copy in copies:
        copy.start()
    n = rows.shape[0]
    earlier = (iota((n, n), 0) < iota((n, n), 1)).astype(jnp.bfloat16)
    copies[0].wait()
    half = place[...] // HALF
    kinds = iota((halves, n), 0) == half
    counts = jnp.dot(kinds.astype(jnp.bfloat16), earlier, preferred_element_type=jnp.float32)
    count = jnp.sum(jnp.where(kinds, counts, 0.0), axis=0, keepdims=True).astype(jnp.int32)
    rank_ref[...] = half * per_half + count
    rank = half * per_half + count
    if len(outs) > 1:
        plane = (half // 2) ^ (lax.axis_index("dev") // QUAD)
        rank = (2 * plane + 1 - half % 2) * per_half + count
    pick = (iota((n, n), 0) == rank).astype(jnp.bfloat16)
    copies[1].wait()
    picked = jnp.dot(pick, rows[...], preferred_element_type=jnp.float32)
    at = 0
    for out in outs:
        out[...] = picked[at : at + out.shape[0], :].astype(out.dtype)
        at += out.shape[0]


def facts_kernel(per_half, position_ref, ids_ref, rank_ref, *refs):
    *pieces, out_ref = refs
    n = position_ref.shape[1]
    pick = iota((n, n), 0) == rank_ref[...]
    where_to = position_ref[...].astype(jnp.float32)
    column = jnp.sum(jnp.where(pick, where_to, 0.0), axis=1, keepdims=True)
    eye = iota((n, n), 0) == iota((n, n), 1)
    positions = jnp.sum(jnp.where(eye, column, 0.0), axis=0, keepdims=True)
    total = jnp.zeros((1, n), jnp.float32)
    k = 0
    for piece in pieces:
        size = n if len(pieces) == 1 else per_half
        for start in range(0, piece.shape[0], size):
            wide = piece[start : start + size, :].astype(jnp.float32)
            inverse = lax.rsqrt(jnp.sum(wide * wide, axis=1, keepdims=True) + 1e-06)
            first = 0
            if len(pieces) > 1:
                plane = (k // 2) ^ (lax.axis_index("dev") // QUAD)
                first = (2 * plane + 1 - k % 2) * per_half
            here = iota((size, n), 0) + first == iota((size, n), 1)
            total += jnp.sum(jnp.where(here, inverse, 0.0), axis=0, keepdims=True)
            k += 1
    ids = ids_ref[...].astype(jnp.float32)
    if len(out_ref.shape) == 2:
        for k, values in enumerate((positions, total, ids, jnp.zeros_like(ids))):
            out_ref[k : k + 1, :] = values
        return
    beyond = jnp.zeros((1, per_half), jnp.float32)
    ids = [ids[:, at : at + LANES] for at in range(0, n, LANES)]
    wide = [jnp.concatenate([beyond, values, beyond], axis=1) for values in (positions, total)]
    for peer in range(out_ref.shape[0]):
        at = peer // QUAD * LANES
        lines = [values[:, at + k : at + k + LANES] for values in wide for k in (0, LANES)]
        for k, line in enumerate(lines + ids):
            out_ref[peer, k : k + 1, :] = line


def labels_kernel(place_ref, table_ref, out_ref):
    place = place_ref[...]
    depth = table_ref.shape[0]
    n = place.shape[1]
    table = table_ref[...]
    high = jnp.floor(table * (1.0 / 256.0))
    low = table - high * 256.0
    line = (iota((depth, n), 0) == place // LANES).astype(jnp.bfloat16)
    high = lax.dot_general(
        high.astype(jnp.bfloat16), line, TN, preferred_element_type=jnp.float32
    )
    low = lax.dot_general(
        low.astype(jnp.bfloat16), line, TN, preferred_element_type=jnp.float32
    )
    here = iota((LANES, n), 0) == place % LANES
    out_ref[...] = jnp.sum(jnp.where(here, high * 256.0 + low, 0.0), axis=0, keepdims=True)


NAMES = ("b0h", "b0l", "b1h", "b1l", "b2h", "b2l", "u", "l", "u1", "l1")
SUMS = ("b0h", "b0l", "b2h", "b2l", "u", "l", "u1", "l1")


class Terms:
    def __init__(self, arrays, rows_ref, columns_ref, out_ref, last_ref):
        self.arrays, self.rows, self.columns, self.out = arrays, rows_ref, columns_ref, out_ref
        self.last = last_ref
        self.sums = {}

    def add(self, name, values):
        self.sums[name] = self.sums[name] + values if name in self.sums else values

    def job(self, down, across):
        n = self.arrays[down].shape[0]
        products = lax.dot_general(
            self.arrays[down][...],
            self.arrays[across][...],
            NT,
            preferred_element_type=jnp.float32,
        )
        at, to = NAMES.index(down) * n, NAMES.index(across) * n
        scale = self.columns[at : at + n, 0:1]
        label = self.columns[at : at + n, 1:2]
        power = products * scale * self.rows[0:1, to : to + n] - SHIFT
        mask = label == self.rows[1:2, to : to + n]
        if down == across:
            mask &= iota((n, n), 0) != iota((n, n), 1)
        values = jnp.where(mask, jnp.exp2(power), 0.0)
        self.add(across, jnp.sum(values, axis=0, keepdims=True))
        if down in ("u", "l", "u1", "l1") or (down, across) == ("b0h", "b0l"):
            side = jnp.zeros((n, LANES), jnp.float32)
            for lane in range(0, n, LANES):
                side += values[:, lane : lane + LANES]
            self.add(down, jnp.sum(side.T, axis=0, keepdims=True))

    def totals(self):
        totals = {}
        for k, name in enumerate(SUMS):
            values = self.sums.get(name)
            last = self.last[k : k + 1, :] if self.last is not None else None
            if values is None:
                n = self.arrays["b0l"].shape[0]
                values = jnp.zeros((1, n), jnp.float32) if last is None else last
            elif last is not None:
                values += last
            totals[name] = values
        return totals

    def write(self):
        for k, values in enumerate(self.totals().values()):
            self.out[k : k + 1, :] = values


def lay_out(sums, m, out_ref):
    me = lax.axis_index("dev")
    slab, lane = me // QUAD, me % QUAD
    even = slab % 2 == 0
    rows = iota((out_ref.shape[0], 2 * m), 0)
    own = jnp.zeros(rows.shape, jnp.float32)
    halo = own

    def piece(name, x):
        return sums[name][:, x * m : (x + 1) * m]

    for x in range(QUAD):
        row = (slab ^ x) * QUAD
        for line, lower, upper in ((0, "b0l", "b0h"), (2, "b2l", "b2h")):
            both = jnp.concatenate([piece(lower, x), piece(upper, x)], axis=1)
            own = jnp.where(rows == row + (lane ^ line), both, own)
        for line, before, after in ((0, "u", "l"), (1, "u1", "l1")):
            before = jnp.where(even, piece(before, x ^ 3), piece(before, x ^ 1))
            after = jnp.where(even, piece(after, x ^ 1), piece(after, x ^ 3))
            both = jnp.concatenate([before, after], axis=1)
            halo = jnp.where(rows == row + (lane ^ line), both, halo)
    out_ref[:, 0, :] = own
    out_ref[:, 1, :] = halo


def masses_call(jobs, arrays, rows, columns, last=None, layout=None):
    names = [name for name in NAMES if any(name in job for job in jobs)]

    def kernel(*refs):
        refs = list(refs)
        held = {name: refs.pop(0) for name in names}
        rows_ref, columns_ref = refs.pop(0), refs.pop(0)
        last_ref = refs.pop(0) if last is not None else None
        t = Terms(held, rows_ref, columns_ref, refs.pop(0), last_ref)
        for job in jobs:
            t.job(*job)
        if layout is None:
            t.write()
        else:
            lay_out(t.totals(), layout[2] // 2, t.out)

    operands = [arrays[name] for name in names] + [rows, columns]
    if last is not None:
        operands.append(last)
    n, width = operands[0].shape
    return call(
        kernel,
        jax.ShapeDtypeStruct(layout or (len(SUMS), n), jnp.float32),
        cost_estimate=pl.CostEstimate(flops=0, transcendentals=0, bytes_accessed=0),
    )(*operands)


def weights_kernel(rank_ref, returned_ref, out_ref):
    peers, _, width = returned_ref.shape
    m = width // 2
    rank = rank_ref[...]
    n = rank.shape[1]
    slab, upper, member = rank // width, rank // m % 2 == 1, rank % m
    plane = iota((peers, n), 0) // QUAD

    def chosen(k, which, column):
        picked = lax.dot_general(
            returned_ref[:, k, :],
            jnp.where(plane == which, 1.0, 0.0),
            TN,
            precision=lax.Precision.HIGHEST,
            preferred_element_type=jnp.float32,
        )
        here = iota((width, n), 0) == column
        return jnp.sum(jnp.where(here, picked, 0.0), axis=0, keepdims=True)

    mass = chosen(0, slab, jnp.where(upper, m + member, member))
    mass += chosen(1, jnp.where(upper, slab + 1, slab - 1), jnp.where(upper, member, m + member))
    out_ref[...] = 1.0 / (1.0 + mass)


def xor_order(array, axis, bits):
    count = array.shape[axis]
    for k in range(count.bit_length() - 1):
        step = 1 << k
        shape = array.shape[:axis] + (count // (2 * step), 2, step) + array.shape[axis + 1 :]
        split = array.reshape(shape)
        split = jnp.where((bits >> k) & 1 == 1, jnp.flip(split, axis + 1), split)
        array = split.reshape(array.shape)
    return array


def shards(embeddings, position, cluster_ids):
    n, width = embeddings.shape
    peers = lax.axis_size("dev")
    me = lax.axis_index("dev")
    planes = peers // QUAD
    slab, lane = me // QUAD, me % QUAD
    per_half = n // (2 * planes)
    by_permutes = planes == 4
    pieces = [per_half] * 2 + [2 * per_half] + [per_half] * 4 if by_permutes else [n]
    f32 = jnp.float32

    def swapped(rows_, bit):
        return lax.ppermute(rows_, "dev", [(i, i ^ bit) for i in range(peers)])

    def passed(rows_, by):
        pairs = [(i, i + by) for i in range(peers) if 0 <= i + by < peers]
        return lax.ppermute(rows_, "dev", pairs)

    def after_all(value, *others):
        return lax.optimization_barrier((value, *others))[0]

    def as_received(values, axis, plane):
        return xor_order(values, axis, plane) if by_permutes else values

    where_to = position.reshape(1, n)
    in_hbm = pl.BlockSpec(memory_space=pltpu.HBM)
    *arranged, rank = call(
        functools.partial(arrange_kernel, per_half, 2 * planes),
        [jax.ShapeDtypeStruct((size, width), embeddings.dtype) for size in pieces]
        + [jax.ShapeDtypeStruct((1, n), jnp.int32)],
        in_specs=[in_hbm, in_hbm],
        scratch_shapes=[
            pltpu.VMEM((1, n), jnp.int32),
            pltpu.VMEM((n, width), embeddings.dtype),
            pltpu.SemaphoreType.DMA((2,)),
        ],
    )(where_to, embeddings)
    if by_permutes:
        own_upper, own_lower, to_1, upper_2, lower_2, upper_3, lower_3 = arranged
        upper_3 = swapped(upper_3, 3 * QUAD)
        upper_2 = swapped(upper_2, 2 * QUAD)
        both_1 = swapped(to_1, QUAD)
        lower_3 = swapped(lower_3, 3 * QUAD)
        lower_2 = swapped(lower_2, 2 * QUAD)
        upper = jnp.concatenate([own_upper, both_1[:per_half], upper_2, upper_3], axis=0)
        lower = jnp.concatenate([own_lower, both_1[per_half:], lower_2, lower_3], axis=0)
    else:
        lines = [[p * QUAD + q for p in range(planes)] for q in range(QUAD)]
        block = lax.all_to_all(
            arranged[0], "dev", split_axis=0, concat_axis=0, axis_index_groups=lines, tiled=True
        ).reshape(planes, 2, per_half, width)
        upper = block[:, 1].reshape(n // 2, width)
        lower = block[:, 0].reshape(n // 2, width)

    aligned = by_permutes and 2 * per_half == LANES
    own_facts = (where_to, cluster_ids.reshape(1, n), rank, *arranged)
    facts_shape = (peers, 4 + n // LANES, LANES) if aligned else (4, n)
    facts = call(
        functools.partial(facts_kernel, per_half), jax.ShapeDtypeStruct(facts_shape, f32)
    )(*own_facts)
    if not aligned:
        seen = jnp.pad(facts[:2], ((0, 0), (per_half, per_half)))
        seen = jnp.stack(
            [seen[:, 2 * p * per_half : (2 * p + 4) * per_half] for p in range(planes)]
        ).reshape(planes, 1, 8 * per_half)
        facts = jnp.concatenate(
            [
                jnp.broadcast_to(seen, (planes, QUAD, 8 * per_half)),
                jnp.broadcast_to(facts[2], (planes, QUAD, n)),
            ],
            axis=2,
        )
        facts = facts.reshape(peers, 8 * per_half + n)
    facts = after_all(facts, both_1 if by_permutes else block)
    facts = lax.all_to_all(facts, "dev", split_axis=0, concat_axis=0, tiled=True)
    arrays = {"b0h": upper}
    arrays["b2h"] = swapped(upper, 2)
    arrays["b1h"] = swapped(upper, 1)
    lower = after_all(lower, arrays["b1h"])
    arrays["b0l"] = lower
    arrays["u"] = passed(upper, QUAD)
    arrays["b2l"] = swapped(lower, 2)
    arrays["l"] = passed(lower, -QUAD)
    arrays["b1l"] = swapped(lower, 1)

    if aligned:
        ids, near = facts[:, 4:].reshape(peers * n), facts[:, :4]
    else:
        ids, near = facts[:, 8 * per_half :].reshape(peers * n), facts[:, : 8 * per_half]
    ids = jnp.pad(ids, (MOST, MOST))
    ids = lax.dynamic_slice_in_dim(ids, slab * MOST, 3 * MOST, 0)
    near = near.reshape(planes, QUAD, 2, 4, per_half)
    near = xor_order(near, 1, lane).transpose(2, 1, 3, 0, 4)
    before = as_received(near[:, :2, 0], 2, slab - 1)
    after = as_received(near[:, :2, 3], 2, slab + 1)
    own = as_received(near[:, :3, 1:3], 3, slab)
    near = jnp.concatenate(
        [
            jnp.stack([own[:, :, 1], own[:, :, 0]], axis=2).reshape(2, 3 * n),
            jnp.stack([before, after], axis=2).reshape(2, 2 * n),
        ],
        axis=1,
    )
    total = 5 * n
    place = near[0].astype(jnp.int32) - (slab - 1) * MOST
    label = call(labels_kernel, jax.ShapeDtypeStruct((1, total), f32))(
        place.reshape(1, total), ids.reshape(3 * MOST // LANES, LANES)
    )[0]
    at = jnp.arange(total)
    absent = (at >= 3 * n) & jnp.where(at % n >= n // 2, slab == planes - 1, slab == 0)
    label = jnp.where(absent, -1.0, label)
    rows = jnp.stack([near[1], label])
    columns = jnp.stack([near[1] * SCALE, label], axis=1)

    def masses_after(jobs, last=None):
        return masses_call(jobs, arrays, rows, columns, last)

    masses = masses_after(
        [("b0h", "b0h"), ("b1h", "b0h"), ("b2h", "b0h"), ("b1h", "b2h")]
        + [("b0l", "b0l"), ("b0h", "b0l"), ("b1h", "b0l"), ("b2h", "b0l")]
        + [("b1l", "b0h"), ("b1l", "b0l"), ("b1l", "b2h")]
    )
    arrays["u1"] = swapped(after_all(arrays['u'], arrays["b2h"]), 1)
    masses = masses_after([(u, b) for u in ("u", "u1") for b in ("b0h", "b0l", "b2h")], masses)
    arrays["l1"] = swapped(after_all(arrays["l"], masses, arrays["b2l"]), 1)
    masses = masses_after(
        [("b2l", "b0h"), ("b2l", "b0l"), ("b1h", "b2l"), ("b1l", "b2l"), ("u", "b2l"), ("u1", "b2l")],
        masses,
    )
    last = [("l", "b0l"), ("l", "b2l"), ("l1", "b0l"), ("l1", "b2l")]
    if by_permutes:
        outgoing = masses_call(last, arrays, rows, columns, masses, (peers, 2, 2 * per_half))
    else:
        masses = masses_after(last, masses)
        masses = masses.reshape(4, 2, planes, per_half)
        slabs = as_received(masses[:2], 2, slab)
        before = as_received(masses[2:, 0], 1, slab - 1)
        after = as_received(masses[2:, 1], 1, slab + 1)
        none = jnp.zeros_like(before[0])
        outgoing = jnp.stack(
            [
                jnp.stack([slabs[0, 1], none, slabs[1, 1], none]),
                jnp.stack([slabs[0, 0], none, slabs[1, 0], none]),
                jnp.stack([before[0], before[1], none, none]),
                jnp.stack([after[0], after[1], none, none]),
            ],
            axis=2,
        )
        outgoing = xor_order(outgoing, 0, lane).transpose(1, 0, 2, 3)
        outgoing = outgoing.reshape(peers, 2, 2 * per_half)
    returned = lax.all_to_all(outgoing, "dev", split_axis=0, concat_axis=0, tiled=True)
    weight = call(
        weights_kernel, jax.ShapeDtypeStruct((1, n), f32)
    )(rank, returned)
    return weight.reshape(n)


def solution(mesh):
    return jax.shard_map(
        shards,
        mesh=mesh,
        in_specs=(P(("grp", "dev"), None), P(("grp", "dev")), P(("grp", "dev"))),
        out_specs=P(("grp", "dev")),
        check_vma=False,
    )
```

```python
import functools
import math

import jax
import jax.numpy as jnp
from jax import lax
from jax.experimental import pallas as pl
from jax.experimental.pallas import tpu as pltpu
from jax.sharding import PartitionSpec as P

MOST = 2048
HALF = MOST // 2
SIMILARITY_CUTOFF = 0.9
SOFTMAX_HEAT = 0.02
SCALE = math.log2(math.e) / SOFTMAX_HEAT
SHIFT = SIMILARITY_CUTOFF * SCALE
QUAD = 4
CHUNK = 256
LANES = 128
VMEM_LIMIT = 16 * 1024 * 1024

NT = (((1,), (1,)), ((), ()))
TN = (((0,), (0,)), ((), ()))


def iota(shape, dim):
    return lax.broadcasted_iota(jnp.int32, shape, dim)


def call(kernel, out_shape, limit=VMEM_LIMIT, **extra):
    return pl.pallas_call(
        kernel,
        out_shape=out_shape,
        compiler_params=pltpu.CompilerParams(vmem_limit_bytes=limit),
        **extra,
    )


def arrange_kernel(per_half, halves, position_hbm, rows_hbm, *refs):
    *outs, rank_ref, place, rows, sems = refs
    copies = [
        pltpu.make_async_copy(position_hbm, place, sems.at[0]),
        pltpu.make_async_copy(rows_hbm, rows, sems.at[1]),
    ]
    for copy in copies:
        copy.start()
    n = rows.shape[0]
    earlier = (iota((n, n), 0) < iota((n, n), 1)).astype(jnp.bfloat16)
    copies[0].wait()
    half = place[...] // HALF
    kinds = iota((halves, n), 0) == half
    counts = jnp.dot(kinds.astype(jnp.bfloat16), earlier, preferred_element_type=jnp.float32)
    count = jnp.sum(jnp.where(kinds, counts, 0.0), axis=0, keepdims=True).astype(jnp.int32)
    rank_ref[0:1, :] = half * per_half + count
    rank_ref[1:2, :] = place[...]
    rank = half * per_half + count
    if len(outs) > 1:
        plane = (half // 2) ^ (lax.axis_index("dev") // QUAD)
        rank = (2 * plane + 1 - half % 2) * per_half + count
    pick = (iota((n, n), 0) == rank).astype(jnp.bfloat16)
    copies[1].wait()
    picked = jnp.dot(pick, rows[...], preferred_element_type=jnp.float32)
    at = 0
    for out in outs:
        out[...] = picked[at : at + out.shape[0], :].astype(out.dtype)
        at += out.shape[0]


def facts_kernel(per_half, ids_hbm, rank_ref, *refs):
    *pieces, out_ref, ids_ref, sem = refs
    copy = pltpu.make_async_copy(ids_hbm, ids_ref, sem)
    copy.start()
    n = rank_ref.shape[1]
    pick = iota((n, n), 0) == rank_ref[0:1, :]
    where_to = rank_ref[1:2, :].astype(jnp.float32)
    column = jnp.sum(jnp.where(pick, where_to, 0.0), axis=1, keepdims=True)
    eye = iota((n, n), 0) == iota((n, n), 1)
    positions = jnp.sum(jnp.where(eye, column, 0.0), axis=0, keepdims=True)
    total = jnp.zeros((1, n), jnp.float32)
    k = 0
    for piece in pieces:
        size = n if len(pieces) == 1 else per_half
        for start in range(0, piece.shape[0], size):
            wide = piece[start : start + size, :].astype(jnp.float32)
            inverse = lax.rsqrt(jnp.sum(wide * wide, axis=1, keepdims=True) + 1e-06)
            first = 0
            if len(pieces) > 1:
                plane = (k // 2) ^ (lax.axis_index("dev") // QUAD)
                first = (2 * plane + 1 - k % 2) * per_half
            here = iota((size, n), 0) + first == iota((size, n), 1)
            total += jnp.sum(jnp.where(here, inverse, 0.0), axis=0, keepdims=True)
            k += 1
    copy.wait()
    ids = ids_ref[...].astype(jnp.float32)
    if len(out_ref.shape) == 2:
        for k, values in enumerate((positions, total, ids, jnp.zeros_like(ids))):
            out_ref[k : k + 1, :] = values
        return
    beyond = jnp.zeros((1, per_half), jnp.float32)
    ids = [ids[:, at : at + LANES] for at in range(0, n, LANES)]
    wide = [jnp.concatenate([beyond, values, beyond], axis=1) for values in (positions, total)]
    for peer in range(out_ref.shape[0]):
        at = peer // QUAD * LANES
        lines = [values[:, at + k : at + k + LANES] for values in wide for k in (0, LANES)]
        for k, line in enumerate(lines + ids):
            out_ref[peer, k : k + 1, :] = line


def labels_kernel(place_ref, table_ref, out_ref):
    place = place_ref[...]
    depth = table_ref.shape[0]
    n = place.shape[1]
    table = table_ref[...]
    high = jnp.floor(table * (1.0 / 256.0))
    low = table - high * 256.0
    line = (iota((depth, n), 0) == place // LANES).astype(jnp.bfloat16)
    high = lax.dot_general(
        high.astype(jnp.bfloat16), line, TN, preferred_element_type=jnp.float32
    )
    low = lax.dot_general(
        low.astype(jnp.bfloat16), line, TN, preferred_element_type=jnp.float32
    )
    here = iota((LANES, n), 0) == place % LANES
    out_ref[...] = jnp.sum(jnp.where(here, high * 256.0 + low, 0.0), axis=0, keepdims=True)


NAMES = ("b0h", "b0l", "b1h", "b1l", "b2h", "b2l", "u", "l", "u1", "l1")
SUMS = ("b0h", "b0l", "b2h", "b2l", "u", "l", "u1", "l1")


class Terms:
    def __init__(self, arrays, rows_ref, columns_ref, out_ref, last_ref):
        self.arrays, self.rows, self.columns, self.out = arrays, rows_ref, columns_ref, out_ref
        self.last = last_ref
        self.sums = {}

    def add(self, name, values):
        self.sums[name] = self.sums[name] + values if name in self.sums else values

    def job(self, down, across):
        n = self.arrays[down].shape[0]
        products = lax.dot_general(
            self.arrays[down][...],
            self.arrays[across][...],
            NT,
            preferred_element_type=jnp.float32,
        )
        at, to = NAMES.index(down) * n, NAMES.index(across) * n
        scale = self.columns[at : at + n, 0:1]
        label = self.columns[at : at + n, 1:2]
        power = products * scale * self.rows[0:1, to : to + n] - SHIFT
        mask = label == self.rows[1:2, to : to + n]
        if down == across:
            mask &= iota((n, n), 0) != iota((n, n), 1)
        values = jnp.where(mask, jnp.exp2(power), 0.0)
        self.add(across, jnp.sum(values, axis=0, keepdims=True))
        if down in ("u", "l", "u1", "l1") or (down, across) == ("b0h", "b0l"):
            side = jnp.zeros((n, LANES), jnp.float32)
            for lane in range(0, n, LANES):
                side += values[:, lane : lane + LANES]
            self.add(down, jnp.sum(side.T, axis=0, keepdims=True))

    def totals(self):
        totals = {}
        for k, name in enumerate(SUMS):
            values = self.sums.get(name)
            last = self.last[k : k + 1, :] if self.last is not None else None
            if values is None:
                n = self.arrays["b0l"].shape[0]
                values = jnp.zeros((1, n), jnp.float32) if last is None else last
            elif last is not None:
                values += last
            totals[name] = values
        return totals

    def write(self):
        for k, values in enumerate(self.totals().values()):
            self.out[k : k + 1, :] = values


def lay_out(sums, m, out_ref):
    me = lax.axis_index("dev")
    slab, lane = me // QUAD, me % QUAD
    even = slab % 2 == 0
    rows = iota((out_ref.shape[0], 2 * m), 0)
    own = jnp.zeros(rows.shape, jnp.float32)
    halo = own

    def piece(name, x):
        return sums[name][:, x * m : (x + 1) * m]

    for x in range(QUAD):
        row = (slab ^ x) * QUAD
        for line, lower, upper in ((0, "b0l", "b0h"), (2, "b2l", "b2h")):
            both = jnp.concatenate([piece(lower, x), piece(upper, x)], axis=1)
            own = jnp.where(rows == row + (lane ^ line), both, own)
        for line, before, after in ((0, "u", "l"), (1, "u1", "l1")):
            before = jnp.where(even, piece(before, x ^ 3), piece(before, x ^ 1))
            after = jnp.where(even, piece(after, x ^ 1), piece(after, x ^ 3))
            both = jnp.concatenate([before, after], axis=1)
            halo = jnp.where(rows == row + (lane ^ line), both, halo)
    out_ref[:, 0, :] = own
    out_ref[:, 1, :] = halo


def masses_call(jobs, arrays, rows, columns, last=None, layout=None):
    names = [name for name in NAMES if any(name in job for job in jobs)]

    def kernel(*refs):
        refs = list(refs)
        held = {name: refs.pop(0) for name in names}
        rows_ref, columns_ref = refs.pop(0), refs.pop(0)
        last_ref = refs.pop(0) if last is not None else None
        t = Terms(held, rows_ref, columns_ref, refs.pop(0), last_ref)
        for job in jobs:
            t.job(*job)
        if layout is None:
            t.write()
        else:
            lay_out(t.totals(), layout[2] // 2, t.out)

    operands = [arrays[name] for name in names] + [rows, columns]
    if last is not None:
        operands.append(last)
    n, width = operands[0].shape
    return call(
        kernel,
        jax.ShapeDtypeStruct(layout or (len(SUMS), n), jnp.float32),
        cost_estimate=pl.CostEstimate(flops=0, transcendentals=0, bytes_accessed=0),
    )(*operands)


def weights_kernel(rank_ref, returned_ref, out_ref):
    peers, _, width = returned_ref.shape
    m = width // 2
    rank = rank_ref[0:1, :]
    n = rank.shape[1]
    slab, upper, member = rank // width, rank // m % 2 == 1, rank % m
    plane = iota((peers, n), 0) // QUAD

    def chosen(k, which, column):
        picked = lax.dot_general(
            returned_ref[:, k, :],
            jnp.where(plane == which, 1.0, 0.0),
            TN,
            precision=lax.Precision.HIGHEST,
            preferred_element_type=jnp.float32,
        )
        here = iota((width, n), 0) == column
        return jnp.sum(jnp.where(here, picked, 0.0), axis=0, keepdims=True)

    mass = chosen(0, slab, jnp.where(upper, m + member, member))
    mass += chosen(1, jnp.where(upper, slab + 1, slab - 1), jnp.where(upper, member, m + member))
    out_ref[...] = 1.0 / (1.0 + mass)


def xor_order(array, axis, bits):
    count = array.shape[axis]
    for k in range(count.bit_length() - 1):
        step = 1 << k
        shape = array.shape[:axis] + (count // (2 * step), 2, step) + array.shape[axis + 1 :]
        split = array.reshape(shape)
        split = jnp.where((bits >> k) & 1 == 1, jnp.flip(split, axis + 1), split)
        array = split.reshape(array.shape)
    return array


def shards(embeddings, position, cluster_ids):
    n, width = embeddings.shape
    peers = lax.axis_size("dev")
    me = lax.axis_index("dev")
    planes = peers // QUAD
    slab, lane = me // QUAD, me % QUAD
    per_half = n // (2 * planes)
    by_permutes = planes == 4
    pieces = [per_half] * 2 + [2 * per_half] + [per_half] * 4 if by_permutes else [n]
    f32 = jnp.float32

    def swapped(rows_, bit):
        return lax.ppermute(rows_, "dev", [(i, i ^ bit) for i in range(peers)])

    def passed(rows_, by):
        pairs = [(i, i + by) for i in range(peers) if 0 <= i + by < peers]
        return lax.ppermute(rows_, "dev", pairs)

    def after_all(value, *others):
        return lax.optimization_barrier((value, *others))[0]

    def as_received(values, axis, plane):
        return xor_order(values, axis, plane) if by_permutes else values

    where_to = position.reshape(1, n)
    in_hbm = pl.BlockSpec(memory_space=pltpu.HBM)
    *arranged, rank = call(
        functools.partial(arrange_kernel, per_half, 2 * planes),
        [jax.ShapeDtypeStruct((size, width), embeddings.dtype) for size in pieces]
        + [jax.ShapeDtypeStruct((2, n), jnp.int32)],
        in_specs=[in_hbm, in_hbm],
        scratch_shapes=[
            pltpu.VMEM((1, n), jnp.int32),
            pltpu.VMEM((n, width), embeddings.dtype),
            pltpu.SemaphoreType.DMA((2,)),
        ],
    )(where_to, embeddings)
    if by_permutes:
        own_upper, own_lower, to_1, upper_2, lower_2, upper_3, lower_3 = arranged
        upper_3 = swapped(upper_3, 3 * QUAD)
        upper_2 = swapped(upper_2, 2 * QUAD)
        both_1 = swapped(to_1, QUAD)
        lower_3 = swapped(lower_3, 3 * QUAD)
        lower_2 = swapped(lower_2, 2 * QUAD)
        upper = jnp.concatenate([own_upper, both_1[:per_half], upper_2, upper_3], axis=0)
        lower = jnp.concatenate([own_lower, both_1[per_half:], lower_2, lower_3], axis=0)
    else:
        lines = [[p * QUAD + q for p in range(planes)] for q in range(QUAD)]
        block = lax.all_to_all(
            arranged[0], "dev", split_axis=0, concat_axis=0, axis_index_groups=lines, tiled=True
        ).reshape(planes, 2, per_half, width)
        upper = block[:, 1].reshape(n // 2, width)
        lower = block[:, 0].reshape(n // 2, width)

    aligned = by_permutes and 2 * per_half == LANES
    own_facts = (cluster_ids.reshape(1, n), rank, *arranged)
    facts_shape = (peers, 4 + n // LANES, LANES) if aligned else (4, n)
    facts = call(
        functools.partial(facts_kernel, per_half),
        jax.ShapeDtypeStruct(facts_shape, f32),
        in_specs=[in_hbm] + [pl.BlockSpec(memory_space=pltpu.VMEM)] * (1 + len(arranged)),
        scratch_shapes=[pltpu.VMEM((1, n), jnp.int32), pltpu.SemaphoreType.DMA],
    )(*own_facts)
    if not aligned:
        seen = jnp.pad(facts[:2], ((0, 0), (per_half, per_half)))
        seen = jnp.stack(
            [seen[:, 2 * p * per_half : (2 * p + 4) * per_half] for p in range(planes)]
        ).reshape(planes, 1, 8 * per_half)
        facts = jnp.concatenate(
            [
                jnp.broadcast_to(seen, (planes, QUAD, 8 * per_half)),
                jnp.broadcast_to(facts[2], (planes, QUAD, n)),
            ],
            axis=2,
        )
        facts = facts.reshape(peers, 8 * per_half + n)
    facts = after_all(facts, both_1 if by_permutes else block)
    facts = lax.all_to_all(facts, "dev", split_axis=0, concat_axis=0, tiled=True)
    arrays = {"b0h": upper}
    arrays["b2h"] = swapped(upper, 2)
    arrays["b1h"] = swapped(upper, 1)
    lower = after_all(lower, arrays["b1h"])
    arrays["b0l"] = lower
    arrays["u"] = passed(upper, QUAD)
    arrays["b2l"] = swapped(lower, 2)
    arrays["l"] = passed(lower, -QUAD)
    arrays["b1l"] = swapped(lower, 1)

    if aligned:
        ids, near = facts[:, 4:].reshape(peers * n), facts[:, :4]
    else:
        ids, near = facts[:, 8 * per_half :].reshape(peers * n), facts[:, : 8 * per_half]
    ids = jnp.pad(ids, (MOST, MOST))
    ids = lax.dynamic_slice_in_dim(ids, slab * MOST, 3 * MOST, 0)
    near = near.reshape(planes, QUAD, 2, 4, per_half)
    near = xor_order(near, 1, lane).transpose(2, 1, 3, 0, 4)
    before = as_received(near[:, :2, 0], 2, slab - 1)
    after = as_received(near[:, :2, 3], 2, slab + 1)
    own = as_received(near[:, :3, 1:3], 3, slab)
    near = jnp.concatenate(
        [
            jnp.stack([own[:, :, 1], own[:, :, 0]], axis=2).reshape(2, 3 * n),
            jnp.stack([before, after], axis=2).reshape(2, 2 * n),
        ],
        axis=1,
    )
    total = 5 * n
    place = near[0].astype(jnp.int32) - (slab - 1) * MOST
    label = call(labels_kernel, jax.ShapeDtypeStruct((1, total), f32))(
        place.reshape(1, total), ids.reshape(3 * MOST // LANES, LANES)
    )[0]
    at = jnp.arange(total)
    absent = (at >= 3 * n) & jnp.where(at % n >= n // 2, slab == planes - 1, slab == 0)
    label = jnp.where(absent, -1.0, label)
    rows = jnp.stack([near[1], label])
    columns = jnp.stack([near[1] * SCALE, label], axis=1)

    def masses_after(jobs, last=None):
        return masses_call(jobs, arrays, rows, columns, last)

    masses = masses_after(
        [("b0h", "b0h"), ("b1h", "b0h"), ("b2h", "b0h"), ("b1h", "b2h")]
        + [("b0l", "b0l"), ("b0h", "b0l"), ("b1h", "b0l"), ("b2h", "b0l")]
        + [("b1l", "b0h"), ("b1l", "b0l"), ("b1l", "b2h")]
    )
    arrays["u1"] = swapped(after_all(arrays['u'], arrays["b2h"]), 1)
    masses = masses_after([(u, b) for u in ("u", "u1") for b in ("b0h", "b0l", "b2h")], masses)
    arrays["l1"] = swapped(after_all(arrays["l"], masses, arrays["b2l"]), 1)
    masses = masses_after(
        [("b2l", "b0h"), ("b2l", "b0l"), ("b1h", "b2l"), ("b1l", "b2l"), ("u", "b2l"), ("u1", "b2l")],
        masses,
    )
    last = [("l", "b0l"), ("l", "b2l"), ("l1", "b0l"), ("l1", "b2l")]
    if by_permutes:
        outgoing = masses_call(last, arrays, rows, columns, masses, (peers, 2, 2 * per_half))
    else:
        masses = masses_after(last, masses)
        masses = masses.reshape(4, 2, planes, per_half)
        slabs = as_received(masses[:2], 2, slab)
        before = as_received(masses[2:, 0], 1, slab - 1)
        after = as_received(masses[2:, 1], 1, slab + 1)
        none = jnp.zeros_like(before[0])
        outgoing = jnp.stack(
            [
                jnp.stack([slabs[0, 1], none, slabs[1, 1], none]),
                jnp.stack([slabs[0, 0], none, slabs[1, 0], none]),
                jnp.stack([before[0], before[1], none, none]),
                jnp.stack([after[0], after[1], none, none]),
            ],
            axis=2,
        )
        outgoing = xor_order(outgoing, 0, lane).transpose(1, 0, 2, 3)
        outgoing = outgoing.reshape(peers, 2, 2 * per_half)
    returned = lax.all_to_all(outgoing, "dev", split_axis=0, concat_axis=0, tiled=True)
    weight = call(
        weights_kernel, jax.ShapeDtypeStruct((1, n), f32)
    )(rank, returned)
    return weight.reshape(n)


def solution(mesh):
    return jax.shard_map(
        shards,
        mesh=mesh,
        in_specs=(P(("grp", "dev"), None), P(("grp", "dev")), P(("grp", "dev"))),
        out_specs=P(("grp", "dev")),
        check_vma=False,
    )
```

```python
import functools
import math

import jax
import jax.numpy as jnp
from jax import lax
from jax.experimental import pallas as pl
from jax.experimental.pallas import tpu as pltpu
from jax.sharding import PartitionSpec as P

MOST = 2048
HALF = MOST // 2
SIMILARITY_CUTOFF = 0.9
SOFTMAX_HEAT = 0.02
SCALE = math.log2(math.e) / SOFTMAX_HEAT
SHIFT = SIMILARITY_CUTOFF * SCALE
QUAD = 4
CHUNK = 256
LANES = 128
VMEM_LIMIT = 16 * 1024 * 1024

NT = (((1,), (1,)), ((), ()))
TN = (((0,), (0,)), ((), ()))


def iota(shape, dim):
    return lax.broadcasted_iota(jnp.int32, shape, dim)


def call(kernel, out_shape, limit=VMEM_LIMIT, **extra):
    return pl.pallas_call(
        kernel,
        out_shape=out_shape,
        compiler_params=pltpu.CompilerParams(vmem_limit_bytes=limit),
        **extra,
    )


def arrange_kernel(per_half, halves, position_hbm, rows_hbm, *refs):
    *outs, rank_ref, place, rows, sems = refs
    copies = [
        pltpu.make_async_copy(position_hbm, place, sems.at[0]),
        pltpu.make_async_copy(rows_hbm, rows, sems.at[1]),
    ]
    for copy in copies:
        copy.start()
    n = rows.shape[0]
    earlier = (iota((n, n), 0) < iota((n, n), 1)).astype(jnp.bfloat16)
    copies[0].wait()
    half = place[...] // HALF
    kinds = iota((halves, n), 0) == half
    counts = jnp.dot(kinds.astype(jnp.bfloat16), earlier, preferred_element_type=jnp.float32)
    count = jnp.sum(jnp.where(kinds, counts, 0.0), axis=0, keepdims=True).astype(jnp.int32)
    rank_ref[...] = half * per_half + count
    rank = half * per_half + count
    if len(outs) > 1:
        plane = (half // 2) ^ (lax.axis_index("dev") // QUAD)
        rank = (2 * plane + 1 - half % 2) * per_half + count
    pick = (iota((n, n), 0) == rank).astype(jnp.bfloat16)
    copies[1].wait()
    picked = jnp.dot(pick, rows[...], preferred_element_type=jnp.float32)
    at = 0
    for out in outs:
        out[...] = picked[at : at + out.shape[0], :].astype(out.dtype)
        at += out.shape[0]


def facts_kernel(per_half, position_ref, ids_ref, rank_ref, *refs):
    *pieces, out_ref = refs
    n = position_ref.shape[1]
    pick = iota((n, n), 0) == rank_ref[...]
    where_to = position_ref[...].astype(jnp.float32)
    column = jnp.sum(jnp.where(pick, where_to, 0.0), axis=1, keepdims=True)
    eye = iota((n, n), 0) == iota((n, n), 1)
    positions = jnp.sum(jnp.where(eye, column, 0.0), axis=0, keepdims=True)
    total = jnp.zeros((1, n), jnp.float32)
    k = 0
    for piece in pieces:
        size = n if len(pieces) == 1 else per_half
        for start in range(0, piece.shape[0], size):
            wide = piece[start : start + size, :].astype(jnp.float32)
            inverse = lax.rsqrt(jnp.sum(wide * wide, axis=1, keepdims=True) + 1e-06)
            first = 0
            if len(pieces) > 1:
                plane = (k // 2) ^ (lax.axis_index("dev") // QUAD)
                first = (2 * plane + 1 - k % 2) * per_half
            here = iota((size, n), 0) + first == iota((size, n), 1)
            total += jnp.sum(jnp.where(here, inverse, 0.0), axis=0, keepdims=True)
            k += 1
    ids = ids_ref[...].astype(jnp.float32)
    if len(out_ref.shape) == 2:
        for k, values in enumerate((positions, total, ids, jnp.zeros_like(ids))):
            out_ref[k : k + 1, :] = values
        return
    beyond = jnp.zeros((1, per_half), jnp.float32)
    ids = [ids[:, at : at + LANES] for at in range(0, n, LANES)]
    wide = [jnp.concatenate([beyond, values, beyond], axis=1) for values in (positions, total)]
    for peer in range(out_ref.shape[0]):
        at = peer // QUAD * LANES
        lines = [values[:, at + k : at + k + LANES] for values in wide for k in (0, LANES)]
        for k, line in enumerate(lines + ids):
            out_ref[peer, k : k + 1, :] = line


def labels_kernel(place_ref, table_ref, out_ref):
    place = place_ref[...]
    depth = table_ref.shape[0]
    n = place.shape[1]
    table = table_ref[...]
    high = jnp.floor(table * (1.0 / 256.0))
    low = table - high * 256.0
    line = (iota((depth, n), 0) == place // LANES).astype(jnp.bfloat16)
    high = lax.dot_general(
        high.astype(jnp.bfloat16), line, TN, preferred_element_type=jnp.float32
    )
    low = lax.dot_general(
        low.astype(jnp.bfloat16), line, TN, preferred_element_type=jnp.float32
    )
    here = iota((LANES, n), 0) == place % LANES
    out_ref[...] = jnp.sum(jnp.where(here, high * 256.0 + low, 0.0), axis=0, keepdims=True)


NAMES = ("b0h", "b0l", "b1h", "b1l", "b2h", "b2l", "u", "l", "u1", "l1")
SUMS = ("b0h", "b0l", "b2h", "b2l", "u", "l", "u1", "l1")


class Terms:
    def __init__(self, arrays, rows_ref, columns_ref, out_ref, last_ref):
        self.arrays, self.rows, self.columns, self.out = arrays, rows_ref, columns_ref, out_ref
        self.last = last_ref
        self.sums = {}

    def add(self, name, values):
        self.sums[name] = self.sums[name] + values if name in self.sums else values

    def job(self, down, across):
        n = self.arrays[down].shape[0]
        products = lax.dot_general(
            self.arrays[down][...],
            self.arrays[across][...],
            NT,
            preferred_element_type=jnp.float32,
        )
        at, to = NAMES.index(down) * n, NAMES.index(across) * n
        scale = self.columns[at : at + n, 0:1]
        label = self.columns[at : at + n, 1:2]
        power = products * scale * self.rows[0:1, to : to + n] - SHIFT
        mask = label == self.rows[1:2, to : to + n]
        if down == across:
            mask &= iota((n, n), 0) != iota((n, n), 1)
        values = jnp.where(mask, jnp.exp2(power), 0.0)
        self.add(across, jnp.sum(values, axis=0, keepdims=True))
        if down in ("u", "l", "u1", "l1") or (down, across) == ("b0h", "b0l"):
            side = jnp.zeros((n, LANES), jnp.float32)
            for lane in range(0, n, LANES):
                side += values[:, lane : lane + LANES]
            self.add(down, jnp.sum(side.T, axis=0, keepdims=True))

    def totals(self):
        totals = {}
        for k, name in enumerate(SUMS):
            values = self.sums.get(name)
            last = self.last[k : k + 1, :] if self.last is not None else None
            if values is None:
                n = self.arrays["b0l"].shape[0]
                values = jnp.zeros((1, n), jnp.float32) if last is None else last
            elif last is not None:
                values += last
            totals[name] = values
        return totals

    def write(self):
        for k, values in enumerate(self.totals().values()):
            self.out[k : k + 1, :] = values


def lay_out(sums, m, out_ref):
    me = lax.axis_index("dev")
    slab, lane = me // QUAD, me % QUAD
    even = slab % 2 == 0
    rows = iota((out_ref.shape[0], 2 * m), 0)
    own = jnp.zeros(rows.shape, jnp.float32)
    halo = own

    def piece(name, x):
        return sums[name][:, x * m : (x + 1) * m]

    for x in range(QUAD):
        row = (slab ^ x) * QUAD
        for line, lower, upper in ((0, "b0l", "b0h"), (2, "b2l", "b2h")):
            both = jnp.concatenate([piece(lower, x), piece(upper, x)], axis=1)
            own = jnp.where(rows == row + (lane ^ line), both, own)
        for line, before, after in ((0, "u", "l"), (1, "u1", "l1")):
            before = jnp.where(even, piece(before, x ^ 3), piece(before, x ^ 1))
            after = jnp.where(even, piece(after, x ^ 1), piece(after, x ^ 3))
            both = jnp.concatenate([before, after], axis=1)
            halo = jnp.where(rows == row + (lane ^ line), both, halo)
    out_ref[:, 0, :] = own
    out_ref[:, 1, :] = halo


def masses_call(jobs, arrays, rows, columns, last=None, layout=None):
    names = [name for name in NAMES if any(name in job for job in jobs)]

    def kernel(*refs):
        refs = list(refs)
        held = {name: refs.pop(0) for name in names}
        rows_ref, columns_ref = refs.pop(0), refs.pop(0)
        last_ref = refs.pop(0) if last is not None else None
        t = Terms(held, rows_ref, columns_ref, refs.pop(0), last_ref)
        for job in jobs:
            t.job(*job)
        if layout is None:
            t.write()
        else:
            lay_out(t.totals(), layout[2] // 2, t.out)

    operands = [arrays[name] for name in names] + [rows, columns]
    if last is not None:
        operands.append(last)
    n, width = operands[0].shape
    return call(
        kernel,
        jax.ShapeDtypeStruct(layout or (len(SUMS), n), jnp.float32),
        cost_estimate=pl.CostEstimate(flops=0, transcendentals=0, bytes_accessed=0),
    )(*operands)


def weights_kernel(rank_ref, returned_ref, out_ref):
    peers, _, width = returned_ref.shape
    m = width // 2
    rank = rank_ref[...]
    n = rank.shape[1]
    slab, upper, member = rank // width, rank // m % 2 == 1, rank % m
    plane = iota((peers, n), 0) // QUAD

    def chosen(k, which, column):
        picked = lax.dot_general(
            returned_ref[:, k, :],
            jnp.where(plane == which, 1.0, 0.0),
            TN,
            precision=lax.Precision.HIGHEST,
            preferred_element_type=jnp.float32,
        )
        here = iota((width, n), 0) == column
        return jnp.sum(jnp.where(here, picked, 0.0), axis=0, keepdims=True)

    mass = chosen(0, slab, jnp.where(upper, m + member, member))
    mass += chosen(1, jnp.where(upper, slab + 1, slab - 1), jnp.where(upper, member, m + member))
    out_ref[...] = 1.0 / (1.0 + mass)


def xor_order(array, axis, bits):
    count = array.shape[axis]
    for k in range(count.bit_length() - 1):
        step = 1 << k
        shape = array.shape[:axis] + (count // (2 * step), 2, step) + array.shape[axis + 1 :]
        split = array.reshape(shape)
        split = jnp.where((bits >> k) & 1 == 1, jnp.flip(split, axis + 1), split)
        array = split.reshape(array.shape)
    return array


def shards(embeddings, position, cluster_ids):
    n, width = embeddings.shape
    peers = lax.axis_size("dev")
    me = lax.axis_index("dev")
    planes = peers // QUAD
    slab, lane = me // QUAD, me % QUAD
    per_half = n // (2 * planes)
    by_permutes = planes == 4
    pieces = [per_half] * 2 + [2 * per_half] + [per_half] * 4 if by_permutes else [n]
    f32 = jnp.float32

    def swapped(rows_, bit):
        return lax.ppermute(rows_, "dev", [(i, i ^ bit) for i in range(peers)])

    def passed(rows_, by):
        pairs = [(i, i + by) for i in range(peers) if 0 <= i + by < peers]
        return lax.ppermute(rows_, "dev", pairs)

    def after_all(value, *others):
        return lax.optimization_barrier((value, *others))[0]

    def as_received(values, axis, plane):
        return xor_order(values, axis, plane) if by_permutes else values

    where_to = position.reshape(1, n)
    in_hbm = pl.BlockSpec(memory_space=pltpu.HBM)
    *arranged, rank = call(
        functools.partial(arrange_kernel, per_half, 2 * planes),
        [jax.ShapeDtypeStruct((size, width), embeddings.dtype) for size in pieces]
        + [jax.ShapeDtypeStruct((1, n), jnp.int32)],
        in_specs=[in_hbm, in_hbm],
        scratch_shapes=[
            pltpu.VMEM((1, n), jnp.int32),
            pltpu.VMEM((n, width), embeddings.dtype),
            pltpu.SemaphoreType.DMA((2,)),
        ],
    )(where_to, embeddings)
    if by_permutes:
        own_upper, own_lower, to_1, upper_2, lower_2, upper_3, lower_3 = arranged
        upper_3 = swapped(upper_3, 3 * QUAD)
        upper_2 = swapped(upper_2, 2 * QUAD)
        both_1 = swapped(to_1, QUAD)
        lower_3 = swapped(lower_3, 3 * QUAD)
        lower_2 = swapped(lower_2, 2 * QUAD)
        upper = jnp.concatenate([own_upper, both_1[:per_half], upper_2, upper_3], axis=0)
        lower = jnp.concatenate([own_lower, both_1[per_half:], lower_2, lower_3], axis=0)
    else:
        lines = [[p * QUAD + q for p in range(planes)] for q in range(QUAD)]
        block = lax.all_to_all(
            arranged[0], "dev", split_axis=0, concat_axis=0, axis_index_groups=lines, tiled=True
        ).reshape(planes, 2, per_half, width)
        upper = block[:, 1].reshape(n // 2, width)
        lower = block[:, 0].reshape(n // 2, width)

    aligned = by_permutes and 2 * per_half == LANES
    own_facts = (where_to, cluster_ids.reshape(1, n), rank, *arranged)
    facts_shape = (peers, 4 + n // LANES, LANES) if aligned else (4, n)
    facts = call(
        functools.partial(facts_kernel, per_half), jax.ShapeDtypeStruct(facts_shape, f32)
    )(*own_facts)
    if not aligned:
        seen = jnp.pad(facts[:2], ((0, 0), (per_half, per_half)))
        seen = jnp.stack(
            [seen[:, 2 * p * per_half : (2 * p + 4) * per_half] for p in range(planes)]
        ).reshape(planes, 1, 8 * per_half)
        facts = jnp.concatenate(
            [
                jnp.broadcast_to(seen, (planes, QUAD, 8 * per_half)),
                jnp.broadcast_to(facts[2], (planes, QUAD, n)),
            ],
            axis=2,
        )
        facts = facts.reshape(peers, 8 * per_half + n)
    facts = after_all(facts, upper_2 if by_permutes else block)
    facts = lax.all_to_all(facts, "dev", split_axis=0, concat_axis=0, tiled=True)
    arrays = {"b0h": upper}
    arrays["b2h"] = swapped(upper, 2)
    arrays["b1h"] = swapped(upper, 1)
    lower = after_all(lower, arrays["b1h"])
    arrays["b0l"] = lower
    arrays["u"] = passed(upper, QUAD)
    arrays["b2l"] = swapped(lower, 2)
    arrays["l"] = passed(lower, -QUAD)
    arrays["b1l"] = swapped(lower, 1)

    if aligned:
        ids, near = facts[:, 4:].reshape(peers * n), facts[:, :4]
    else:
        ids, near = facts[:, 8 * per_half :].reshape(peers * n), facts[:, : 8 * per_half]
    ids = jnp.pad(ids, (MOST, MOST))
    ids = lax.dynamic_slice_in_dim(ids, slab * MOST, 3 * MOST, 0)
    near = near.reshape(planes, QUAD, 2, 4, per_half)
    near = xor_order(near, 1, lane).transpose(2, 1, 3, 0, 4)
    before = as_received(near[:, :2, 0], 2, slab - 1)
    after = as_received(near[:, :2, 3], 2, slab + 1)
    own = as_received(near[:, :3, 1:3], 3, slab)
    near = jnp.concatenate(
        [
            jnp.stack([own[:, :, 1], own[:, :, 0]], axis=2).reshape(2, 3 * n),
            jnp.stack([before, after], axis=2).reshape(2, 2 * n),
        ],
        axis=1,
    )
    total = 5 * n
    place = near[0].astype(jnp.int32) - (slab - 1) * MOST
    label = call(labels_kernel, jax.ShapeDtypeStruct((1, total), f32))(
        place.reshape(1, total), ids.reshape(3 * MOST // LANES, LANES)
    )[0]
    at = jnp.arange(total)
    absent = (at >= 3 * n) & jnp.where(at % n >= n // 2, slab == planes - 1, slab == 0)
    label = jnp.where(absent, -1.0, label)
    rows = jnp.stack([near[1], label])
    columns = jnp.stack([near[1] * SCALE, label], axis=1)

    def masses_after(jobs, last=None):
        return masses_call(jobs, arrays, rows, columns, last)

    masses = masses_after(
        [("b0h", "b0h"), ("b1h", "b0h"), ("b2h", "b0h"), ("b1h", "b2h")]
        + [("b0l", "b0l"), ("b0h", "b0l"), ("b1h", "b0l"), ("b2h", "b0l")]
        + [("b1l", "b0h"), ("b1l", "b0l"), ("b1l", "b2h")]
    )
    arrays["u1"] = swapped(after_all(arrays['u'], arrays["b2h"]), 1)
    masses = masses_after([(u, b) for u in ("u", "u1") for b in ("b0h", "b0l", "b2h")], masses)
    arrays["l1"] = swapped(after_all(arrays["l"], masses, arrays["b2l"]), 1)
    masses = masses_after(
        [("b2l", "b0h"), ("b2l", "b0l"), ("b1h", "b2l"), ("b1l", "b2l"), ("u", "b2l"), ("u1", "b2l")],
        masses,
    )
    last = [("l", "b0l"), ("l", "b2l"), ("l1", "b0l"), ("l1", "b2l")]
    if by_permutes:
        outgoing = masses_call(last, arrays, rows, columns, masses, (peers, 2, 2 * per_half))
    else:
        masses = masses_after(last, masses)
        masses = masses.reshape(4, 2, planes, per_half)
        slabs = as_received(masses[:2], 2, slab)
        before = as_received(masses[2:, 0], 1, slab - 1)
        after = as_received(masses[2:, 1], 1, slab + 1)
        none = jnp.zeros_like(before[0])
        outgoing = jnp.stack(
            [
                jnp.stack([slabs[0, 1], none, slabs[1, 1], none]),
                jnp.stack([slabs[0, 0], none, slabs[1, 0], none]),
                jnp.stack([before[0], before[1], none, none]),
                jnp.stack([after[0], after[1], none, none]),
            ],
            axis=2,
        )
        outgoing = xor_order(outgoing, 0, lane).transpose(1, 0, 2, 3)
        outgoing = outgoing.reshape(peers, 2, 2 * per_half)
    returned = lax.all_to_all(outgoing, "dev", split_axis=0, concat_axis=0, tiled=True)
    weight = call(
        weights_kernel, jax.ShapeDtypeStruct((1, n), f32)
    )(rank, returned)
    return weight.reshape(n)


def solution(mesh):
    return jax.shard_map(
        shards,
        mesh=mesh,
        in_specs=(P(("grp", "dev"), None), P(("grp", "dev")), P(("grp", "dev"))),
        out_specs=P(("grp", "dev")),
        check_vma=False,
    )
```

```python
import functools
import math

import jax
import jax.numpy as jnp
from jax import lax
from jax.experimental import pallas as pl
from jax.experimental.pallas import tpu as pltpu
from jax.sharding import PartitionSpec as P

MOST = 2048
HALF = MOST // 2
SIMILARITY_CUTOFF = 0.9
SOFTMAX_HEAT = 0.02
SCALE = math.log2(math.e) / SOFTMAX_HEAT
FACTOR = math.exp(-SIMILARITY_CUTOFF / SOFTMAX_HEAT)
QUAD = 4
CHUNK = 256
LANES = 128
VMEM_LIMIT = 16 * 1024 * 1024

NT = (((1,), (1,)), ((), ()))
TN = (((0,), (0,)), ((), ()))


def iota(shape, dim):
    return lax.broadcasted_iota(jnp.int32, shape, dim)


def call(kernel, out_shape, limit=VMEM_LIMIT, **extra):
    return pl.pallas_call(
        kernel,
        out_shape=out_shape,
        compiler_params=pltpu.CompilerParams(vmem_limit_bytes=limit),
        **extra,
    )


def arrange_kernel(per_half, halves, position_hbm, rows_hbm, *refs):
    *outs, rank_ref, place, rows, sems = refs
    copies = [
        pltpu.make_async_copy(position_hbm, place, sems.at[0]),
        pltpu.make_async_copy(rows_hbm, rows, sems.at[1]),
    ]
    for copy in copies:
        copy.start()
    n = rows.shape[0]
    earlier = (iota((n, n), 0) < iota((n, n), 1)).astype(jnp.bfloat16)
    copies[0].wait()
    half = place[...] // HALF
    kinds = iota((halves, n), 0) == half
    counts = jnp.dot(kinds.astype(jnp.bfloat16), earlier, preferred_element_type=jnp.float32)
    count = jnp.sum(jnp.where(kinds, counts, 0.0), axis=0, keepdims=True).astype(jnp.int32)
    rank_ref[...] = half * per_half + count
    rank = half * per_half + count
    if len(outs) > 1:
        plane = (half // 2) ^ (lax.axis_index("dev") // QUAD)
        rank = (2 * plane + 1 - half % 2) * per_half + count
    pick = (iota((n, n), 0) == rank).astype(jnp.bfloat16)
    copies[1].wait()
    picked = jnp.dot(pick, rows[...], preferred_element_type=jnp.float32)
    at = 0
    for out in outs:
        out[...] = picked[at : at + out.shape[0], :].astype(out.dtype)
        at += out.shape[0]


def facts_kernel(per_half, position_ref, ids_ref, rank_ref, *refs):
    *pieces, out_ref = refs
    n = position_ref.shape[1]
    pick = iota((n, n), 0) == rank_ref[...]
    where_to = position_ref[...].astype(jnp.float32)
    column = jnp.sum(jnp.where(pick, where_to, 0.0), axis=1, keepdims=True)
    eye = iota((n, n), 0) == iota((n, n), 1)
    positions = jnp.sum(jnp.where(eye, column, 0.0), axis=0, keepdims=True)
    total = jnp.zeros((1, n), jnp.float32)
    k = 0
    for piece in pieces:
        size = n if len(pieces) == 1 else per_half
        for start in range(0, piece.shape[0], size):
            wide = piece[start : start + size, :].astype(jnp.float32)
            inverse = lax.rsqrt(jnp.sum(wide * wide, axis=1, keepdims=True) + 1e-06)
            first = 0
            if len(pieces) > 1:
                plane = (k // 2) ^ (lax.axis_index("dev") // QUAD)
                first = (2 * plane + 1 - k % 2) * per_half
            here = iota((size, n), 0) + first == iota((size, n), 1)
            total += jnp.sum(jnp.where(here, inverse, 0.0), axis=0, keepdims=True)
            k += 1
    ids = ids_ref[...].astype(jnp.float32)
    if len(out_ref.shape) == 2:
        for k, values in enumerate((positions, total, ids, jnp.zeros_like(ids))):
            out_ref[k : k + 1, :] = values
        return
    beyond = jnp.zeros((1, per_half), jnp.float32)
    ids = [ids[:, at : at + LANES] for at in range(0, n, LANES)]
    wide = [jnp.concatenate([beyond, values, beyond], axis=1) for values in (positions, total)]
    for peer in range(out_ref.shape[0]):
        at = peer // QUAD * LANES
        lines = [values[:, at + k : at + k + LANES] for values in wide for k in (0, LANES)]
        for k, line in enumerate(lines + ids):
            out_ref[peer, k : k + 1, :] = line


def labels_kernel(place_ref, table_ref, out_ref):
    place = place_ref[...]
    depth = table_ref.shape[0]
    n = place.shape[1]
    table = table_ref[...]
    high = jnp.floor(table * (1.0 / 256.0))
    low = table - high * 256.0
    line = (iota((depth, n), 0) == place // LANES).astype(jnp.bfloat16)
    high = lax.dot_general(
        high.astype(jnp.bfloat16), line, TN, preferred_element_type=jnp.float32
    )
    low = lax.dot_general(
        low.astype(jnp.bfloat16), line, TN, preferred_element_type=jnp.float32
    )
    here = iota((LANES, n), 0) == place % LANES
    out_ref[...] = jnp.sum(jnp.where(here, high * 256.0 + low, 0.0), axis=0, keepdims=True)


NAMES = ("b0h", "b0l", "b1h", "b1l", "b2h", "b2l", "u", "l", "u1", "l1")
SUMS = ("b0h", "b0l", "b2h", "b2l", "u", "l", "u1", "l1")


class Terms:
    def __init__(self, arrays, rows_ref, columns_ref, out_ref, last_ref):
        self.arrays, self.rows, self.columns, self.out = arrays, rows_ref, columns_ref, out_ref
        self.last = last_ref
        self.sums = {}

    def add(self, name, values):
        self.sums[name] = self.sums[name] + values if name in self.sums else values

    def job(self, down, across):
        n = self.arrays[down].shape[0]
        products = lax.dot_general(
            self.arrays[down][...],
            self.arrays[across][...],
            NT,
            preferred_element_type=jnp.float32,
        )
        at, to = NAMES.index(down) * n, NAMES.index(across) * n
        scale = self.columns[at : at + n, 0:1]
        label = self.columns[at : at + n, 1:2]
        power = products * scale * self.rows[0:1, to : to + n]
        mask = label == self.rows[1:2, to : to + n]
        if down == across:
            mask &= iota((n, n), 0) != iota((n, n), 1)
        values = jnp.where(mask, jnp.exp2(power), 0.0)
        self.add(across, jnp.sum(values, axis=0, keepdims=True))
        if down in ("u", "l", "u1", "l1") or (down, across) == ("b0h", "b0l"):
            side = jnp.zeros((n, LANES), jnp.float32)
            for lane in range(0, n, LANES):
                side += values[:, lane : lane + LANES]
            self.add(down, jnp.sum(side.T, axis=0, keepdims=True))

    def totals(self):
        totals = {}
        for k, name in enumerate(SUMS):
            values = self.sums.get(name)
            last = self.last[k : k + 1, :] if self.last is not None else None
            if values is None:
                n = self.arrays["b0l"].shape[0]
                values = jnp.zeros((1, n), jnp.float32) if last is None else last
            elif last is not None:
                values += last
            totals[name] = values
        return totals

    def write(self):
        for k, values in enumerate(self.totals().values()):
            self.out[k : k + 1, :] = values


def lay_out(sums, m, out_ref):
    me = lax.axis_index("dev")
    slab, lane = me // QUAD, me % QUAD
    even = slab % 2 == 0
    rows = iota((out_ref.shape[0], 2 * m), 0)
    own = jnp.zeros(rows.shape, jnp.float32)
    halo = own

    def piece(name, x):
        return sums[name][:, x * m : (x + 1) * m]

    for x in range(QUAD):
        row = (slab ^ x) * QUAD
        for line, lower, upper in ((0, "b0l", "b0h"), (2, "b2l", "b2h")):
            both = jnp.concatenate([piece(lower, x), piece(upper, x)], axis=1)
            own = jnp.where(rows == row + (lane ^ line), both, own)
        for line, before, after in ((0, "u", "l"), (1, "u1", "l1")):
            before = jnp.where(even, piece(before, x ^ 3), piece(before, x ^ 1))
            after = jnp.where(even, piece(after, x ^ 1), piece(after, x ^ 3))
            both = jnp.concatenate([before, after], axis=1)
            halo = jnp.where(rows == row + (lane ^ line), both, halo)
    out_ref[:, 0, :] = own
    out_ref[:, 1, :] = halo


def masses_call(jobs, arrays, rows, columns, last=None, layout=None):
    names = [name for name in NAMES if any(name in job for job in jobs)]

    def kernel(*refs):
        refs = list(refs)
        held = {name: refs.pop(0) for name in names}
        rows_ref, columns_ref = refs.pop(0), refs.pop(0)
        last_ref = refs.pop(0) if last is not None else None
        t = Terms(held, rows_ref, columns_ref, refs.pop(0), last_ref)
        for job in jobs:
            t.job(*job)
        if layout is None:
            t.write()
        else:
            lay_out(t.totals(), layout[2] // 2, t.out)

    operands = [arrays[name] for name in names] + [rows, columns]
    if last is not None:
        operands.append(last)
    n, width = operands[0].shape
    return call(
        kernel,
        jax.ShapeDtypeStruct(layout or (len(SUMS), n), jnp.float32),
        cost_estimate=pl.CostEstimate(flops=0, transcendentals=0, bytes_accessed=0),
    )(*operands)


def weights_kernel(rank_ref, returned_ref, out_ref):
    peers, _, width = returned_ref.shape
    m = width // 2
    rank = rank_ref[...]
    n = rank.shape[1]
    slab, upper, member = rank // width, rank // m % 2 == 1, rank % m
    plane = iota((peers, n), 0) // QUAD

    def chosen(k, which, column):
        picked = lax.dot_general(
            returned_ref[:, k, :],
            jnp.where(plane == which, 1.0, 0.0),
            TN,
            precision=lax.Precision.HIGHEST,
            preferred_element_type=jnp.float32,
        )
        here = iota((width, n), 0) == column
        return jnp.sum(jnp.where(here, picked, 0.0), axis=0, keepdims=True)

    mass = chosen(0, slab, jnp.where(upper, m + member, member))
    mass += chosen(1, jnp.where(upper, slab + 1, slab - 1), jnp.where(upper, member, m + member))
    out_ref[...] = 1.0 / (1.0 + mass * FACTOR)


def xor_order(array, axis, bits):
    count = array.shape[axis]
    for k in range(count.bit_length() - 1):
        step = 1 << k
        shape = array.shape[:axis] + (count // (2 * step), 2, step) + array.shape[axis + 1 :]
        split = array.reshape(shape)
        split = jnp.where((bits >> k) & 1 == 1, jnp.flip(split, axis + 1), split)
        array = split.reshape(array.shape)
    return array


def shards(embeddings, position, cluster_ids):
    n, width = embeddings.shape
    peers = lax.axis_size("dev")
    me = lax.axis_index("dev")
    planes = peers // QUAD
    slab, lane = me // QUAD, me % QUAD
    per_half = n // (2 * planes)
    by_permutes = planes == 4
    pieces = [per_half] * 2 + [2 * per_half] + [per_half] * 4 if by_permutes else [n]
    f32 = jnp.float32

    def swapped(rows_, bit):
        return lax.ppermute(rows_, "dev", [(i, i ^ bit) for i in range(peers)])

    def passed(rows_, by):
        pairs = [(i, i + by) for i in range(peers) if 0 <= i + by < peers]
        return lax.ppermute(rows_, "dev", pairs)

    def after_all(value, *others):
        return lax.optimization_barrier((value, *others))[0]

    def as_received(values, axis, plane):
        return xor_order(values, axis, plane) if by_permutes else values

    where_to = position.reshape(1, n)
    in_hbm = pl.BlockSpec(memory_space=pltpu.HBM)
    *arranged, rank = call(
        functools.partial(arrange_kernel, per_half, 2 * planes),
        [jax.ShapeDtypeStruct((size, width), embeddings.dtype) for size in pieces]
        + [jax.ShapeDtypeStruct((1, n), jnp.int32)],
        in_specs=[in_hbm, in_hbm],
        scratch_shapes=[
            pltpu.VMEM((1, n), jnp.int32),
            pltpu.VMEM((n, width), embeddings.dtype),
            pltpu.SemaphoreType.DMA((2,)),
        ],
    )(where_to, embeddings)
    if by_permutes:
        own_upper, own_lower, to_1, upper_2, lower_2, upper_3, lower_3 = arranged
        upper_3 = swapped(upper_3, 3 * QUAD)
        upper_2 = swapped(upper_2, 2 * QUAD)
        both_1 = swapped(to_1, QUAD)
        lower_3 = swapped(lower_3, 3 * QUAD)
        lower_2 = swapped(lower_2, 2 * QUAD)
        upper = jnp.concatenate([own_upper, both_1[:per_half], upper_2, upper_3], axis=0)
        lower = jnp.concatenate([own_lower, both_1[per_half:], lower_2, lower_3], axis=0)
    else:
        lines = [[p * QUAD + q for p in range(planes)] for q in range(QUAD)]
        block = lax.all_to_all(
            arranged[0], "dev", split_axis=0, concat_axis=0, axis_index_groups=lines, tiled=True
        ).reshape(planes, 2, per_half, width)
        upper = block[:, 1].reshape(n // 2, width)
        lower = block[:, 0].reshape(n // 2, width)

    aligned = by_permutes and 2 * per_half == LANES
    own_facts = (where_to, cluster_ids.reshape(1, n), rank, *arranged)
    facts_shape = (peers, 4 + n // LANES, LANES) if aligned else (4, n)
    facts = call(
        functools.partial(facts_kernel, per_half), jax.ShapeDtypeStruct(facts_shape, f32)
    )(*own_facts)
    if not aligned:
        seen = jnp.pad(facts[:2], ((0, 0), (per_half, per_half)))
        seen = jnp.stack(
            [seen[:, 2 * p * per_half : (2 * p + 4) * per_half] for p in range(planes)]
        ).reshape(planes, 1, 8 * per_half)
        facts = jnp.concatenate(
            [
                jnp.broadcast_to(seen, (planes, QUAD, 8 * per_half)),
                jnp.broadcast_to(facts[2], (planes, QUAD, n)),
            ],
            axis=2,
        )
        facts = facts.reshape(peers, 8 * per_half + n)
    facts = after_all(facts, both_1 if by_permutes else block)
    facts = lax.all_to_all(facts, "dev", split_axis=0, concat_axis=0, tiled=True)
    arrays = {"b0h": upper}
    arrays["b2h"] = swapped(upper, 2)
    arrays["b1h"] = swapped(upper, 1)
    lower = after_all(lower, arrays["b1h"])
    arrays["b0l"] = lower
    arrays["u"] = passed(upper, QUAD)
    arrays["b2l"] = swapped(lower, 2)
    arrays["l"] = passed(lower, -QUAD)
    arrays["b1l"] = swapped(lower, 1)

    if aligned:
        ids, near = facts[:, 4:].reshape(peers * n), facts[:, :4]
    else:
        ids, near = facts[:, 8 * per_half :].reshape(peers * n), facts[:, : 8 * per_half]
    ids = jnp.pad(ids, (MOST, MOST))
    ids = lax.dynamic_slice_in_dim(ids, slab * MOST, 3 * MOST, 0)
    near = near.reshape(planes, QUAD, 2, 4, per_half)
    near = xor_order(near, 1, lane).transpose(2, 1, 3, 0, 4)
    before = as_received(near[:, :2, 0], 2, slab - 1)
    after = as_received(near[:, :2, 3], 2, slab + 1)
    own = as_received(near[:, :3, 1:3], 3, slab)
    near = jnp.concatenate(
        [
            jnp.stack([own[:, :, 1], own[:, :, 0]], axis=2).reshape(2, 3 * n),
            jnp.stack([before, after], axis=2).reshape(2, 2 * n),
        ],
        axis=1,
    )
    total = 5 * n
    place = near[0].astype(jnp.int32) - (slab - 1) * MOST
    label = call(labels_kernel, jax.ShapeDtypeStruct((1, total), f32))(
        place.reshape(1, total), ids.reshape(3 * MOST // LANES, LANES)
    )[0]
    at = jnp.arange(total)
    absent = (at >= 3 * n) & jnp.where(at % n >= n // 2, slab == planes - 1, slab == 0)
    label = jnp.where(absent, -1.0, label)
    rows = jnp.stack([near[1], label])
    columns = jnp.stack([near[1] * SCALE, label], axis=1)

    def masses_after(jobs, last=None):
        return masses_call(jobs, arrays, rows, columns, last)

    masses = masses_after(
        [("b0h", "b0h"), ("b1h", "b0h"), ("b2h", "b0h"), ("b1h", "b2h")]
        + [("b0l", "b0l"), ("b0h", "b0l"), ("b1h", "b0l"), ("b2h", "b0l")]
        + [("b1l", "b0h"), ("b1l", "b0l"), ("b1l", "b2h")]
    )
    arrays["u1"] = swapped(after_all(arrays['u'], arrays["b2h"]), 1)
    masses = masses_after([(u, b) for u in ("u", "u1") for b in ("b0h", "b0l", "b2h")], masses)
    arrays["l1"] = swapped(after_all(arrays["l"], masses, arrays["b2l"]), 1)
    masses = masses_after(
        [("b2l", "b0h"), ("b2l", "b0l"), ("b1h", "b2l"), ("b1l", "b2l"), ("u", "b2l"), ("u1", "b2l")],
        masses,
    )
    last = [("l", "b0l"), ("l", "b2l"), ("l1", "b0l"), ("l1", "b2l")]
    if by_permutes:
        outgoing = masses_call(last, arrays, rows, columns, masses, (peers, 2, 2 * per_half))
    else:
        masses = masses_after(last, masses)
        masses = masses.reshape(4, 2, planes, per_half)
        slabs = as_received(masses[:2], 2, slab)
        before = as_received(masses[2:, 0], 1, slab - 1)
        after = as_received(masses[2:, 1], 1, slab + 1)
        none = jnp.zeros_like(before[0])
        outgoing = jnp.stack(
            [
                jnp.stack([slabs[0, 1], none, slabs[1, 1], none]),
                jnp.stack([slabs[0, 0], none, slabs[1, 0], none]),
                jnp.stack([before[0], before[1], none, none]),
                jnp.stack([after[0], after[1], none, none]),
            ],
            axis=2,
        )
        outgoing = xor_order(outgoing, 0, lane).transpose(1, 0, 2, 3)
        outgoing = outgoing.reshape(peers, 2, 2 * per_half)
    returned = lax.all_to_all(outgoing, "dev", split_axis=0, concat_axis=0, tiled=True)
    weight = call(
        weights_kernel, jax.ShapeDtypeStruct((1, n), f32)
    )(rank, returned)
    return weight.reshape(n)


def solution(mesh):
    return jax.shard_map(
        shards,
        mesh=mesh,
        in_specs=(P(("grp", "dev"), None), P(("grp", "dev")), P(("grp", "dev"))),
        out_specs=P(("grp", "dev")),
        check_vma=False,
    )
```

```python
import functools
import math

import jax
import jax.numpy as jnp
from jax import lax
from jax.experimental import pallas as pl
from jax.experimental.pallas import tpu as pltpu
from jax.sharding import PartitionSpec as P

MOST = 2048
HALF = MOST // 2
SIMILARITY_CUTOFF = 0.9
SOFTMAX_HEAT = 0.02
SCALE = math.log2(math.e) / SOFTMAX_HEAT
FACTOR = math.exp(-SIMILARITY_CUTOFF / SOFTMAX_HEAT)
QUAD = 4
CHUNK = 256
LANES = 128
VMEM_LIMIT = 16 * 1024 * 1024

NT = (((1,), (1,)), ((), ()))
TN = (((0,), (0,)), ((), ()))


def iota(shape, dim):
    return lax.broadcasted_iota(jnp.int32, shape, dim)


def call(kernel, out_shape, limit=VMEM_LIMIT, **extra):
    return pl.pallas_call(
        kernel,
        out_shape=out_shape,
        compiler_params=pltpu.CompilerParams(vmem_limit_bytes=limit),
        **extra,
    )


def arrange_kernel(per_half, halves, position_hbm, rows_hbm, *refs):
    *outs, rank_ref, place, rows, sems = refs
    copies = [
        pltpu.make_async_copy(position_hbm, place, sems.at[0]),
        pltpu.make_async_copy(rows_hbm, rows, sems.at[1]),
    ]
    for copy in copies:
        copy.start()
    n = rows.shape[0]
    earlier = (iota((n, n), 0) < iota((n, n), 1)).astype(jnp.bfloat16)
    copies[0].wait()
    half = place[...] // HALF
    kinds = iota((halves, n), 0) == half
    counts = jnp.dot(kinds.astype(jnp.bfloat16), earlier, preferred_element_type=jnp.float32)
    count = jnp.sum(jnp.where(kinds, counts, 0.0), axis=0, keepdims=True).astype(jnp.int32)
    rank_ref[...] = half * per_half + count
    rank = half * per_half + count
    if len(outs) > 1:
        plane = (half // 2) ^ (lax.axis_index("dev") // QUAD)
        rank = (2 * plane + 1 - half % 2) * per_half + count
    pick = (iota((n, n), 0) == rank).astype(jnp.bfloat16)
    copies[1].wait()
    picked = jnp.dot(pick, rows[...], preferred_element_type=jnp.float32)
    at = 0
    for out in outs:
        out[...] = picked[at : at + out.shape[0], :].astype(out.dtype)
        at += out.shape[0]


def facts_kernel(per_half, position_ref, ids_ref, rank_ref, *refs):
    *pieces, out_ref = refs
    n = position_ref.shape[1]
    pick = iota((n, n), 0) == rank_ref[...]
    where_to = position_ref[...].astype(jnp.float32)
    column = jnp.sum(jnp.where(pick, where_to, 0.0), axis=1, keepdims=True)
    eye = iota((n, n), 0) == iota((n, n), 1)
    positions = jnp.sum(jnp.where(eye, column, 0.0), axis=0, keepdims=True)
    total = jnp.zeros((1, n), jnp.float32)
    k = 0
    for piece in pieces:
        size = n if len(pieces) == 1 else per_half
        for start in range(0, piece.shape[0], size):
            wide = piece[start : start + size, :].astype(jnp.float32)
            inverse = lax.rsqrt(jnp.sum(wide * wide, axis=1, keepdims=True) + 1e-06)
            first = 0
            if len(pieces) > 1:
                plane = (k // 2) ^ (lax.axis_index("dev") // QUAD)
                first = (2 * plane + 1 - k % 2) * per_half
            here = iota((size, n), 0) + first == iota((size, n), 1)
            total += jnp.sum(jnp.where(here, inverse, 0.0), axis=0, keepdims=True)
            k += 1
    ids = ids_ref[...].astype(jnp.float32)
    if len(out_ref.shape) == 2:
        for k, values in enumerate((positions, total, ids, jnp.zeros_like(ids))):
            out_ref[k : k + 1, :] = values
        return
    beyond = jnp.zeros((1, per_half), jnp.float32)
    ids = [ids[:, at : at + LANES] for at in range(0, n, LANES)]
    wide = [jnp.concatenate([beyond, values, beyond], axis=1) for values in (positions, total)]
    for peer in range(out_ref.shape[0]):
        at = peer // QUAD * LANES
        lines = [values[:, at + k : at + k + LANES] for values in wide for k in (0, LANES)]
        for k, line in enumerate(lines + ids):
            out_ref[peer, k : k + 1, :] = line


def labels_kernel(place_ref, table_ref, out_ref):
    place = place_ref[...]
    depth = table_ref.shape[0]
    n = place.shape[1]
    table = table_ref[...]
    high = jnp.floor(table * (1.0 / 256.0))
    low = table - high * 256.0
    line = (iota((depth, n), 0) == place // LANES).astype(jnp.bfloat16)
    high = lax.dot_general(
        high.astype(jnp.bfloat16), line, TN, preferred_element_type=jnp.float32
    )
    low = lax.dot_general(
        low.astype(jnp.bfloat16), line, TN, preferred_element_type=jnp.float32
    )
    here = iota((LANES, n), 0) == place % LANES
    out_ref[...] = jnp.sum(jnp.where(here, high * 256.0 + low, 0.0), axis=0, keepdims=True)


NAMES = ("b0h", "b0l", "b1h", "b1l", "b2h", "b2l", "u", "l", "u1", "l1")
SUMS = ("b0h", "b0l", "b2h", "b2l", "u", "l", "u1", "l1")


class Terms:
    def __init__(self, arrays, rows_ref, columns_ref, out_ref, last_ref):
        self.arrays, self.rows, self.columns, self.out = arrays, rows_ref, columns_ref, out_ref
        self.last = last_ref
        self.sums = {}

    def add(self, name, values):
        self.sums[name] = self.sums[name] + values if name in self.sums else values

    def job(self, down, across):
        n = self.arrays[down].shape[0]
        products = lax.dot_general(
            self.arrays[down][...],
            self.arrays[across][...],
            NT,
            preferred_element_type=jnp.float32,
        )
        at, to = NAMES.index(down) * n, NAMES.index(across) * n
        scale = self.columns[at : at + n, 0:1]
        label = self.columns[at : at + n, 1:2]
        power = products * scale * self.rows[0:1, to : to + n]
        mask = label == self.rows[1:2, to : to + n]
        if down == across:
            mask &= iota((n, n), 0) != iota((n, n), 1)
        values = jnp.where(mask, jnp.exp2(power), 0.0)
        self.add(across, jnp.sum(values, axis=0, keepdims=True))
        if down in ("u", "l", "u1", "l1") or (down, across) == ("b0h", "b0l"):
            side = jnp.zeros((n, LANES), jnp.float32)
            for lane in range(0, n, LANES):
                side += values[:, lane : lane + LANES]
            self.add(down, jnp.sum(side.T, axis=0, keepdims=True))

    def totals(self):
        totals = {}
        for k, name in enumerate(SUMS):
            values = self.sums.get(name)
            last = self.last[k : k + 1, :] if self.last is not None else None
            if values is None:
                n = self.arrays["b0l"].shape[0]
                values = jnp.zeros((1, n), jnp.float32) if last is None else last
            elif last is not None:
                values += last
            totals[name] = values
        return totals

    def write(self):
        for k, values in enumerate(self.totals().values()):
            self.out[k : k + 1, :] = values


def masses_call(jobs, arrays, rows, columns, last=None):
    names = [name for name in NAMES if any(name in job for job in jobs)]

    def kernel(*refs):
        refs = list(refs)
        held = {name: refs.pop(0) for name in names}
        rows_ref, columns_ref = refs.pop(0), refs.pop(0)
        last_ref = refs.pop(0) if last is not None else None
        t = Terms(held, rows_ref, columns_ref, refs.pop(0), last_ref)
        for job in jobs:
            t.job(*job)
        t.write()

    operands = [arrays[name] for name in names] + [rows, columns]
    if last is not None:
        operands.append(last)
    n, width = operands[0].shape
    return call(
        kernel,
        jax.ShapeDtypeStruct((len(SUMS), n), jnp.float32),
        cost_estimate=pl.CostEstimate(flops=0, transcendentals=0, bytes_accessed=0),
    )(*operands)


def combine_kernel(masses_ref, across_ref, beside_ref, *out_refs):
    slab = lax.axis_index("dev") // QUAD
    upper = masses_ref[0:1, :] + across_ref[0:1, :]
    lower = masses_ref[1:2, :] + across_ref[1:2, :]
    before = masses_ref[4:5, :] + beside_ref[0:1, :]
    after = masses_ref[5:6, :] + beside_ref[1:2, :]
    m = out_refs[0].shape[1]

    def piece(values, x):
        return values[:, x * m : (x + 1) * m]

    for x, out in enumerate(out_refs):
        out[0:1, :] = piece(lower, x)
        out[1:2, :] = piece(upper, x)
        out[2:3, :] = jnp.where(slab == 2, piece(before, x ^ 3), piece(before, x ^ 1))
        out[3:4, :] = jnp.where(slab == 1, piece(after, x ^ 3), piece(after, x ^ 1))


def weights_kernel(relative, rank_ref, *refs):
    *returned, out_ref = refs
    parts = [ref[...] for ref in returned]
    returned = parts[0] if len(parts) == 1 else jnp.concatenate(parts, axis=0)
    count, m = returned.shape
    rank = rank_ref[0:1, :]
    n = rank.shape[1]
    slab, upper, member = rank // (2 * m), rank // m % 2 == 1, rank % m
    shape = (count, n)
    plane = iota(shape, 0) // (count * 2 * m // n)
    if relative:
        plane = plane ^ (lax.axis_index("dev") // QUAD)
    kind = iota(shape, 0) % 4
    own = (plane == slab) & (kind == jnp.where(upper, 1, 0))
    halo = (plane == jnp.where(upper, slab + 1, slab - 1)) & (kind == jnp.where(upper, 2, 3))
    picked = lax.dot_general(
        returned,
        jnp.where(own | halo, 1.0, 0.0),
        TN,
        precision=lax.Precision.HIGHEST,
        preferred_element_type=jnp.float32,
    )
    mass = jnp.sum(jnp.where(iota((m, n), 0) == member, picked, 0.0), axis=0, keepdims=True)
    out_ref[...] = 1.0 / (1.0 + mass * FACTOR)


def xor_order(array, axis, bits):
    count = array.shape[axis]
    for k in range(count.bit_length() - 1):
        step = 1 << k
        shape = array.shape[:axis] + (count // (2 * step), 2, step) + array.shape[axis + 1 :]
        split = array.reshape(shape)
        split = jnp.where((bits >> k) & 1 == 1, jnp.flip(split, axis + 1), split)
        array = split.reshape(array.shape)
    return array


def shards(embeddings, position, cluster_ids):
    n, width = embeddings.shape
    peers = lax.axis_size("dev")
    me = lax.axis_index("dev")
    planes = peers // QUAD
    slab, lane = me // QUAD, me % QUAD
    per_half = n // (2 * planes)
    by_permutes = planes == 4
    pieces = [per_half] * 2 + [2 * per_half] + [per_half] * 4 if by_permutes else [n]
    f32 = jnp.float32

    def swapped(rows_, bit):
        return lax.ppermute(rows_, "dev", [(i, i ^ bit) for i in range(peers)])

    def passed(rows_, by):
        pairs = [(i, i + by) for i in range(peers) if 0 <= i + by < peers]
        return lax.ppermute(rows_, "dev", pairs)

    def after_all(value, *others):
        return lax.optimization_barrier((value, *others))[0]

    def as_received(values, axis, plane):
        return xor_order(values, axis, plane) if by_permutes else values

    where_to = position.reshape(1, n)
    in_hbm = pl.BlockSpec(memory_space=pltpu.HBM)
    *arranged, rank = call(
        functools.partial(arrange_kernel, per_half, 2 * planes),
        [jax.ShapeDtypeStruct((size, width), embeddings.dtype) for size in pieces]
        + [jax.ShapeDtypeStruct((1, n), jnp.int32)],
        in_specs=[in_hbm, in_hbm],
        scratch_shapes=[
            pltpu.VMEM((1, n), jnp.int32),
            pltpu.VMEM((n, width), embeddings.dtype),
            pltpu.SemaphoreType.DMA((2,)),
        ],
    )(where_to, embeddings)
    if by_permutes:
        own_upper, own_lower, to_1, upper_2, lower_2, upper_3, lower_3 = arranged
        upper_3 = swapped(upper_3, 3 * QUAD)
        upper_2 = swapped(upper_2, 2 * QUAD)
        both_1 = swapped(to_1, QUAD)
        lower_3 = swapped(lower_3, 3 * QUAD)
        lower_2 = swapped(lower_2, 2 * QUAD)
        upper = jnp.concatenate([own_upper, both_1[:per_half], upper_2, upper_3], axis=0)
        lower = jnp.concatenate([own_lower, both_1[per_half:], lower_2, lower_3], axis=0)
    else:
        lines = [[p * QUAD + q for p in range(planes)] for q in range(QUAD)]
        block = lax.all_to_all(
            arranged[0], "dev", split_axis=0, concat_axis=0, axis_index_groups=lines, tiled=True
        ).reshape(planes, 2, per_half, width)
        upper = block[:, 1].reshape(n // 2, width)
        lower = block[:, 0].reshape(n // 2, width)

    aligned = by_permutes and 2 * per_half == LANES
    own_facts = (where_to, cluster_ids.reshape(1, n), rank, *arranged)
    facts_shape = (peers, 4 + n // LANES, LANES) if aligned else (4, n)
    facts = call(
        functools.partial(facts_kernel, per_half), jax.ShapeDtypeStruct(facts_shape, f32)
    )(*own_facts)
    if not aligned:
        seen = jnp.pad(facts[:2], ((0, 0), (per_half, per_half)))
        seen = jnp.stack(
            [seen[:, 2 * p * per_half : (2 * p + 4) * per_half] for p in range(planes)]
        ).reshape(planes, 1, 8 * per_half)
        facts = jnp.concatenate(
            [
                jnp.broadcast_to(seen, (planes, QUAD, 8 * per_half)),
                jnp.broadcast_to(facts[2], (planes, QUAD, n)),
            ],
            axis=2,
        )
        facts = facts.reshape(peers, 8 * per_half + n)
    facts = after_all(facts, both_1 if by_permutes else block)
    facts = lax.all_to_all(facts, "dev", split_axis=0, concat_axis=0, tiled=True)
    arrays = {"b0h": upper}
    arrays["b2h"] = swapped(upper, 2)
    arrays["b1h"] = swapped(upper, 1)
    lower = after_all(lower, arrays["b1h"])
    arrays["b0l"] = lower
    arrays["u"] = passed(upper, QUAD)
    arrays["b2l"] = swapped(lower, 2)
    arrays["l"] = passed(lower, -QUAD)
    arrays["b1l"] = swapped(lower, 1)

    if aligned:
        ids, near = facts[:, 4:].reshape(peers * n), facts[:, :4]
    else:
        ids, near = facts[:, 8 * per_half :].reshape(peers * n), facts[:, : 8 * per_half]
    ids = jnp.pad(ids, (MOST, MOST))
    ids = lax.dynamic_slice_in_dim(ids, slab * MOST, 3 * MOST, 0)
    near = near.reshape(planes, QUAD, 2, 4, per_half)
    near = xor_order(near, 1, lane).transpose(2, 1, 3, 0, 4)
    before = as_received(near[:, :2, 0], 2, slab - 1)
    after = as_received(near[:, :2, 3], 2, slab + 1)
    own = as_received(near[:, :3, 1:3], 3, slab)
    near = jnp.concatenate(
        [
            jnp.stack([own[:, :, 1], own[:, :, 0]], axis=2).reshape(2, 3 * n),
            jnp.stack([before, after], axis=2).reshape(2, 2 * n),
        ],
        axis=1,
    )
    total = 5 * n
    place = near[0].astype(jnp.int32) - (slab - 1) * MOST
    label = call(labels_kernel, jax.ShapeDtypeStruct((1, total), f32))(
        place.reshape(1, total), ids.reshape(3 * MOST // LANES, LANES)
    )[0]
    at = jnp.arange(total)
    absent = (at >= 3 * n) & jnp.where(at % n >= n // 2, slab == planes - 1, slab == 0)
    label = jnp.where(absent, -1.0, label)
    rows = jnp.stack([near[1], label])
    columns = jnp.stack([near[1] * SCALE, label], axis=1)

    def masses_after(jobs, last=None):
        return masses_call(jobs, arrays, rows, columns, last)

    masses = masses_after(
        [("b0h", "b0h"), ("b1h", "b0h"), ("b2h", "b0h"), ("b1h", "b2h")]
        + [("b0l", "b0l"), ("b0h", "b0l"), ("b1h", "b0l"), ("b2h", "b0l")]
        + [("b1l", "b0h"), ("b1l", "b0l"), ("b1l", "b2h")]
    )
    arrays["u1"] = swapped(after_all(arrays['u'], arrays["b2h"]), 1)
    masses = masses_after([(u, b) for u in ("u", "u1") for b in ("b0h", "b0l", "b2h")], masses)
    arrays["l1"] = swapped(after_all(arrays["l"], masses, arrays["b2l"]), 1)
    masses = masses_after(
        [("b2l", "b0h"), ("b2l", "b0l"), ("b1h", "b2l"), ("b1l", "b2l"), ("u", "b2l"), ("u1", "b2l")],
        masses,
    )
    last = [("l", "b0l"), ("l", "b2l"), ("l1", "b0l"), ("l1", "b2l")]
    masses = masses_after(last, masses)
    if by_permutes:
        across = swapped(masses[2:4], 2)
        beside = swapped(masses[6:8], 1)
        sums = call(combine_kernel, [jax.ShapeDtypeStruct((4, per_half), f32)] * planes)(
            masses, across, beside
        )
        returned = [sums[0]] + [swapped(sums[x], x * QUAD) for x in range(1, planes)]
    else:
        masses = masses.reshape(4, 2, planes, per_half)
        slabs = as_received(masses[:2], 2, slab)
        before = as_received(masses[2:, 0], 1, slab - 1)
        after = as_received(masses[2:, 1], 1, slab + 1)
        none = jnp.zeros_like(before[0])
        outgoing = jnp.stack(
            [
                jnp.stack([slabs[0, 1], none, slabs[1, 1], none]),
                jnp.stack([slabs[0, 0], none, slabs[1, 0], none]),
                jnp.stack([before[0], before[1], none, none]),
                jnp.stack([after[0], after[1], none, none]),
            ],
            axis=2,
        )
        outgoing = xor_order(outgoing, 0, lane).transpose(1, 0, 2, 3)
        returned = lax.all_to_all(
            outgoing.reshape(peers, 4 * per_half), "dev", split_axis=0, concat_axis=0, tiled=True
        )
        returned = [returned.reshape(4 * peers, per_half)]
    weight = call(
        functools.partial(weights_kernel, by_permutes), jax.ShapeDtypeStruct((1, n), f32)
    )(rank, *returned)
    return weight.reshape(n)


def solution(mesh):
    return jax.shard_map(
        shards,
        mesh=mesh,
        in_specs=(P(("grp", "dev"), None), P(("grp", "dev")), P(("grp", "dev"))),
        out_specs=P(("grp", "dev")),
        check_vma=False,
    )
```

```python
import functools
import math

import jax
import jax.numpy as jnp
from jax import lax
from jax.experimental import pallas as pl
from jax.experimental.pallas import tpu as pltpu
from jax.sharding import PartitionSpec as P

MOST = 2048
HALF = MOST // 2
SIMILARITY_CUTOFF = 0.9
SOFTMAX_HEAT = 0.02
SCALE = math.log2(math.e) / SOFTMAX_HEAT
SHIFT = SIMILARITY_CUTOFF * SCALE
QUAD = 4
CHUNK = 256
LANES = 128
VMEM_LIMIT = 16 * 1024 * 1024

NT = (((1,), (1,)), ((), ()))
TN = (((0,), (0,)), ((), ()))


def iota(shape, dim):
    return lax.broadcasted_iota(jnp.int32, shape, dim)


def call(kernel, out_shape, limit=VMEM_LIMIT, **extra):
    return pl.pallas_call(
        kernel,
        out_shape=out_shape,
        compiler_params=pltpu.CompilerParams(vmem_limit_bytes=limit),
        **extra,
    )


def arrange_kernel(per_half, halves, position_hbm, rows_hbm, *refs):
    *outs, rank_ref, place, rows, sems = refs
    copies = [
        pltpu.make_async_copy(position_hbm, place, sems.at[0]),
        pltpu.make_async_copy(rows_hbm, rows, sems.at[1]),
    ]
    for copy in copies:
        copy.start()
    n = rows.shape[0]
    earlier = (iota((n, n), 0) < iota((n, n), 1)).astype(jnp.bfloat16)
    copies[0].wait()
    half = place[...] // HALF
    kinds = iota((halves, n), 0) == half
    counts = jnp.dot(kinds.astype(jnp.bfloat16), earlier, preferred_element_type=jnp.float32)
    count = jnp.sum(jnp.where(kinds, counts, 0.0), axis=0, keepdims=True).astype(jnp.int32)
    rank_ref[...] = half * per_half + count
    rank = half * per_half + count
    if len(outs) > 1:
        plane = (half // 2) ^ (lax.axis_index("dev") // QUAD)
        rank = (2 * plane + 1 - half % 2) * per_half + count
    pick = (iota((n, n), 0) == rank).astype(jnp.bfloat16)
    copies[1].wait()
    picked = jnp.dot(pick, rows[...], preferred_element_type=jnp.float32)
    at = 0
    for out in outs:
        out[...] = picked[at : at + out.shape[0], :].astype(out.dtype)
        at += out.shape[0]


def facts_kernel(per_half, position_ref, ids_ref, rank_ref, *refs):
    *pieces, out_ref = refs
    n = position_ref.shape[1]
    pick = iota((n, n), 0) == rank_ref[...]
    where_to = position_ref[...].astype(jnp.float32)
    column = jnp.sum(jnp.where(pick, where_to, 0.0), axis=1, keepdims=True)
    eye = iota((n, n), 0) == iota((n, n), 1)
    positions = jnp.sum(jnp.where(eye, column, 0.0), axis=0, keepdims=True)
    total = jnp.zeros((1, n), jnp.float32)
    k = 0
    for piece in pieces:
        size = n if len(pieces) == 1 else per_half
        for start in range(0, piece.shape[0], size):
            wide = piece[start : start + size, :].astype(jnp.float32)
            inverse = lax.rsqrt(jnp.sum(wide * wide, axis=1, keepdims=True) + 1e-06)
            first = 0
            if len(pieces) > 1:
                plane = (k // 2) ^ (lax.axis_index("dev") // QUAD)
                first = (2 * plane + 1 - k % 2) * per_half
            here = iota((size, n), 0) + first == iota((size, n), 1)
            total += jnp.sum(jnp.where(here, inverse, 0.0), axis=0, keepdims=True)
            k += 1
    ids = ids_ref[...].astype(jnp.float32)
    if len(out_ref.shape) == 2:
        for k, values in enumerate((positions, total, ids, jnp.zeros_like(ids))):
            out_ref[k : k + 1, :] = values
        return
    beyond = jnp.zeros((1, per_half), jnp.float32)
    ids = [ids[:, at : at + LANES] for at in range(0, n, LANES)]
    wide = [jnp.concatenate([beyond, values, beyond], axis=1) for values in (positions, total)]
    for peer in range(out_ref.shape[0]):
        at = peer // QUAD * LANES
        lines = [values[:, at + k : at + k + LANES] for values in wide for k in (0, LANES)]
        for k, line in enumerate(lines + ids):
            out_ref[peer, k : k + 1, :] = line


def labels_kernel(place_ref, table_ref, out_ref):
    place = place_ref[...]
    depth = table_ref.shape[0]
    n = place.shape[1]
    table = table_ref[...]
    high = jnp.floor(table * (1.0 / 256.0))
    low = table - high * 256.0
    line = (iota((depth, n), 0) == place // LANES).astype(jnp.bfloat16)
    high = lax.dot_general(
        high.astype(jnp.bfloat16), line, TN, preferred_element_type=jnp.float32
    )
    low = lax.dot_general(
        low.astype(jnp.bfloat16), line, TN, preferred_element_type=jnp.float32
    )
    here = iota((LANES, n), 0) == place % LANES
    out_ref[...] = jnp.sum(jnp.where(here, high * 256.0 + low, 0.0), axis=0, keepdims=True)


NAMES = ("b0h", "b0l", "b1h", "b1l", "b2h", "b2l", "u", "l", "u1", "l1")
SUMS = ("b0h", "b0l", "b2h", "b2l", "u", "l", "u1", "l1")


class Terms:
    def __init__(self, arrays, rows_ref, columns_ref, out_ref, last_ref):
        self.arrays, self.rows, self.columns, self.out = arrays, rows_ref, columns_ref, out_ref
        self.last = last_ref
        self.sums = {}

    def add(self, name, values):
        self.sums[name] = self.sums[name] + values if name in self.sums else values

    def job(self, down, across):
        n = self.arrays[down].shape[0]
        products = lax.dot_general(
            self.arrays[down][...],
            self.arrays[across][...],
            NT,
            preferred_element_type=jnp.float32,
        )
        at, to = NAMES.index(down) * n, NAMES.index(across) * n
        scale = self.columns[at : at + n, 0:1]
        label = self.columns[at : at + n, 1:2]
        power = products * scale * self.rows[0:1, to : to + n] - SHIFT
        mask = label == self.rows[1:2, to : to + n]
        if down == across:
            mask &= iota((n, n), 0) != iota((n, n), 1)
        values = jnp.where(mask, jnp.exp2(power), 0.0)
        self.add(across, jnp.sum(values, axis=0, keepdims=True))
        if down in ("u", "l", "u1", "l1") or (down, across) == ("b0h", "b0l"):
            side = jnp.zeros((n, LANES), jnp.float32)
            for lane in range(0, n, LANES):
                side += values[:, lane : lane + LANES]
            self.add(down, jnp.sum(side.T, axis=0, keepdims=True))

    def totals(self):
        totals = {}
        for k, name in enumerate(SUMS):
            values = self.sums.get(name)
            last = self.last[k : k + 1, :] if self.last is not None else None
            if values is None:
                n = self.arrays["b0l"].shape[0]
                values = jnp.zeros((1, n), jnp.float32) if last is None else last
            elif last is not None:
                values += last
            totals[name] = values
        return totals

    def write(self):
        for k, values in enumerate(self.totals().values()):
            self.out[k : k + 1, :] = values


def lay_out(sums, m, out_ref):
    me = lax.axis_index("dev")
    slab, lane = me // QUAD, me % QUAD
    even = slab % 2 == 0
    rows = iota((out_ref.shape[0], 2 * m), 0)
    own = jnp.zeros(rows.shape, jnp.float32)
    halo = own

    def piece(name, x):
        return sums[name][:, x * m : (x + 1) * m]

    for x in range(QUAD):
        row = (slab ^ x) * QUAD
        for line, lower, upper in ((0, "b0l", "b0h"), (2, "b2l", "b2h")):
            both = jnp.concatenate([piece(lower, x), piece(upper, x)], axis=1)
            own = jnp.where(rows == row + (lane ^ line), both, own)
        for line, before, after in ((0, "u", "l"), (1, "u1", "l1")):
            before = jnp.where(even, piece(before, x ^ 3), piece(before, x ^ 1))
            after = jnp.where(even, piece(after, x ^ 1), piece(after, x ^ 3))
            both = jnp.concatenate([before, after], axis=1)
            halo = jnp.where(rows == row + (lane ^ line), both, halo)
    out_ref[:, 0, :] = own
    out_ref[:, 1, :] = halo


def masses_call(jobs, arrays, rows, columns, last=None, layout=None):
    names = [name for name in NAMES if any(name in job for job in jobs)]

    def kernel(*refs):
        refs = list(refs)
        held = {name: refs.pop(0) for name in names}
        rows_ref, columns_ref = refs.pop(0), refs.pop(0)
        last_ref = refs.pop(0) if last is not None else None
        t = Terms(held, rows_ref, columns_ref, refs.pop(0), last_ref)
        for job in jobs:
            t.job(*job)
        if layout is None:
            t.write()
        else:
            lay_out(t.totals(), layout[2] // 2, t.out)

    operands = [arrays[name] for name in names] + [rows, columns]
    if last is not None:
        operands.append(last)
    n, width = operands[0].shape
    return call(
        kernel,
        jax.ShapeDtypeStruct(layout or (len(SUMS), n), jnp.float32),
        cost_estimate=pl.CostEstimate(flops=0, transcendentals=0, bytes_accessed=0),
    )(*operands)


def weights_kernel(rank_ref, returned_ref, out_ref):
    peers, _, width = returned_ref.shape
    m = width // 2
    rank = rank_ref[...]
    n = rank.shape[1]
    slab, upper, member = rank // width, rank // m % 2 == 1, rank % m
    plane = iota((peers, n), 0) // QUAD

    def chosen(k, which, column):
        picked = lax.dot_general(
            returned_ref[:, k, :],
            jnp.where(plane == which, 1.0, 0.0),
            TN,
            precision=lax.Precision.HIGHEST,
            preferred_element_type=jnp.float32,
        )
        here = iota((width, n), 0) == column
        return jnp.sum(jnp.where(here, picked, 0.0), axis=0, keepdims=True)

    mass = chosen(0, slab, jnp.where(upper, m + member, member))
    mass += chosen(1, jnp.where(upper, slab + 1, slab - 1), jnp.where(upper, member, m + member))
    out_ref[...] = 1.0 / (1.0 + mass)


def xor_order(array, axis, bits):
    count = array.shape[axis]
    for k in range(count.bit_length() - 1):
        step = 1 << k
        shape = array.shape[:axis] + (count // (2 * step), 2, step) + array.shape[axis + 1 :]
        split = array.reshape(shape)
        split = jnp.where((bits >> k) & 1 == 1, jnp.flip(split, axis + 1), split)
        array = split.reshape(array.shape)
    return array


def shards(embeddings, position, cluster_ids):
    n, width = embeddings.shape
    peers = lax.axis_size("dev")
    me = lax.axis_index("dev")
    planes = peers // QUAD
    slab, lane = me // QUAD, me % QUAD
    per_half = n // (2 * planes)
    by_permutes = planes == 4
    pieces = [per_half] * 2 + [2 * per_half] + [per_half] * 4 if by_permutes else [n]
    f32 = jnp.float32

    def swapped(rows_, bit):
        return lax.ppermute(rows_, "dev", [(i, i ^ bit) for i in range(peers)])

    def passed(rows_, by):
        pairs = [(i, i + by) for i in range(peers) if 0 <= i + by < peers]
        return lax.ppermute(rows_, "dev", pairs)

    def after_all(value, *others):
        return lax.optimization_barrier((value, *others))[0]

    def as_received(values, axis, plane):
        return xor_order(values, axis, plane) if by_permutes else values

    where_to = position.reshape(1, n)
    in_hbm = pl.BlockSpec(memory_space=pltpu.HBM)
    *arranged, rank = call(
        functools.partial(arrange_kernel, per_half, 2 * planes),
        [jax.ShapeDtypeStruct((size, width), embeddings.dtype) for size in pieces]
        + [jax.ShapeDtypeStruct((1, n), jnp.int32)],
        in_specs=[in_hbm, in_hbm],
        scratch_shapes=[
            pltpu.VMEM((1, n), jnp.int32),
            pltpu.VMEM((n, width), embeddings.dtype),
            pltpu.SemaphoreType.DMA((2,)),
        ],
    )(where_to, embeddings)
    if by_permutes:
        own_upper, own_lower, to_1, upper_2, lower_2, upper_3, lower_3 = arranged
        upper_3 = swapped(upper_3, 3 * QUAD)
        upper_2 = swapped(upper_2, 2 * QUAD)
        both_1 = swapped(to_1, QUAD)
        lower_3 = swapped(lower_3, 3 * QUAD)
        lower_2 = swapped(lower_2, 2 * QUAD)
        upper = jnp.concatenate([own_upper, both_1[:per_half], upper_2, upper_3], axis=0)
        lower = jnp.concatenate([own_lower, both_1[per_half:], lower_2, lower_3], axis=0)
    else:
        lines = [[p * QUAD + q for p in range(planes)] for q in range(QUAD)]
        block = lax.all_to_all(
            arranged[0], "dev", split_axis=0, concat_axis=0, axis_index_groups=lines, tiled=True
        ).reshape(planes, 2, per_half, width)
        upper = block[:, 1].reshape(n // 2, width)
        lower = block[:, 0].reshape(n // 2, width)

    aligned = by_permutes and 2 * per_half == LANES
    own_facts = (where_to, cluster_ids.reshape(1, n), rank, *arranged)
    facts_shape = (peers, 4 + n // LANES, LANES) if aligned else (4, n)
    facts = call(
        functools.partial(facts_kernel, per_half), jax.ShapeDtypeStruct(facts_shape, f32)
    )(*own_facts)
    if not aligned:
        seen = jnp.pad(facts[:2], ((0, 0), (per_half, per_half)))
        seen = jnp.stack(
            [seen[:, 2 * p * per_half : (2 * p + 4) * per_half] for p in range(planes)]
        ).reshape(planes, 1, 8 * per_half)
        facts = jnp.concatenate(
            [
                jnp.broadcast_to(seen, (planes, QUAD, 8 * per_half)),
                jnp.broadcast_to(facts[2], (planes, QUAD, n)),
            ],
            axis=2,
        )
        facts = facts.reshape(peers, 8 * per_half + n)
    facts = after_all(facts, both_1 if by_permutes else block)
    facts = lax.all_to_all(facts, "dev", split_axis=0, concat_axis=0, tiled=True)
    arrays = {"b0h": upper}
    arrays["b2h"] = swapped(upper, 2)
    arrays["b1h"] = swapped(upper, 1)
    lower = after_all(lower, arrays["b1h"])
    arrays["b0l"] = lower
    arrays["u"] = passed(upper, QUAD)
    arrays["b2l"] = swapped(lower, 2)
    arrays["l"] = passed(lower, -QUAD)
    arrays["b1l"] = swapped(lower, 1)

    if aligned:
        ids, near = facts[:, 4:].reshape(peers * n), facts[:, :4]
    else:
        ids, near = facts[:, 8 * per_half :].reshape(peers * n), facts[:, : 8 * per_half]
    ids = jnp.pad(ids, (MOST, MOST))
    ids = lax.dynamic_slice_in_dim(ids, slab * MOST, 3 * MOST, 0)
    near = near.reshape(planes, QUAD, 2, 4, per_half)
    near = xor_order(near, 1, lane).transpose(2, 1, 3, 0, 4)
    before = as_received(near[:, :2, 0], 2, slab - 1)
    after = as_received(near[:, :2, 3], 2, slab + 1)
    own = as_received(near[:, :3, 1:3], 3, slab)
    near = jnp.concatenate(
        [
            jnp.stack([own[:, :, 1], own[:, :, 0]], axis=2).reshape(2, 3 * n),
            jnp.stack([before, after], axis=2).reshape(2, 2 * n),
        ],
        axis=1,
    )
    total = 5 * n
    place = near[0].astype(jnp.int32) - (slab - 1) * MOST
    label = call(labels_kernel, jax.ShapeDtypeStruct((1, total), f32))(
        place.reshape(1, total), ids.reshape(3 * MOST // LANES, LANES)
    )[0]
    at = jnp.arange(total)
    absent = (at >= 3 * n) & jnp.where(at % n >= n // 2, slab == planes - 1, slab == 0)
    label = jnp.where(absent, -1.0, label)
    rows = jnp.stack([near[1], label])
    columns = jnp.stack([near[1] * SCALE, label], axis=1)

    def masses_after(jobs, last=None):
        return masses_call(jobs, arrays, rows, columns, last)

    masses = masses_after(
        [("b0h", "b0h"), ("b1h", "b0h"), ("b2h", "b0h"), ("b1h", "b2h")]
        + [("b0l", "b0l"), ("b0h", "b0l"), ("b1h", "b0l"), ("b2h", "b0l")]
        + [("b1l", "b0h"), ("b1l", "b0l"), ("b1l", "b2h")]
    )
    masses = masses_after([("u", "b0h"), ("u", "b0l"), ("u", "b2h")], masses)
    arrays["u1"] = swapped(after_all(arrays["u"], arrays["l"]), 1)
    arrays["l1"] = swapped(after_all(arrays["l"], masses), 1)
    masses = masses_after(
        [("b2l", "b0h"), ("b2l", "b0l"), ("b1h", "b2l"), ("b1l", "b2l")]
        + [("u", "b2l"), ("l", "b0l"), ("l", "b2l")],
        masses,
    )
    last = [("u1", b) for b in ("b0h", "b0l", "b2h", "b2l")] + [("l1", "b0l"), ("l1", "b2l")]
    if by_permutes:
        outgoing = masses_call(last, arrays, rows, columns, masses, (peers, 2, 2 * per_half))
    else:
        masses = masses_after(last, masses)
        masses = masses.reshape(4, 2, planes, per_half)
        slabs = as_received(masses[:2], 2, slab)
        before = as_received(masses[2:, 0], 1, slab - 1)
        after = as_received(masses[2:, 1], 1, slab + 1)
        none = jnp.zeros_like(before[0])
        outgoing = jnp.stack(
            [
                jnp.stack([slabs[0, 1], none, slabs[1, 1], none]),
                jnp.stack([slabs[0, 0], none, slabs[1, 0], none]),
                jnp.stack([before[0], before[1], none, none]),
                jnp.stack([after[0], after[1], none, none]),
            ],
            axis=2,
        )
        outgoing = xor_order(outgoing, 0, lane).transpose(1, 0, 2, 3)
        outgoing = outgoing.reshape(peers, 2, 2 * per_half)
    returned = lax.all_to_all(outgoing, "dev", split_axis=0, concat_axis=0, tiled=True)
    weight = call(
        weights_kernel, jax.ShapeDtypeStruct((1, n), f32)
    )(rank, returned)
    return weight.reshape(n)


def solution(mesh):
    return jax.shard_map(
        shards,
        mesh=mesh,
        in_specs=(P(("grp", "dev"), None), P(("grp", "dev")), P(("grp", "dev"))),
        out_specs=P(("grp", "dev")),
        check_vma=False,
    )
```

```python
import functools
import math

import jax
import jax.numpy as jnp
from jax import lax
from jax.experimental import pallas as pl
from jax.experimental.pallas import tpu as pltpu
from jax.sharding import PartitionSpec as P

MOST = 2048
HALF = MOST // 2
SIMILARITY_CUTOFF = 0.9
SOFTMAX_HEAT = 0.02
SCALE = math.log2(math.e) / SOFTMAX_HEAT
FACTOR = math.exp(-SIMILARITY_CUTOFF / SOFTMAX_HEAT)
QUAD = 4
CHUNK = 256
LANES = 128
VMEM_LIMIT = 16 * 1024 * 1024

NT = (((1,), (1,)), ((), ()))
TN = (((0,), (0,)), ((), ()))


def iota(shape, dim):
    return lax.broadcasted_iota(jnp.int32, shape, dim)


def call(kernel, out_shape, limit=VMEM_LIMIT, **extra):
    return pl.pallas_call(
        kernel,
        out_shape=out_shape,
        compiler_params=pltpu.CompilerParams(vmem_limit_bytes=limit),
        **extra,
    )


def arrange_kernel(per_half, halves, position_hbm, rows_hbm, *refs):
    *outs, rank_ref, place, rows, sems = refs
    copies = [
        pltpu.make_async_copy(position_hbm, place, sems.at[0]),
        pltpu.make_async_copy(rows_hbm, rows, sems.at[1]),
    ]
    for copy in copies:
        copy.start()
    n = rows.shape[0]
    earlier = (iota((n, n), 0) < iota((n, n), 1)).astype(jnp.bfloat16)
    copies[0].wait()
    half = place[...] // HALF
    kinds = iota((halves, n), 0) == half
    counts = jnp.dot(kinds.astype(jnp.bfloat16), earlier, preferred_element_type=jnp.float32)
    count = jnp.sum(jnp.where(kinds, counts, 0.0), axis=0, keepdims=True).astype(jnp.int32)
    rank_ref[0:1, :] = half * per_half + count
    rank_ref[1:2, :] = place[...]
    rank = half * per_half + count
    if len(outs) > 1:
        plane = (half // 2) ^ (lax.axis_index("dev") // QUAD)
        rank = (2 * plane + 1 - half % 2) * per_half + count
    pick = (iota((n, n), 0) == rank).astype(jnp.bfloat16)
    copies[1].wait()
    picked = jnp.dot(pick, rows[...], preferred_element_type=jnp.float32)
    at = 0
    for out in outs:
        out[...] = picked[at : at + out.shape[0], :].astype(out.dtype)
        at += out.shape[0]


def facts_kernel(per_half, ids_hbm, rank_ref, *refs):
    *pieces, out_ref, ids_ref, sem = refs
    copy = pltpu.make_async_copy(ids_hbm, ids_ref, sem)
    copy.start()
    n = rank_ref.shape[1]
    pick = iota((n, n), 0) == rank_ref[0:1, :]
    where_to = rank_ref[1:2, :].astype(jnp.float32)
    column = jnp.sum(jnp.where(pick, where_to, 0.0), axis=1, keepdims=True)
    eye = iota((n, n), 0) == iota((n, n), 1)
    positions = jnp.sum(jnp.where(eye, column, 0.0), axis=0, keepdims=True)
    total = jnp.zeros((1, n), jnp.float32)
    k = 0
    for piece in pieces:
        size = n if len(pieces) == 1 else per_half
        for start in range(0, piece.shape[0], size):
            wide = piece[start : start + size, :].astype(jnp.float32)
            inverse = lax.rsqrt(jnp.sum(wide * wide, axis=1, keepdims=True) + 1e-06)
            first = 0
            if len(pieces) > 1:
                plane = (k // 2) ^ (lax.axis_index("dev") // QUAD)
                first = (2 * plane + 1 - k % 2) * per_half
            here = iota((size, n), 0) + first == iota((size, n), 1)
            total += jnp.sum(jnp.where(here, inverse, 0.0), axis=0, keepdims=True)
            k += 1
    copy.wait()
    ids = ids_ref[...].astype(jnp.float32)
    if len(out_ref.shape) == 2:
        for k, values in enumerate((positions, total, ids, jnp.zeros_like(ids))):
            out_ref[k : k + 1, :] = values
        return
    beyond = jnp.zeros((1, per_half), jnp.float32)
    ids = [ids[:, at : at + LANES] for at in range(0, n, LANES)]
    wide = [jnp.concatenate([beyond, values, beyond], axis=1) for values in (positions, total)]
    for peer in range(out_ref.shape[0]):
        at = peer // QUAD * LANES
        lines = [values[:, at + k : at + k + LANES] for values in wide for k in (0, LANES)]
        for k, line in enumerate(lines + ids):
            out_ref[peer, k : k + 1, :] = line


def labels_kernel(place_ref, table_ref, out_ref):
    place = place_ref[...]
    depth = table_ref.shape[0]
    n = place.shape[1]
    table = table_ref[...]
    high = jnp.floor(table * (1.0 / 256.0))
    low = table - high * 256.0
    line = (iota((depth, n), 0) == place // LANES).astype(jnp.bfloat16)
    high = lax.dot_general(
        high.astype(jnp.bfloat16), line, TN, preferred_element_type=jnp.float32
    )
    low = lax.dot_general(
        low.astype(jnp.bfloat16), line, TN, preferred_element_type=jnp.float32
    )
    here = iota((LANES, n), 0) == place % LANES
    out_ref[...] = jnp.sum(jnp.where(here, high * 256.0 + low, 0.0), axis=0, keepdims=True)


NAMES = ("b0h", "b0l", "b1h", "b1l", "b2h", "b2l", "u", "l", "u1", "l1")
SUMS = ("b0h", "b0l", "b2h", "b2l", "u", "l", "u1", "l1")


class Terms:
    def __init__(self, arrays, rows_ref, columns_ref, out_ref, last_ref):
        self.arrays, self.rows, self.columns, self.out = arrays, rows_ref, columns_ref, out_ref
        self.last = last_ref
        self.sums = {}

    def add(self, name, values):
        self.sums[name] = self.sums[name] + values if name in self.sums else values

    def job(self, down, across):
        n = self.arrays[down].shape[0]
        products = lax.dot_general(
            self.arrays[down][...],
            self.arrays[across][...],
            NT,
            preferred_element_type=jnp.float32,
        )
        at, to = NAMES.index(down) * n, NAMES.index(across) * n
        scale = self.columns[at : at + n, 0:1]
        label = self.columns[at : at + n, 1:2]
        power = products * scale * self.rows[0:1, to : to + n]
        mask = label == self.rows[1:2, to : to + n]
        if down == across:
            mask &= iota((n, n), 0) != iota((n, n), 1)
        values = jnp.where(mask, jnp.exp2(power), 0.0)
        self.add(across, jnp.sum(values, axis=0, keepdims=True))
        if down in ("u", "l", "u1", "l1") or (down, across) == ("b0h", "b0l"):
            side = jnp.zeros((n, LANES), jnp.float32)
            for lane in range(0, n, LANES):
                side += values[:, lane : lane + LANES]
            self.add(down, jnp.sum(side.T, axis=0, keepdims=True))

    def totals(self):
        totals = {}
        for k, name in enumerate(SUMS):
            values = self.sums.get(name)
            last = self.last[k : k + 1, :] if self.last is not None else None
            if values is None:
                n = self.arrays["b0l"].shape[0]
                values = jnp.zeros((1, n), jnp.float32) if last is None else last
            elif last is not None:
                values += last
            totals[name] = values
        return totals

    def write(self):
        for k, values in enumerate(self.totals().values()):
            self.out[k : k + 1, :] = values


def lay_out(sums, m, out_ref):
    me = lax.axis_index("dev")
    slab, lane = me // QUAD, me % QUAD
    even = slab % 2 == 0
    rows = iota((out_ref.shape[0], 2 * m), 0)
    own = jnp.zeros(rows.shape, jnp.float32)
    halo = own

    def piece(name, x):
        return sums[name][:, x * m : (x + 1) * m]

    for x in range(QUAD):
        row = (slab ^ x) * QUAD
        for line, lower, upper in ((0, "b0l", "b0h"), (2, "b2l", "b2h")):
            both = jnp.concatenate([piece(lower, x), piece(upper, x)], axis=1)
            own = jnp.where(rows == row + (lane ^ line), both, own)
        for line, before, after in ((0, "u", "l"), (1, "u1", "l1")):
            before = jnp.where(even, piece(before, x ^ 3), piece(before, x ^ 1))
            after = jnp.where(even, piece(after, x ^ 1), piece(after, x ^ 3))
            both = jnp.concatenate([before, after], axis=1)
            halo = jnp.where(rows == row + (lane ^ line), both, halo)
    out_ref[:, 0, :] = own
    out_ref[:, 1, :] = halo


def masses_call(jobs, arrays, rows, columns, last=None, layout=None):
    names = [name for name in NAMES if any(name in job for job in jobs)]

    def kernel(*refs):
        refs = list(refs)
        held = {name: refs.pop(0) for name in names}
        rows_ref, columns_ref = refs.pop(0), refs.pop(0)
        last_ref = refs.pop(0) if last is not None else None
        t = Terms(held, rows_ref, columns_ref, refs.pop(0), last_ref)
        for job in jobs:
            t.job(*job)
        if layout is None:
            t.write()
        else:
            lay_out(t.totals(), layout[2] // 2, t.out)

    operands = [arrays[name] for name in names] + [rows, columns]
    if last is not None:
        operands.append(last)
    n, width = operands[0].shape
    return call(
        kernel,
        jax.ShapeDtypeStruct(layout or (len(SUMS), n), jnp.float32),
        cost_estimate=pl.CostEstimate(flops=0, transcendentals=0, bytes_accessed=0),
    )(*operands)


def weights_kernel(rank_ref, returned_ref, out_ref):
    peers, _, width = returned_ref.shape
    m = width // 2
    rank = rank_ref[0:1, :]
    n = rank.shape[1]
    slab, upper, member = rank // width, rank // m % 2 == 1, rank % m
    plane = iota((peers, n), 0) // QUAD

    def chosen(k, which, column):
        picked = lax.dot_general(
            returned_ref[:, k, :],
            jnp.where(plane == which, 1.0, 0.0),
            TN,
            precision=lax.Precision.HIGHEST,
            preferred_element_type=jnp.float32,
        )
        here = iota((width, n), 0) == column
        return jnp.sum(jnp.where(here, picked, 0.0), axis=0, keepdims=True)

    mass = chosen(0, slab, jnp.where(upper, m + member, member))
    mass += chosen(1, jnp.where(upper, slab + 1, slab - 1), jnp.where(upper, member, m + member))
    out_ref[...] = 1.0 / (1.0 + mass * FACTOR)


def xor_order(array, axis, bits):
    count = array.shape[axis]
    for k in range(count.bit_length() - 1):
        step = 1 << k
        shape = array.shape[:axis] + (count // (2 * step), 2, step) + array.shape[axis + 1 :]
        split = array.reshape(shape)
        split = jnp.where((bits >> k) & 1 == 1, jnp.flip(split, axis + 1), split)
        array = split.reshape(array.shape)
    return array


def shards(embeddings, position, cluster_ids):
    n, width = embeddings.shape
    peers = lax.axis_size("dev")
    me = lax.axis_index("dev")
    planes = peers // QUAD
    slab, lane = me // QUAD, me % QUAD
    per_half = n // (2 * planes)
    by_permutes = planes == 4
    pieces = [per_half] * 2 + [2 * per_half] + [per_half] * 4 if by_permutes else [n]
    f32 = jnp.float32

    def swapped(rows_, bit):
        return lax.ppermute(rows_, "dev", [(i, i ^ bit) for i in range(peers)])

    def passed(rows_, by):
        pairs = [(i, i + by) for i in range(peers) if 0 <= i + by < peers]
        return lax.ppermute(rows_, "dev", pairs)

    def after_all(value, *others):
        return lax.optimization_barrier((value, *others))[0]

    def as_received(values, axis, plane):
        return xor_order(values, axis, plane) if by_permutes else values

    where_to = position.reshape(1, n)
    in_hbm = pl.BlockSpec(memory_space=pltpu.HBM)
    *arranged, rank = call(
        functools.partial(arrange_kernel, per_half, 2 * planes),
        [jax.ShapeDtypeStruct((size, width), embeddings.dtype) for size in pieces]
        + [jax.ShapeDtypeStruct((2, n), jnp.int32)],
        in_specs=[in_hbm, in_hbm],
        scratch_shapes=[
            pltpu.VMEM((1, n), jnp.int32),
            pltpu.VMEM((n, width), embeddings.dtype),
            pltpu.SemaphoreType.DMA((2,)),
        ],
    )(where_to, embeddings)
    if by_permutes:
        own_upper, own_lower, to_1, upper_2, lower_2, upper_3, lower_3 = arranged
        upper_3 = swapped(upper_3, 3 * QUAD)
        upper_2 = swapped(upper_2, 2 * QUAD)
        both_1 = swapped(to_1, QUAD)
        lower_3 = swapped(lower_3, 3 * QUAD)
        lower_2 = swapped(lower_2, 2 * QUAD)
        upper = jnp.concatenate([own_upper, both_1[:per_half], upper_2, upper_3], axis=0)
        lower = jnp.concatenate([own_lower, both_1[per_half:], lower_2, lower_3], axis=0)
    else:
        lines = [[p * QUAD + q for p in range(planes)] for q in range(QUAD)]
        block = lax.all_to_all(
            arranged[0], "dev", split_axis=0, concat_axis=0, axis_index_groups=lines, tiled=True
        ).reshape(planes, 2, per_half, width)
        upper = block[:, 1].reshape(n // 2, width)
        lower = block[:, 0].reshape(n // 2, width)

    aligned = by_permutes and 2 * per_half == LANES
    own_facts = (cluster_ids.reshape(1, n), rank, *arranged)
    facts_shape = (peers, 4 + n // LANES, LANES) if aligned else (4, n)
    facts = call(
        functools.partial(facts_kernel, per_half),
        jax.ShapeDtypeStruct(facts_shape, f32),
        in_specs=[in_hbm] + [pl.BlockSpec(memory_space=pltpu.VMEM)] * (1 + len(arranged)),
        scratch_shapes=[pltpu.VMEM((1, n), jnp.int32), pltpu.SemaphoreType.DMA],
    )(*own_facts)
    if not aligned:
        seen = jnp.pad(facts[:2], ((0, 0), (per_half, per_half)))
        seen = jnp.stack(
            [seen[:, 2 * p * per_half : (2 * p + 4) * per_half] for p in range(planes)]
        ).reshape(planes, 1, 8 * per_half)
        facts = jnp.concatenate(
            [
                jnp.broadcast_to(seen, (planes, QUAD, 8 * per_half)),
                jnp.broadcast_to(facts[2], (planes, QUAD, n)),
            ],
            axis=2,
        )
        facts = facts.reshape(peers, 8 * per_half + n)
    facts = after_all(facts, both_1 if by_permutes else block)
    facts = lax.all_to_all(facts, "dev", split_axis=0, concat_axis=0, tiled=True)
    arrays = {"b0h": upper}
    arrays["b2h"] = swapped(upper, 2)
    arrays["b1h"] = swapped(upper, 1)
    lower = after_all(lower, arrays["b1h"])
    arrays["b0l"] = lower
    arrays["u"] = passed(upper, QUAD)
    arrays["b2l"] = swapped(lower, 2)
    arrays["l"] = passed(lower, -QUAD)
    arrays["b1l"] = swapped(lower, 1)

    if aligned:
        ids, near = facts[:, 4:].reshape(peers * n), facts[:, :4]
    else:
        ids, near = facts[:, 8 * per_half :].reshape(peers * n), facts[:, : 8 * per_half]
    ids = jnp.pad(ids, (MOST, MOST))
    ids = lax.dynamic_slice_in_dim(ids, slab * MOST, 3 * MOST, 0)
    near = near.reshape(planes, QUAD, 2, 4, per_half)
    near = xor_order(near, 1, lane).transpose(2, 1, 3, 0, 4)
    before = as_received(near[:, :2, 0], 2, slab - 1)
    after = as_received(near[:, :2, 3], 2, slab + 1)
    own = as_received(near[:, :3, 1:3], 3, slab)
    near = jnp.concatenate(
        [
            jnp.stack([own[:, :, 1], own[:, :, 0]], axis=2).reshape(2, 3 * n),
            jnp.stack([before, after], axis=2).reshape(2, 2 * n),
        ],
        axis=1,
    )
    total = 5 * n
    place = near[0].astype(jnp.int32) - (slab - 1) * MOST
    label = call(labels_kernel, jax.ShapeDtypeStruct((1, total), f32))(
        place.reshape(1, total), ids.reshape(3 * MOST // LANES, LANES)
    )[0]
    at = jnp.arange(total)
    absent = (at >= 3 * n) & jnp.where(at % n >= n // 2, slab == planes - 1, slab == 0)
    label = jnp.where(absent, -1.0, label)
    rows = jnp.stack([near[1], label])
    columns = jnp.stack([near[1] * SCALE, label], axis=1)

    def masses_after(jobs, last=None):
        return masses_call(jobs, arrays, rows, columns, last)

    masses = masses_after(
        [("b0h", "b0h"), ("b1h", "b0h"), ("b2h", "b0h"), ("b1h", "b2h")]
        + [("b0l", "b0l"), ("b0h", "b0l"), ("b1h", "b0l"), ("b2h", "b0l")]
        + [("b1l", "b0h"), ("b1l", "b0l"), ("b1l", "b2h")]
    )
    masses = masses_after([("u", "b0h"), ("u", "b0l"), ("u", "b2h")], masses)
    arrays["u1"] = swapped(after_all(arrays["u"], arrays["l"]), 1)
    arrays["l1"] = swapped(after_all(arrays["l"], masses), 1)
    masses = masses_after(
        [("b2l", "b0h"), ("b2l", "b0l"), ("b1h", "b2l"), ("b1l", "b2l")]
        + [("u", "b2l"), ("l", "b0l"), ("l", "b2l")],
        masses,
    )
    last = [("u1", b) for b in ("b0h", "b0l", "b2h", "b2l")] + [("l1", "b0l"), ("l1", "b2l")]
    if by_permutes:
        outgoing = masses_call(last, arrays, rows, columns, masses, (peers, 2, 2 * per_half))
    else:
        masses = masses_after(last, masses)
        masses = masses.reshape(4, 2, planes, per_half)
        slabs = as_received(masses[:2], 2, slab)
        before = as_received(masses[2:, 0], 1, slab - 1)
        after = as_received(masses[2:, 1], 1, slab + 1)
        none = jnp.zeros_like(before[0])
        outgoing = jnp.stack(
            [
                jnp.stack([slabs[0, 1], none, slabs[1, 1], none]),
                jnp.stack([slabs[0, 0], none, slabs[1, 0], none]),
                jnp.stack([before[0], before[1], none, none]),
                jnp.stack([after[0], after[1], none, none]),
            ],
            axis=2,
        )
        outgoing = xor_order(outgoing, 0, lane).transpose(1, 0, 2, 3)
        outgoing = outgoing.reshape(peers, 2, 2 * per_half)
    returned = lax.all_to_all(outgoing, "dev", split_axis=0, concat_axis=0, tiled=True)
    weight = call(
        weights_kernel, jax.ShapeDtypeStruct((1, n), f32)
    )(rank, returned)
    return weight.reshape(n)


def solution(mesh):
    return jax.shard_map(
        shards,
        mesh=mesh,
        in_specs=(P(("grp", "dev"), None), P(("grp", "dev")), P(("grp", "dev"))),
        out_specs=P(("grp", "dev")),
        check_vma=False,
    )
```

```python
import functools
import math

import jax
import jax.numpy as jnp
from jax import lax
from jax.experimental import pallas as pl
from jax.experimental.pallas import tpu as pltpu
from jax.sharding import PartitionSpec as P

MOST = 2048
HALF = MOST // 2
SIMILARITY_CUTOFF = 0.9
SOFTMAX_HEAT = 0.02
SCALE = math.log2(math.e) / SOFTMAX_HEAT
SHIFT = SIMILARITY_CUTOFF * SCALE
QUAD = 4
CHUNK = 256
LANES = 128
VMEM_LIMIT = 16 * 1024 * 1024

NT = (((1,), (1,)), ((), ()))
TN = (((0,), (0,)), ((), ()))


def iota(shape, dim):
    return lax.broadcasted_iota(jnp.int32, shape, dim)


def call(kernel, out_shape, limit=VMEM_LIMIT, **extra):
    return pl.pallas_call(
        kernel,
        out_shape=out_shape,
        compiler_params=pltpu.CompilerParams(vmem_limit_bytes=limit),
        **extra,
    )


def arrange_kernel(per_half, halves, position_hbm, rows_hbm, *refs):
    *outs, rank_ref, place, rows, sems = refs
    copies = [
        pltpu.make_async_copy(position_hbm, place, sems.at[0]),
        pltpu.make_async_copy(rows_hbm, rows, sems.at[1]),
    ]
    for copy in copies:
        copy.start()
    n = rows.shape[0]
    earlier = (iota((n, n), 0) < iota((n, n), 1)).astype(jnp.bfloat16)
    copies[0].wait()
    half = place[...] // HALF
    kinds = iota((halves, n), 0) == half
    counts = jnp.dot(kinds.astype(jnp.bfloat16), earlier, preferred_element_type=jnp.float32)
    count = jnp.sum(jnp.where(kinds, counts, 0.0), axis=0, keepdims=True).astype(jnp.int32)
    rank_ref[...] = half * per_half + count
    rank = half * per_half + count
    if len(outs) > 1:
        plane = (half // 2) ^ (lax.axis_index("dev") // QUAD)
        rank = (2 * plane + 1 - half % 2) * per_half + count
    pick = (iota((n, n), 0) == rank).astype(jnp.bfloat16)
    copies[1].wait()
    picked = jnp.dot(pick, rows[...], preferred_element_type=jnp.float32)
    at = 0
    for out in outs:
        out[...] = picked[at : at + out.shape[0], :].astype(out.dtype)
        at += out.shape[0]


def facts_kernel(per_half, position_ref, ids_ref, rank_ref, *refs):
    *pieces, out_ref = refs
    n = position_ref.shape[1]
    pick = iota((n, n), 0) == rank_ref[...]
    where_to = position_ref[...].astype(jnp.float32)
    column = jnp.sum(jnp.where(pick, where_to, 0.0), axis=1, keepdims=True)
    eye = iota((n, n), 0) == iota((n, n), 1)
    positions = jnp.sum(jnp.where(eye, column, 0.0), axis=0, keepdims=True)
    total = jnp.zeros((1, n), jnp.float32)
    k = 0
    for piece in pieces:
        size = n if len(pieces) == 1 else per_half
        for start in range(0, piece.shape[0], size):
            wide = piece[start : start + size, :].astype(jnp.float32)
            inverse = lax.rsqrt(jnp.sum(wide * wide, axis=1, keepdims=True) + 1e-06)
            first = 0
            if len(pieces) > 1:
                plane = (k // 2) ^ (lax.axis_index("dev") // QUAD)
                first = (2 * plane + 1 - k % 2) * per_half
            here = iota((size, n), 0) + first == iota((size, n), 1)
            total += jnp.sum(jnp.where(here, inverse, 0.0), axis=0, keepdims=True)
            k += 1
    ids = ids_ref[...].astype(jnp.float32)
    if len(out_ref.shape) == 2:
        for k, values in enumerate((positions, total, ids, jnp.zeros_like(ids))):
            out_ref[k : k + 1, :] = values
        return
    beyond = jnp.zeros((1, per_half), jnp.float32)
    ids = [ids[:, at : at + LANES] for at in range(0, n, LANES)]
    wide = [jnp.concatenate([beyond, values, beyond], axis=1) for values in (positions, total)]
    for peer in range(out_ref.shape[0]):
        at = peer // QUAD * LANES
        lines = [values[:, at + k : at + k + LANES] for values in wide for k in (0, LANES)]
        for k, line in enumerate(lines + ids):
            out_ref[peer, k : k + 1, :] = line


def labels_kernel(place_ref, table_ref, out_ref):
    place = place_ref[...]
    depth = table_ref.shape[0]
    n = place.shape[1]
    table = table_ref[...]
    high = jnp.floor(table * (1.0 / 256.0))
    low = table - high * 256.0
    line = (iota((depth, n), 0) == place // LANES).astype(jnp.bfloat16)
    high = lax.dot_general(
        high.astype(jnp.bfloat16), line, TN, preferred_element_type=jnp.float32
    )
    low = lax.dot_general(
        low.astype(jnp.bfloat16), line, TN, preferred_element_type=jnp.float32
    )
    here = iota((LANES, n), 0) == place % LANES
    out_ref[...] = jnp.sum(jnp.where(here, high * 256.0 + low, 0.0), axis=0, keepdims=True)


NAMES = ("b0h", "b0l", "b1h", "b1l", "b2h", "b2l", "u", "l", "u1", "l1")
SUMS = ("b0h", "b0l", "b2h", "b2l", "u", "l", "u1", "l1")


class Terms:
    def __init__(self, arrays, rows_ref, columns_ref, out_ref, last_ref):
        self.arrays, self.rows, self.columns, self.out = arrays, rows_ref, columns_ref, out_ref
        self.last = last_ref
        self.sums = {}

    def add(self, name, values):
        self.sums[name] = self.sums[name] + values if name in self.sums else values

    def job(self, down, across):
        n = self.arrays[down].shape[0]
        products = lax.dot_general(
            self.arrays[down][...],
            self.arrays[across][...],
            NT,
            preferred_element_type=jnp.float32,
        )
        at, to = NAMES.index(down) * n, NAMES.index(across) * n
        scale = self.columns[at : at + n, 0:1]
        label = self.columns[at : at + n, 1:2]
        power = products * scale * self.rows[0:1, to : to + n] - SHIFT
        mask = label == self.rows[1:2, to : to + n]
        if down == across:
            mask &= iota((n, n), 0) != iota((n, n), 1)
        values = jnp.where(mask, jnp.exp2(power), 0.0)
        self.add(across, jnp.sum(values, axis=0, keepdims=True))
        if down in ("u", "l", "u1", "l1") or (down, across) == ("b0h", "b0l"):
            side = jnp.zeros((n, LANES), jnp.float32)
            for lane in range(0, n, LANES):
                side += values[:, lane : lane + LANES]
            self.add(down, jnp.sum(side.T, axis=0, keepdims=True))

    def totals(self):
        totals = {}
        for k, name in enumerate(SUMS):
            values = self.sums.get(name)
            last = self.last[k : k + 1, :] if self.last is not None else None
            if values is None:
                n = self.arrays["b0l"].shape[0]
                values = jnp.zeros((1, n), jnp.float32) if last is None else last
            elif last is not None:
                values += last
            totals[name] = values
        return totals

    def write(self):
        for k, values in enumerate(self.totals().values()):
            self.out[k : k + 1, :] = values


def lay_out(sums, m, out_ref):
    me = lax.axis_index("dev")
    slab, lane = me // QUAD, me % QUAD
    even = slab % 2 == 0
    rows = iota((out_ref.shape[0], 2 * m), 0)
    own = jnp.zeros(rows.shape, jnp.float32)
    halo = own

    def piece(name, x):
        return sums[name][:, x * m : (x + 1) * m]

    for x in range(QUAD):
        row = (slab ^ x) * QUAD
        for line, lower, upper in ((0, "b0l", "b0h"), (2, "b2l", "b2h")):
            both = jnp.concatenate([piece(lower, x), piece(upper, x)], axis=1)
            own = jnp.where(rows == row + (lane ^ line), both, own)
        for line, before, after in ((0, "u", "l"), (1, "u1", "l1")):
            before = jnp.where(even, piece(before, x ^ 3), piece(before, x ^ 1))
            after = jnp.where(even, piece(after, x ^ 1), piece(after, x ^ 3))
            both = jnp.concatenate([before, after], axis=1)
            halo = jnp.where(rows == row + (lane ^ line), both, halo)
    out_ref[:, 0, :] = own
    out_ref[:, 1, :] = halo


def masses_call(jobs, arrays, rows, columns, last=None, layout=None):
    names = [name for name in NAMES if any(name in job for job in jobs)]

    def kernel(*refs):
        refs = list(refs)
        held = {name: refs.pop(0) for name in names}
        rows_ref, columns_ref = refs.pop(0), refs.pop(0)
        last_ref = refs.pop(0) if last is not None else None
        t = Terms(held, rows_ref, columns_ref, refs.pop(0), last_ref)
        for job in jobs:
            t.job(*job)
        if layout is None:
            t.write()
        else:
            lay_out(t.totals(), layout[2] // 2, t.out)

    operands = [arrays[name] for name in names] + [rows, columns]
    if last is not None:
        operands.append(last)
    n, width = operands[0].shape
    return call(
        kernel,
        jax.ShapeDtypeStruct(layout or (len(SUMS), n), jnp.float32),
        cost_estimate=pl.CostEstimate(
            flops=2 * len(jobs) * n * n * width,
            transcendentals=len(jobs) * n * n,
            bytes_accessed=2 * len(names) * n * width,
        ),
    )(*operands)


def weights_kernel(rank_ref, returned_ref, out_ref):
    peers, _, width = returned_ref.shape
    m = width // 2
    rank = rank_ref[...]
    n = rank.shape[1]
    slab, upper, member = rank // width, rank // m % 2 == 1, rank % m
    plane = iota((peers, n), 0) // QUAD

    def chosen(k, which, column):
        picked = lax.dot_general(
            returned_ref[:, k, :],
            jnp.where(plane == which, 1.0, 0.0),
            TN,
            precision=lax.Precision.HIGHEST,
            preferred_element_type=jnp.float32,
        )
        here = iota((width, n), 0) == column
        return jnp.sum(jnp.where(here, picked, 0.0), axis=0, keepdims=True)

    mass = chosen(0, slab, jnp.where(upper, m + member, member))
    mass += chosen(1, jnp.where(upper, slab + 1, slab - 1), jnp.where(upper, member, m + member))
    out_ref[...] = 1.0 / (1.0 + mass)


def xor_order(array, axis, bits):
    count = array.shape[axis]
    for k in range(count.bit_length() - 1):
        step = 1 << k
        shape = array.shape[:axis] + (count // (2 * step), 2, step) + array.shape[axis + 1 :]
        split = array.reshape(shape)
        split = jnp.where((bits >> k) & 1 == 1, jnp.flip(split, axis + 1), split)
        array = split.reshape(array.shape)
    return array


def shards(embeddings, position, cluster_ids):
    n, width = embeddings.shape
    peers = lax.axis_size("dev")
    me = lax.axis_index("dev")
    planes = peers // QUAD
    slab, lane = me // QUAD, me % QUAD
    per_half = n // (2 * planes)
    by_permutes = planes == 4
    pieces = [per_half] * 2 + [2 * per_half] + [per_half] * 4 if by_permutes else [n]
    f32 = jnp.float32

    def swapped(rows_, bit):
        return lax.ppermute(rows_, "dev", [(i, i ^ bit) for i in range(peers)])

    def passed(rows_, by):
        pairs = [(i, i + by) for i in range(peers) if 0 <= i + by < peers]
        return lax.ppermute(rows_, "dev", pairs)

    def after_all(value, *others):
        return lax.optimization_barrier((value, *others))[0]

    def as_received(values, axis, plane):
        return xor_order(values, axis, plane) if by_permutes else values

    where_to = position.reshape(1, n)
    in_hbm = pl.BlockSpec(memory_space=pltpu.HBM)
    *arranged, rank = call(
        functools.partial(arrange_kernel, per_half, 2 * planes),
        [jax.ShapeDtypeStruct((size, width), embeddings.dtype) for size in pieces]
        + [jax.ShapeDtypeStruct((1, n), jnp.int32)],
        in_specs=[in_hbm, in_hbm],
        scratch_shapes=[
            pltpu.VMEM((1, n), jnp.int32),
            pltpu.VMEM((n, width), embeddings.dtype),
            pltpu.SemaphoreType.DMA((2,)),
        ],
    )(where_to, embeddings)
    if by_permutes:
        own_upper, own_lower, to_1, upper_2, lower_2, upper_3, lower_3 = arranged
        upper_3 = swapped(upper_3, 3 * QUAD)
        upper_2 = swapped(upper_2, 2 * QUAD)
        both_1 = swapped(to_1, QUAD)
        lower_3 = swapped(lower_3, 3 * QUAD)
        lower_2 = swapped(lower_2, 2 * QUAD)
        upper = jnp.concatenate([own_upper, both_1[:per_half], upper_2, upper_3], axis=0)
        lower = jnp.concatenate([own_lower, both_1[per_half:], lower_2, lower_3], axis=0)
    else:
        lines = [[p * QUAD + q for p in range(planes)] for q in range(QUAD)]
        block = lax.all_to_all(
            arranged[0], "dev", split_axis=0, concat_axis=0, axis_index_groups=lines, tiled=True
        ).reshape(planes, 2, per_half, width)
        upper = block[:, 1].reshape(n // 2, width)
        lower = block[:, 0].reshape(n // 2, width)

    aligned = by_permutes and 2 * per_half == LANES
    own_facts = (where_to, cluster_ids.reshape(1, n), rank, *arranged)
    facts_shape = (peers, 4 + n // LANES, LANES) if aligned else (4, n)
    facts = call(
        functools.partial(facts_kernel, per_half), jax.ShapeDtypeStruct(facts_shape, f32)
    )(*own_facts)
    if not aligned:
        seen = jnp.pad(facts[:2], ((0, 0), (per_half, per_half)))
        seen = jnp.stack(
            [seen[:, 2 * p * per_half : (2 * p + 4) * per_half] for p in range(planes)]
        ).reshape(planes, 1, 8 * per_half)
        facts = jnp.concatenate(
            [
                jnp.broadcast_to(seen, (planes, QUAD, 8 * per_half)),
                jnp.broadcast_to(facts[2], (planes, QUAD, n)),
            ],
            axis=2,
        )
        facts = facts.reshape(peers, 8 * per_half + n)
    facts = after_all(facts, both_1 if by_permutes else block)
    facts = lax.all_to_all(facts, "dev", split_axis=0, concat_axis=0, tiled=True)
    arrays = {"b0h": upper}
    arrays["b2h"] = swapped(upper, 2)
    arrays["b1h"] = swapped(upper, 1)
    lower = after_all(lower, arrays["b1h"])
    arrays["b0l"] = lower
    arrays["u"] = passed(upper, QUAD)
    arrays["b2l"] = swapped(lower, 2)
    arrays["l"] = passed(lower, -QUAD)
    arrays["b1l"] = swapped(lower, 1)

    if aligned:
        ids, near = facts[:, 4:].reshape(peers * n), facts[:, :4]
    else:
        ids, near = facts[:, 8 * per_half :].reshape(peers * n), facts[:, : 8 * per_half]
    ids = jnp.pad(ids, (MOST, MOST))
    ids = lax.dynamic_slice_in_dim(ids, slab * MOST, 3 * MOST, 0)
    near = near.reshape(planes, QUAD, 2, 4, per_half)
    near = xor_order(near, 1, lane).transpose(2, 1, 3, 0, 4)
    before = as_received(near[:, :2, 0], 2, slab - 1)
    after = as_received(near[:, :2, 3], 2, slab + 1)
    own = as_received(near[:, :3, 1:3], 3, slab)
    near = jnp.concatenate(
        [
            jnp.stack([own[:, :, 1], own[:, :, 0]], axis=2).reshape(2, 3 * n),
            jnp.stack([before, after], axis=2).reshape(2, 2 * n),
        ],
        axis=1,
    )
    total = 5 * n
    place = near[0].astype(jnp.int32) - (slab - 1) * MOST
    label = call(labels_kernel, jax.ShapeDtypeStruct((1, total), f32))(
        place.reshape(1, total), ids.reshape(3 * MOST // LANES, LANES)
    )[0]
    at = jnp.arange(total)
    absent = (at >= 3 * n) & jnp.where(at % n >= n // 2, slab == planes - 1, slab == 0)
    label = jnp.where(absent, -1.0, label)
    rows = jnp.stack([near[1], label])
    columns = jnp.stack([near[1] * SCALE, label], axis=1)

    def masses_after(jobs, last=None):
        return masses_call(jobs, arrays, rows, columns, last)

    masses = masses_after(
        [("b0h", "b0h"), ("b1h", "b0h"), ("b2h", "b0h"), ("b1h", "b2h")]
        + [("b0l", "b0l"), ("b0h", "b0l"), ("b1h", "b0l"), ("b2h", "b0l")]
        + [("b1l", "b0h"), ("b1l", "b0l"), ("b1l", "b2h")]
    )
    arrays["u1"] = swapped(after_all(arrays['u'], arrays["b2h"]), 1)
    masses = masses_after([(u, b) for u in ("u", "u1") for b in ("b0h", "b0l", "b2h")], masses)
    arrays["l1"] = swapped(after_all(arrays["l"], masses, arrays["b2l"]), 1)
    masses = masses_after(
        [("b2l", "b0h"), ("b2l", "b0l"), ("b1h", "b2l"), ("b1l", "b2l"), ("u", "b2l"), ("u1", "b2l")],
        masses,
    )
    last = [("l", "b0l"), ("l", "b2l"), ("l1", "b0l"), ("l1", "b2l")]
    if by_permutes:
        outgoing = masses_call(last, arrays, rows, columns, masses, (peers, 2, 2 * per_half))
    else:
        masses = masses_after(last, masses)
        masses = masses.reshape(4, 2, planes, per_half)
        slabs = as_received(masses[:2], 2, slab)
        before = as_received(masses[2:, 0], 1, slab - 1)
        after = as_received(masses[2:, 1], 1, slab + 1)
        none = jnp.zeros_like(before[0])
        outgoing = jnp.stack(
            [
                jnp.stack([slabs[0, 1], none, slabs[1, 1], none]),
                jnp.stack([slabs[0, 0], none, slabs[1, 0], none]),
                jnp.stack([before[0], before[1], none, none]),
                jnp.stack([after[0], after[1], none, none]),
            ],
            axis=2,
        )
        outgoing = xor_order(outgoing, 0, lane).transpose(1, 0, 2, 3)
        outgoing = outgoing.reshape(peers, 2, 2 * per_half)
    returned = lax.all_to_all(outgoing, "dev", split_axis=0, concat_axis=0, tiled=True)
    weight = call(
        weights_kernel, jax.ShapeDtypeStruct((1, n), f32)
    )(rank, returned)
    return weight.reshape(n)


def solution(mesh):
    return jax.shard_map(
        shards,
        mesh=mesh,
        in_specs=(P(("grp", "dev"), None), P(("grp", "dev")), P(("grp", "dev"))),
        out_specs=P(("grp", "dev")),
        check_vma=False,
    )
```
